128 devices in a mesh: blk: 32 (over y_lo, z, x), uly: 4 (over y_hi, core).
Axes of the slice: x: 4, y: 4 (y_hi: 2, y_lo: 2; y = y_hi * 2 + y_lo), z: 4, core: 2. Of those that a mesh axis runs over, the one named last changes fastest.
Arguments:
- tokens: bfloat16 [2, 8192, 1536], P(None, ('blk', 'uly')), may hold values from -6 to 6
- cotangent: bfloat16 [2, 8192, 1536], P(None, ('blk', 'uly')), may hold values from -6 to 6
- lengths: int32 [2], replicated, may hold values from 4097 to 8192, as said below
- set_index: int32 [2], replicated, may hold values from 0 to 7
- norm_in: float32 [1536], replicated, may hold values from 0.25 to 1.75
- norm_ff: float32 [1536], replicated, may hold values from 0.25 to 1.75
- qkv_bias: float32 [2048], replicated, may hold values from -3 to 3
- w_qkv: bfloat16 [1536, 2048], P(('blk', 'uly')), may hold values from -0.15625 to 0.15625
- w_out: bfloat16 [1536, 1536], P(('blk', 'uly')), may hold values from -2.5 to 2.5
- w_gate_up: bfloat16 [2, 1536, 8960], P(None, 'blk', 'uly'), may hold values from -0.15625 to 0.15625
- w_down: bfloat16 [8960, 1536], P('uly', 'blk'), may hold values from -0.0625 to 0.0625
- a_wide: bfloat16 [6, 8, 16, 1536], replicated, may hold values from -0.15625 to 0.15625
- a_down: bfloat16 [8, 16, 8960], replicated, may hold values from -0.0625 to 0.0625
- b_wide: bfloat16 [3, 8, 16, 1536], replicated, may hold values from -1.5 to 1.5
- b_kv: bfloat16 [2, 8, 16, 256], replicated, may hold values from -1.5 to 1.5
- b_ff: bfloat16 [2, 8, 16, 8960], replicated, may hold values from -1.5 to 1.5
Outputs:
- result_tokens: bfloat16 [2, 8192, 1536], P(None, ('blk', 'uly'))
- input_grad: float32 [2, 8192, 1536], P(None, ('blk', 'uly'))
- grad_a_wide: float32 [6, 8, 16, 1536], replicated
- grad_a_down: float32 [8, 16, 8960], replicated
- grad_b_wide: float32 [3, 8, 16, 1536], replicated
- grad_b_kv: float32 [2, 8, 16, 256], replicated
- grad_b_ff: float32 [2, 8, 16, 8960], replicated
The draws below stay inside these ranges and needn't reach their ends.
Inputs may be any that keep to these rules, and one draw needn't show every extreme that they name: Each sequence's valid slots are its first lengths[s]; one sequence, drawn from the seed, fills all 8192 slots.
All inputs are finite; a program needn't handle non-finite values.
Results may differ from the reference program's by a relative error of at most 0.024.
Values may be sent and summed in bfloat16 or wider, within the bound.
A program may use at most 320 MiB of HBM per device.

```python
import jax
import jax.numpy as jnp
from jax import lax

D = 1536
HEADS = 12
KV_HEADS = 2
HEAD = 128
FF = 8960
RANK = 16
SETS = 8
SEQS = 2
LEN = 8192
QKV = 2048


def draw_lengths(key, part):
    key = jax.random.fold_in(key, 11)
    first_key, second_key = jax.random.split(key)
    drawn = jax.random.randint(first_key, (SEQS,), LEN // 2 + 1, LEN + 1, dtype=jnp.int32)
    longest = jax.random.randint(second_key, (), 0, SEQS, dtype=jnp.int32)
    return jnp.where(jnp.arange(SEQS, dtype=jnp.int32) == longest, LEN, drawn).astype(jnp.int32)


def levels(own_key, extent, cuts, low, top_value):
    level = 1.0
    for dim, parts in cuts:
        draws = jax.random.uniform(jax.random.fold_in(jax.random.fold_in(own_key, 6), dim), (parts,), jnp.float32, low / len(cuts), top_value / len(cuts))
        level = level * jnp.repeat(jnp.exp(draws), extent[dim] // parts).reshape((-1,) + (1,) * (len(extent) - 1 - dim))
    return level


def centred(own_key, extent, scale, limit, cuts=(), held_as=jnp.bfloat16):
    entries = jax.random.normal(own_key, extent, jnp.float32) * scale
    if len(cuts) > 0:
        entries = levels(own_key, extent, cuts, -0.22, 0.18) * entries
    return jnp.clip(entries, min=-limit, max=limit).astype(held_as)


def setup_inputs(seed: int = 0) -> dict:
    keys = jax.random.split(jax.random.key(seed), 17)
    tokens = centred(keys[0], (SEQS, LEN, D), 1.0, 6.0, ((1, 128),))
    cotangent = centred(keys[1], (SEQS, LEN, D), 1.0, 6.0, ((1, 128),))
    lengths = draw_lengths(jax.random.fold_in(keys[16], 71), 0)
    set_index = jax.random.randint(keys[3], (SEQS,), 0, SETS).astype(jnp.int32)
    norm_in = jnp.clip(1.0 + 0.15 * jax.random.normal(keys[4], (D,), jnp.float32), 0.25, 1.75)
    norm_ff = jnp.clip(1.0 + 0.15 * jax.random.normal(keys[5], (D,), jnp.float32), 0.25, 1.75)
    qkv_bias = centred(keys[6], (QKV,), 0.5, 3.0, (), jnp.float32)
    w_qkv = centred(keys[7], (D, QKV), D ** -0.5, 0.15625, ((0, 128),))
    w_out = centred(keys[8], (D, D), (max(D // 256, 1)) ** -0.5, 2.5, ((0, 128),))
    w_gate_up = centred(keys[9], (2, D, FF), D ** -0.5, 0.15625, ((1, 32), (2, 4)))
    w_down = centred(keys[10], (FF, D), FF ** -0.5, 0.0625, ((0, 4), (1, 32)))
    a_wide = centred(keys[11], (6, SETS, RANK, D), D ** -0.5, 0.15625)
    a_down = centred(keys[12], (SETS, RANK, FF), FF ** -0.5, 0.0625)
    b_wide = centred(keys[13], (3, SETS, RANK, D), RANK ** -0.5, 1.5)
    b_kv = centred(keys[14], (2, SETS, RANK, KV_HEADS * HEAD), RANK ** -0.5, 1.5)
    b_ff = centred(keys[15], (2, SETS, RANK, FF), RANK ** -0.5, 1.5)
    return dict(tokens=tokens, cotangent=cotangent, lengths=lengths, set_index=set_index, norm_in=norm_in, norm_ff=norm_ff, qkv_bias=qkv_bias, w_qkv=w_qkv, w_out=w_out, w_gate_up=w_gate_up, w_down=w_down, a_wide=a_wide, a_down=a_down, b_wide=b_wide, b_kv=b_kv, b_ff=b_ff)


@jax.custom_vjp
def low(v):
    return lax.optimization_barrier(v.astype(jnp.bfloat16)).astype(jnp.float32)

@jax.custom_vjp
def low_back(v):
    return v

def low_keep(v):
    return (low(v), None)

def low_pass(kept, grad):
    return (grad,)

def back_keep(v):
    return (v, None)

def back_low(kept, grad):
    return (low(grad),)
low.defvjp(low_keep, low_pass)
low_back.defvjp(back_keep, back_low)
EPS = 1e-06
THETA = 1000000.0
HIGH = lax.Precision.HIGHEST

def rms_norm(hidden, gain_vec):
    inverse = lax.rsqrt(lax.optimization_barrier(jnp.mean(hidden * hidden, axis=-1, keepdims=True)) + EPS)
    return hidden * inverse * gain_vec

def rope_tables(positions):
    halves = jnp.arange(0, HEAD, 2, dtype=jnp.int32).astype(jnp.float32)
    freq_table = THETA ** (-halves / HEAD)
    angles = positions.astype(jnp.float32)[:, None] * freq_table[None, :]
    angles = jnp.concatenate([angles, angles], axis=-1)
    return (jnp.cos(angles), jnp.sin(angles))

def rope_turn(values, cos_table, sine_table):
    middle = values.shape[-1] // 2
    turned = jnp.concatenate([-values[..., middle:], values[..., :middle]], axis=-1)
    return values * cos_table + turned * sine_table

def low_rank(values, down_mat, up_mat):
    latent = jnp.dot(values, down_mat.T, precision=HIGH)
    return jnp.dot(latent, up_mat, precision=HIGH)

def attend(queries, key_heads, value_heads, length):
    rows_block = min(512, LEN)
    blocks = LEN // rows_block
    key_at = jnp.arange(LEN, dtype=jnp.int32)
    score_scale = HEAD ** (-0.5)

    def one_block(mapped):
        query_part, first_row = mapped
        row_at = first_row + jnp.arange(rows_block, dtype=jnp.int32)
        scores = low_back(jnp.einsum('qhd,khd->hqk', query_part, key_heads, precision=HIGH) * score_scale)
        allowed = (key_at[None, :] <= row_at[:, None]) & (key_at[None, :] < length)
        scores = jnp.where(allowed[None], scores, -1e+30)
        row_top = lax.optimization_barrier(jnp.max(scores, axis=-1, keepdims=True))
        exponent = jnp.exp(scores - row_top)
        attn_probs = exponent / lax.optimization_barrier(jnp.sum(exponent, axis=-1, keepdims=True))
        return jnp.einsum('hqk,khd->qhd', low(attn_probs), value_heads, precision=HIGH)
    starts = jnp.arange(blocks, dtype=jnp.int32) * rows_block
    outputs = lax.map(jax.checkpoint(one_block), (queries.reshape(blocks, rows_block, HEADS, HEAD), starts))
    return outputs.reshape(LEN, HEADS * HEAD)

def reference(tokens, cotangent, lengths, set_index, norm_in, norm_ff, qkv_bias, w_qkv, w_out, w_gate_up, w_down, a_wide, a_down, b_wide, b_kv, b_ff):
    qkv_full = w_qkv.astype(jnp.float32)
    out_full = w_out.astype(jnp.float32)
    gate_up_full = w_gate_up.astype(jnp.float32)
    down_full = w_down.astype(jnp.float32)
    cos_table, sine_table = rope_tables(jnp.arange(LEN, dtype=jnp.int32))
    cos_heads = cos_table[:, None, :]
    sine_heads = sine_table[:, None, :]
    group_size = HEADS // KV_HEADS
    q_width = HEADS * HEAD
    k_width = KV_HEADS * HEAD

    def forward(inputs, adapt_wide, adapt_down, lift_wide, lift_pair, lift_ff):

        def one_sequence(mapped):
            seq_tokens, length, chosen = mapped
            down_sel = adapt_wide[:, chosen]
            normed_in = low(rms_norm(seq_tokens, norm_in))
            adapter_qkv = jnp.concatenate([low_rank(normed_in, down_sel[0], lift_wide[0, chosen]), low_rank(normed_in, down_sel[1], lift_pair[0, chosen]), low_rank(normed_in, down_sel[2], lift_pair[1, chosen])], axis=-1)
            projected = low_back(jnp.dot(normed_in, qkv_full, precision=HIGH) + qkv_bias + adapter_qkv)
            queries = projected[:, :q_width].reshape(LEN, HEADS, HEAD)
            key_heads = projected[:, q_width:q_width + k_width].reshape(LEN, KV_HEADS, HEAD)
            value_heads = projected[:, q_width + k_width:].reshape(LEN, KV_HEADS, HEAD)
            queries = low(rope_turn(queries, cos_heads, sine_heads))
            key_heads = low(rope_turn(key_heads, cos_heads, sine_heads))
            value_heads = low(value_heads)
            mixed_out = attend(queries, jnp.repeat(key_heads, group_size, axis=1), jnp.repeat(value_heads, group_size, axis=1), length)
            mixed_out = low(low_back(mixed_out))
            attn_out = low_back(jnp.dot(mixed_out, out_full, precision=HIGH) + low_rank(mixed_out, down_sel[3], lift_wide[1, chosen]))
            residual = seq_tokens + attn_out
            normed_ff = low(rms_norm(residual, norm_ff))
            gate_value = low_back(jnp.dot(normed_ff, gate_up_full[0], precision=HIGH) + low_rank(normed_ff, down_sel[4], lift_ff[0, chosen]))
            up_value = low_back(jnp.dot(normed_ff, gate_up_full[1], precision=HIGH) + low_rank(normed_ff, down_sel[5], lift_ff[1, chosen]))
            hidden = low(gate_value * jax.nn.sigmoid(gate_value) * up_value)
            return residual + jnp.dot(hidden, down_full, precision=HIGH) + low_rank(hidden, adapt_down[chosen], lift_wide[2, chosen])
        return lax.map(jax.checkpoint(one_sequence), (inputs, lengths, set_index))
    primals = (tokens.astype(jnp.float32), a_wide.astype(jnp.float32), a_down.astype(jnp.float32), b_wide.astype(jnp.float32), b_kv.astype(jnp.float32), b_ff.astype(jnp.float32))
    result, pullback = jax.vjp(forward, *primals)
    valid_rows = (jnp.arange(LEN, dtype=jnp.int32)[None, :] < lengths[:, None]).astype(jnp.float32)
    gradients = pullback(cotangent.astype(jnp.float32) * valid_rows[:, :, None])
    return (result.astype(jnp.bfloat16), gradients[0], gradients[1], gradients[2], gradients[3], gradients[4], gradients[5])
```

```python
import functools

import jax
import jax.numpy as jnp
import numpy as np
from jax import lax
from jax.experimental import pallas as pl
from jax.experimental.pallas import tpu as pltpu
from jax.sharding import PartitionSpec as P

HEADS = 12
KV_HEADS = 2
HEAD = 128
GROUP = HEADS // KV_HEADS
FF = 8960
SETS = 8
D = 1536
CHUNK = 128
CHUNKS = 64
PADDED = 2304
EPS = 1e-06
THETA = 1000000.0
LOG2E = 1.4426950408889634
LN2 = 0.6931471805599453
MESH = pl.DeviceIdType.MESH
BF = jnp.bfloat16
F32 = jnp.float32
ANY = pl.BlockSpec(memory_space=pl.ANY)
IN_VMEM = pl.BlockSpec(memory_space=pltpu.VMEM)


def blk_of(y, z, x):
    return y * 16 + z * 4 + x


def place():
    blk = lax.axis_index("blk")
    return blk // 16, (blk // 4) % 4, blk % 4, blk, lax.axis_index("uly")


def ring_others():
    y, z, x, blk, uly = place()
    return [
        (blk_of(1 - y, z, x), uly),
        (blk_of(y, z, (x + 1) % 4), uly),
        (blk_of(y, z, (x + 3) % 4), uly),
        (blk_of(y, (z + 1) % 4, x), uly),
        (blk_of(y, (z + 3) % 4, x), uly),
    ]


def greet(others):
    barrier = pltpu.get_barrier_semaphore()
    for other in others:
        pl.semaphore_signal(barrier, inc=1, device_id=other, device_id_type=MESH)
    pl.semaphore_wait(barrier, len(others))


class Gather:
    sends = 31

    def __init__(self, src, dst, send_sem, recv_sem, local_sem):
        self.src, self.dst = src, dst
        self.send_sem, self.recv_sem, self.local_sem = send_sem, recv_sem, local_sem
        self.y, self.z, self.x, self.blk, self.uly = place()
        self.count = [0, 0]
        self.sent = []
        self.local = []

    def at(self, half, y, p, q):
        return blk_of(y, q, p) if half == 0 else blk_of(y, p, q)

    def pq(self, half):
        return (self.x, self.z) if half == 0 else (self.z, self.x)

    def send(self, half, item, target, src=None):
        copy = pltpu.make_async_remote_copy(
            src_ref=self.dst(half, item) if src is None else src,
            dst_ref=self.dst(half, item),
            send_sem=self.send_sem.at[half, self.count[half]],
            recv_sem=self.recv_sem.at[half, item],
            device_id=(target, self.uly),
            device_id_type=MESH,
        )
        self.count[half] += 1
        copy.start()
        self.sent.append(copy)

    def wait(self, half, item):
        ref = self.dst(half, item)
        pltpu.make_async_remote_copy(
            src_ref=ref,
            dst_ref=ref,
            send_sem=self.send_sem.at[half, 0],
            recv_sem=self.recv_sem.at[half, item],
            device_id=(self.blk, self.uly),
            device_id_type=MESH,
        ).wait_recv()

    def start(self):
        for half in (0, 1):
            p, q = self.pq(half)
            self.send(half, self.blk, self.at(half, 1 - self.y, p, q), self.src(half))
        for half in (0, 1):
            p, q = self.pq(half)
            for d in (1, 3):
                self.send(half, self.blk, self.at(half, self.y, (p + d) % 4, q), self.src(half))
            copy = pltpu.make_async_copy(
                self.src(half), self.dst(half, self.blk), self.local_sem.at[half]
            )
            copy.start()
            self.local.append(copy)

    def second(self):
        for half in (0, 1):
            p, q = self.pq(half)
            item = self.at(half, 1 - self.y, p, q)
            self.wait(half, item)
            for d in (1, 3):
                self.send(half, item, self.at(half, self.y, (p + d) % 4, q))
            for d in (1, 3):
                onward = self.at(half, self.y, p, (q + d) % 4)
                self.send(half, self.blk, onward, self.src(half))
                self.send(half, item, onward)

    def spread(self, half, item):
        p, q = self.pq(half)
        for d in (1, 3):
            self.send(half, item, self.at(half, self.y, p, (q + d) % 4))

    def third(self):
        for k, y in enumerate((self.y, 1 - self.y)):
            for half in (0, 1):
                p, q = self.pq(half)
                for d in (3, 1):
                    item = self.at(half, y, (p + d) % 4, q)
                    self.wait(half, item)
                    if (d == 3) == (k == 0):
                        self.send(half, item, self.at(half, self.y, (p + 4 - d) % 4, q))
                    self.spread(half, item)
        for y in (self.y, 1 - self.y):
            for half in (0, 1):
                p, q = self.pq(half)
                item = self.at(half, y, (p + 2) % 4, q)
                self.wait(half, item)
                self.spread(half, item)

    def fourth(self):
        for e in (0, 1, 3, 2):
            for k, y in enumerate((self.y, 1 - self.y)):
                for half in (0, 1):
                    p, q = self.pq(half)
                    for d in (3, 1):
                        item = self.at(half, y, (p + e) % 4, (q + d) % 4)
                        self.wait(half, item)
                        if (d == 3) == (k == 0):
                            self.send(half, item, self.at(half, self.y, p, (q + 4 - d) % 4))

    def last(self):
        for e in (0, 1, 3, 2):
            for y in (self.y, 1 - self.y):
                for half in (0, 1):
                    p, q = self.pq(half)
                    self.wait(half, self.at(half, y, (p + e) % 4, (q + 2) % 4))
        for copy in self.local:
            copy.wait()
        for copy in self.sent:
            copy.wait_send()

    def all(self):
        self.start()
        self.second()
        self.third()
        self.fourth()
        self.last()


GATHER_SEMS = lambda *lead: [
    pltpu.SemaphoreType.DMA(lead + (2, Gather.sends)),
    pltpu.SemaphoreType.DMA(lead + (2, 32)),
    pltpu.SemaphoreType.DMA(lead + (2,)),
]


def proj_kernel(qkv_ref, out_ref, qkv_all, out_all, *sems):
    y, z, x, blk, uly = place()
    core = uly % 2
    sibling = (blk, uly + 1 - 2 * core)
    greet(ring_others() + [sibling])
    (send_a, recv_a, local_a, send_b, recv_b, local_b, pair_send, pair_recv) = sems

    def columns(item, half):
        start = ((item % 2) * 2 + core) * 384
        return pl.ds(pl.multiple_of(start + 128 * half, 128), 128 + 128 * half)

    a = Gather(
        lambda half: qkv_ref.at[:, pl.ds(256 * half, 256)],
        lambda half, item: qkv_all.at[
            core, pl.ds(pl.multiple_of(item * 48, 16), 48), pl.ds(256 * half, 256)
        ],
        send_a, recv_a, local_a,
    )
    b = Gather(
        lambda half: out_ref.at[:, pl.ds(128 * half, 128 + 128 * half)],
        lambda half, item: out_all.at[
            pl.ds(pl.multiple_of((item // 2) * 48, 16), 48), columns(item, half)
        ],
        send_b, recv_b, local_b,
    )
    a.start()
    b.start()
    a.second()
    b.second()
    a.third()
    b.third()
    a.fourth()
    b.fourth()
    a.last()
    b.last()
    parts = [lambda c: qkv_all.at[c]] + [
        lambda c, n=n: out_all.at[:, pl.ds(pl.multiple_of((2 * n + c) * 384, 128), 384)]
        for n in (0, 1)
    ]
    copies = []
    for n, part in enumerate(parts):
        copy = pltpu.make_async_remote_copy(
            src_ref=part(core), dst_ref=part(core),
            send_sem=pair_send.at[n], recv_sem=pair_recv.at[n],
            device_id=sibling, device_id_type=MESH,
        )
        copy.start()
        copies.append(copy)
    for n, part in enumerate(parts):
        copies[n].wait_send()
        pltpu.make_async_remote_copy(
            src_ref=part(1 - core), dst_ref=part(1 - core),
            send_sem=pair_send.at[n], recv_sem=pair_recv.at[n],
            device_id=sibling, device_id_type=MESH,
        ).wait_recv()


def gather_proj(qkv_part, out_part):
    return pl.pallas_call(
        proj_kernel,
        out_shape=(
            jax.ShapeDtypeStruct((2, D, 512), BF),
            jax.ShapeDtypeStruct((D // 2, D), BF),
        ),
        in_specs=[ANY, ANY],
        out_specs=(ANY, ANY),
        scratch_shapes=GATHER_SEMS() + GATHER_SEMS() + [pltpu.SemaphoreType.DMA((3,))] * 2,
        compiler_params=pltpu.CompilerParams(collective_id=0, has_side_effects=True),
        name="gather_proj",
    )(qkv_part, out_part)


KEYS = 512
STEP = KEYS // CHUNK
ROWS = GROUP * CHUNK


def head_columns(ref, slot):
    return jnp.concatenate(
        [
            ref[slot * CHUNK : (slot + 1) * CHUNK, n * HEAD : (n + 1) * HEAD].T
            for n in range(GROUP)
        ],
        axis=1,
    )


def head_rows(ref, slot):
    return jnp.concatenate(
        [
            ref[slot * CHUNK : (slot + 1) * CHUNK, n * HEAD : (n + 1) * HEAD]
            for n in range(GROUP)
        ],
        axis=0,
    )


def key_block(kv_ref, step):
    rows = kv_ref[pl.ds(step * STEP, STEP)].reshape(KEYS, 2 * HEAD)
    return rows[:, :HEAD], rows[:, HEAD:]


def dot(a, b):
    return jnp.dot(a, b, preferred_element_type=F32)


def key_places(step):
    return lax.broadcasted_iota(jnp.int32, (KEYS, ROWS), 0) + step * KEYS


def attend_slot(slot, chunk, q_ref, kv_ref, limit_ref, mixed_ref, lse_ref, acc_ref):
    turned = head_columns(q_ref, slot)
    limit = limit_ref[slot, 0:1, :]
    acc_ref[...] = jnp.zeros_like(acc_ref)

    def step(n, carry):
        top, total = carry
        keys, values = key_block(kv_ref, n)
        scores = jnp.where(key_places(n) <= limit, dot(keys, turned), -1e30)
        new_top = jnp.maximum(top, jnp.max(scores, axis=0, keepdims=True))
        fade = jnp.exp2(top - new_top)
        probs = jnp.exp2(scores - new_top)
        total = total * fade + jnp.sum(probs, axis=0, keepdims=True)
        acc_ref[...] = acc_ref[...] * fade + dot(values.T, probs.astype(BF))
        return new_top, total

    top, total = lax.fori_loop(
        0,
        chunk // STEP + 1,
        step,
        (jnp.full((1, ROWS), -1e30, F32), jnp.zeros((1, ROWS), F32)),
    )
    out = acc_ref[...] / total
    for n in range(GROUP):
        mixed_ref[slot * CHUNK : (slot + 1) * CHUNK, n * HEAD : (n + 1) * HEAD] = out[
            :, n * CHUNK : (n + 1) * CHUNK
        ].T.astype(BF)
    lse_ref[slot] = jnp.broadcast_to(top + jnp.log2(total), (8, ROWS))


def forward_kernel(
    q_ref, kv_ref, limit_ref, ff_ref, mixed_ref, lse_ref, kv_out, gate_all, up_all, down_all,
    kv_all, acc_ref, *sems,
):
    y, z, x, blk, uly = place()
    greet(ring_others())
    kv_send, kv_recv, kv_local, ff_send, ff_recv, ff_local, out_sem = sems
    kv = Gather(
        lambda half: kv_ref.at[half],
        lambda half, item: kv_all.at[item if half == 0 else 63 - item],
        kv_send, kv_recv, kv_local,
    )
    wide = PADDED // 2
    weights = [
        Gather(
            lambda half, n=n: ff_ref.at[n, :, pl.ds(wide * half, wide)],
            lambda half, item, ref=ref: ref.at[item, :, pl.ds(wide * half, wide)],
            ff_send.at[n], ff_recv.at[n], ff_local.at[n],
        )
        for n, ref in enumerate((gate_all, up_all, down_all))
    ]
    kv.start()
    for w in weights:
        w.start()
    kv.second()
    kv.third()
    kv.fourth()
    for w in weights:
        w.second()
    kv.last()
    out_copy = pltpu.make_async_copy(kv_all, kv_out, out_sem)
    out_copy.start()
    attend_slot(0, blk, q_ref, kv_all, limit_ref, mixed_ref, lse_ref, acc_ref)
    for w in weights:
        w.third()
    attend_slot(1, 63 - blk, q_ref, kv_all, limit_ref, mixed_ref, lse_ref, acc_ref)
    for w in weights:
        w.fourth()
    for w in weights:
        w.last()
    out_copy.wait()


def attend_forward(q, kv, limit, ff):
    weight = jax.ShapeDtypeStruct((32, 48, PADDED), BF)
    return pl.pallas_call(
        forward_kernel,
        out_shape=(
            jax.ShapeDtypeStruct((2 * CHUNK, GROUP * HEAD), BF),
            jax.ShapeDtypeStruct((2, 8, ROWS), F32),
            jax.ShapeDtypeStruct((CHUNKS, CHUNK, 2 * HEAD), BF),
            weight, weight, weight,
        ),
        in_specs=[IN_VMEM, ANY, IN_VMEM, ANY],
        out_specs=(IN_VMEM, IN_VMEM, ANY, ANY, ANY, ANY),
        scratch_shapes=[
            pltpu.VMEM((CHUNKS, CHUNK, 2 * HEAD), BF),
            pltpu.VMEM((HEAD, ROWS), F32),
        ]
        + GATHER_SEMS()
        + GATHER_SEMS(3)
        + [pltpu.SemaphoreType.DMA],
        compiler_params=pltpu.CompilerParams(
            collective_id=1, has_side_effects=True, vmem_limit_bytes=40 * 2**20
        ),
        name="attend_forward",
    )(q, kv, limit, ff)


def backward_slot(slot, chunk, q_ref, kv_ref, limit_ref, mixed_ref, grad_ref, lse_ref, dq_ref, dkv_ref, acc_ref):
    turned = head_columns(q_ref, slot)
    rows = head_rows(q_ref, slot)
    grad_turned = head_columns(grad_ref, slot)
    grad_rows = head_rows(grad_ref, slot)
    mixed_turned = head_columns(mixed_ref, slot)
    row_dot = jnp.sum(
        grad_turned.astype(F32) * mixed_turned.astype(F32), axis=0, keepdims=True
    )
    limit = limit_ref[slot, 0:1, :]
    lse = lse_ref[slot, 0:1, :]
    acc_ref[...] = jnp.zeros_like(acc_ref)

    def step(n, carry):
        keys, values = key_block(kv_ref, n)
        scores = jnp.where(key_places(n) <= limit, dot(keys, turned), -1e30)
        probs = jnp.exp2(scores - lse)
        grad_probs = dot(values, grad_turned)
        grad_scores = (probs * (grad_probs - row_dot)).astype(BF)
        acc_ref[...] += dot(keys.T, grad_scores)
        at = pl.ds(pl.multiple_of(n * KEYS, KEYS), KEYS)
        dkv_ref[at, :HEAD] += dot(grad_scores, rows)
        dkv_ref[at, HEAD:] += dot(probs.astype(BF), grad_rows)
        return carry

    lax.fori_loop(0, chunk // STEP + 1, step, 0)
    for n in range(GROUP):
        dq_ref[slot * CHUNK : (slot + 1) * CHUNK, n * HEAD : (n + 1) * HEAD] = (
            acc_ref[:, n * CHUNK : (n + 1) * CHUNK].T * HEAD ** (-0.5)
        )


def reduce_dkv(part, own_ref, bufs, sums, sems):
    y, z, x, blk, uly = place()
    buf_q, buf_p, buf_y = bufs
    sum_p, sum_y = sums
    send_sem, recv_sem = sems

    def index(half, y, p, q):
        item = blk_of(y, q, p) if half == 0 else blk_of(y, p, q)
        return item if half == 0 else 63 - item

    def pq(half):
        return (x, z) if half == 0 else (z, x)

    def device(half, y, p, q):
        return (blk_of(y, q, p) if half == 0 else blk_of(y, p, q), uly)

    def remote(src, dst, half, n, target):
        return pltpu.make_async_remote_copy(
            src_ref=src, dst_ref=dst, send_sem=send_sem.at[half, n], recv_sem=recv_sem.at[half, n],
            device_id=target, device_id_type=MESH,
        )

    done = []
    for d in (2, 1, 3):
        for half in (0, 1):
            p, q = pq(half)
            for yy in (0, 1):
                for pp in range(4):
                    copy = remote(
                        part.at[index(half, yy, pp, (q + d) % 4)],
                        buf_q.at[half, d - 1, yy, pp],
                        half, (d - 1) * 8 + yy * 4 + pp,
                        device(half, y, p, (q + d) % 4),
                    )
                    copy.start()
                    done.append(copy)
    for copy in done:
        copy.wait()
    done = []
    for d in (2, 1, 3, 0):
        for half in (0, 1):
            p, q = pq(half)
            to = (p + d) % 4
            for yy in (0, 1):
                total = part[index(half, yy, to, q)].astype(F32)
                for n in range(3):
                    total += buf_q[half, n, yy, to].astype(F32)
                sum_p[half, d, yy] = total.astype(BF)
            if d > 0:
                copy = remote(
                    sum_p.at[half, d], buf_p.at[half, d - 1], half, 24 + d - 1,
                    device(half, y, to, q),
                )
                copy.start()
                done.append(copy)
    for copy in done:
        copy.wait()
    done = []
    for k in (1, 0):
        for half in (0, 1):
            p, q = pq(half)
            yy = y if k == 0 else 1 - y
            total = sum_p[half, 0, yy].astype(F32)
            for n in range(3):
                total += buf_p[half, n, yy].astype(F32)
            sum_y[half, k] = total.astype(BF)
            if k == 1:
                copy = remote(
                    sum_y.at[half, 1], buf_y.at[half], half, 27, device(half, 1 - y, p, q)
                )
                copy.start()
                done.append(copy)
    for copy in done:
        copy.wait()
    for half in (0, 1):
        own_ref[half] = sum_y[half, 0].astype(F32) + buf_y[half].astype(F32)


def reduce_others():
    y, z, x, blk, uly = place()
    return (
        [(blk_of(1 - y, z, x), uly)]
        + [(blk_of(y, z, (x + d) % 4), uly) for d in (1, 2, 3)]
        + [(blk_of(y, (z + d) % 4, x), uly) for d in (1, 2, 3)]
    )


def backward_kernel(
    q_ref, kv_ref, limit_ref, mixed_ref, grad_ref, lse_ref, dq_ref, own_ref,
    dkv_ref, acc_ref, part, buf_q, buf_p, buf_y, sum_p, sum_y, send_sem, recv_sem,
):
    y, z, x, blk, uly = place()
    greet(reduce_others())
    dkv_ref[...] = jnp.zeros_like(dkv_ref)
    args = (q_ref, kv_ref, limit_ref, mixed_ref, grad_ref, lse_ref, dq_ref, dkv_ref, acc_ref)
    backward_slot(0, blk, *args)
    backward_slot(1, 63 - blk, *args)

    def pack(n, carry):
        rows = dkv_ref[pl.ds(pl.multiple_of(n * CHUNK, CHUNK), CHUNK), :]
        part[n] = jnp.concatenate([rows[:, :HEAD] * LN2, rows[:, HEAD:]], axis=1).astype(BF)
        return carry

    lax.fori_loop(0, CHUNKS, pack, 0)
    reduce_dkv(part, own_ref, (buf_q, buf_p, buf_y), (sum_p, sum_y), (send_sem, recv_sem))


def attend_backward(q, kv, limit, mixed, grad, lse):
    return pl.pallas_call(
        backward_kernel,
        out_shape=(
            jax.ShapeDtypeStruct((2 * CHUNK, GROUP * HEAD), F32),
            jax.ShapeDtypeStruct((2, CHUNK, 2 * HEAD), F32),
        ),
        in_specs=[IN_VMEM] * 6,
        out_specs=(IN_VMEM, IN_VMEM),
        scratch_shapes=[
            pltpu.VMEM((CHUNKS * CHUNK, 2 * HEAD), F32),
            pltpu.VMEM((HEAD, ROWS), F32),
            pltpu.VMEM((CHUNKS, CHUNK, 2 * HEAD), BF),
            pltpu.VMEM((2, 3, 2, 4, CHUNK, 2 * HEAD), BF),
            pltpu.VMEM((2, 3, 2, CHUNK, 2 * HEAD), BF),
            pltpu.VMEM((2, CHUNK, 2 * HEAD), BF),
            pltpu.VMEM((2, 4, 2, CHUNK, 2 * HEAD), BF),
            pltpu.VMEM((2, 2, CHUNK, 2 * HEAD), BF),
            pltpu.SemaphoreType.DMA((2, 28)),
            pltpu.SemaphoreType.DMA((2, 28)),
        ],
        compiler_params=pltpu.CompilerParams(
            collective_id=2, has_side_effects=True, vmem_limit_bytes=56 * 2**20
        ),
        name="attend_backward",
    )(q, kv, limit, mixed, grad, lse)


def device_at(blk, h, core):
    return blk * 4 + h * 2 + core


def moves():
    def home(blk, h):
        chunk = 2 * blk + h
        return (chunk, 0) if chunk < 32 else (63 - chunk, 1)

    fetch = {}
    for j in (0, 1):
        for k in (0, 1):
            fetch[k, j] = [
                (device_at(b, h, c), device_at(home(b, h)[0], h ^ k, c ^ j))
                for b in range(32) for h in (0, 1) for c in (0, 1)
            ]
    own = [
        [
            (device_at(b, h, c), device_at(home(b, h)[0], home(b, h)[1], c ^ j))
            for b in range(32) for h in (0, 1) for c in (0, 1)
        ]
        for j in (0, 1)
    ]
    back = [[(t, s) for s, t in pairs] for pairs in own]
    out_rows = [
        [
            (device_at(b, u // 2, u % 2), device_at(2 * (b % 16) + q // 2, b // 16, q % 2))
            for b in range(32) for u in range(4) for q in ((u + t) % 4,)
        ]
        for t in range(4)
    ]
    return fetch, own, back, out_rows


ALL = ("blk", "uly")
OVER_H = [(0, 2), (2, 0), (1, 3), (3, 1)]
OVER_CORE = [(0, 1), (1, 0), (2, 3), (3, 2)]
OVER_BOTH = [(0, 3), (3, 0), (1, 2), (2, 1)]


def flip(parts, first, second):
    return jnp.where(parts, second, first), jnp.where(parts, first, second)


def rope_tables(positions):
    halves = jnp.arange(0, HEAD, 2, dtype=jnp.int32).astype(F32)
    freq_table = THETA ** (-halves / HEAD)
    angles = positions.astype(F32)[:, None] * freq_table[None, :]
    angles = jnp.concatenate([angles, angles], axis=-1)
    return jnp.cos(angles), jnp.sin(angles)


def rope_turn(values, cos_table, sine_table):
    middle = HEAD // 2
    turned = jnp.concatenate([-values[..., middle:], values[..., :middle]], axis=-1)
    return values * cos_table + turned * sine_table


def rope_back(values, cos_table, sine_table):
    middle = HEAD // 2
    turned = jnp.concatenate([values[..., middle:], -values[..., :middle]], axis=-1)
    return values * cos_table + turned * sine_table


def norm_scale(hidden):
    return lax.rsqrt(jnp.mean(hidden * hidden, axis=-1, keepdims=True) + EPS)


def norm_back(hidden, scaled, gain_vec, upstream):
    normed = hidden * scaled
    weighted = upstream * gain_vec
    return scaled * (weighted - normed * jnp.mean(weighted * normed, axis=-1, keepdims=True))


def mm(spec, a, b):
    return jnp.einsum(spec, a.astype(BF), b.astype(BF), preferred_element_type=F32)


def body(
    tokens, cotangent, lengths, set_index, norm_in, norm_ff, qkv_bias, w_qkv, w_out, w_gate_up, w_down,
    a_wide, a_down, b_wide, b_kv, b_ff,
):
    blk = lax.axis_index("blk")
    uly = lax.axis_index("uly")
    h = uly // 2
    core = uly % 2
    fetch, own_moves, back_moves, out_moves = moves()
    local_ff = w_down.shape[0]
    group_cols = GROUP * HEAD

    by_head = jnp.concatenate(
        [
            w_qkv[:, : HEADS * HEAD].reshape(12, 2, group_cols),
            w_qkv[:, HEADS * HEAD : HEADS * HEAD + 256].reshape(12, 2, HEAD),
            w_qkv[:, HEADS * HEAD + 256 :].reshape(12, 2, HEAD),
        ],
        axis=2,
    )
    quarters = jnp.moveaxis(by_head.reshape(12, 4, 512), 1, 0)
    qkv_part = lax.all_to_all(quarters, "uly", split_axis=0, concat_axis=0, tiled=True).reshape(48, 512)
    out_quarters = jnp.moveaxis(w_out.reshape(12, 4, 384), 1, 0)
    got = [
        lax.ppermute(
            lax.dynamic_index_in_dim(out_quarters, (uly + t) % 4, 0, keepdims=False), ALL, out_moves[t]
        )
        for t in range(4)
    ]
    quarter = (blk % 2) * 2 + core
    got = jnp.stack(got)
    out_part = jnp.take(got, (quarter - jnp.arange(4)) % 4, axis=0).reshape(48, 384)
    qkv_w, out_w = gather_proj(qkv_part, out_part)

    pieces = [
        [
            lax.ppermute(lax.dynamic_index_in_dim(tokens, core ^ j, 0, keepdims=False), ALL, fetch[k, j])
            for j in (0, 1)
        ]
        for k in (0, 1)
    ]
    first, second = flip((blk % 2) != h, jnp.stack(pieces[0]), jnp.stack(pieces[1]))
    rows = jnp.stack([first, second])
    rows = jnp.stack(flip(core == 1, rows[:, 0], rows[:, 1]), axis=1)
    rows = rows.reshape(2, CHUNK, D).astype(F32)
    cot_pieces = [
        lax.ppermute(lax.dynamic_index_in_dim(cotangent, core ^ j, 0, keepdims=False), ALL, own_moves[j])
        for j in (0, 1)
    ]
    cot_rows = jnp.concatenate(flip(core == 1, cot_pieces[0], cot_pieces[1]), axis=0)
    chunks = jnp.stack([blk, 63 - blk])
    positions = (chunks[:, None] * CHUNK + jnp.arange(CHUNK, dtype=jnp.int32)[None, :]).reshape(-1)
    length = lengths[core]
    own_positions = jnp.where(h == 0, blk, 63 - blk) * CHUNK + jnp.arange(CHUNK, dtype=jnp.int32)
    grad_out = jnp.where((own_positions < length)[:, None], cot_rows, 0).astype(BF)

    own_set = set_index[core]
    sets = jnp.stack([set_index[core], set_index[1 - core]])
    a_own = jnp.take(a_wide, own_set, axis=1)
    bq = lax.dynamic_slice_in_dim(jnp.take(b_wide[0], own_set, axis=0), h * group_cols, group_cols, 1)
    bo = jnp.take(b_wide[1], own_set, axis=0)
    bk, bv = (
        lax.dynamic_slice_in_dim(jnp.take(b_kv[n], own_set, axis=0), h * HEAD, HEAD, 1) for n in (0, 1)
    )
    ao = lax.dynamic_slice_in_dim(a_own[3], h * group_cols, group_cols, 1)
    bias = jnp.concatenate(
        [
            lax.dynamic_slice_in_dim(qkv_bias, h * group_cols, group_cols, 0),
            lax.dynamic_slice_in_dim(qkv_bias, HEADS * HEAD + h * HEAD, HEAD, 0),
            lax.dynamic_slice_in_dim(qkv_bias, HEADS * HEAD + 256 + h * HEAD, HEAD, 0),
        ]
    )
    zero = jnp.zeros
    a_qkv = a_own[:3].reshape(48, D)
    b_qkv = jnp.concatenate(
        [
            jnp.concatenate([bq, zero((16, 256), BF)], axis=1),
            jnp.concatenate([zero((16, group_cols), BF), bk, zero((16, HEAD), BF)], axis=1),
            jnp.concatenate([zero((16, group_cols + HEAD), BF), bv], axis=1),
        ],
        axis=0,
    )
    a_ff = jnp.take(a_wide[4:6], sets, axis=1).transpose(1, 0, 2, 3).reshape(2, 32, D)
    b_cols = lax.dynamic_slice_in_dim(jnp.take(b_ff, sets, axis=1), uly * local_ff, local_ff, 3)
    b_cols = jnp.pad(b_cols, ((0, 0), (0, 0), (0, 0), (0, PADDED - local_ff)))
    a_cols = lax.dynamic_slice_in_dim(jnp.take(a_down, sets, axis=0), uly * local_ff, local_ff, 2)
    a_cols = jnp.pad(a_cols, ((0, 0), (0, 0), (0, PADDED - local_ff)))
    b_out = jnp.take(b_wide[2], sets, axis=0)

    scale_in = norm_scale(rows)
    normed = (rows * scale_in * norm_in).astype(BF).reshape(2 * CHUNK, D)
    latent_qkv = mm("td,rd->tr", normed, a_qkv)
    projected = jnp.concatenate([dot(normed, qkv_w[0]), dot(normed, qkv_w[1])], axis=1)
    projected = projected + bias + mm("tr,ro->to", latent_qkv, b_qkv)
    cos_table, sine_table = rope_tables(positions)
    cos_heads, sine_heads = cos_table[:, None, :], sine_table[:, None, :]
    queries = projected[:, :group_cols].reshape(2 * CHUNK, GROUP, HEAD)
    q = rope_turn(queries, cos_heads, sine_heads) * (HEAD ** (-0.5) * LOG2E)
    q = q.astype(BF).reshape(2 * CHUNK, group_cols)
    k = rope_turn(projected[:, group_cols : group_cols + HEAD], cos_table, sine_table)
    kv = jnp.concatenate([k, projected[:, group_cols + HEAD :]], axis=1).astype(BF)
    kv = kv.reshape(2, CHUNK, 2 * HEAD)
    limit = jnp.minimum(positions, length - 1).reshape(2, 1, 1, CHUNK)
    limit = jnp.broadcast_to(limit, (2, 8, GROUP, CHUNK)).reshape(2, 8, ROWS)
    ff_part = jnp.pad(
        jnp.concatenate([w_gate_up, w_down.T[None]], axis=0), ((0, 0), (0, 0), (0, PADDED - local_ff))
    )
    mixed, lse, kv_all, gate_w, up_w, down_w = attend_forward(q, kv, limit, ff_part)
    gate_w, up_w, down_w = (w.reshape(D, PADDED) for w in (gate_w, up_w, down_w))

    def swap_h(v):
        return lax.ppermute(v, "uly", OVER_H)

    def own_slot(v):
        return flip(h == 1, v[0], v[1])

    latent_o = mm("tc,rc->tr", mixed, ao)
    part = (dot(mixed, out_w) + mm("tr,ro->to", latent_o, bo)).reshape(2, CHUNK, D)
    mine, theirs = own_slot(part)
    attn_out = mine + swap_h(theirs.astype(BF)).astype(F32)
    own_rows = jnp.where(h == 0, rows[0], rows[1])
    residual = own_rows + attn_out
    scale_ff = norm_scale(residual)
    normed_ff = (residual * scale_ff * norm_ff).astype(BF)

    def spread(v):
        across, beside, both = (lax.ppermute(v, "uly", over) for over in (OVER_H, OVER_CORE, OVER_BOTH))
        return jnp.stack([jnp.concatenate([v, across]), jnp.concatenate([beside, both])])

    def collect(v):
        low = v.astype(BF)
        total = v[0, :CHUNK]
        for over, part in ((OVER_H, low[0, CHUNK:]), (OVER_CORE, low[1, :CHUNK]), (OVER_BOTH, low[1, CHUNK:])):
            total = total + lax.ppermute(part, "uly", over).astype(F32)
        return total

    gathered = spread(normed_ff)
    grad_gathered = spread(grad_out)
    latent_ff = mm("std,srd->str", gathered, a_ff)
    gate = mm("std,df->stf", gathered, gate_w) + mm("str,srf->stf", latent_ff[..., :16], b_cols[0])
    up = mm("std,df->stf", gathered, up_w) + mm("str,srf->stf", latent_ff[..., 16:], b_cols[1])
    sigmoid = jax.nn.sigmoid(gate)
    silu = gate * sigmoid
    hidden = (silu * up).astype(BF)
    latent_down = mm("stf,srf->str", hidden, a_cols)
    down = mm("stf,df->std", hidden, down_w) + mm("str,srd->std", latent_down, b_out)
    ff_out = collect(down)
    result = (residual + ff_out).astype(BF)

    latent_back = mm("std,srd->str", grad_gathered, b_out)
    grad_hidden = mm("std,df->stf", grad_gathered, down_w) + mm("str,srf->stf", latent_back, a_cols)
    grad_a_cols = mm("str,stf->srf", latent_back, hidden)
    grad_b_out = mm("str,std->srd", latent_down, grad_gathered)
    grad_up = (grad_hidden * silu).astype(BF)
    grad_gate = (grad_hidden * up * (sigmoid * (1.0 + gate * (1.0 - sigmoid)))).astype(BF)
    back_gate = mm("stf,srf->str", grad_gate, b_cols[0])
    back_up = mm("stf,srf->str", grad_up, b_cols[1])
    back_ff = jnp.concatenate([back_gate, back_up], axis=-1)
    grad_a_ff = mm("str,std->srd", back_ff, gathered)
    grad_b_gate = mm("str,stf->srf", latent_ff[..., :16], grad_gate)
    grad_b_up = mm("str,stf->srf", latent_ff[..., 16:], grad_up)
    grad_ff_in = (
        mm("stf,df->std", grad_gate, gate_w)
        + mm("stf,df->std", grad_up, up_w)
        + mm("str,srd->std", back_ff, a_ff)
    )
    grad_normed_ff = collect(grad_ff_in)
    grad_resid = grad_out.astype(F32) + norm_back(residual, scale_ff, norm_ff, grad_normed_ff)
    grad_attn = grad_resid.astype(BF)
    grad_attn = jnp.concatenate(flip(h == 1, grad_attn, swap_h(grad_attn)), axis=0)

    back_o = mm("td,rd->tr", grad_attn, bo)
    grad_a_o = mm("tr,tc->rc", back_o, mixed)
    grad_b_o = mm("tr,td->rd", latent_o, grad_attn)
    grad_mixed = (mm("td,cd->tc", grad_attn, out_w) + mm("tr,rc->tc", back_o, ao)).astype(BF)
    dq, dkv = attend_backward(q, kv_all, limit, mixed, grad_mixed, lse)
    dkv = dkv.reshape(2 * CHUNK, 2 * HEAD)
    grad_q = rope_back(dq.reshape(2 * CHUNK, GROUP, HEAD), cos_heads, sine_heads)
    grad_k = rope_back(dkv[:, :HEAD], cos_table, sine_table)
    grad_qkv = jnp.concatenate(
        [grad_q.reshape(2 * CHUNK, group_cols), grad_k, dkv[:, HEAD:]], axis=1
    ).astype(BF)
    back_qkv = mm("to,ro->tr", grad_qkv, b_qkv)
    grad_a_qkv = mm("tr,td->rd", back_qkv, normed)
    grad_b_qkv = mm("tr,to->ro", latent_qkv, grad_qkv)
    grad_normed = (
        mm("to,do->td", grad_qkv[:, :512], qkv_w[0])
        + mm("to,do->td", grad_qkv[:, 512:], qkv_w[1])
        + mm("tr,rd->td", back_qkv, a_qkv)
    ).reshape(2, CHUNK, D)
    mine, theirs = own_slot(grad_normed)
    grad_normed = mine + swap_h(theirs.astype(BF)).astype(F32)
    own_scale = jnp.where(h == 0, scale_in[0], scale_in[1])
    input_grad = grad_resid + norm_back(own_rows, own_scale, norm_in, grad_normed)

    def home(v):
        halves = v.astype(BF).reshape(2, CHUNK // 2, D)
        got = [
            lax.ppermute(lax.dynamic_index_in_dim(halves, core ^ j, 0, keepdims=False), ALL, back_moves[j])
            for j in (0, 1)
        ]
        return jnp.stack(flip(core == 1, got[0], got[1]))

    result_tokens = home(result)
    input_grad = home(input_grad).astype(F32)

    def ordered(v):
        return jnp.stack(flip(core == 1, v[0], v[1]))

    def by_sequence(v):
        return jnp.where((core == jnp.arange(2)).reshape((2,) + (1,) * v.ndim), v[None], 0.0)

    def widen(v, total, start):
        full = zero(v.shape[:-1] + (total,), F32)
        return lax.dynamic_update_slice_in_dim(full, v, start, v.ndim - 1)

    col_parts = ordered(jnp.stack([grad_a_cols, grad_b_gate, grad_b_up], axis=1)[..., :local_ff])
    ff_parts = ordered(
        jnp.concatenate([grad_a_ff.reshape(2, 2, 16, D), grad_b_out[:, None]], axis=1)
    )
    o_parts = by_sequence(jnp.stack([widen(grad_a_o, D, h * group_cols), grad_b_o]))
    qkv_parts = by_sequence(
        jnp.concatenate(
            [grad_a_qkv.reshape(3, 16, D), widen(grad_b_qkv[:16, :group_cols], D, h * group_cols)[None]]
        )
    )
    kv_parts = by_sequence(
        jnp.stack(
            [
                widen(grad_b_qkv[16:32, group_cols : group_cols + HEAD], 2 * HEAD, h * HEAD),
                widen(grad_b_qkv[32:, group_cols + HEAD :], 2 * HEAD, h * HEAD),
            ]
        )
    )
    cols = lax.psum(col_parts, "blk")
    cols = lax.all_gather(cols, "uly", axis=3, tiled=True)
    ff_parts, o_parts = lax.psum((ff_parts, o_parts), ALL)
    qkv_parts, kv_parts = lax.psum((qkv_parts, kv_parts), ALL)
    chosen = (jnp.arange(SETS, dtype=jnp.int32)[:, None] == set_index[None, :]).astype(F32)

    def fold(v):
        v = jnp.moveaxis(v, 0, 1)
        pick = chosen[None, :, :, None, None]
        return pick[:, :, 0] * v[:, 0][:, None] + pick[:, :, 1] * v[:, 1][:, None]

    wide_a = jnp.concatenate([qkv_parts[:, :3], o_parts[:, :1], ff_parts[:, :2]], axis=1)
    wide_b = jnp.concatenate([qkv_parts[:, 3:], o_parts[:, 1:], ff_parts[:, 2:]], axis=1)
    return (
        result_tokens,
        input_grad,
        fold(wide_a),
        fold(cols[:, :1])[0],
        fold(wide_b),
        fold(kv_parts),
        fold(cols[:, 1:]),
    )


def solution(mesh):
    spread = P(None, ("blk", "uly"), None)
    in_specs = (
        spread, spread, P(), P(), P(), P(), P(),
        P(("blk", "uly"), None), P(("blk", "uly"), None), P(None, "blk", "uly"), P("uly", "blk"),
        P(), P(), P(), P(), P(),
    )
    out_specs = (spread, spread, P(), P(), P(), P(), P())
    return jax.shard_map(body, mesh=mesh, in_specs=in_specs, out_specs=out_specs, check_vma=False)
```

```python
import functools

import jax
import jax.numpy as jnp
import numpy as np
from jax import lax
from jax.experimental import pallas as pl
from jax.experimental.pallas import tpu as pltpu
from jax.sharding import PartitionSpec as P

HEADS = 12
KV_HEADS = 2
HEAD = 128
GROUP = HEADS // KV_HEADS
FF = 8960
SETS = 8
D = 1536
CHUNK = 128
CHUNKS = 64
PADDED = 2304
EPS = 1e-06
THETA = 1000000.0
LOG2E = 1.4426950408889634
LN2 = 0.6931471805599453
MESH = pl.DeviceIdType.MESH
BF = jnp.bfloat16
F32 = jnp.float32
ANY = pl.BlockSpec(memory_space=pl.ANY)
IN_VMEM = pl.BlockSpec(memory_space=pltpu.VMEM)


def blk_of(y, z, x):
    return y * 16 + z * 4 + x


def place():
    blk = lax.axis_index("blk")
    return blk // 16, (blk // 4) % 4, blk % 4, blk, lax.axis_index("uly")


def ring_others():
    y, z, x, blk, uly = place()
    return [
        (blk_of(1 - y, z, x), uly),
        (blk_of(y, z, (x + 1) % 4), uly),
        (blk_of(y, z, (x + 3) % 4), uly),
        (blk_of(y, (z + 1) % 4, x), uly),
        (blk_of(y, (z + 3) % 4, x), uly),
    ]


def greet(others):
    barrier = pltpu.get_barrier_semaphore()
    for other in others:
        pl.semaphore_signal(barrier, inc=1, device_id=other, device_id_type=MESH)
    pl.semaphore_wait(barrier, len(others))


class Gather:
    sends = 31

    def __init__(self, src, dst, send_sem, recv_sem, local_sem, orders=(0, 1)):
        self.src, self.dst, self.orders = src, dst, orders
        self.streams = range(len(orders))
        self.send_sem, self.recv_sem, self.local_sem = send_sem, recv_sem, local_sem
        self.y, self.z, self.x, self.blk, self.uly = place()
        self.count = [0] * len(orders)
        self.sent = []
        self.local = []

    def at(self, stream, y, p, q):
        order = self.orders[stream]
        return blk_of(y, order * p + (1 - order) * q, order * q + (1 - order) * p)

    def pq(self, stream):
        order = self.orders[stream]
        return (
            order * self.z + (1 - order) * self.x,
            order * self.x + (1 - order) * self.z,
        )

    def send(self, stream, item, target, src=None):
        copy = pltpu.make_async_remote_copy(
            src_ref=self.dst(stream, item) if src is None else src,
            dst_ref=self.dst(stream, item),
            send_sem=self.send_sem.at[stream, self.count[stream]],
            recv_sem=self.recv_sem.at[stream, item],
            device_id=(target, self.uly),
            device_id_type=MESH,
        )
        self.count[stream] += 1
        copy.start()
        self.sent.append(copy)

    def wait(self, stream, item):
        ref = self.dst(stream, item)
        pltpu.make_async_remote_copy(
            src_ref=ref,
            dst_ref=ref,
            send_sem=self.send_sem.at[stream, 0],
            recv_sem=self.recv_sem.at[stream, item],
            device_id=(self.blk, self.uly),
            device_id_type=MESH,
        ).wait_recv()

    def start(self):
        for s in self.streams:
            p, q = self.pq(s)
            self.send(s, self.blk, self.at(s, 1 - self.y, p, q), self.src(s))
        for s in self.streams:
            p, q = self.pq(s)
            for d in (1, 3):
                self.send(s, self.blk, self.at(s, self.y, (p + d) % 4, q), self.src(s))
            copy = pltpu.make_async_copy(self.src(s), self.dst(s, self.blk), self.local_sem.at[s])
            copy.start()
            self.local.append(copy)

    def second(self):
        for s in self.streams:
            p, q = self.pq(s)
            item = self.at(s, 1 - self.y, p, q)
            self.wait(s, item)
            for d in (1, 3):
                self.send(s, item, self.at(s, self.y, (p + d) % 4, q))
            for d in (1, 3):
                onward = self.at(s, self.y, p, (q + d) % 4)
                self.send(s, self.blk, onward, self.src(s))
                self.send(s, item, onward)

    def spread(self, s, item):
        p, q = self.pq(s)
        for d in (1, 3):
            self.send(s, item, self.at(s, self.y, p, (q + d) % 4))

    def third(self):
        for k, y in enumerate((self.y, 1 - self.y)):
            for s in self.streams:
                p, q = self.pq(s)
                for d in (3, 1):
                    item = self.at(s, y, (p + d) % 4, q)
                    self.wait(s, item)
                    if (d == 3) == (k == 0):
                        self.send(s, item, self.at(s, self.y, (p + 4 - d) % 4, q))
                    self.spread(s, item)
        for y in (self.y, 1 - self.y):
            for s in self.streams:
                p, q = self.pq(s)
                item = self.at(s, y, (p + 2) % 4, q)
                self.wait(s, item)
                self.spread(s, item)

    def fourth(self):
        for e in (0, 1, 3, 2):
            for k, y in enumerate((self.y, 1 - self.y)):
                for s in self.streams:
                    p, q = self.pq(s)
                    for d in (3, 1):
                        item = self.at(s, y, (p + e) % 4, (q + d) % 4)
                        self.wait(s, item)
                        if (d == 3) == (k == 0):
                            self.send(s, item, self.at(s, self.y, p, (q + 4 - d) % 4))

    def last(self):
        for e in (0, 1, 3, 2):
            for y in (self.y, 1 - self.y):
                for s in self.streams:
                    p, q = self.pq(s)
                    self.wait(s, self.at(s, y, (p + e) % 4, (q + 2) % 4))
        for copy in self.local:
            copy.wait()
        for copy in self.sent:
            copy.wait_send()


GATHER_SEMS = lambda *lead: [
    pltpu.SemaphoreType.DMA(lead + (2, Gather.sends)),
    pltpu.SemaphoreType.DMA(lead + (2, 32)),
    pltpu.SemaphoreType.DMA(lead + (2,)),
]


KEYS = 512
STEP = KEYS // CHUNK
ROWS = GROUP * CHUNK


def head_columns(ref, slot):
    return jnp.concatenate(
        [
            ref[slot * CHUNK : (slot + 1) * CHUNK, n * HEAD : (n + 1) * HEAD].T
            for n in range(GROUP)
        ],
        axis=1,
    )


def head_rows(ref, slot):
    return jnp.concatenate(
        [
            ref[slot * CHUNK : (slot + 1) * CHUNK, n * HEAD : (n + 1) * HEAD]
            for n in range(GROUP)
        ],
        axis=0,
    )


def key_block(kv_ref, step):
    rows = kv_ref[pl.ds(step * STEP, STEP)].reshape(KEYS, 2 * HEAD)
    return rows[:, :HEAD], rows[:, HEAD:]


def dot(a, b):
    return jnp.dot(a, b, preferred_element_type=F32)


def key_places(step):
    return lax.broadcasted_iota(jnp.int32, (KEYS, ROWS), 0) + step * KEYS


def dot_nt(a, b):
    return lax.dot_general(a, b, (((1,), (1,)), ((), ())), preferred_element_type=F32)


def forward_slot(slot, chunk, part, q_ref, kv_ref, limit_ref, mixed_ref, lse_ref, acc_ref, stat_ref):
    turned = head_columns(q_ref, slot)
    limit = limit_ref[slot, 0:1, :]
    if part == 0:
        acc_ref[...] = jnp.zeros_like(acc_ref)
        stat_ref[0] = jnp.full(stat_ref.shape[1:], -1e30, F32)
        stat_ref[1] = jnp.zeros(stat_ref.shape[1:], F32)

    def step(n, carry):
        top, total = carry
        keys, values = key_block(kv_ref, n)
        scores = jnp.where(key_places(n) <= limit, dot(keys, turned), -1e30)
        new_top = jnp.maximum(top, jnp.max(scores, axis=0, keepdims=True))
        fade = jnp.exp2(top - new_top)
        probs = jnp.exp2(scores - new_top)
        total = total * fade + jnp.sum(probs, axis=0, keepdims=True)
        acc_ref[...] = acc_ref[...] * fade + dot(values.T, probs.astype(BF))
        return new_top, total

    blocks = chunk // STEP + 1
    top, total = lax.fori_loop(
        blocks * part // 4, blocks * (part + 1) // 4, step, (stat_ref[0, 0:1, :], stat_ref[1, 0:1, :])
    )
    if part < 3:
        stat_ref[0, 0:1, :] = top
        stat_ref[1, 0:1, :] = total
        return
    out = acc_ref[...] / total
    for n in range(GROUP):
        mixed_ref[slot * CHUNK : (slot + 1) * CHUNK, n * HEAD : (n + 1) * HEAD] = out[
            :, n * CHUNK : (n + 1) * CHUNK
        ].T.astype(BF)
    lse_ref[slot] = jnp.broadcast_to(top + jnp.log2(total), (8, ROWS))


def uly_others():
    y, z, x, blk, uly = place()
    return [(blk, (uly + 2) % 4), (blk, uly + 1 - 2 * (uly % 2)), (blk, 3 - uly)]


def ring_place(w):
    y, z, x, blk, uly = place()
    return (blk_of(w % 2, z, x), (w // 2) * 2 + uly % 2)


def ring_at():
    y, z, x, blk, uly = place()
    return (uly // 2) * 2 + y


def wait_arrival(ref, sem):
    pltpu.make_async_copy(ref, ref, sem).wait()


def remote(src, dst, send, recv, device):
    return pltpu.make_async_remote_copy(
        src_ref=src, dst_ref=dst, send_sem=send, recv_sem=recv, device_id=device, device_id_type=MESH
    )


class Deliver:
    def __init__(self):
        self.sent = []

    def send(self, src, dst, send, recv, device):
        y, z, x, blk, uly = place()
        here = jnp.logical_and(device[0] == blk, device[1] == uly)

        @pl.when(here)
        def _():
            pltpu.make_async_copy(src, dst, recv).start()

        @pl.when(jnp.logical_not(here))
        def _():
            remote(src, dst, send, recv, device).start()

        self.sent.append((here, src, dst, send, recv, device))

    def end(self):
        for here, *copy in self.sent:

            @pl.when(jnp.logical_not(here))
            def _():
                remote(*copy).wait_send()


class Ring:
    sends = 15

    def __init__(self, src, dst, y, order, way, send_sem, recv_sem):
        self.src, self.dst, self.y, self.order, self.way = src, dst, y, order, way
        self.send_sem, self.recv_sem = send_sem, recv_sem
        self.own_y, self.z, self.x, self.blk, self.uly = place()
        self.p = order * self.z + (1 - order) * self.x
        self.q = order * self.x + (1 - order) * self.z
        self.sent = []

    def at(self, y, p, q):
        order = self.order
        return blk_of(y, order * p + (1 - order) * q, order * q + (1 - order) * p)

    def index(self, p, q):
        return self.at(0, p, q)

    def send(self, p, q, dp, dq, src=None):
        ref = self.dst(self.at(self.y, p, q))
        target = self.at(self.own_y, (self.p + dp) % 4, (self.q + dq) % 4)
        copy = remote(
            ref if src is None else src, ref, self.send_sem.at[len(self.sent)],
            self.recv_sem.at[self.index(p, q)], (target, self.uly),
        )
        copy.start()
        self.sent.append(copy)

    def wait(self, p, q):
        wait_arrival(self.dst(self.at(self.y, p, q)), self.recv_sem.at[self.index(p, q)])

    def start(self):
        for d in (1, 3):
            self.send(self.p, self.q, d, 0, self.src)
        for d in (1, 3):
            self.send(self.p, self.q, 0, d, self.src)

    def third(self):
        for d in (4 - self.way, self.way):
            p = (self.p + d) % 4
            self.wait(p, self.q)
            if d == 4 - self.way:
                self.send(p, self.q, self.way, 0)
            for e in (1, 3):
                self.send(p, self.q, 0, e)

    def third_late(self):
        p = (self.p + 2) % 4
        self.wait(p, self.q)
        for e in (1, 3):
            self.send(p, self.q, 0, e)

    def fourth(self, e):
        p = (self.p + e) % 4
        for d in (4 - self.way, self.way):
            q = (self.q + d) % 4
            self.wait(p, q)
            if d == 4 - self.way:
                self.send(p, q, 0, self.way)

    def last(self):
        for e in (0, 1, 3, 2):
            self.wait((self.p + e) % 4, (self.q + 2) % 4)
        for copy in self.sent:
            copy.wait_send()


class Spread:
    def __init__(self, own, all_ref, send_sem, recv_sem, local_sem):
        self.own, self.all_ref = own, all_ref
        self.send_sem, self.recv_sem, self.local_sem = send_sem, recv_sem, local_sem
        self.w = ring_at()
        self.core = lax.axis_index("uly") % 2
        self.sibling = uly_others()[1]
        self.sent = []

    def piece(self, d, rows=slice(None), core=None):
        core = self.core if core is None else core
        ref = self.all_ref.at[core, (self.w + d) % 4]
        return ref if rows == slice(None) else ref.at[pl.ds(rows.start, rows.stop - rows.start)]

    def send(self, src, dst, recv, device):
        copy = remote(src, dst, self.send_sem.at[len(self.sent)], self.recv_sem.at[recv], device)
        copy.start()
        self.sent.append(copy)

    def pair(self, d, src=None):
        self.send(self.piece(d) if src is None else src, self.piece(d), 4 + d, self.sibling)

    def start(self):
        self.local = pltpu.make_async_copy(self.own, self.piece(0), self.local_sem)
        self.local.start()
        self.send(self.own, self.piece(0), 0, ring_place((self.w + 1) % 4))
        self.send(self.own, self.piece(0), 1, ring_place((self.w + 3) % 4))
        self.pair(0, self.own)

    def second(self):
        half = CHUNK // 2
        wait_arrival(self.piece(3), self.recv_sem.at[0])
        low = self.piece(3, slice(0, half))
        self.send(low, low, 2, ring_place((self.w + 1) % 4))
        self.pair(3)
        wait_arrival(self.piece(1), self.recv_sem.at[1])
        high = self.piece(1, slice(half, CHUNK))
        self.send(high, high, 3, ring_place((self.w + 3) % 4))
        self.pair(1)

    def third(self):
        half = CHUNK // 2
        wait_arrival(self.piece(2, slice(0, half)), self.recv_sem.at[2])
        wait_arrival(self.piece(2, slice(half, CHUNK)), self.recv_sem.at[3])
        self.pair(2)

    def last(self):
        for d in range(4):
            wait_arrival(self.piece(d, core=1 - self.core), self.recv_sem.at[4 + d])
        for copy in self.sent:
            copy.wait_send()
        self.local.wait()


SPREAD_SEMS = [pltpu.SemaphoreType.DMA((8,)), pltpu.SemaphoreType.DMA((8,)), pltpu.SemaphoreType.DMA]
FF_COLS = PADDED // 2


def forward_kernel(
    qkv_ref, out_ref, tokens_ref, cot_ref, ff_ref, limit_ref, length_ref, norm_in_ref, norm_ff_ref, bias_ref, cos_ref, sin_ref,
    a_qkv_ref, b_qkv_ref, ao_ref, bo_ref,
    q_ref, mixed_ref, lse_ref, kv_out, wq_out, wo_out, gate_all, up_all, down_all, rows_out, normed_ref,
    latent_ref, resid_ref, cot_own, nf_all, cot_all,
    kv_all, wq_all, wo_all, rows, cot_in, kv_part, acc_ref, stat_ref, qkv_in, out_in, qkv_part, out_part,
    nf_own, cross_out, cross_in,
    *sems,
):
    y, z, x, blk, uly = place()
    core, h = uly % 2, uly // 2
    sems = list(sems)

    def take(count):
        got = sems[:count]
        del sems[:count]
        return got

    chunk = 2 * blk + h
    upper = chunk // 32
    home = (1 - upper) * chunk + upper * (63 - chunk)
    row_to = [[(home, hh * 2 + s) for hh in (0, 1)] for s in (0, 1)]
    row_from = [(c // 2, (c % 2) * 2 + half) for c in (blk, 63 - blk) for half in (0, 1)]
    out_to = [(2 * (blk % 16) + q // 2, (blk // 16) * 2 + q % 2) for q in range(4)]
    out_from = [(16 * h + blk // 2, u) for u in range(4)]
    sibling = uly_others()[1]
    greet(
        ring_others() + uly_others() + [(blk_of(1 - y, z, x), (uly + 2) % 4)]
        + row_to[0] + row_to[1] + row_from + out_to + out_from
    )

    deliver = Deliver()
    piece_send, piece_recv, row_send, row_recv = take(4)
    for q in range(4):
        deliver.send(qkv_ref.at[q], qkv_in.at[uly], piece_send.at[q], piece_recv.at[uly], (blk, q))
    for q in range(4):
        deliver.send(out_ref.at[q], out_in.at[uly], piece_send.at[4 + q], piece_recv.at[4 + uly], out_to[q])
    for s in (0, 1):
        for hh in (0, 1):
            deliver.send(
                tokens_ref.at[s], rows.at[upper, core], row_send.at[s * 2 + hh],
                row_recv.at[upper * 2 + core], row_to[s][hh],
            )

    wide = PADDED // 2
    gathered = (gate_all, up_all, down_all)
    ff_send, ff_recv, y_send, y_recv, y_local = take(5)
    other_blk = blk_of(1 - y, z, x)

    def ff_part(n, half):
        return ff_ref.at[n, :, pl.ds(pl.multiple_of(half * wide, 128), wide)]

    picked = lax.broadcasted_iota(jnp.int32, (48, 64), 1)
    picked = jnp.where(picked % 16 < 12, picked // 16 * 12 + picked % 16, -1)
    picked = jnp.where(picked == lax.broadcasted_iota(jnp.int32, (48, 64), 0), 1.0, 0.0).astype(BF)
    for u in range(4):
        wait_arrival(qkv_in.at[u], piece_recv.at[u])
    qkv_part[...] = dot(picked, qkv_in[...].reshape(64, 512)).astype(BF)
    wq = Gather(
        lambda s: qkv_part.at[:, pl.ds(256 * s, 256)],
        lambda s, item: wq_all.at[
            core, pl.ds(pl.multiple_of(item * 48, 16), 48), pl.ds(256 * s, 256)
        ],
        *take(3),
    )
    wq.start()
    for u in range(4):
        wait_arrival(out_in.at[u], piece_recv.at[4 + u])
    out_part[...] = dot(picked, out_in[...].reshape(64, 384)).astype(BF)
    y_copies = []
    for n, ref in enumerate(gathered):
        copy = remote(ff_part(n, 1 - y), ref.at[blk], y_send.at[n], y_recv.at[n], (other_blk, uly))
        copy.start()
        y_copies.append(copy)
        copy = pltpu.make_async_copy(ff_part(n, y), ref.at[blk], y_local.at[n])
        copy.start()
        y_copies.append(copy)
    for s in (0, 1):
        deliver.send(
            cot_ref.at[s], cot_in.at[core], row_send.at[4 + s], row_recv.at[4 + core], (home, upper * 2 + s)
        )

    def out_columns(item, s):
        start = ((item % 2) * 2 + core) * 384
        return pl.ds(pl.multiple_of(start + 128 * s, 128), 128 + 128 * s)

    wo = Gather(
        lambda s: out_part.at[:, pl.ds(128 * s, 128 + 128 * s)],
        lambda s, item: wo_all.at[pl.ds(pl.multiple_of((item // 2) * 48, 16), 48), out_columns(item, s)],
        *take(3),
    )
    own_ff, other_ff = (
        [
            Ring(
                ff_part(n, y) if k == 0 else ref.at[other_blk],
                lambda item, ref=ref: ref.at[item],
                y if k == 0 else 1 - y,
                y if k == 0 else 1 - y,
                (1, 3, 1 + 2 * k)[n],
                ff_send.at[k, n], ff_recv.at[k, n],
            )
            for n, ref in enumerate(gathered)
        ]
        for k in (0, 1)
    )
    wq.second()
    for ring in own_ff:
        ring.start()

    for n in range(4):
        wait_arrival(rows.at[n // 2, n % 2], row_recv.at[n])
        value = rows[n // 2, n % 2].astype(F32)
        at = slice(n * 64, (n + 1) * 64)
        rows_out[at, :] = rows[n // 2, n % 2]
        normed_ref[at, :] = (value * norm_scale(value) * norm_in_ref[...]).astype(BF)
    latent = dot_nt(normed_ref[...], a_qkv_ref[...])
    latent_ref[...] = latent
    wq.third()
    wo.start()
    wq.fourth()
    wo.second()
    for n in range(3):
        y_copies[2 * n].wait_recv()
    for ring in other_ff:
        ring.start()
    wq.last()
    pair_send, pair_recv = take(2)

    def pair_copy(ref, n):
        return remote(ref, ref, pair_send.at[n], pair_recv.at[n], sibling)

    pair_copy(wq_all.at[core], 0).start()
    wo.third()
    pair_copy(wq_all.at[core], 0).wait_send()
    pair_copy(wq_all.at[1 - core], 0).wait_recv()

    adapted = dot(latent.astype(BF), b_qkv_ref[...]) + bias_ref[...]
    cos_table, sine_table = cos_ref[...], sin_ref[...]
    for c in (0, 1):
        columns = dot(normed_ref[...], wq_all[c]) + adapted[:, c * 512 : (c + 1) * 512]
        for n in range(4):
            head = columns[:, n * HEAD : (n + 1) * HEAD]
            if c * 4 + n < GROUP + 1:
                head = head * cos_table + pltpu.roll(head, HEAD // 2, 1) * sine_table
            if c * 4 + n < GROUP:
                at = (c * 4 + n) * HEAD
                q_ref[:, at : at + HEAD] = (head * (HEAD ** (-0.5) * LOG2E)).astype(BF)
            else:
                at = (n - 2) * HEAD
                kv_part[0, :, at : at + HEAD] = head[:CHUNK].astype(BF)
                kv_part[1, :, at : at + HEAD] = head[CHUNK:].astype(BF)
    kv = Gather(
        lambda s: kv_part.at[s],
        lambda s, item: kv_all.at[item if s == 0 else 63 - item],
        *take(3),
    )
    kv.start()
    for ring in own_ff:
        ring.third()
    kv.second()
    for ring in own_ff:
        ring.third_late()
    for ring in other_ff:
        ring.third()
    kv.third()
    wo.fourth()
    for ring in other_ff:
        ring.third_late()
    kv.fourth()

    for half in (0, 1):
        wait_arrival(cot_in.at[half], row_recv.at[4 + half])
        start = ((1 - h) * blk + h * (63 - blk)) * CHUNK + half * 64
        at = lax.broadcasted_iota(jnp.int32, (64, D), 0) + start
        cot_own[half * 64 : (half + 1) * 64, :] = jnp.where(
            at < length_ref[...], cot_in[half].astype(F32), 0.0
        ).astype(BF)
    cot_spread = Spread(cot_own, cot_all, *take(3))
    cot_spread.start()
    kv.last()
    (out_sem,) = take(1)
    copies = [
        pltpu.make_async_copy(src, dst, out_sem.at[n])
        for n, (src, dst) in enumerate(((kv_all, kv_out), (wq_all, wq_out), (wo_all, wo_out)))
    ]
    copies[0].start()
    copies[1].start()
    wo.last()

    def wo_columns(c, n):
        return wo_all.at[:, pl.ds(pl.multiple_of((2 * n + c) * 384, 128), 384)]

    for n in (0, 1):
        pair_copy(wo_columns(core, n), 1 + n).start()
    args = (q_ref, kv_all, limit_ref, mixed_ref, lse_ref, acc_ref, stat_ref)
    beside = [
        lambda: [ring.fourth(0) for ring in own_ff],
        lambda: [ring.fourth(0) for ring in other_ff] + [cot_spread.second()],
        lambda: [ring.fourth(1) for ring in own_ff],
        lambda: [ring.fourth(1) for ring in other_ff] + [cot_spread.third()],
        lambda: [ring.fourth(3) for ring in own_ff],
        lambda: [ring.fourth(3) for ring in other_ff],
        lambda: [ring.fourth(2) for ring in own_ff],
        lambda: [ring.fourth(2) for ring in other_ff],
    ]
    for slot, at in ((0, blk), (1, 63 - blk)):
        for part in range(4):
            forward_slot(slot, at, part, *args)
            beside.pop(0)()
    for n in (0, 1):
        pair_copy(wo_columns(core, n), 1 + n).wait_send()
        pair_copy(wo_columns(1 - core, n), 1 + n).wait_recv()
    copies[2].start()

    def project(slot):
        mixed = mixed_ref[pl.ds(pl.multiple_of(slot * CHUNK, CHUNK), CHUNK), :]
        lifted = dot(dot_nt(mixed, ao_ref[...]).astype(BF), bo_ref[...])
        return dot(mixed, wo_all[...]) + lifted

    (cross_sem,) = take(1)
    cross_out[...] = project(1 - h).astype(BF)
    cross = remote(cross_out, cross_in, cross_sem.at[0], cross_sem.at[1], uly_others()[0])
    cross.start()
    mine = project(h) + rows_out[pl.ds(pl.multiple_of(h * CHUNK, CHUNK), CHUNK), :].astype(F32)
    cross.wait()
    residual = mine + cross_in[...].astype(F32)
    resid_ref[...] = residual
    nf_own[...] = (residual * norm_scale(residual) * norm_ff_ref[...]).astype(BF)
    nf_spread = Spread(nf_own, nf_all, *take(3))
    nf_spread.start()
    nf_spread.second()
    nf_spread.third()
    nf_spread.last()
    cot_spread.last()
    for ring in own_ff + other_ff:
        ring.last()
    for n in range(3):
        y_copies[2 * n].wait_send()
        y_copies[2 * n + 1].wait()
    deliver.end()
    for copy in copies:
        copy.wait()


def forward(*args):
    weight = jax.ShapeDtypeStruct((32, 48, FF_COLS), BF)
    group = GROUP * HEAD
    dma = pltpu.SemaphoreType.DMA
    spread = jax.ShapeDtypeStruct((2, 4, CHUNK, D), BF)
    return pl.pallas_call(
        forward_kernel,
        out_shape=(
            jax.ShapeDtypeStruct((2 * CHUNK, group), BF),
            jax.ShapeDtypeStruct((2 * CHUNK, group), BF),
            jax.ShapeDtypeStruct((2, 8, ROWS), F32),
            jax.ShapeDtypeStruct((CHUNKS, CHUNK, 2 * HEAD), BF),
            jax.ShapeDtypeStruct((2, D, 512), BF),
            jax.ShapeDtypeStruct((D // 2, D), BF),
            weight, weight, weight,
            jax.ShapeDtypeStruct((2 * CHUNK, D), BF),
            jax.ShapeDtypeStruct((2 * CHUNK, D), BF),
            jax.ShapeDtypeStruct((2 * CHUNK, 48), F32),
            jax.ShapeDtypeStruct((CHUNK, D), F32),
            jax.ShapeDtypeStruct((CHUNK, D), BF),
            spread, spread,
        ),
        in_specs=[ANY] * 5 + [IN_VMEM] * 11,
        out_specs=(IN_VMEM,) * 3 + (ANY,) * 6 + (IN_VMEM,) * 5 + (ANY,) * 2,
        scratch_shapes=[
            pltpu.VMEM((CHUNKS, CHUNK, 2 * HEAD), BF),
            pltpu.VMEM((2, D, 512), BF),
            pltpu.VMEM((D // 2, D), BF),
            pltpu.VMEM((2, 2, 64, D), BF),
            pltpu.VMEM((2, 64, D), BF),
            pltpu.VMEM((2, CHUNK, 2 * HEAD), BF),
            pltpu.VMEM((HEAD, ROWS), F32),
            pltpu.VMEM((2, 8, ROWS), F32),
            pltpu.VMEM((4, 16, 512), BF),
            pltpu.VMEM((4, 16, 384), BF),
            pltpu.VMEM((48, 512), BF),
            pltpu.VMEM((48, 384), BF),
            pltpu.VMEM((CHUNK, D), BF),
            pltpu.VMEM((CHUNK, D), BF),
            pltpu.VMEM((CHUNK, D), BF),
            dma((8,)), dma((8,)), dma((6,)), dma((6,)),
            dma((2, 3, Ring.sends)), dma((2, 3, 16)), dma((3,)), dma((3,)), dma((3,)),
        ]
        + GATHER_SEMS()
        + GATHER_SEMS()
        + [dma((3,)), dma((3,))]
        + GATHER_SEMS()
        + SPREAD_SEMS
        + [dma((3,)), dma((2,))]
        + SPREAD_SEMS,
        compiler_params=pltpu.CompilerParams(
            collective_id=1, has_side_effects=True, vmem_limit_bytes=48 * 2**20
        ),
        name="forward",
    )(*args)


class Collect:
    @staticmethod
    def scratch():
        piece, half = (CHUNK, D), (CHUNK // 2, D)
        return [
            pltpu.VMEM((4,) + piece, BF),
            pltpu.VMEM((4,) + piece, BF),
            pltpu.VMEM((2,) + half, BF),
            pltpu.VMEM((2,) + piece, BF),
            pltpu.VMEM(piece, BF),
            pltpu.VMEM((2,) + piece, BF),
            pltpu.SemaphoreType.DMA((8,)),
            pltpu.SemaphoreType.DMA((8,)),
            pltpu.SemaphoreType.DMA,
        ]

    scratches = 9

    def __init__(self, src, scratch):
        self.src = src
        (
            self.mine, self.pair, self.halves, self.last_in, self.far, self.near,
            self.send_sem, self.recv_sem, self.local_sem,
        ) = scratch
        self.w = ring_at()
        self.core = lax.axis_index("uly") % 2
        self.sent = []

    def send(self, src, dst, recv, device):
        copy = remote(src, dst, self.send_sem.at[recv], self.recv_sem.at[recv], device)
        copy.start()
        self.sent.append(copy)

    def start(self):
        self.local = pltpu.make_async_copy(self.src.at[self.core], self.mine, self.local_sem)
        self.local.start()
        for d in (2, 1, 3, 0):
            at = (self.w + d) % 4
            self.send(self.src.at[1 - self.core, at], self.pair.at[at], d, uly_others()[1])

    def both(self, d):
        at = (self.w + d) % 4
        wait_arrival(self.pair.at[at], self.recv_sem.at[d])
        return self.mine[at].astype(F32) + self.pair[at].astype(F32)

    def second(self):
        half = CHUNK // 2
        self.local.wait()
        self.far[...] = self.both(2).astype(BF)
        self.send(self.far.at[pl.ds(0, half)], self.halves.at[0], 4, ring_place((self.w + 1) % 4))
        self.send(self.far.at[pl.ds(half, half)], self.halves.at[1], 5, ring_place((self.w + 3) % 4))

    def third(self):
        half = CHUNK // 2
        for k, d in ((0, 1), (1, 3)):
            total = self.both(d)
            wait_arrival(self.halves.at[k], self.recv_sem.at[4 + k])
            rows = slice(k * half, (k + 1) * half)
            other = slice((1 - k) * half, (2 - k) * half)
            self.near[k, rows] = (total[rows] + self.halves[k].astype(F32)).astype(BF)
            self.near[k, other] = total[other].astype(BF)
            self.send(self.near.at[k], self.last_in.at[k], 6 + k, ring_place((self.w + d) % 4))

    def fourth(self):
        total = self.both(0)
        for k in (0, 1):
            wait_arrival(self.last_in.at[k], self.recv_sem.at[6 + k])
            total += self.last_in[k].astype(F32)
        for copy in self.sent:
            copy.wait_send()
        return total


def collect_kernel(a_ref, b_ref, a_out, b_out, *scratch):
    y, z, x, blk, uly = place()
    greet([uly_others()[1], (blk_of(1 - y, z, x), uly), (blk_of(1 - y, z, x), (uly + 2) % 4)])
    a = Collect(a_ref, scratch[: Collect.scratches])
    b = Collect(b_ref, scratch[Collect.scratches :])
    a.start()
    a.second()
    a.third()
    b.start()
    a_out[...] = a.fourth()
    b.second()
    b.third()
    b_out[...] = b.fourth()


def collect(a, b):
    out = jax.ShapeDtypeStruct((CHUNK, D), F32)
    return pl.pallas_call(
        collect_kernel,
        out_shape=(out, out),
        in_specs=[ANY, ANY],
        out_specs=(IN_VMEM, IN_VMEM),
        scratch_shapes=Collect.scratch() * 2,
        compiler_params=pltpu.CompilerParams(
            collective_id=4, has_side_effects=True, vmem_limit_bytes=24 * 2**20
        ),
        name="collect",
    )(a, b)


def backward_slot(
    slot, chunk, part, q_ref, kv_ref, limit_ref, mixed_ref, grad_ref, lse_ref, dq_ref, dkv_ref, acc_ref
):
    turned = head_columns(q_ref, slot)
    rows = head_rows(q_ref, slot)
    grad_turned = head_columns(grad_ref, slot)
    grad_rows = head_rows(grad_ref, slot)
    mixed_turned = head_columns(mixed_ref, slot)
    row_dot = jnp.sum(
        grad_turned.astype(F32) * mixed_turned.astype(F32), axis=0, keepdims=True
    )
    limit = limit_ref[slot, 0:1, :]
    lse = lse_ref[slot, 0:1, :]
    if part == 0:
        acc_ref[...] = jnp.zeros_like(acc_ref)

    def step(n, carry):
        keys, values = key_block(kv_ref, n)
        scores = jnp.where(key_places(n) <= limit, dot(keys, turned), -1e30)
        probs = jnp.exp2(scores - lse)
        grad_probs = dot(values, grad_turned)
        grad_scores = (probs * (grad_probs - row_dot)).astype(BF)
        acc_ref[...] += dot(keys.T, grad_scores)
        at = pl.ds(pl.multiple_of(n * KEYS, KEYS), KEYS)
        dkv_ref[at, :HEAD] += dot(grad_scores, rows)
        dkv_ref[at, HEAD:] += dot(probs.astype(BF), grad_rows)
        return carry

    blocks = chunk // STEP + 1
    lax.fori_loop(blocks * part // 4, blocks * (part + 1) // 4, step, 0)
    if part == 3:
        for n in range(GROUP):
            dq_ref[slot * CHUNK : (slot + 1) * CHUNK, n * HEAD : (n + 1) * HEAD] = (
                acc_ref[:, n * CHUNK : (n + 1) * CHUNK].T * HEAD ** (-0.5)
            )


class Reduce:
    sends = 28

    @staticmethod
    def scratch(shape):
        return [
            pltpu.VMEM((2, 3, 2, 4) + shape, BF),
            pltpu.VMEM((2, 3, 2) + shape, BF),
            pltpu.VMEM((2,) + shape, BF),
            pltpu.VMEM((2, 4, 2) + shape, BF),
            pltpu.VMEM((2, 2) + shape, BF),
            pltpu.SemaphoreType.DMA((2, Reduce.sends)),
            pltpu.SemaphoreType.DMA((2, Reduce.sends)),
        ]

    def __init__(self, part, index, scratch):
        self.part, self.index = part, index
        self.buf_q, self.buf_p, self.buf_y, self.sum_p, self.sum_y, self.send_sem, self.recv_sem = scratch
        self.y, self.z, self.x, self.blk, self.uly = place()
        self.pq = ((self.x, self.z), (self.z, self.x))
        self.flying = []

    def at(self, half, y, p, q):
        return blk_of(y, q, p) if half == 0 else blk_of(y, p, q)

    def send(self, src, dst, half, n, y, p, q):
        copy = pltpu.make_async_remote_copy(
            src_ref=src, dst_ref=dst,
            send_sem=self.send_sem.at[half, n], recv_sem=self.recv_sem.at[half, n],
            device_id=(self.at(half, y, p, q), self.uly), device_id_type=MESH,
        )
        copy.start()
        self.flying.append(copy)

    def land(self):
        for copy in self.flying:
            copy.wait()
        self.flying = []

    def first(self):
        for d in (2, 1, 3):
            for half in (0, 1):
                p, q = self.pq[half]
                to = (q + d) % 4
                for y in (0, 1):
                    for pp in range(4):
                        self.send(
                            self.part.at[self.index(half, self.at(half, y, pp, to))],
                            self.buf_q.at[half, d - 1, y, pp],
                            half, (d - 1) * 8 + y * 4 + pp, self.y, p, to,
                        )

    def second(self):
        self.land()
        for d in (2, 1, 3, 0):
            for half in (0, 1):
                p, q = self.pq[half]
                to = (p + d) % 4
                for y in (0, 1):
                    total = self.part[self.index(half, self.at(half, y, to, q))].astype(F32)
                    for n in range(3):
                        total += self.buf_q[half, n, y, to].astype(F32)
                    self.sum_p[half, d, y] = total.astype(BF)
                if d > 0:
                    self.send(
                        self.sum_p.at[half, d], self.buf_p.at[half, d - 1], half, 23 + d, self.y, to, q
                    )

    def third(self):
        self.land()
        for k in (1, 0):
            for half in (0, 1):
                p, q = self.pq[half]
                y = self.y if k == 0 else 1 - self.y
                total = self.sum_p[half, 0, y].astype(F32)
                for n in range(3):
                    total += self.buf_p[half, n, y].astype(F32)
                self.sum_y[half, k] = total.astype(BF)
                if k == 1:
                    self.send(self.sum_y.at[half, 1], self.buf_y.at[half], half, 27, 1 - self.y, p, q)

    def fourth(self):
        self.land()
        return [self.sum_y[half, 0].astype(F32) + self.buf_y[half].astype(F32) for half in (0, 1)]


def reduce_others():
    y, z, x, blk, uly = place()
    return (
        [(blk_of(1 - y, z, x), uly)]
        + [(blk_of(y, z, (x + d) % 4), uly) for d in (1, 2, 3)]
        + [(blk_of(y, (z + d) % 4, x), uly) for d in (1, 2, 3)]
    )


UNIT = (16, 128)


class Total:
    @staticmethod
    def scratch(kept, summed):
        shape = (kept + summed,) + UNIT
        return (
            [pltpu.VMEM((64,) + shape, BF)]
            + Reduce.scratch(shape)
            + [
                pltpu.VMEM((2,) + shape, BF),
                pltpu.VMEM((3, 2) + shape, BF),
                pltpu.VMEM((2, 4 * kept + summed) + UNIT, BF),
                pltpu.SemaphoreType.DMA((3,)),
                pltpu.SemaphoreType.DMA((3,)),
                pltpu.SemaphoreType.DMA((1, Gather.sends)),
                pltpu.SemaphoreType.DMA((1, 32)),
                pltpu.SemaphoreType.DMA((1,)),
                pltpu.SemaphoreType.DMA,
                pltpu.SemaphoreType.DMA,
            ]
        )

    scratches = 18

    @staticmethod
    def shape(kept, summed):
        return jax.ShapeDtypeStruct((2, 32, 4 * kept + summed) + UNIT, BF)

    def __init__(self, kept, summed, all_ref, scratch):
        self.kept, self.summed, self.all_ref = kept, summed, all_ref
        self.part = scratch[0]
        self.reduce = Reduce(self.part, lambda half, item: half * 32 + item, scratch[1:8])
        self.own, self.buf, self.full, self.send_sem, self.recv_sem = scratch[8:13]
        self.pair_send, self.pair_recv = scratch[16:18]
        self.y, self.z, self.x, self.blk, self.uly = place()
        self.core = self.uly % 2
        self.gather = Gather(
            lambda s: self.full.at[self.core],
            lambda s, item: self.all_ref.at[self.core, item],
            *scratch[13:16],
            orders=(self.core,),
        )

    def pack(self, kept, summed):
        for n in range(64 * self.kept):
            self.part[n // self.kept, n % self.kept] = (
                kept[n].astype(BF) if n < len(kept) else jnp.zeros(UNIT, BF)
            )
        for n in range(64 * self.summed):
            self.part[n // self.summed, self.kept + n % self.summed] = (
                summed[n].astype(BF) if n < len(summed) else jnp.zeros(UNIT, BF)
            )

    def across(self):
        for half, total in enumerate(self.reduce.fourth()):
            self.own[half] = total.astype(BF)
        self.copies = []
        for n, other in enumerate(uly_others()):
            copy = pltpu.make_async_remote_copy(
                src_ref=self.own, dst_ref=self.buf.at[n],
                send_sem=self.send_sem.at[n], recv_sem=self.recv_sem.at[n],
                device_id=other, device_id_type=MESH,
            )
            copy.start()
            self.copies.append(copy)

    def join(self):
        for copy in self.copies:
            copy.wait()
        kept = self.kept
        terms = [self.own] + [self.buf.at[n] for n in range(3)]
        who = [self.uly] + [other[1] for other in uly_others()]
        for half in (0, 1):
            for term, uly in zip(terms, who):
                self.full[half, pl.ds(uly * kept, kept)] = term[half, :kept]
            if self.summed:
                self.full[half, 4 * kept :] = sum(
                    term[half, kept:].astype(F32) for term in terms
                ).astype(BF)
        self.gather.start()

    def hand(self):
        self.gather.last()
        self.pair(self.core).start()

    def pair(self, core):
        return pltpu.make_async_remote_copy(
            src_ref=self.all_ref.at[core], dst_ref=self.all_ref.at[core],
            send_sem=self.pair_send, recv_sem=self.pair_recv,
            device_id=uly_others()[1], device_id_type=MESH,
        )

    def end(self):
        self.pair(self.core).wait_send()
        self.pair(1 - self.core).wait_recv()

    def steps(self):
        return [
            self.reduce.first, self.reduce.second, self.reduce.third, self.across, self.join,
            self.gather.second, self.gather.third, self.gather.fourth, self.hand, self.end,
        ]


def units(ref, tiles):
    return [
        ref[n, :, t * 128 : (t + 1) * 128] for n in range(ref.shape[0]) for t in range(tiles)
    ]


FF_KEPT, FF_SUMMED = 2, 2
COL_TILES = PADDED // 128
D_TILES = D // 128


def backward_kernel(
    q_ref, kv_ref, limit_ref, mixed_ref, grad_ref, lse_ref, cols_ref, oa_ref, ob_ref, ff_ref,
    dq_ref, own_ref, all_ref, dkv_ref, acc_ref, part, *scratch,
):
    y, z, x, blk, uly = place()
    greet(reduce_others() + uly_others())
    reduce = Reduce(
        part, lambda half, item: item if half == 0 else 63 - item, scratch[:7]
    )
    total = Total(FF_KEPT, FF_SUMMED, all_ref, scratch[7:])
    total.pack(
        units(cols_ref, COL_TILES) + units(oa_ref, D_TILES // 2) + units(ob_ref, D_TILES),
        units(ff_ref, D_TILES),
    )
    steps = total.steps()
    steps.pop(0)()
    dkv_ref[...] = jnp.zeros_like(dkv_ref)
    args = (q_ref, kv_ref, limit_ref, mixed_ref, grad_ref, lse_ref, dq_ref, dkv_ref, acc_ref)
    for slot, chunk in ((0, blk), (1, 63 - blk)):
        for part_of in range(4):
            backward_slot(slot, chunk, part_of, *args)
            if steps:
                steps.pop(0)()

    def pack(n, carry):
        rows = dkv_ref[pl.ds(pl.multiple_of(n * CHUNK, CHUNK), CHUNK), :]
        part[n] = jnp.concatenate([rows[:, :HEAD] * LN2, rows[:, HEAD:]], axis=1).astype(BF)
        return carry

    lax.fori_loop(0, CHUNKS, pack, 0)
    reduce.first()
    while steps:
        steps.pop(0)()
    reduce.second()
    reduce.third()
    for half, value in enumerate(reduce.fourth()):
        own_ref[half] = value


def attend_backward(q, kv, limit, mixed, grad, lse, cols, oa, ob, ff):
    return pl.pallas_call(
        backward_kernel,
        out_shape=(
            jax.ShapeDtypeStruct((2 * CHUNK, GROUP * HEAD), F32),
            jax.ShapeDtypeStruct((2, CHUNK, 2 * HEAD), F32),
            Total.shape(FF_KEPT, FF_SUMMED),
        ),
        in_specs=[IN_VMEM] * 10,
        out_specs=(IN_VMEM, IN_VMEM, ANY),
        scratch_shapes=[
            pltpu.VMEM((CHUNKS * CHUNK, 2 * HEAD), F32),
            pltpu.VMEM((HEAD, ROWS), F32),
            pltpu.VMEM((CHUNKS, CHUNK, 2 * HEAD), BF),
        ]
        + Reduce.scratch((CHUNK, 2 * HEAD))
        + Total.scratch(FF_KEPT, FF_SUMMED),
        compiler_params=pltpu.CompilerParams(
            collective_id=2, has_side_effects=True, vmem_limit_bytes=56 * 2**20
        ),
        name="attend_backward",
    )(q, kv, limit, mixed, grad, lse, cols, oa, ob, ff)


QKV_KEPT = 1


def qkv_total_kernel(a_ref, bq_ref, bkv_ref, all_ref, *scratch):
    greet(reduce_others() + uly_others())
    total = Total(QKV_KEPT, 0, all_ref, scratch)
    total.pack(units(a_ref, D_TILES) + units(bq_ref, D_TILES // 2) + units(bkv_ref, 1), [])
    for step in total.steps():
        step()


def qkv_total(a, bq, bkv):
    return pl.pallas_call(
        qkv_total_kernel,
        out_shape=Total.shape(QKV_KEPT, 0),
        in_specs=[IN_VMEM] * 3,
        out_specs=ANY,
        scratch_shapes=Total.scratch(QKV_KEPT, 0),
        compiler_params=pltpu.CompilerParams(
            collective_id=3, has_side_effects=True, vmem_limit_bytes=24 * 2**20
        ),
        name="qkv_total",
    )(a, bq, bkv)


def fold_kernel(pick_ref, ff_ref, qkv_ref, a_wide, a_down, b_wide, b_kv, b_ff):
    c = pl.program_id(0)

    def kept(ref, per, n, u):
        return ref[n // per // 32, n // per % 32, u * per + n % per].astype(F32)

    def ff_kept(n, u):
        return kept(ff_ref, FF_KEPT, n, u)

    def qkv_kept(n, u):
        return kept(qkv_ref, QKV_KEPT, n, u)

    def summed(n):
        item = n // FF_SUMMED
        return ff_ref[item // 32, item % 32, 4 * FF_KEPT + n % FF_SUMMED].astype(F32)

    def put(ref, at, tile, value):
        ref[at + (slice(None), slice(tile * 128, (tile + 1) * 128))] = (
            pick_ref[c, 0] * value(0) + pick_ref[c, 1] * value(1)
        )

    for n in range(3):
        for t in range(D_TILES):
            put(a_wide, (n, 0), t, lambda s: qkv_kept(n * D_TILES + t, s) + qkv_kept(n * D_TILES + t, 2 + s))
    at_o = 6 * COL_TILES
    half = D_TILES // 2
    for t in range(D_TILES):
        h, part = t // half, t % half
        put(a_wide, (3, 0), t, lambda s: ff_kept(at_o + part, 2 * h + s))
        put(b_wide, (0, 0), t, lambda s: qkv_kept(3 * D_TILES + part, 2 * h + s))
        put(
            b_wide, (1, 0), t,
            lambda s: ff_kept(at_o + half + t, s) + ff_kept(at_o + half + t, 2 + s),
        )
        for n, (ref, at) in enumerate(((a_wide, (4, 0)), (a_wide, (5, 0)), (b_wide, (2, 0)))):
            put(ref, at, t, lambda s: summed((2 * n + s) * D_TILES + t))
    for n in (0, 1):
        for h in (0, 1):
            put(b_kv, (n, 0), h, lambda s: qkv_kept(3 * D_TILES + half + n, 2 * h + s))
    for n, (ref, at) in enumerate(((a_down, (0,)), (b_ff, (0, 0)), (b_ff, (1, 0)))):
        for t in range(FF // 128):
            where = [
                (u, t - start) for u, start in enumerate((0, 17, 35, 52)) if 0 <= t - start < COL_TILES
            ]
            put(
                ref, at, t,
                lambda s: sum(ff_kept((2 * n + s) * COL_TILES + tile, u) for u, tile in where),
            )


def fold(pick, ff_all, qkv_all):
    def whole(v):
        return pl.BlockSpec(v.shape, lambda c: (0,) * v.ndim)

    def by_set(lead, columns):
        shape = lead + (1, 16, columns)
        return pl.BlockSpec(shape, lambda c: (0,) * len(lead) + (c, 0, 0))

    def out(lead, columns):
        return jax.ShapeDtypeStruct(lead + (SETS, 16, columns), F32)

    outs = (((6,), D), ((), FF), ((3,), D), ((2,), 2 * HEAD), ((2,), FF))
    return pl.pallas_call(
        fold_kernel,
        grid=(SETS,),
        out_shape=tuple(out(*o) for o in outs),
        in_specs=[pl.BlockSpec(memory_space=pltpu.SMEM), whole(ff_all), whole(qkv_all)],
        out_specs=tuple(by_set(*o) for o in outs),
        compiler_params=pltpu.CompilerParams(vmem_limit_bytes=40 * 2**20),
        name="fold",
    )(pick, ff_all, qkv_all)


def device_at(blk, h, core):
    return blk * 4 + h * 2 + core


def moves():
    def home(blk, h):
        chunk = 2 * blk + h
        return (chunk, 0) if chunk < 32 else (63 - chunk, 1)

    return [
        [
            (device_at(home(b, h)[0], home(b, h)[1], c ^ j), device_at(b, h, c))
            for b in range(32) for h in (0, 1) for c in (0, 1)
        ]
        for j in (0, 1)
    ]


ALL = ("blk", "uly")
OVER_H = [(0, 2), (2, 0), (1, 3), (3, 1)]
OVER_CORE = [(0, 1), (1, 0), (2, 3), (3, 2)]
OVER_BOTH = [(0, 3), (3, 0), (1, 2), (2, 1)]


def flip(parts, first, second):
    return jnp.where(parts, second, first), jnp.where(parts, first, second)


def rope_tables(positions):
    halves = jnp.arange(0, HEAD, 2, dtype=jnp.int32).astype(F32)
    freq_table = THETA ** (-halves / HEAD)
    angles = positions.astype(F32)[:, None] * freq_table[None, :]
    angles = jnp.concatenate([angles, angles], axis=-1)
    return jnp.cos(angles), jnp.sin(angles)


def rope_turn(values, cos_table, sine_table):
    middle = HEAD // 2
    turned = jnp.concatenate([-values[..., middle:], values[..., :middle]], axis=-1)
    return values * cos_table + turned * sine_table


def rope_back(values, cos_table, sine_table):
    middle = HEAD // 2
    turned = jnp.concatenate([values[..., middle:], -values[..., :middle]], axis=-1)
    return values * cos_table + turned * sine_table


def norm_scale(hidden):
    return lax.rsqrt(jnp.mean(hidden * hidden, axis=-1, keepdims=True) + EPS)


def norm_back(hidden, scaled, gain_vec, upstream):
    normed = hidden * scaled
    weighted = upstream * gain_vec
    return scaled * (weighted - normed * jnp.mean(weighted * normed, axis=-1, keepdims=True))


def mm(spec, a, b):
    return jnp.einsum(spec, a.astype(BF), b.astype(BF), preferred_element_type=F32)


def body(
    tokens, cotangent, lengths, set_index, norm_in, norm_ff, qkv_bias, w_qkv, w_out, w_gate_up, w_down,
    a_wide, a_down, b_wide, b_kv, b_ff,
):
    blk = lax.axis_index("blk")
    uly = lax.axis_index("uly")
    h = uly // 2
    core = uly % 2
    y_lo = blk // 16
    back_moves = moves()
    local_ff = w_down.shape[0]
    group_cols = GROUP * HEAD
    zero = jnp.zeros

    def pick_set(table, axis, at):
        return lax.dynamic_index_in_dim(table, at, axis, keepdims=False)

    def halve(v, size, axis):
        return lax.dynamic_slice_in_dim(v, h * size, size, axis)

    def widen(v):
        left, right = (
            jnp.pad(v, ((0, 0),) * (v.ndim - 1) + (side,))
            for side in ((0, PADDED - local_ff), (PADDED - local_ff, 0))
        )
        return jnp.where(core == 1, right, left)

    quarters = jnp.concatenate(
        [
            w_qkv[:, : HEADS * HEAD].reshape(12, 2, group_cols),
            w_qkv[:, HEADS * HEAD : HEADS * HEAD + 256].reshape(12, 2, HEAD),
            w_qkv[:, HEADS * HEAD + 256 :].reshape(12, 2, HEAD),
        ],
        axis=2,
    )
    quarters = jnp.moveaxis(quarters.reshape(12, 4, 512), 1, 0)
    quarters = jnp.pad(quarters, ((0, 0), (0, 4), (0, 0)))
    out_quarters = jnp.pad(jnp.moveaxis(w_out.reshape(12, 4, 384), 1, 0), ((0, 0), (0, 4), (0, 0)))
    ff_part = widen(jnp.concatenate([w_gate_up, w_down.T[None]], axis=0))

    chunks = jnp.stack([blk, 63 - blk])
    positions = (chunks[:, None] * CHUNK + jnp.arange(CHUNK, dtype=jnp.int32)[None, :]).reshape(-1)
    length = lengths[core]
    limit = jnp.minimum(positions, length - 1).reshape(2, 1, 1, CHUNK)
    limit = jnp.broadcast_to(limit, (2, 8, GROUP, CHUNK)).reshape(2, 8, ROWS)
    cos_table, sine_table = rope_tables(positions)
    cos_heads, sine_heads = cos_table[:, None, :], sine_table[:, None, :]
    signed = jnp.where(jnp.arange(HEAD) < HEAD // 2, -sine_table, sine_table)

    own_set = set_index[core]
    a_own = pick_set(a_wide, 1, own_set)
    bq = halve(pick_set(b_wide[0], 0, own_set), group_cols, 1)
    bo = pick_set(b_wide[1], 0, own_set)
    bk, bv = (halve(pick_set(b_kv[n], 0, own_set), HEAD, 1) for n in (0, 1))
    ao = halve(a_own[3], group_cols, 1)
    bias = jnp.concatenate(
        [
            halve(qkv_bias[: HEADS * HEAD], group_cols, 0),
            halve(qkv_bias[HEADS * HEAD : HEADS * HEAD + 256], HEAD, 0),
            halve(qkv_bias[HEADS * HEAD + 256 :], HEAD, 0),
        ]
    )
    a_qkv = a_own[:3].reshape(48, D)
    b_qkv = jnp.concatenate(
        [
            jnp.concatenate([bq, zero((16, 256), BF)], axis=1),
            jnp.concatenate([zero((16, group_cols), BF), bk, zero((16, HEAD), BF)], axis=1),
            jnp.concatenate([zero((16, group_cols + HEAD), BF), bv], axis=1),
        ],
        axis=0,
    )
    (
        q, mixed, lse, kv_all, qkv_w, out_w, gate_w, up_w, down_w, rows, normed, latent_qkv, residual,
        grad_out, gathered, grad_gathered,
    ) = forward(
        quarters, out_quarters, tokens, cotangent, ff_part, limit,
        jnp.broadcast_to(length, (1, D)), norm_in[None], norm_ff[None], bias[None], cos_table, signed,
        a_qkv, b_qkv, ao, bo,
    )
    gate_w, up_w, down_w = (w.reshape(D, FF_COLS) for w in (gate_w, up_w, down_w))
    gathered, grad_gathered = (v.reshape(2, 4 * CHUNK, D) for v in (gathered, grad_gathered))
    rows = rows.reshape(2, CHUNK, D).astype(F32)
    scale_in = norm_scale(rows)
    own_rows = jnp.where(h == 0, rows[0], rows[1])
    scale_ff = norm_scale(residual)
    latent_o = mm("tc,rc->tr", mixed, ao)

    def swap_h(v):
        return lax.ppermute(v, "uly", OVER_H)

    def own_slot(v):
        return flip(h == 1, v[0], v[1])

    def by_sequence(table, axis):
        return jnp.stack([pick_set(table, axis, set_index[s]) for s in (0, 1)])

    def own_cols(v):
        v = lax.dynamic_slice_in_dim(v, uly * local_ff, local_ff, v.ndim - 1)
        return lax.dynamic_slice_in_dim(widen(v), y_lo * FF_COLS, FF_COLS, v.ndim - 1)

    a_ff = by_sequence(a_wide[4:6], 1).reshape(2, 32, D)
    b_cols = own_cols(by_sequence(b_ff, 1))
    a_cols = own_cols(by_sequence(a_down, 0))
    b_out = by_sequence(b_wide[2], 0)
    latent_ff = mm("std,srd->str", gathered, a_ff)
    gate = mm("std,df->stf", gathered, gate_w) + mm("str,srf->stf", latent_ff[..., :16], b_cols[:, 0])
    up = mm("std,df->stf", gathered, up_w) + mm("str,srf->stf", latent_ff[..., 16:], b_cols[:, 1])
    sigmoid = jax.nn.sigmoid(gate)
    silu = gate * sigmoid
    hidden = (silu * up).astype(BF)
    latent_down = mm("stf,srf->str", hidden, a_cols)
    down = mm("stf,df->std", hidden, down_w) + mm("str,srd->std", latent_down, b_out)
    latent_back = mm("std,srd->str", grad_gathered, b_out)
    grad_hidden = mm("std,df->stf", grad_gathered, down_w) + mm("str,srf->stf", latent_back, a_cols)
    grad_a_cols = mm("str,stf->srf", latent_back, hidden)
    grad_b_out = mm("str,std->srd", latent_down, grad_gathered)
    grad_up = (grad_hidden * silu).astype(BF)
    grad_gate = (grad_hidden * up * (sigmoid * (1.0 + gate * (1.0 - sigmoid)))).astype(BF)
    back_gate = mm("stf,srf->str", grad_gate, b_cols[:, 0])
    back_up = mm("stf,srf->str", grad_up, b_cols[:, 1])
    back_ff = jnp.concatenate([back_gate, back_up], axis=-1)
    grad_a_ff = mm("str,std->srd", back_ff, gathered)
    grad_b_gate = mm("str,stf->srf", latent_ff[..., :16], grad_gate)
    grad_b_up = mm("str,stf->srf", latent_ff[..., 16:], grad_up)
    grad_ff_in = (
        mm("stf,df->std", grad_gate, gate_w)
        + mm("stf,df->std", grad_up, up_w)
        + mm("str,srd->std", back_ff, a_ff)
    )
    grad_normed_ff, ff_out = collect(
        grad_ff_in.astype(BF).reshape(2, 4, CHUNK, D), down.astype(BF).reshape(2, 4, CHUNK, D)
    )
    result = (residual + ff_out).astype(BF)
    grad_resid = grad_out.astype(F32) + norm_back(residual, scale_ff, norm_ff, grad_normed_ff)
    grad_attn = grad_resid.astype(BF)
    grad_attn = jnp.concatenate(flip(h == 1, grad_attn, swap_h(grad_attn)), axis=0)

    back_o = mm("td,rd->tr", grad_attn, bo)
    grad_a_o = mm("tr,tc->rc", back_o, mixed)
    grad_b_o = mm("tr,td->rd", latent_o, grad_attn)
    grad_mixed = (mm("td,cd->tc", grad_attn, out_w) + mm("tr,rc->tc", back_o, ao)).astype(BF)

    cols = jnp.stack([grad_a_cols, grad_b_gate, grad_b_up]).reshape(6, 16, FF_COLS).astype(BF)
    none = jnp.zeros_like(cols)
    cols = jnp.concatenate(flip(y_lo == 1, cols, none), axis=2)
    ff_wide = jnp.concatenate([grad_a_ff.reshape(2, 2, 16, D), grad_b_out[:, None]], axis=1)
    ff_wide = jnp.moveaxis(ff_wide, 0, 1).reshape(6, 16, D).astype(BF)
    dq, dkv, ff_all = attend_backward(
        q, kv_all, limit, mixed, grad_mixed, lse, cols, grad_a_o.astype(BF)[None],
        grad_b_o.astype(BF)[None], ff_wide,
    )
    dkv = dkv.reshape(2 * CHUNK, 2 * HEAD)
    grad_q = rope_back(dq.reshape(2 * CHUNK, GROUP, HEAD), cos_heads, sine_heads)
    grad_k = rope_back(dkv[:, :HEAD], cos_table, sine_table)
    grad_qkv = jnp.concatenate(
        [grad_q.reshape(2 * CHUNK, group_cols), grad_k, dkv[:, HEAD:]], axis=1
    ).astype(BF)
    back_qkv = mm("to,ro->tr", grad_qkv, b_qkv)
    grad_a_qkv = mm("tr,td->rd", back_qkv, normed)
    grad_b_qkv = mm("tr,to->ro", latent_qkv, grad_qkv)
    grad_normed = (
        mm("to,do->td", grad_qkv[:, :512], qkv_w[0])
        + mm("to,do->td", grad_qkv[:, 512:], qkv_w[1])
        + mm("tr,rd->td", back_qkv, a_qkv)
    ).reshape(2, CHUNK, D)
    mine, theirs = own_slot(grad_normed)
    grad_normed = mine + swap_h(theirs.astype(BF)).astype(F32)
    own_scale = jnp.where(h == 0, scale_in[0], scale_in[1])
    input_grad = grad_resid + norm_back(own_rows, own_scale, norm_in, grad_normed)

    def home(v):
        halves = v.astype(BF).reshape(2, CHUNK // 2, D)
        got = [
            lax.ppermute(lax.dynamic_index_in_dim(halves, core ^ j, 0, keepdims=False), ALL, back_moves[j])
            for j in (0, 1)
        ]
        return jnp.stack(flip(core == 1, got[0], got[1]))

    result_tokens = home(result)
    input_grad = home(input_grad).astype(F32)

    qkv_all = qkv_total(
        grad_a_qkv.reshape(3, 16, D).astype(BF),
        grad_b_qkv[:16, :group_cols].astype(BF)[None],
        jnp.stack(
            [
                grad_b_qkv[16:32, group_cols : group_cols + HEAD],
                grad_b_qkv[32:, group_cols + HEAD :],
            ]
        ).astype(BF),
    )
    pick = (jnp.arange(SETS, dtype=jnp.int32)[:, None] == set_index[None, :]).astype(F32)
    return (result_tokens, input_grad) + tuple(fold(pick, ff_all, qkv_all))


def solution(mesh):
    spread = P(None, ("blk", "uly"), None)
    in_specs = (
        spread, spread, P(), P(), P(), P(), P(),
        P(("blk", "uly"), None), P(("blk", "uly"), None), P(None, "blk", "uly"), P("uly", "blk"),
        P(), P(), P(), P(), P(),
    )
    out_specs = (spread, spread, P(), P(), P(), P(), P())
    return jax.shard_map(body, mesh=mesh, in_specs=in_specs, out_specs=out_specs, check_vma=False)
```

```python
import functools

import jax
import jax.numpy as jnp
import numpy as np
from jax import lax
from jax.experimental import pallas as pl
from jax.experimental.pallas import tpu as pltpu
from jax.sharding import PartitionSpec as P

HEADS = 12
KV_HEADS = 2
HEAD = 128
GROUP = HEADS // KV_HEADS
FF = 8960
SETS = 8
D = 1536
CHUNK = 128
CHUNKS = 64
PADDED = 2304
EPS = 1e-06
THETA = 1000000.0
LOG2E = 1.4426950408889634
LN2 = 0.6931471805599453
MESH = pl.DeviceIdType.MESH
BF = jnp.bfloat16
F32 = jnp.float32
ANY = pl.BlockSpec(memory_space=pl.ANY)
IN_VMEM = pl.BlockSpec(memory_space=pltpu.VMEM)


def blk_of(y, z, x):
    return y * 16 + z * 4 + x


def place():
    blk = lax.axis_index("blk")
    return blk // 16, (blk // 4) % 4, blk % 4, blk, lax.axis_index("uly")


def ring_others():
    y, z, x, blk, uly = place()
    return [
        (blk_of(1 - y, z, x), uly),
        (blk_of(y, z, (x + 1) % 4), uly),
        (blk_of(y, z, (x + 3) % 4), uly),
        (blk_of(y, (z + 1) % 4, x), uly),
        (blk_of(y, (z + 3) % 4, x), uly),
    ]


def greet(others, meanwhile=None):
    barrier = pltpu.get_barrier_semaphore()
    for other in others:
        pl.semaphore_signal(barrier, inc=1, device_id=other, device_id_type=MESH)
    if meanwhile is not None:
        meanwhile()
    pl.semaphore_wait(barrier, len(others))


class Gather:
    sends = 31

    def __init__(self, src, dst, send_sem, recv_sem, local_sem, orders=(0, 1)):
        self.src, self.dst, self.orders = src, dst, orders
        self.streams = range(len(orders))
        self.send_sem, self.recv_sem, self.local_sem = send_sem, recv_sem, local_sem
        self.y, self.z, self.x, self.blk, self.uly = place()
        self.count = [0] * len(orders)
        self.sent = []
        self.local = []

    def at(self, stream, y, p, q):
        order = self.orders[stream]
        return blk_of(y, order * p + (1 - order) * q, order * q + (1 - order) * p)

    def pq(self, stream):
        order = self.orders[stream]
        return (
            order * self.z + (1 - order) * self.x,
            order * self.x + (1 - order) * self.z,
        )

    def send(self, stream, item, target, src=None):
        copy = pltpu.make_async_remote_copy(
            src_ref=self.dst(stream, item) if src is None else src,
            dst_ref=self.dst(stream, item),
            send_sem=self.send_sem.at[stream, self.count[stream]],
            recv_sem=self.recv_sem.at[stream, item],
            device_id=(target, self.uly),
            device_id_type=MESH,
        )
        self.count[stream] += 1
        copy.start()
        self.sent.append(copy)

    def wait(self, stream, item):
        ref = self.dst(stream, item)
        pltpu.make_async_remote_copy(
            src_ref=ref,
            dst_ref=ref,
            send_sem=self.send_sem.at[stream, 0],
            recv_sem=self.recv_sem.at[stream, item],
            device_id=(self.blk, self.uly),
            device_id_type=MESH,
        ).wait_recv()

    def start(self):
        for s in self.streams:
            p, q = self.pq(s)
            self.send(s, self.blk, self.at(s, 1 - self.y, p, q), self.src(s))
        for s in self.streams:
            p, q = self.pq(s)
            for d in (1, 3):
                self.send(s, self.blk, self.at(s, self.y, (p + d) % 4, q), self.src(s))
            copy = pltpu.make_async_copy(self.src(s), self.dst(s, self.blk), self.local_sem.at[s])
            copy.start()
            self.local.append(copy)

    def second(self):
        for s in self.streams:
            p, q = self.pq(s)
            item = self.at(s, 1 - self.y, p, q)
            self.wait(s, item)
            for d in (1, 3):
                self.send(s, item, self.at(s, self.y, (p + d) % 4, q))
            for d in (1, 3):
                onward = self.at(s, self.y, p, (q + d) % 4)
                self.send(s, self.blk, onward, self.src(s))
                self.send(s, item, onward)

    def spread(self, s, item):
        p, q = self.pq(s)
        for d in (1, 3):
            self.send(s, item, self.at(s, self.y, p, (q + d) % 4))

    def third(self):
        for k, y in enumerate((self.y, 1 - self.y)):
            for s in self.streams:
                p, q = self.pq(s)
                for d in (3, 1):
                    item = self.at(s, y, (p + d) % 4, q)
                    self.wait(s, item)
                    if (d == 3) == (k == 0):
                        self.send(s, item, self.at(s, self.y, (p + 4 - d) % 4, q))
                    self.spread(s, item)
        for y in (self.y, 1 - self.y):
            for s in self.streams:
                p, q = self.pq(s)
                item = self.at(s, y, (p + 2) % 4, q)
                self.wait(s, item)
                self.spread(s, item)

    def fourth(self):
        for e in (0, 1, 3, 2):
            for k, y in enumerate((self.y, 1 - self.y)):
                for s in self.streams:
                    p, q = self.pq(s)
                    for d in (3, 1):
                        item = self.at(s, y, (p + e) % 4, (q + d) % 4)
                        self.wait(s, item)
                        if (d == 3) == (k == 0):
                            self.send(s, item, self.at(s, self.y, p, (q + 4 - d) % 4))

    def last(self):
        for e in (0, 1, 3, 2):
            for y in (self.y, 1 - self.y):
                for s in self.streams:
                    p, q = self.pq(s)
                    self.wait(s, self.at(s, y, (p + e) % 4, (q + 2) % 4))
        for copy in self.local:
            copy.wait()
        for copy in self.sent:
            copy.wait_send()


GATHER_SEMS = lambda *lead: [
    pltpu.SemaphoreType.DMA(lead + (2, Gather.sends)),
    pltpu.SemaphoreType.DMA(lead + (2, 32)),
    pltpu.SemaphoreType.DMA(lead + (2,)),
]


KEYS = 512
STEP = KEYS // CHUNK
ROWS = GROUP * CHUNK


def head_columns(ref, slot):
    return jnp.concatenate(
        [
            ref[slot * CHUNK : (slot + 1) * CHUNK, n * HEAD : (n + 1) * HEAD].T
            for n in range(GROUP)
        ],
        axis=1,
    )


def head_rows(ref, slot):
    return jnp.concatenate(
        [
            ref[slot * CHUNK : (slot + 1) * CHUNK, n * HEAD : (n + 1) * HEAD]
            for n in range(GROUP)
        ],
        axis=0,
    )


def key_block(kv_ref, step):
    rows = kv_ref[pl.ds(step * STEP, STEP)].reshape(KEYS, 2 * HEAD)
    return rows[:, :HEAD], rows[:, HEAD:]


def dot(a, b):
    return jnp.dot(a, b, preferred_element_type=F32)


def key_places(step):
    return lax.broadcasted_iota(jnp.int32, (KEYS, ROWS), 0) + step * KEYS


def dot_nt(a, b):
    return lax.dot_general(a, b, (((1,), (1,)), ((), ())), preferred_element_type=F32)


def forward_slot(slot, chunk, part, q_ref, kv_ref, limit_ref, mixed_ref, lse_ref, acc_ref, stat_ref):
    turned = head_columns(q_ref, slot)
    limit = limit_ref[slot, 0:1, :]
    if part == 0:
        acc_ref[...] = jnp.zeros_like(acc_ref)
        stat_ref[0] = jnp.full(stat_ref.shape[1:], -1e30, F32)
        stat_ref[1] = jnp.zeros(stat_ref.shape[1:], F32)

    def step(n, carry):
        top, total = carry
        keys, values = key_block(kv_ref, n)
        scores = jnp.where(key_places(n) <= limit, dot(keys, turned), -1e30)
        new_top = jnp.maximum(top, jnp.max(scores, axis=0, keepdims=True))
        fade = jnp.exp2(top - new_top)
        probs = jnp.exp2(scores - new_top)
        total = total * fade + jnp.sum(probs, axis=0, keepdims=True)
        acc_ref[...] = acc_ref[...] * fade + dot(values.T, probs.astype(BF))
        return new_top, total

    blocks = chunk // STEP + 1
    top, total = lax.fori_loop(
        blocks * part // 4, blocks * (part + 1) // 4, step, (stat_ref[0, 0:1, :], stat_ref[1, 0:1, :])
    )
    if part < 3:
        stat_ref[0, 0:1, :] = top
        stat_ref[1, 0:1, :] = total
        return
    out = acc_ref[...] / total
    for n in range(GROUP):
        mixed_ref[slot * CHUNK : (slot + 1) * CHUNK, n * HEAD : (n + 1) * HEAD] = out[
            :, n * CHUNK : (n + 1) * CHUNK
        ].T.astype(BF)
    lse_ref[slot] = jnp.broadcast_to(top + jnp.log2(total), (8, ROWS))


def uly_others():
    y, z, x, blk, uly = place()
    return [(blk, (uly + 2) % 4), (blk, uly + 1 - 2 * (uly % 2)), (blk, 3 - uly)]


def ring_place(w):
    y, z, x, blk, uly = place()
    return (blk_of(w % 2, z, x), (w // 2) * 2 + uly % 2)


def ring_at():
    y, z, x, blk, uly = place()
    return (uly // 2) * 2 + y


def wait_arrival(ref, sem):
    pltpu.make_async_copy(ref, ref, sem).wait()


def remote(src, dst, send, recv, device):
    return pltpu.make_async_remote_copy(
        src_ref=src, dst_ref=dst, send_sem=send, recv_sem=recv, device_id=device, device_id_type=MESH
    )


class Deliver:
    def __init__(self):
        self.sent = []

    def send(self, src, dst, send, recv, device):
        y, z, x, blk, uly = place()
        here = jnp.logical_and(device[0] == blk, device[1] == uly)

        @pl.when(here)
        def _():
            pltpu.make_async_copy(src, dst, recv).start()

        @pl.when(jnp.logical_not(here))
        def _():
            remote(src, dst, send, recv, device).start()

        self.sent.append((here, src, dst, send, recv, device))

    def end(self):
        for here, *copy in self.sent:

            @pl.when(jnp.logical_not(here))
            def _():
                remote(*copy).wait_send()


class Ring:
    sends = 15

    def __init__(self, src, dst, y, order, way, send_sem, recv_sem):
        self.src, self.dst, self.y, self.order, self.way = src, dst, y, order, way
        self.send_sem, self.recv_sem = send_sem, recv_sem
        self.own_y, self.z, self.x, self.blk, self.uly = place()
        self.p = order * self.z + (1 - order) * self.x
        self.q = order * self.x + (1 - order) * self.z
        self.sent = []

    def at(self, y, p, q):
        order = self.order
        return blk_of(y, order * p + (1 - order) * q, order * q + (1 - order) * p)

    def index(self, p, q):
        return self.at(0, p, q)

    def send(self, p, q, dp, dq, src=None):
        ref = self.dst(self.at(self.y, p, q))
        target = self.at(self.own_y, (self.p + dp) % 4, (self.q + dq) % 4)
        copy = remote(
            ref if src is None else src, ref, self.send_sem.at[len(self.sent)],
            self.recv_sem.at[self.index(p, q)], (target, self.uly),
        )
        copy.start()
        self.sent.append(copy)

    def wait(self, p, q):
        wait_arrival(self.dst(self.at(self.y, p, q)), self.recv_sem.at[self.index(p, q)])

    def start(self):
        for d in (1, 3):
            self.send(self.p, self.q, d, 0, self.src)

    def second(self):
        for d in (4 - self.way, self.way):
            p = (self.p + d) % 4
            self.wait(p, self.q)
            if d == 4 - self.way:
                self.send(p, self.q, self.way, 0)

    def third(self):
        self.wait((self.p + 2) % 4, self.q)

    def spread(self, e):
        p = (self.p + e) % 4
        for d in (1, 3):
            self.send(p, self.q, 0, d, self.src if e == 0 else None)

    def fourth(self, e):
        p = (self.p + e) % 4
        for d in (4 - self.way, self.way):
            q = (self.q + d) % 4
            self.wait(p, q)
            if d == 4 - self.way:
                self.send(p, q, 0, self.way)

    def last(self):
        for e in (0, 1, 3, 2):
            self.wait((self.p + e) % 4, (self.q + 2) % 4)
        for copy in self.sent:
            copy.wait_send()


class Spread:
    def __init__(self, own, all_ref, send_sem, recv_sem, local_sem):
        self.own, self.all_ref = own, all_ref
        self.send_sem, self.recv_sem, self.local_sem = send_sem, recv_sem, local_sem
        self.w = ring_at()
        self.core = lax.axis_index("uly") % 2
        self.sibling = uly_others()[1]
        self.sent = []

    def piece(self, d, rows=slice(None), core=None):
        core = self.core if core is None else core
        ref = self.all_ref.at[core, (self.w + d) % 4]
        return ref if rows == slice(None) else ref.at[pl.ds(rows.start, rows.stop - rows.start)]

    def send(self, src, dst, recv, device):
        copy = remote(src, dst, self.send_sem.at[len(self.sent)], self.recv_sem.at[recv], device)
        copy.start()
        self.sent.append(copy)

    def pair(self, d, src=None):
        self.send(self.piece(d) if src is None else src, self.piece(d), 4 + d, self.sibling)

    def start(self):
        self.local = pltpu.make_async_copy(self.own, self.piece(0), self.local_sem)
        self.local.start()
        self.send(self.own, self.piece(0), 0, ring_place((self.w + 1) % 4))
        self.send(self.own, self.piece(0), 1, ring_place((self.w + 3) % 4))
        self.pair(0, self.own)

    def second(self):
        half = CHUNK // 2
        wait_arrival(self.piece(3), self.recv_sem.at[0])
        low = self.piece(3, slice(0, half))
        self.send(low, low, 2, ring_place((self.w + 1) % 4))
        self.pair(3)
        wait_arrival(self.piece(1), self.recv_sem.at[1])
        high = self.piece(1, slice(half, CHUNK))
        self.send(high, high, 3, ring_place((self.w + 3) % 4))
        self.pair(1)

    def third(self):
        half = CHUNK // 2
        wait_arrival(self.piece(2, slice(0, half)), self.recv_sem.at[2])
        wait_arrival(self.piece(2, slice(half, CHUNK)), self.recv_sem.at[3])
        self.pair(2)

    def last(self):
        for d in range(4):
            wait_arrival(self.piece(d, core=1 - self.core), self.recv_sem.at[4 + d])
        for copy in self.sent:
            copy.wait_send()
        self.local.wait()


SPREAD_SEMS = [pltpu.SemaphoreType.DMA((8,)), pltpu.SemaphoreType.DMA((8,)), pltpu.SemaphoreType.DMA]
FF_COLS = PADDED // 2


def forward_kernel(
    tokens_ref, cot_ref, length_ref, qkv_ref, out_ref, gate_up_ref, down_ref, norm_in_ref, norm_ff_ref,
    bias_ref, freq_ref, a_ref, b_ref, bkv_ref,
    q_ref, mixed_ref, lse_ref, kv_out, wq_out, wo_out, gate_all, up_all, down_all, rows_out, normed_ref,
    resid_ref, cot_own, nf_all, cot_all, limit_ref, cos_ref, sin_ref, b_qkv_ref, ao_ref,
    kv_all, wq_all, wo_all, rows, cot_in, kv_part, acc_ref, stat_ref, qkv_in, out_in, qkv_part, out_part,
    nf_own, cross_out, cross_in, qkv_pieces, out_pieces, ff_ref,
    *sems,
):
    y, z, x, blk, uly = place()
    core, h = uly % 2, uly // 2
    sems = list(sems)

    def take(count):
        got = sems[:count]
        del sems[:count]
        return got

    chunk = 2 * blk + h
    upper = chunk // 32
    home = (1 - upper) * chunk + upper * (63 - chunk)
    row_to = [[(home, hh * 2 + s) for hh in (0, 1)] for s in (0, 1)]
    row_from = [(c // 2, (c % 2) * 2 + half) for c in (blk, 63 - blk) for half in (0, 1)]
    out_to = [(2 * (blk % 16) + q // 2, (blk // 16) * 2 + q % 2) for q in range(4)]
    out_from = [(16 * h + blk // 2, u) for u in range(4)]
    sibling = uly_others()[1]
    length = length_ref[0] * (1 - core) + length_ref[1] * core

    def prepare():
        qkv_pieces[...] = jnp.zeros_like(qkv_pieces)
        out_pieces[...] = jnp.zeros_like(out_pieces)
        group = GROUP * HEAD
        for hh in (0, 1):
            qkv_pieces[2 * hh, :12] = qkv_ref[:, hh * group : hh * group + 512]
            for place_at, start, size in (
                (0, hh * group + 512, 256),
                (256, HEADS * HEAD + hh * HEAD, HEAD),
                (384, HEADS * HEAD + 256 + hh * HEAD, HEAD),
            ):
                qkv_pieces[2 * hh + 1, :12, place_at : place_at + size] = qkv_ref[:, start : start + size]
        for q in range(4):
            out_pieces[q, :12] = out_ref[:, q * 384 : (q + 1) * 384]
        for n in range(3):
            part = (gate_up_ref[n] if n < 2 else down_ref[...]).astype(F32)
            none = jnp.zeros((48, 64), F32)
            left = jnp.concatenate([part, none], axis=1)
            right = jnp.concatenate([none, part], axis=1)
            ff_ref[n] = jnp.where(jnp.broadcast_to(core, (48, PADDED)) == 1, right, left).astype(BF)

    greet(
        ring_others() + uly_others() + [(blk_of(1 - y, z, x), (uly + 2) % 4)]
        + row_to[0] + row_to[1] + row_from + out_to + out_from,
        prepare,
    )

    deliver = Deliver()
    piece_send, piece_recv, row_send, row_recv = take(4)
    for q in range(4):
        deliver.send(qkv_pieces.at[q], qkv_in.at[uly], piece_send.at[q], piece_recv.at[uly], (blk, q))
    for q in range(4):
        deliver.send(out_pieces.at[q], out_in.at[uly], piece_send.at[4 + q], piece_recv.at[4 + uly], out_to[q])
    for s in (0, 1):
        for hh in (0, 1):
            deliver.send(
                tokens_ref.at[s], rows.at[upper, core], row_send.at[s * 2 + hh],
                row_recv.at[upper * 2 + core], row_to[s][hh],
            )

    wide = PADDED // 2
    gathered = (gate_all, up_all, down_all)
    ff_send, ff_recv, y_send, y_recv, y_local = take(5)
    other_blk = blk_of(1 - y, z, x)

    def ff_part(n, half):
        return ff_ref.at[n, :, pl.ds(pl.multiple_of(half * wide, 128), wide)]

    picked = lax.broadcasted_iota(jnp.int32, (48, 64), 1)
    picked = jnp.where(picked % 16 < 12, picked // 16 * 12 + picked % 16, -1)
    picked = jnp.where(picked == lax.broadcasted_iota(jnp.int32, (48, 64), 0), 1.0, 0.0).astype(BF)
    for u in range(4):
        wait_arrival(qkv_in.at[u], piece_recv.at[u])
    qkv_part[...] = dot(picked, qkv_in[...].reshape(64, 512)).astype(BF)
    wq = Gather(
        lambda s: qkv_part.at[:, pl.ds(256 * s, 256)],
        lambda s, item: wq_all.at[
            core, pl.ds(pl.multiple_of(item * 48, 16), 48), pl.ds(256 * s, 256)
        ],
        *take(3),
    )
    wq.start()
    for u in range(4):
        wait_arrival(out_in.at[u], piece_recv.at[4 + u])
    out_part[...] = dot(picked, out_in[...].reshape(64, 384)).astype(BF)
    y_copies = []
    for n, ref in enumerate(gathered):
        copy = remote(ff_part(n, 1 - y), ref.at[blk], y_send.at[n], y_recv.at[n], (other_blk, uly))
        copy.start()
        y_copies.append(copy)
        copy = pltpu.make_async_copy(ff_part(n, y), ref.at[blk], y_local.at[n])
        copy.start()
        y_copies.append(copy)
    for s in (0, 1):
        deliver.send(
            cot_ref.at[s], cot_in.at[core], row_send.at[4 + s], row_recv.at[4 + core], (home, upper * 2 + s)
        )

    def out_columns(item, s):
        start = ((item % 2) * 2 + core) * 384
        return pl.ds(pl.multiple_of(start + 128 * s, 128), 128 + 128 * s)

    wo = Gather(
        lambda s: out_part.at[:, pl.ds(128 * s, 128 + 128 * s)],
        lambda s, item: wo_all.at[pl.ds(pl.multiple_of((item // 2) * 48, 16), 48), out_columns(item, s)],
        *take(3),
    )
    own_ff, other_ff = (
        [
            Ring(
                ff_part(n, y) if k == 0 else ref.at[other_blk],
                lambda item, ref=ref: ref.at[item],
                y if k == 0 else 1 - y,
                y if k == 0 else 1 - y,
                (1, 3, 1 + 2 * k)[n],
                ff_send.at[k, n], ff_recv.at[k, n],
            )
            for n, ref in enumerate(gathered)
        ]
        for k in (0, 1)
    )
    rings = own_ff + other_ff
    wq.second()
    wq.third()
    wq.fourth()
    for ring in own_ff:
        ring.start()
    for n in range(3):
        y_copies[2 * n].wait_recv()
    for ring in other_ff:
        ring.start()

    for slot, at in ((0, blk), (1, 63 - blk)):
        row = lax.broadcasted_iota(jnp.int32, (CHUNK, HEAD), 0) + at * CHUNK
        angle = row.astype(F32) * freq_ref[...]
        first = lax.broadcasted_iota(jnp.int32, (CHUNK, HEAD), 1) < HEAD // 2
        sine = jnp.sin(angle)
        cos_ref[slot * CHUNK : (slot + 1) * CHUNK, :] = jnp.cos(angle)
        sin_ref[slot * CHUNK : (slot + 1) * CHUNK, :] = jnp.where(first, -sine, sine)
        row = lax.broadcasted_iota(jnp.int32, (8, ROWS), 1) % CHUNK + at * CHUNK
        limit_ref[slot] = jnp.minimum(row, length - 1)
    group = GROUP * HEAD
    group_at = pl.ds(pl.multiple_of(h * group, 128), group)
    head_at = pl.ds(pl.multiple_of(h * HEAD, 128), HEAD)
    ao_ref[...] = a_ref[3, :, group_at]
    b_qkv_ref[...] = jnp.zeros_like(b_qkv_ref)
    b_qkv_ref[:16, :group] = b_ref[0, :, group_at]
    b_qkv_ref[16:32, group : group + HEAD] = bkv_ref[0, :, head_at]
    b_qkv_ref[32:, group + HEAD :] = bkv_ref[1, :, head_at]
    a_qkv = a_ref[:3].reshape(48, D)
    bo_ref = b_ref.at[1]

    def bias(n):
        at = h * GROUP + n if n < GROUP else HEADS + 2 * (n - GROUP) + h
        return bias_ref[pl.ds(at, 1), :]

    for n in range(4):
        wait_arrival(rows.at[n // 2, n % 2], row_recv.at[n])
        value = rows[n // 2, n % 2].astype(F32)
        at = slice(n * 64, (n + 1) * 64)
        rows_out[at, :] = rows[n // 2, n % 2]
        normed_ref[at, :] = (value * norm_scale(value) * norm_in_ref[...]).astype(BF)
    latent = dot_nt(normed_ref[...], a_qkv)
    adapted = dot(latent.astype(BF), b_qkv_ref[...])
    wq.last()
    pair_send, pair_recv = take(2)

    def pair_copy(ref, n):
        return remote(ref, ref, pair_send.at[n], pair_recv.at[n], sibling)

    pair_copy(wq_all.at[core], 0).start()
    wo.start()
    pair_copy(wq_all.at[core], 0).wait_send()
    pair_copy(wq_all.at[1 - core], 0).wait_recv()

    cos_table, sine_table = cos_ref[...], sin_ref[...]

    def turn(head):
        return head * cos_table + pltpu.roll(head, HEAD // 2, 1) * sine_table

    def query(n, head):
        q_ref[:, n * HEAD : (n + 1) * HEAD] = (turn(head + bias(n)) * (HEAD ** (-0.5) * LOG2E)).astype(BF)

    pairs = dot(normed_ref[...], wq_all[1, :, 256:]) + adapted[:, 768:]
    for n, head in ((0, turn(pairs[:, :HEAD] + bias(6))), (1, pairs[:, HEAD:] + bias(7))):
        at = slice(n * HEAD, (n + 1) * HEAD)
        kv_part[0, :, at] = head[:CHUNK].astype(BF)
        kv_part[1, :, at] = head[CHUNK:].astype(BF)
    kv = Gather(
        lambda s: kv_part.at[s],
        lambda s, item: kv_all.at[item if s == 0 else 63 - item],
        *take(3),
    )
    kv.start()
    heads = dot(normed_ref[...], wq_all[1, :, :256]) + adapted[:, 512:768]
    for n in (4, 5):
        query(n, heads[:, (n - 4) * HEAD : (n - 3) * HEAD])
    kv.second()
    for ring in rings:
        ring.second()
    wo.second()
    heads = dot(normed_ref[...], wq_all[0]) + adapted[:, :512]
    for n in range(4):
        query(n, heads[:, n * HEAD : (n + 1) * HEAD])
    kv.third()
    for ring in rings:
        ring.third()
    wo.third()
    kv.fourth()
    wo.fourth()

    for half in (0, 1):
        wait_arrival(cot_in.at[half], row_recv.at[4 + half])
        start = ((1 - h) * blk + h * (63 - blk)) * CHUNK + half * 64
        at = lax.broadcasted_iota(jnp.int32, (64, D), 0) + start
        cot_own[half * 64 : (half + 1) * 64, :] = jnp.where(
            at < length, cot_in[half].astype(F32), 0.0
        ).astype(BF)
    cot_spread = Spread(cot_own, cot_all, *take(3))
    cot_spread.start()
    kv.last()
    for e in (0, 1, 3, 2):
        for ring in rings:
            ring.spread(e)
    (out_sem,) = take(1)
    copies = [
        pltpu.make_async_copy(src, dst, out_sem.at[n])
        for n, (src, dst) in enumerate(((kv_all, kv_out), (wq_all, wq_out), (wo_all, wo_out)))
    ]
    copies[0].start()
    copies[1].start()
    wo.last()

    def wo_columns(c, n):
        return wo_all.at[:, pl.ds(pl.multiple_of((2 * n + c) * 384, 128), 384)]

    for n in (0, 1):
        pair_copy(wo_columns(core, n), 1 + n).start()
    args = (q_ref, kv_all, limit_ref, mixed_ref, lse_ref, acc_ref, stat_ref)
    beside = {
        3: lambda: [ring.fourth(0) for ring in rings] + [cot_spread.second()],
        5: lambda: [ring.fourth(1) for ring in rings],
        6: lambda: [ring.fourth(3) for ring in rings] + [cot_spread.third()],
        7: lambda: [ring.fourth(2) for ring in rings],
    }
    for slot, at in ((0, blk), (1, 63 - blk)):
        for part in range(4):
            forward_slot(slot, at, part, *args)
            if slot * 4 + part in beside:
                beside[slot * 4 + part]()
    for n in (0, 1):
        pair_copy(wo_columns(core, n), 1 + n).wait_send()
        pair_copy(wo_columns(1 - core, n), 1 + n).wait_recv()
    copies[2].start()

    def project(slot):
        mixed = mixed_ref[pl.ds(pl.multiple_of(slot * CHUNK, CHUNK), CHUNK), :]
        lifted = dot(dot_nt(mixed, ao_ref[...]).astype(BF), bo_ref[...])
        return dot(mixed, wo_all[...]) + lifted

    (cross_sem,) = take(1)
    cross_out[...] = project(1 - h).astype(BF)
    cross = remote(cross_out, cross_in, cross_sem.at[0], cross_sem.at[1], uly_others()[0])
    cross.start()
    mine = project(h) + rows_out[pl.ds(pl.multiple_of(h * CHUNK, CHUNK), CHUNK), :].astype(F32)
    cross.wait()
    residual = mine + cross_in[...].astype(F32)
    resid_ref[...] = residual
    nf_own[...] = (residual * norm_scale(residual) * norm_ff_ref[...]).astype(BF)
    nf_spread = Spread(nf_own, nf_all, *take(3))
    nf_spread.start()
    nf_spread.second()
    nf_spread.third()
    nf_spread.last()
    cot_spread.last()
    for ring in rings:
        ring.last()
    for n in range(3):
        y_copies[2 * n].wait_send()
        y_copies[2 * n + 1].wait()
    deliver.end()
    for copy in copies:
        copy.wait()


def forward(*args):
    weight = jax.ShapeDtypeStruct((32, 48, FF_COLS), BF)
    group = GROUP * HEAD
    dma = pltpu.SemaphoreType.DMA
    spread = jax.ShapeDtypeStruct((2, 4, CHUNK, D), BF)
    return pl.pallas_call(
        forward_kernel,
        out_shape=(
            jax.ShapeDtypeStruct((2 * CHUNK, group), BF),
            jax.ShapeDtypeStruct((2 * CHUNK, group), BF),
            jax.ShapeDtypeStruct((2, 8, ROWS), F32),
            jax.ShapeDtypeStruct((CHUNKS, CHUNK, 2 * HEAD), BF),
            jax.ShapeDtypeStruct((2, D, 512), BF),
            jax.ShapeDtypeStruct((D // 2, D), BF),
            weight, weight, weight,
            jax.ShapeDtypeStruct((2 * CHUNK, D), BF),
            jax.ShapeDtypeStruct((2 * CHUNK, D), BF),
            jax.ShapeDtypeStruct((CHUNK, D), F32),
            jax.ShapeDtypeStruct((CHUNK, D), BF),
            spread, spread,
            jax.ShapeDtypeStruct((2, 8, ROWS), jnp.int32),
            jax.ShapeDtypeStruct((2 * CHUNK, HEAD), F32),
            jax.ShapeDtypeStruct((2 * CHUNK, HEAD), F32),
            jax.ShapeDtypeStruct((48, 1024), BF),
            jax.ShapeDtypeStruct((16, group), BF),
        ),
        in_specs=[ANY] * 2 + [pl.BlockSpec(memory_space=pltpu.SMEM)] + [IN_VMEM] * 11,
        out_specs=(IN_VMEM,) * 3 + (ANY,) * 6 + (IN_VMEM,) * 4 + (ANY,) * 2 + (IN_VMEM,) * 5,
        scratch_shapes=[
            pltpu.VMEM((CHUNKS, CHUNK, 2 * HEAD), BF),
            pltpu.VMEM((2, D, 512), BF),
            pltpu.VMEM((D // 2, D), BF),
            pltpu.VMEM((2, 2, 64, D), BF),
            pltpu.VMEM((2, 64, D), BF),
            pltpu.VMEM((2, CHUNK, 2 * HEAD), BF),
            pltpu.VMEM((HEAD, ROWS), F32),
            pltpu.VMEM((2, 8, ROWS), F32),
            pltpu.VMEM((4, 16, 512), BF),
            pltpu.VMEM((4, 16, 384), BF),
            pltpu.VMEM((48, 512), BF),
            pltpu.VMEM((48, 384), BF),
            pltpu.VMEM((CHUNK, D), BF),
            pltpu.VMEM((CHUNK, D), BF),
            pltpu.VMEM((CHUNK, D), BF),
            pltpu.VMEM((4, 16, 512), BF),
            pltpu.VMEM((4, 16, 384), BF),
            pltpu.VMEM((3, 48, PADDED), BF),
            dma((8,)), dma((8,)), dma((6,)), dma((6,)),
            dma((2, 3, Ring.sends)), dma((2, 3, 16)), dma((3,)), dma((3,)), dma((3,)),
        ]
        + GATHER_SEMS()
        + GATHER_SEMS()
        + [dma((3,)), dma((3,))]
        + GATHER_SEMS()
        + SPREAD_SEMS
        + [dma((3,)), dma((2,))]
        + SPREAD_SEMS,
        compiler_params=pltpu.CompilerParams(
            collective_id=1, has_side_effects=True, vmem_limit_bytes=48 * 2**20
        ),
        name="forward",
    )(*args)


class Collect:
    @staticmethod
    def scratch():
        piece, half = (CHUNK, D), (CHUNK // 2, D)
        return [
            pltpu.VMEM((4,) + piece, BF),
            pltpu.VMEM((4,) + piece, BF),
            pltpu.VMEM((2,) + half, BF),
            pltpu.VMEM((2,) + piece, BF),
            pltpu.VMEM(piece, BF),
            pltpu.VMEM((2,) + piece, BF),
            pltpu.SemaphoreType.DMA((8,)),
            pltpu.SemaphoreType.DMA((8,)),
            pltpu.SemaphoreType.DMA,
        ]

    scratches = 9

    def __init__(self, src, scratch):
        self.src = src
        (
            self.mine, self.pair, self.halves, self.last_in, self.far, self.near,
            self.send_sem, self.recv_sem, self.local_sem,
        ) = scratch
        self.w = ring_at()
        self.core = lax.axis_index("uly") % 2
        self.sent = []

    def send(self, src, dst, recv, device):
        copy = remote(src, dst, self.send_sem.at[recv], self.recv_sem.at[recv], device)
        copy.start()
        self.sent.append(copy)

    def start(self):
        self.local = pltpu.make_async_copy(self.src.at[self.core], self.mine, self.local_sem)
        self.local.start()
        for d in (2, 1, 3, 0):
            at = (self.w + d) % 4
            self.send(self.src.at[1 - self.core, at], self.pair.at[at], d, uly_others()[1])

    def both(self, d):
        at = (self.w + d) % 4
        wait_arrival(self.pair.at[at], self.recv_sem.at[d])
        return self.mine[at].astype(F32) + self.pair[at].astype(F32)

    def second(self):
        half = CHUNK // 2
        self.local.wait()
        self.far[...] = self.both(2).astype(BF)
        self.send(self.far.at[pl.ds(0, half)], self.halves.at[0], 4, ring_place((self.w + 1) % 4))
        self.send(self.far.at[pl.ds(half, half)], self.halves.at[1], 5, ring_place((self.w + 3) % 4))

    def third(self):
        half = CHUNK // 2
        for k, d in ((0, 1), (1, 3)):
            total = self.both(d)
            wait_arrival(self.halves.at[k], self.recv_sem.at[4 + k])
            rows = slice(k * half, (k + 1) * half)
            other = slice((1 - k) * half, (2 - k) * half)
            self.near[k, rows] = (total[rows] + self.halves[k].astype(F32)).astype(BF)
            self.near[k, other] = total[other].astype(BF)
            self.send(self.near.at[k], self.last_in.at[k], 6 + k, ring_place((self.w + d) % 4))

    def fourth(self):
        total = self.both(0)
        for k in (0, 1):
            wait_arrival(self.last_in.at[k], self.recv_sem.at[6 + k])
            total += self.last_in[k].astype(F32)
        for copy in self.sent:
            copy.wait_send()
        return total


def ff_kernel(
    set_ref, x_hbm, cot_hbm, gate_hbm, up_hbm, down_hbm, a_wide, a_down, b_wide, b_ff,
    grad_out, down_out, cols_ref, wide_ref,
    x_ref, cot_ref, gate_w, up_w, down_w, a_ff, b_cols, a_cols, b_out, hidden_ref, grad_gate, grad_up,
    out_buf, sems, out_sems,
):
    y, z, x, blk, uly = place()
    core = uly % 2
    first = (35 * uly) // 2 * 128 + y * FF_COLS
    columns = pl.ds(pl.multiple_of(first, 128), FF_COLS)
    pairs = [(down_hbm, down_w), (cot_hbm, cot_ref), (x_hbm, x_ref), (gate_hbm, gate_w), (up_hbm, up_w)]
    for s in (0, 1):
        chosen = set_ref[s]
        for n in (0, 1):
            pairs.append((a_wide.at[4 + n, chosen], a_ff.at[s, pl.ds(16 * n, 16)]))
            pairs.append((b_ff.at[n, chosen, :, columns], b_cols.at[s, n]))
        pairs.append((a_down.at[chosen, :, columns], a_cols.at[s]))
        pairs.append((b_wide.at[2, chosen], b_out.at[s]))
    copies = [pltpu.make_async_copy(src, dst, sems.at[n]) for n, (src, dst) in enumerate(pairs)]
    for copy in copies[5:] + copies[:5]:
        copy.start()
    for copy in copies[5:]:
        copy.wait()
    at = lax.broadcasted_iota(jnp.int32, (16, FF_COLS), 1) + (y * FF_COLS - 64 * core)
    inside = jnp.logical_and(at >= 0, at < FF // 4)

    def keep(v):
        return jnp.where(inside, v.astype(F32), 0.0).astype(BF)

    for s in (0, 1):
        a_cols[s] = keep(a_cols[s])
        for n in (0, 1):
            b_cols[s, n] = keep(b_cols[s, n])
    cols_ref[...] = jnp.zeros_like(cols_ref)
    here = pl.ds(pl.multiple_of(y * FF_COLS, 128), FF_COLS)
    copies[0].wait()
    copies[1].wait()

    def flat(ref, s):
        return ref[s].reshape(4 * CHUNK, D)

    out_copies = []
    for s in (0, 1):
        cot = flat(cot_ref, s)
        latent_cot = dot_nt(cot, b_out[s])
        grad_hidden = dot(cot, down_w[...]) + dot(latent_cot.astype(BF), a_cols[s])
        if s == 0:
            for copy in copies[2:5]:
                copy.wait()
        rows = flat(x_ref, s)
        latent = dot_nt(rows, a_ff[s])
        low = latent.astype(BF)
        gate = dot(rows, gate_w[...]) + dot(low[:, :16], b_cols[s, 0])
        sigmoid = jax.nn.sigmoid(gate)
        silu = gate * sigmoid
        grad_up[...] = (grad_hidden * silu).astype(BF)
        slope = grad_hidden * (sigmoid * (1.0 + gate * (1.0 - sigmoid)))
        up = dot(rows, up_w[...]) + dot(low[:, 16:], b_cols[s, 1])
        grad_gate[...] = (slope * up).astype(BF)
        hidden_ref[...] = (silu * up).astype(BF)
        back_gate = dot_nt(grad_gate[...], b_cols[s, 0])
        back_up = dot_nt(grad_up[...], b_cols[s, 1])
        grads = (
            dot_nt(grad_gate[...], gate_w[...])
            + dot_nt(grad_up[...], up_w[...])
            + dot(back_gate.astype(BF), a_ff[s, :16])
            + dot(back_up.astype(BF), a_ff[s, 16:])
        )
        out_buf[0, s] = grads.astype(BF).reshape(4, CHUNK, D)
        copy = pltpu.make_async_copy(out_buf.at[0, s], grad_out.at[s], out_sems.at[0, s])
        copy.start()
        out_copies.append(copy)
        latent_down = dot_nt(hidden_ref[...], a_cols[s])
        down = dot_nt(hidden_ref[...], down_w[...]) + dot(latent_down.astype(BF), b_out[s])
        out_buf[1, s] = down.astype(BF).reshape(4, CHUNK, D)
        copy = pltpu.make_async_copy(out_buf.at[1, s], down_out.at[s], out_sems.at[1, s])
        copy.start()
        out_copies.append(copy)

        def put(ref, n, value, at=slice(None)):
            ref[(2 * n + s) * 16 : (2 * n + s + 1) * 16, at] = value.astype(BF)

        def turned(value):
            return value.T.astype(BF)

        put(cols_ref, 0, dot(turned(latent_cot), hidden_ref[...]), here)
        put(cols_ref, 1, dot(turned(latent[:, :16]), grad_gate[...]), here)
        put(cols_ref, 2, dot(turned(latent[:, 16:]), grad_up[...]), here)
        put(wide_ref, 0, dot(turned(back_gate), rows))
        put(wide_ref, 1, dot(turned(back_up), rows))
        put(wide_ref, 2, dot(turned(latent_down), cot))
    for copy in out_copies:
        copy.wait()


def feed_forward(set_index, x, cot, gate_w, up_w, down_w, a_wide, a_down, b_wide, b_ff):
    spread = jax.ShapeDtypeStruct((2, 4, CHUNK, D), BF)
    weight = pltpu.VMEM((D, FF_COLS), BF)
    rows = pltpu.VMEM((4 * CHUNK, FF_COLS), BF)
    return pl.pallas_call(
        ff_kernel,
        out_shape=(
            spread, spread,
            jax.ShapeDtypeStruct((96, PADDED), BF),
            jax.ShapeDtypeStruct((96, D), BF),
        ),
        in_specs=[pl.BlockSpec(memory_space=pltpu.SMEM)] + [ANY] * 9,
        out_specs=(ANY, ANY, IN_VMEM, IN_VMEM),
        scratch_shapes=[
            pltpu.VMEM((2, 4, CHUNK, D), BF), pltpu.VMEM((2, 4, CHUNK, D), BF),
            weight, weight, weight,
            pltpu.VMEM((2, 32, D), BF), pltpu.VMEM((2, 2, 16, FF_COLS), BF),
            pltpu.VMEM((2, 16, FF_COLS), BF), pltpu.VMEM((2, 16, D), BF),
            rows, rows, rows,
            pltpu.VMEM((2, 2, 4, CHUNK, D), BF),
            pltpu.SemaphoreType.DMA((17,)), pltpu.SemaphoreType.DMA((2, 2)),
        ],
        compiler_params=pltpu.CompilerParams(vmem_limit_bytes=60 * 2**20),
        name="feed_forward",
    )(set_index, x, cot, gate_w, up_w, down_w, a_wide, a_down, b_wide, b_ff)


def backward_slot(
    slot, chunk, part, q_ref, kv_ref, limit_ref, mixed_ref, grad_ref, lse_ref, dq_ref, dkv_ref, acc_ref
):
    turned = head_columns(q_ref, slot)
    rows = head_rows(q_ref, slot)
    grad_turned = head_columns(grad_ref, slot)
    grad_rows = head_rows(grad_ref, slot)
    mixed_turned = head_columns(mixed_ref, slot)
    row_dot = jnp.sum(
        grad_turned.astype(F32) * mixed_turned.astype(F32), axis=0, keepdims=True
    )
    limit = limit_ref[slot, 0:1, :]
    lse = lse_ref[slot, 0:1, :]
    if part == 0:
        acc_ref[...] = jnp.zeros_like(acc_ref)

    def step(n, carry):
        keys, values = key_block(kv_ref, n)
        scores = jnp.where(key_places(n) <= limit, dot(keys, turned), -1e30)
        probs = jnp.exp2(scores - lse)
        grad_probs = dot(values, grad_turned)
        grad_scores = (probs * (grad_probs - row_dot)).astype(BF)
        acc_ref[...] += dot(keys.T, grad_scores)
        at = pl.ds(pl.multiple_of(n * KEYS, KEYS), KEYS)
        dkv_ref[at, :HEAD] += dot(grad_scores, rows)
        dkv_ref[at, HEAD:] += dot(probs.astype(BF), grad_rows)
        return carry

    blocks = chunk // STEP + 1
    lax.fori_loop(blocks * part // 4, blocks * (part + 1) // 4, step, 0)
    if part == 3:
        for n in range(GROUP):
            dq_ref[slot * CHUNK : (slot + 1) * CHUNK, n * HEAD : (n + 1) * HEAD] = (
                acc_ref[:, n * CHUNK : (n + 1) * CHUNK].T * HEAD ** (-0.5)
            )


class Reduce:
    sends = 28

    @staticmethod
    def scratch(shape):
        return [
            pltpu.VMEM((2, 3, 2, 4) + shape, BF),
            pltpu.VMEM((2, 3, 2) + shape, BF),
            pltpu.VMEM((2,) + shape, BF),
            pltpu.VMEM((2, 4, 2) + shape, BF),
            pltpu.VMEM((2, 2) + shape, BF),
            pltpu.SemaphoreType.DMA((2, Reduce.sends)),
            pltpu.SemaphoreType.DMA((2, Reduce.sends)),
        ]

    def __init__(self, part, index, scratch):
        self.part, self.index = part, index
        self.buf_q, self.buf_p, self.buf_y, self.sum_p, self.sum_y, self.send_sem, self.recv_sem = scratch
        self.y, self.z, self.x, self.blk, self.uly = place()
        self.pq = ((self.x, self.z), (self.z, self.x))
        self.flying = []

    def at(self, half, y, p, q):
        return blk_of(y, q, p) if half == 0 else blk_of(y, p, q)

    def send(self, src, dst, half, n, y, p, q):
        copy = pltpu.make_async_remote_copy(
            src_ref=src, dst_ref=dst,
            send_sem=self.send_sem.at[half, n], recv_sem=self.recv_sem.at[half, n],
            device_id=(self.at(half, y, p, q), self.uly), device_id_type=MESH,
        )
        copy.start()
        self.flying.append(copy)

    def land(self):
        for copy in self.flying:
            copy.wait()
        self.flying = []

    def first(self):
        for d in (2, 1, 3):
            for half in (0, 1):
                p, q = self.pq[half]
                to = (q + d) % 4
                for y in (0, 1):
                    for pp in range(4):
                        self.send(
                            self.part.at[self.index(half, self.at(half, y, pp, to))],
                            self.buf_q.at[half, d - 1, y, pp],
                            half, (d - 1) * 8 + y * 4 + pp, self.y, p, to,
                        )

    def second(self):
        self.land()
        for d in (2, 1, 3, 0):
            for half in (0, 1):
                p, q = self.pq[half]
                to = (p + d) % 4
                for y in (0, 1):
                    total = self.part[self.index(half, self.at(half, y, to, q))].astype(F32)
                    for n in range(3):
                        total += self.buf_q[half, n, y, to].astype(F32)
                    self.sum_p[half, d, y] = total.astype(BF)
                if d > 0:
                    self.send(
                        self.sum_p.at[half, d], self.buf_p.at[half, d - 1], half, 23 + d, self.y, to, q
                    )

    def third(self):
        self.land()
        for k in (1, 0):
            for half in (0, 1):
                p, q = self.pq[half]
                y = self.y if k == 0 else 1 - self.y
                total = self.sum_p[half, 0, y].astype(F32)
                for n in range(3):
                    total += self.buf_p[half, n, y].astype(F32)
                self.sum_y[half, k] = total.astype(BF)
                if k == 1:
                    self.send(self.sum_y.at[half, 1], self.buf_y.at[half], half, 27, 1 - self.y, p, q)

    def fourth(self):
        self.land()
        return [self.sum_y[half, 0].astype(F32) + self.buf_y[half].astype(F32) for half in (0, 1)]


def reduce_others():
    y, z, x, blk, uly = place()
    return (
        [(blk_of(1 - y, z, x), uly)]
        + [(blk_of(y, z, (x + d) % 4), uly) for d in (1, 2, 3)]
        + [(blk_of(y, (z + d) % 4, x), uly) for d in (1, 2, 3)]
    )


UNIT = (16, 128)


class Total:
    @staticmethod
    def scratch(kept, summed):
        shape = (kept + summed,) + UNIT
        return (
            [pltpu.VMEM((64,) + shape, BF)]
            + Reduce.scratch(shape)
            + [
                pltpu.VMEM((2,) + shape, BF),
                pltpu.VMEM((3, 2) + shape, BF),
                pltpu.VMEM((2, 4 * kept + summed) + UNIT, BF),
                pltpu.SemaphoreType.DMA((3,)),
                pltpu.SemaphoreType.DMA((3,)),
                pltpu.SemaphoreType.DMA((1, Gather.sends)),
                pltpu.SemaphoreType.DMA((1, 32)),
                pltpu.SemaphoreType.DMA((1,)),
                pltpu.SemaphoreType.DMA,
                pltpu.SemaphoreType.DMA,
            ]
        )

    scratches = 18

    @staticmethod
    def shape(kept, summed):
        return jax.ShapeDtypeStruct((2, 32, 4 * kept + summed) + UNIT, BF)

    def __init__(self, kept, summed, all_ref, scratch):
        self.kept, self.summed, self.all_ref = kept, summed, all_ref
        self.part = scratch[0]
        self.reduce = Reduce(self.part, lambda half, item: half * 32 + item, scratch[1:8])
        self.own, self.buf, self.full, self.send_sem, self.recv_sem = scratch[8:13]
        self.pair_send, self.pair_recv = scratch[16:18]
        self.y, self.z, self.x, self.blk, self.uly = place()
        self.core = self.uly % 2
        self.gather = Gather(
            lambda s: self.full.at[self.core],
            lambda s, item: self.all_ref.at[self.core, item],
            *scratch[13:16],
            orders=(self.core,),
        )

    def pack(self, values, first, per, at):
        for n, value in enumerate(values, first):
            self.part[n // per, at + n % per] = value.astype(BF)

    def pack_kept(self, values, first=0):
        self.pack(values, first, self.kept, 0)

    def pack_summed(self, values, first=0):
        self.pack(values, first, self.summed, self.kept)

    def clear(self, kept, summed):
        nothing = jnp.zeros(UNIT, BF)
        self.pack_kept([nothing] * (64 * self.kept - kept), kept)
        self.pack_summed([nothing] * (64 * self.summed - summed), summed)

    def across(self):
        for half, total in enumerate(self.reduce.fourth()):
            self.own[half] = total.astype(BF)
        self.copies = []
        for n, other in enumerate(uly_others()):
            copy = pltpu.make_async_remote_copy(
                src_ref=self.own, dst_ref=self.buf.at[n],
                send_sem=self.send_sem.at[n], recv_sem=self.recv_sem.at[n],
                device_id=other, device_id_type=MESH,
            )
            copy.start()
            self.copies.append(copy)

    def join(self):
        for copy in self.copies:
            copy.wait()
        kept = self.kept
        terms = [self.own] + [self.buf.at[n] for n in range(3)]
        who = [self.uly] + [other[1] for other in uly_others()]
        for half in (0, 1):
            for term, uly in zip(terms, who):
                self.full[half, pl.ds(uly * kept, kept)] = term[half, :kept]
            if self.summed:
                self.full[half, 4 * kept :] = sum(
                    term[half, kept:].astype(F32) for term in terms
                ).astype(BF)
        self.gather.start()

    def hand(self):
        self.gather.last()
        self.pair(self.core).start()

    def pair(self, core):
        return pltpu.make_async_remote_copy(
            src_ref=self.all_ref.at[core], dst_ref=self.all_ref.at[core],
            send_sem=self.pair_send, recv_sem=self.pair_recv,
            device_id=uly_others()[1], device_id_type=MESH,
        )

    def end(self):
        self.pair(self.core).wait_send()
        self.pair(1 - self.core).wait_recv()

    def steps(self):
        return [
            self.reduce.first, self.reduce.second, self.reduce.third, self.across, self.join,
            self.gather.second, self.gather.third, self.gather.fourth, self.hand, self.end,
        ]


def units(value):
    rows, columns = value.shape
    return [
        value[n * 16 : (n + 1) * 16, t * 128 : (t + 1) * 128]
        for n in range(rows // 16) for t in range(columns // 128)
    ]


FF_KEPT, FF_SUMMED, QKV_KEPT = 2, 2, 1
COL_TILES = PADDED // 128
D_TILES = D // 128
DKV_SCRATCH = 7


def backward_kernel(
    grad_part_ref, down_part_ref, kv_hbm, wq_hbm, wo_hbm, resid_ref, cot_ref, norm_ff_ref, norm_in_ref,
    rows_ref, normed_ref, a_qkv_ref, b_qkv_ref, ao_ref, bo_ref, q_ref, mixed_ref, limit_ref, lse_ref,
    cos_ref, sin_ref, cols_ref, ff_ref,
    result_ref, input_grad_ref, ff_all, qkv_all,
    kv_ref, wq_ref, wo_ref, dkv_ref, acc_ref, part, dq_ref, grad_ref, grad_attn, grad_resid, grad_qkv,
    cross_out, cross_in, home_out, home_in, copy_sem, cross_sem, home_send, home_recv,
    *scratch,
):
    y, z, x, blk, uly = place()
    core, h = uly % 2, uly // 2
    scratch = list(scratch)

    def take(count):
        got = scratch[:count]
        del scratch[:count]
        return got

    chunk = 2 * blk + h
    upper = chunk // 32
    home = (1 - upper) * chunk + upper * (63 - chunk)
    home_from = [(home, upper * 2 + s) for s in (0, 1)]
    own_chunk = (1 - h) * blk + h * (63 - blk)
    home_to = [(own_chunk // 2, (own_chunk % 2) * 2 + half) for half in (0, 1)]
    greet(
        reduce_others() + uly_others() + [(blk_of(1 - y, z, x), (uly + 2) % 4)] + home_from + home_to
    )
    copies = [
        pltpu.make_async_copy(src, dst, copy_sem.at[n])
        for n, (src, dst) in enumerate(((wo_hbm, wo_ref), (kv_hbm, kv_ref), (wq_hbm, wq_ref)))
    ]
    for copy in copies:
        copy.start()
    collect_grad = Collect(grad_part_ref, take(Collect.scratches))
    collect_out = Collect(down_part_ref, take(Collect.scratches))
    reduce = Reduce(
        part, lambda half, item: item if half == 0 else 63 - item, take(DKV_SCRATCH)
    )
    ff_total = Total(FF_KEPT, FF_SUMMED, ff_all, take(Total.scratches))
    qkv_total = Total(QKV_KEPT, 0, qkv_all, take(Total.scratches))
    deliver = Deliver()

    def send_home(n, value):
        home_out[n] = value.astype(BF)
        for half in (0, 1):
            deliver.send(
                home_out.at[n, pl.ds(half * 64, 64)], home_in.at[n, core],
                home_send.at[n, half], home_recv.at[n, core], home_to[half],
            )

    def arrived_home(n):
        for s in (0, 1):
            wait_arrival(home_in.at[n, s], home_recv.at[n, s])
        return home_in[n].astype(F32)

    collect_grad.start()
    ff_total.pack_kept(units(cols_ref))
    ff_total.pack_summed(units(ff_ref))
    at_o = 6 * COL_TILES
    ff_total.clear(at_o + D_TILES // 2 + D_TILES, 6 * D_TILES)
    qkv_total.clear(3 * D_TILES + D_TILES // 2 + 2, 0)
    collect_grad.second()
    collect_grad.third()
    residual = resid_ref[...]
    total = collect_grad.fourth()
    value = cot_ref[...].astype(F32) + norm_back(residual, norm_scale(residual), norm_ff_ref[...], total)
    grad_resid[...] = value
    own_rows = pl.ds(pl.multiple_of(h * CHUNK, CHUNK), CHUNK)
    other_rows = pl.ds(pl.multiple_of((1 - h) * CHUNK, CHUNK), CHUNK)
    grad_attn[own_rows, :] = value.astype(BF)
    partner = uly_others()[0]
    cross = remote(
        grad_attn.at[own_rows], grad_attn.at[own_rows], cross_sem.at[0], cross_sem.at[1], partner
    )
    cross.start()
    collect_out.start()
    dkv_ref[...] = jnp.zeros_like(dkv_ref)
    latent_o = dot_nt(ao_ref[...], mixed_ref[...]).astype(BF)
    cross.wait_send()
    wait_arrival(grad_attn.at[other_rows], cross_sem.at[1])
    copies[0].wait()
    back_o = dot_nt(grad_attn[...], bo_ref[...]).astype(BF)
    grad_ref[...] = (dot_nt(grad_attn[...], wo_ref[...]) + dot(back_o, ao_ref[...])).astype(BF)
    back_o = dot_nt(bo_ref[...], grad_attn[...]).astype(BF)
    ff_total.pack_kept(
        units(dot(back_o, mixed_ref[...])) + units(dot(latent_o, grad_attn[...])), at_o
    )

    copies[1].wait()
    steps = ff_total.steps()
    steps.pop(0)()
    more = [collect_out.second, collect_out.third]
    args = (q_ref, kv_ref, limit_ref, mixed_ref, grad_ref, lse_ref, dq_ref, dkv_ref, acc_ref)
    for slot, at in ((0, blk), (1, 63 - blk)):
        for part_of in range(4):
            backward_slot(slot, at, part_of, *args)
            if more:
                more.pop(0)()
            steps.pop(0)()

    def pack(n, carry):
        rows = dkv_ref[pl.ds(pl.multiple_of(n * CHUNK, CHUNK), CHUNK), :]
        part[n] = jnp.concatenate([rows[:, :HEAD] * LN2, rows[:, HEAD:]], axis=1).astype(BF)
        return carry

    lax.fori_loop(0, CHUNKS, pack, 0)
    reduce.first()
    send_home(0, resid_ref[...] + collect_out.fourth())
    while steps:
        steps.pop(0)()
    cos_table, sine_table = cos_ref[...], sin_ref[...]

    def turn_back(value, rows=slice(None)):
        return value * cos_table[rows] - pltpu.roll(value, HEAD // 2, 1) * sine_table[rows]

    for n in range(GROUP):
        at = slice(n * HEAD, (n + 1) * HEAD)
        grad_qkv[:, at] = turn_back(dq_ref[:, at]).astype(BF)
    latent_qkv = dot_nt(a_qkv_ref[...], normed_ref[...]).astype(BF)
    copies[2].wait()
    reduce.second()
    reduce.third()
    group = GROUP * HEAD
    for half, value in enumerate(reduce.fourth()):
        rows = slice(half * CHUNK, (half + 1) * CHUNK)
        grad_qkv[rows, group : group + HEAD] = turn_back(value[:, :HEAD], rows).astype(BF)
        grad_qkv[rows, group + HEAD :] = value[:, HEAD:].astype(BF)

    def project_back(rows):
        grads = grad_qkv[rows, :]
        lifted = dot(dot_nt(grads, b_qkv_ref[...]).astype(BF), a_qkv_ref[...])
        return dot_nt(grads[:, :512], wq_ref[0]) + dot_nt(grads[:, 512:], wq_ref[1]) + lifted

    cross_out[...] = project_back(other_rows).astype(BF)
    cross = remote(cross_out, cross_in, cross_sem.at[2], cross_sem.at[3], partner)
    cross.start()
    back_qkv = dot_nt(b_qkv_ref[...], grad_qkv[...]).astype(BF)
    grad_b = dot(latent_qkv, grad_qkv[...])
    qkv_total.pack_kept(
        units(dot(back_qkv, normed_ref[...]))
        + units(grad_b[:16, :group])
        + units(grad_b[16:32, group : group + HEAD])
        + units(grad_b[32:, group + HEAD :])
    )
    steps = qkv_total.steps()
    steps.pop(0)()
    mine = project_back(own_rows)
    steps.pop(0)()
    cross.wait()
    mine = mine + cross_in[...].astype(F32)
    tokens = rows_ref[own_rows, :].astype(F32)
    send_home(1, grad_resid[...] + norm_back(tokens, norm_scale(tokens), norm_in_ref[...], mine))
    while steps:
        steps.pop(0)()
    result_ref[...] = arrived_home(0).astype(BF)
    input_grad_ref[...] = arrived_home(1)
    deliver.end()


def backward(*args):
    dma = pltpu.SemaphoreType.DMA
    group = GROUP * HEAD
    return pl.pallas_call(
        backward_kernel,
        out_shape=(
            jax.ShapeDtypeStruct((2, CHUNK // 2, D), BF),
            jax.ShapeDtypeStruct((2, CHUNK // 2, D), F32),
            Total.shape(FF_KEPT, FF_SUMMED),
            Total.shape(QKV_KEPT, 0),
        ),
        in_specs=[ANY] * 5 + [IN_VMEM] * 18,
        out_specs=(IN_VMEM, IN_VMEM, ANY, ANY),
        scratch_shapes=[
            pltpu.VMEM((CHUNKS, CHUNK, 2 * HEAD), BF),
            pltpu.VMEM((2, D, 512), BF),
            pltpu.VMEM((D // 2, D), BF),
            pltpu.VMEM((CHUNKS * CHUNK, 2 * HEAD), F32),
            pltpu.VMEM((HEAD, ROWS), F32),
            pltpu.VMEM((CHUNKS, CHUNK, 2 * HEAD), BF),
            pltpu.VMEM((2 * CHUNK, group), F32),
            pltpu.VMEM((2 * CHUNK, group), BF),
            pltpu.VMEM((2 * CHUNK, D), BF),
            pltpu.VMEM((CHUNK, D), F32),
            pltpu.VMEM((2 * CHUNK, 1024), BF),
            pltpu.VMEM((CHUNK, D), BF),
            pltpu.VMEM((CHUNK, D), BF),
            pltpu.VMEM((2, CHUNK, D), BF),
            pltpu.VMEM((2, 2, CHUNK // 2, D), BF),
            dma((3,)), dma((4,)), dma((2, 2)), dma((2, 2)),
        ]
        + Collect.scratch() * 2
        + Reduce.scratch((CHUNK, 2 * HEAD))
        + Total.scratch(FF_KEPT, FF_SUMMED)
        + Total.scratch(QKV_KEPT, 0),
        compiler_params=pltpu.CompilerParams(
            collective_id=2, has_side_effects=True, vmem_limit_bytes=60 * 2**20
        ),
        name="backward",
    )(*args)


def fold_kernel(pick_ref, ff_ref, qkv_ref, a_wide, a_down, b_wide, b_kv, b_ff):
    c = pl.program_id(0)

    def kept(ref, per, n, u):
        return ref[n // per // 32, n // per % 32, u * per + n % per].astype(F32)

    def ff_kept(n, u):
        return kept(ff_ref, FF_KEPT, n, u)

    def qkv_kept(n, u):
        return kept(qkv_ref, QKV_KEPT, n, u)

    def summed(n):
        item = n // FF_SUMMED
        return ff_ref[item // 32, item % 32, 4 * FF_KEPT + n % FF_SUMMED].astype(F32)

    def put(ref, at, tile, value):
        ref[at + (slice(None), slice(tile * 128, (tile + 1) * 128))] = (
            pick_ref[c, 0] * value(0) + pick_ref[c, 1] * value(1)
        )

    for n in range(3):
        for t in range(D_TILES):
            put(a_wide, (n, 0), t, lambda s: qkv_kept(n * D_TILES + t, s) + qkv_kept(n * D_TILES + t, 2 + s))
    at_o = 6 * COL_TILES
    half = D_TILES // 2
    for t in range(D_TILES):
        h, part = t // half, t % half
        put(a_wide, (3, 0), t, lambda s: ff_kept(at_o + part, 2 * h + s))
        put(b_wide, (0, 0), t, lambda s: qkv_kept(3 * D_TILES + part, 2 * h + s))
        put(
            b_wide, (1, 0), t,
            lambda s: ff_kept(at_o + half + t, s) + ff_kept(at_o + half + t, 2 + s),
        )
        for n, (ref, at) in enumerate(((a_wide, (4, 0)), (a_wide, (5, 0)), (b_wide, (2, 0)))):
            put(ref, at, t, lambda s: summed((2 * n + s) * D_TILES + t))
    for n in (0, 1):
        for h in (0, 1):
            put(b_kv, (n, 0), h, lambda s: qkv_kept(3 * D_TILES + half + n, 2 * h + s))
    for n, (ref, at) in enumerate(((a_down, (0,)), (b_ff, (0, 0)), (b_ff, (1, 0)))):
        for t in range(FF // 128):
            where = [
                (u, t - start) for u, start in enumerate((0, 17, 35, 52)) if 0 <= t - start < COL_TILES
            ]
            put(
                ref, at, t,
                lambda s: sum(ff_kept((2 * n + s) * COL_TILES + tile, u) for u, tile in where),
            )


def fold(pick, ff_all, qkv_all):
    def whole(v):
        return pl.BlockSpec(v.shape, lambda c: (0,) * v.ndim)

    def by_set(lead, columns):
        shape = lead + (1, 16, columns)
        return pl.BlockSpec(shape, lambda c: (0,) * len(lead) + (c, 0, 0))

    def out(lead, columns):
        return jax.ShapeDtypeStruct(lead + (SETS, 16, columns), F32)

    outs = (((6,), D), ((), FF), ((3,), D), ((2,), 2 * HEAD), ((2,), FF))
    return pl.pallas_call(
        fold_kernel,
        grid=(SETS,),
        out_shape=tuple(out(*o) for o in outs),
        in_specs=[pl.BlockSpec(memory_space=pltpu.SMEM), whole(ff_all), whole(qkv_all)],
        out_specs=tuple(by_set(*o) for o in outs),
        compiler_params=pltpu.CompilerParams(vmem_limit_bytes=40 * 2**20),
        name="fold",
    )(pick, ff_all, qkv_all)


def norm_scale(hidden):
    return lax.rsqrt(jnp.mean(hidden * hidden, axis=-1, keepdims=True) + EPS)


def norm_back(hidden, scaled, gain_vec, upstream):
    normed = hidden * scaled
    weighted = upstream * gain_vec
    return scaled * (weighted - normed * jnp.mean(weighted * normed, axis=-1, keepdims=True))


def body(
    tokens, cotangent, lengths, set_index, norm_in, norm_ff, qkv_bias, w_qkv, w_out, w_gate_up, w_down,
    a_wide, a_down, b_wide, b_kv, b_ff,
):
    own_set = set_index[lax.axis_index("uly") % 2]

    def chosen(table):
        return lax.dynamic_index_in_dim(table, own_set, 1, keepdims=False)

    a_own, b_own = chosen(a_wide[:4]), chosen(b_wide[:2])
    frequencies = np.float64(THETA) ** (-np.arange(0, HEAD, 2, dtype=np.float64) / HEAD)
    frequencies = np.concatenate([frequencies, frequencies])[None].astype(np.float32)
    (
        q, mixed, lse, kv_all, qkv_w, out_w, gate_w, up_w, down_w, rows, normed, residual, grad_out,
        gathered, grad_gathered, limit, cos_table, sine_table, b_qkv, ao,
    ) = forward(
        tokens, cotangent, lengths, w_qkv, w_out, w_gate_up, w_down.T, norm_in[None], norm_ff[None],
        qkv_bias.reshape(16, HEAD), frequencies, a_own, b_own, chosen(b_kv),
    )
    gate_w, up_w, down_w = (w.reshape(D, FF_COLS) for w in (gate_w, up_w, down_w))
    grad_part, down_part, cols, ff_wide = feed_forward(
        set_index, gathered, grad_gathered, gate_w, up_w, down_w, a_wide, a_down, b_wide, b_ff
    )
    result, input_grad, ff_all, qkv_all = backward(
        grad_part, down_part, kv_all, qkv_w, out_w, residual, grad_out, norm_ff[None], norm_in[None], rows, normed,
        a_own[:3].reshape(48, D), b_qkv, ao, b_own[1], q, mixed, limit, lse, cos_table, sine_table, cols, ff_wide,
    )
    pick = (jnp.arange(SETS, dtype=jnp.int32)[:, None] == set_index[None, :]).astype(F32)
    return (result, input_grad) + tuple(fold(pick, ff_all, qkv_all))


def solution(mesh):
    spread = P(None, ("blk", "uly"), None)
    in_specs = (
        spread, spread, P(), P(), P(), P(), P(),
        P(("blk", "uly"), None), P(("blk", "uly"), None), P(None, "blk", "uly"), P("uly", "blk"),
        P(), P(), P(), P(), P(),
    )
    out_specs = (spread, spread, P(), P(), P(), P(), P())
    return jax.shard_map(body, mesh=mesh, in_specs=in_specs, out_specs=out_specs, check_vma=False)
```

```python
import functools

import jax
import jax.numpy as jnp
import numpy as np
from jax import lax
from jax.experimental import pallas as pl
from jax.experimental.pallas import tpu as pltpu
from jax.sharding import PartitionSpec as P

HEADS = 12
KV_HEADS = 2
HEAD = 128
GROUP = HEADS // KV_HEADS
FF = 8960
SETS = 8
D = 1536
CHUNK = 128
CHUNKS = 64
PADDED = 2304
EPS = 1e-06
THETA = 1000000.0
LOG2E = 1.4426950408889634
LN2 = 0.6931471805599453
MESH = pl.DeviceIdType.MESH
BF = jnp.bfloat16
F32 = jnp.float32
ANY = pl.BlockSpec(memory_space=pl.ANY)
IN_VMEM = pl.BlockSpec(memory_space=pltpu.VMEM)


def blk_of(y, z, x):
    return y * 16 + z * 4 + x


def place():
    blk = lax.axis_index("blk")
    return blk // 16, (blk // 4) % 4, blk % 4, blk, lax.axis_index("uly")


def ring_others():
    y, z, x, blk, uly = place()
    return [
        (blk_of(1 - y, z, x), uly),
        (blk_of(y, z, (x + 1) % 4), uly),
        (blk_of(y, z, (x + 3) % 4), uly),
        (blk_of(y, (z + 1) % 4, x), uly),
        (blk_of(y, (z + 3) % 4, x), uly),
    ]


def greet(others, meanwhile=None):
    barrier = pltpu.get_barrier_semaphore()
    for other in others:
        pl.semaphore_signal(barrier, inc=1, device_id=other, device_id_type=MESH)
    if meanwhile is not None:
        meanwhile()
    pl.semaphore_wait(barrier, len(others))


class Gather:
    sends = 31

    def __init__(self, src, dst, send_sem, recv_sem, local_sem, orders=(0, 1)):
        self.src, self.dst, self.orders = src, dst, orders
        self.streams = range(len(orders))
        self.send_sem, self.recv_sem, self.local_sem = send_sem, recv_sem, local_sem
        self.y, self.z, self.x, self.blk, self.uly = place()
        self.count = [0] * len(orders)
        self.sent = []
        self.local = []

    def at(self, stream, y, p, q):
        order = self.orders[stream]
        return blk_of(y, order * p + (1 - order) * q, order * q + (1 - order) * p)

    def pq(self, stream):
        order = self.orders[stream]
        return (
            order * self.z + (1 - order) * self.x,
            order * self.x + (1 - order) * self.z,
        )

    def send(self, stream, item, target, src=None):
        copy = pltpu.make_async_remote_copy(
            src_ref=self.dst(stream, item) if src is None else src,
            dst_ref=self.dst(stream, item),
            send_sem=self.send_sem.at[stream, self.count[stream]],
            recv_sem=self.recv_sem.at[stream, item],
            device_id=(target, self.uly),
            device_id_type=MESH,
        )
        self.count[stream] += 1
        copy.start()
        self.sent.append(copy)

    def wait(self, stream, item):
        ref = self.dst(stream, item)
        pltpu.make_async_remote_copy(
            src_ref=ref,
            dst_ref=ref,
            send_sem=self.send_sem.at[stream, 0],
            recv_sem=self.recv_sem.at[stream, item],
            device_id=(self.blk, self.uly),
            device_id_type=MESH,
        ).wait_recv()

    def start(self):
        for s in self.streams:
            p, q = self.pq(s)
            self.send(s, self.blk, self.at(s, 1 - self.y, p, q), self.src(s))
        for s in self.streams:
            p, q = self.pq(s)
            for d in (1, 3):
                self.send(s, self.blk, self.at(s, self.y, (p + d) % 4, q), self.src(s))
            copy = pltpu.make_async_copy(self.src(s), self.dst(s, self.blk), self.local_sem.at[s])
            copy.start()
            self.local.append(copy)

    def second(self):
        for s in self.streams:
            p, q = self.pq(s)
            item = self.at(s, 1 - self.y, p, q)
            self.wait(s, item)
            for d in (1, 3):
                self.send(s, item, self.at(s, self.y, (p + d) % 4, q))
            for d in (1, 3):
                onward = self.at(s, self.y, p, (q + d) % 4)
                self.send(s, self.blk, onward, self.src(s))
                self.send(s, item, onward)

    def spread(self, s, item):
        p, q = self.pq(s)
        for d in (1, 3):
            self.send(s, item, self.at(s, self.y, p, (q + d) % 4))

    def third(self):
        for k, y in enumerate((self.y, 1 - self.y)):
            for s in self.streams:
                p, q = self.pq(s)
                for d in (3, 1):
                    item = self.at(s, y, (p + d) % 4, q)
                    self.wait(s, item)
                    if (d == 3) == (k == 0):
                        self.send(s, item, self.at(s, self.y, (p + 4 - d) % 4, q))
                    self.spread(s, item)
        for y in (self.y, 1 - self.y):
            for s in self.streams:
                p, q = self.pq(s)
                item = self.at(s, y, (p + 2) % 4, q)
                self.wait(s, item)
                self.spread(s, item)

    def fourth(self):
        for e in (0, 1, 3, 2):
            for k, y in enumerate((self.y, 1 - self.y)):
                for s in self.streams:
                    p, q = self.pq(s)
                    for d in (3, 1):
                        item = self.at(s, y, (p + e) % 4, (q + d) % 4)
                        self.wait(s, item)
                        if (d == 3) == (k == 0):
                            self.send(s, item, self.at(s, self.y, p, (q + 4 - d) % 4))

    def last(self):
        for e in (0, 1, 3, 2):
            for y in (self.y, 1 - self.y):
                for s in self.streams:
                    p, q = self.pq(s)
                    self.wait(s, self.at(s, y, (p + e) % 4, (q + 2) % 4))
        for copy in self.local:
            copy.wait()
        for copy in self.sent:
            copy.wait_send()


GATHER_SEMS = lambda *lead: [
    pltpu.SemaphoreType.DMA(lead + (2, Gather.sends)),
    pltpu.SemaphoreType.DMA(lead + (2, 32)),
    pltpu.SemaphoreType.DMA(lead + (2,)),
]


KEYS = 1024
STEP = KEYS // CHUNK
ROWS = GROUP * CHUNK


def head_columns(ref, slot):
    return jnp.concatenate(
        [
            ref[slot * CHUNK : (slot + 1) * CHUNK, n * HEAD : (n + 1) * HEAD].T
            for n in range(GROUP)
        ],
        axis=1,
    )


def head_rows(ref, slot):
    return jnp.concatenate(
        [
            ref[slot * CHUNK : (slot + 1) * CHUNK, n * HEAD : (n + 1) * HEAD]
            for n in range(GROUP)
        ],
        axis=0,
    )


def key_block(kv_ref, step):
    rows = kv_ref[pl.ds(step * STEP, STEP)].reshape(KEYS, 2 * HEAD)
    return rows[:, :HEAD], rows[:, HEAD:]


def dot(a, b):
    return jnp.dot(a, b, preferred_element_type=F32)


def key_places(step):
    return lax.broadcasted_iota(jnp.int32, (KEYS, ROWS), 0) + step * KEYS


def dot_nt(a, b):
    return lax.dot_general(a, b, (((1,), (1,)), ((), ())), preferred_element_type=F32)


def forward_slot(slot, chunk, part, q_ref, kv_ref, limit_ref, mixed_ref, lse_ref, acc_ref, stat_ref):
    turned = head_columns(q_ref, slot)
    limit = limit_ref[slot, 0:1, :]
    if part == 0:
        acc_ref[...] = jnp.zeros_like(acc_ref)
        stat_ref[0] = jnp.full(stat_ref.shape[1:], -1e30, F32)
        stat_ref[1] = jnp.zeros(stat_ref.shape[1:], F32)

    def step(n, carry):
        top, total = carry
        keys, values = key_block(kv_ref, n)
        scores = jnp.where(key_places(n) <= limit, dot(keys, turned), -1e30)
        new_top = jnp.maximum(top, jnp.max(scores, axis=0, keepdims=True))
        fade = jnp.exp2(top - new_top)
        probs = jnp.exp2(scores - new_top)
        total = total * fade + jnp.sum(probs, axis=0, keepdims=True)
        acc_ref[...] = acc_ref[...] * fade + dot(values.T, probs.astype(BF))
        return new_top, total

    blocks = chunk // STEP + 1
    top, total = lax.fori_loop(
        blocks * part // 4, blocks * (part + 1) // 4, step, (stat_ref[0, 0:1, :], stat_ref[1, 0:1, :])
    )
    if part < 3:
        stat_ref[0, 0:1, :] = top
        stat_ref[1, 0:1, :] = total
        return
    out = acc_ref[...] / total
    for n in range(GROUP):
        mixed_ref[slot * CHUNK : (slot + 1) * CHUNK, n * HEAD : (n + 1) * HEAD] = out[
            :, n * CHUNK : (n + 1) * CHUNK
        ].T.astype(BF)
    lse_ref[slot] = jnp.broadcast_to(top + jnp.log2(total), (8, ROWS))


def uly_others():
    y, z, x, blk, uly = place()
    return [(blk, (uly + 2) % 4), (blk, uly + 1 - 2 * (uly % 2)), (blk, 3 - uly)]


def ring_place(w):
    y, z, x, blk, uly = place()
    return (blk_of(w % 2, z, x), (w // 2) * 2 + uly % 2)


def ring_at():
    y, z, x, blk, uly = place()
    return (uly // 2) * 2 + y


def wait_arrival(ref, sem):
    pltpu.make_async_copy(ref, ref, sem).wait()


def remote(src, dst, send, recv, device):
    return pltpu.make_async_remote_copy(
        src_ref=src, dst_ref=dst, send_sem=send, recv_sem=recv, device_id=device, device_id_type=MESH
    )


class Deliver:
    def __init__(self):
        self.sent = []

    def send(self, src, dst, send, recv, device):
        y, z, x, blk, uly = place()
        here = jnp.logical_and(device[0] == blk, device[1] == uly)

        @pl.when(here)
        def _():
            pltpu.make_async_copy(src, dst, recv).start()

        @pl.when(jnp.logical_not(here))
        def _():
            remote(src, dst, send, recv, device).start()

        self.sent.append((here, src, dst, send, recv, device))

    def end(self):
        for here, *copy in self.sent:

            @pl.when(jnp.logical_not(here))
            def _():
                remote(*copy).wait_send()


class Ring:
    sends = 15

    def __init__(self, src, dst, y, order, way, send_sem, recv_sem):
        self.src, self.dst, self.y, self.order, self.way = src, dst, y, order, way
        self.send_sem, self.recv_sem = send_sem, recv_sem
        self.own_y, self.z, self.x, self.blk, self.uly = place()
        self.p = order * self.z + (1 - order) * self.x
        self.q = order * self.x + (1 - order) * self.z
        self.sent = []

    def at(self, y, p, q):
        order = self.order
        return blk_of(y, order * p + (1 - order) * q, order * q + (1 - order) * p)

    def index(self, p, q):
        return self.at(0, p, q)

    def send(self, p, q, dp, dq, src=None):
        ref = self.dst(self.at(self.y, p, q))
        target = self.at(self.own_y, (self.p + dp) % 4, (self.q + dq) % 4)
        copy = remote(
            ref if src is None else src, ref, self.send_sem.at[len(self.sent)],
            self.recv_sem.at[self.index(p, q)], (target, self.uly),
        )
        copy.start()
        self.sent.append(copy)

    def wait(self, p, q):
        wait_arrival(self.dst(self.at(self.y, p, q)), self.recv_sem.at[self.index(p, q)])

    def start(self):
        for d in (1, 3):
            self.send(self.p, self.q, d, 0, self.src)

    def second(self):
        for d in (4 - self.way, self.way):
            p = (self.p + d) % 4
            self.wait(p, self.q)
            if d == 4 - self.way:
                self.send(p, self.q, self.way, 0)

    def third(self):
        self.wait((self.p + 2) % 4, self.q)

    def spread(self, e):
        p = (self.p + e) % 4
        for d in (1, 3):
            self.send(p, self.q, 0, d, self.src if e == 0 else None)

    def fourth(self, e):
        p = (self.p + e) % 4
        for d in (4 - self.way, self.way):
            q = (self.q + d) % 4
            self.wait(p, q)
            if d == 4 - self.way:
                self.send(p, q, 0, self.way)

    def last(self):
        for e in (0, 1, 3, 2):
            self.wait((self.p + e) % 4, (self.q + 2) % 4)
        for copy in self.sent:
            copy.wait_send()


class Spread:
    def __init__(self, own, all_ref, send_sem, recv_sem, local_sem):
        self.own, self.all_ref = own, all_ref
        self.send_sem, self.recv_sem, self.local_sem = send_sem, recv_sem, local_sem
        self.w = ring_at()
        self.core = lax.axis_index("uly") % 2
        self.sibling = uly_others()[1]
        self.sent = []

    def piece(self, d, rows=slice(None), core=None):
        core = self.core if core is None else core
        ref = self.all_ref.at[core, (self.w + d) % 4]
        return ref if rows == slice(None) else ref.at[pl.ds(rows.start, rows.stop - rows.start)]

    def send(self, src, dst, recv, device):
        copy = remote(src, dst, self.send_sem.at[len(self.sent)], self.recv_sem.at[recv], device)
        copy.start()
        self.sent.append(copy)

    def pair(self, d, src=None):
        self.send(self.piece(d) if src is None else src, self.piece(d), 4 + d, self.sibling)

    def start(self):
        self.local = pltpu.make_async_copy(self.own, self.piece(0), self.local_sem)
        self.local.start()
        self.send(self.own, self.piece(0), 0, ring_place((self.w + 1) % 4))
        self.send(self.own, self.piece(0), 1, ring_place((self.w + 3) % 4))
        self.pair(0, self.own)

    def second(self):
        half = CHUNK // 2
        wait_arrival(self.piece(3), self.recv_sem.at[0])
        low = self.piece(3, slice(0, half))
        self.send(low, low, 2, ring_place((self.w + 1) % 4))
        self.pair(3)
        wait_arrival(self.piece(1), self.recv_sem.at[1])
        high = self.piece(1, slice(half, CHUNK))
        self.send(high, high, 3, ring_place((self.w + 3) % 4))
        self.pair(1)

    def third(self):
        half = CHUNK // 2
        wait_arrival(self.piece(2, slice(0, half)), self.recv_sem.at[2])
        wait_arrival(self.piece(2, slice(half, CHUNK)), self.recv_sem.at[3])
        self.pair(2)

    def last(self):
        for d in range(4):
            wait_arrival(self.piece(d, core=1 - self.core), self.recv_sem.at[4 + d])
        for copy in self.sent:
            copy.wait_send()
        self.local.wait()


SPREAD_SEMS = [pltpu.SemaphoreType.DMA((8,)), pltpu.SemaphoreType.DMA((8,)), pltpu.SemaphoreType.DMA]
FF_COLS = PADDED // 2


def forward_kernel(
    tokens_ref, cot_ref, length_ref, qkv_ref, out_ref, gate_up_ref, down_ref, norm_in_ref, norm_ff_ref,
    bias_ref, freq_ref, a_ref, b_ref, bkv_ref,
    q_out, mixed_out, lse_out, kv_out, wq_out, wo_out, gate_all, up_all, down_all, rows_hbm, normed_out,
    resid_out, cot_out, nf_all, cot_all, limit_out, cos_out, sin_out, b_qkv_out, ao_out,
    q_ref, mixed_ref, lse_ref, rows_out, normed_ref, resid_ref, cot_own, limit_ref, cos_ref, sin_ref,
    b_qkv_ref, ao_ref, kv_all, wq_all, wo_all, rows, cot_in, kv_part, acc_ref, stat_ref, qkv_in, out_in, qkv_part, out_part,
    nf_own, cross_out, cross_in, qkv_pieces, out_pieces, ff_ref,
    *sems,
):
    y, z, x, blk, uly = place()
    core, h = uly % 2, uly // 2
    sems = list(sems)

    def take(count):
        got = sems[:count]
        del sems[:count]
        return got

    chunk = 2 * blk + h
    upper = chunk // 32
    home = (1 - upper) * chunk + upper * (63 - chunk)
    row_to = [[(home, hh * 2 + s) for hh in (0, 1)] for s in (0, 1)]
    row_from = [(c // 2, (c % 2) * 2 + half) for c in (blk, 63 - blk) for half in (0, 1)]
    out_to = [(2 * (blk % 16) + q // 2, (blk // 16) * 2 + q % 2) for q in range(4)]
    out_from = [(16 * h + blk // 2, u) for u in range(4)]
    sibling = uly_others()[1]
    length = length_ref[0] * (1 - core) + length_ref[1] * core

    def prepare():
        qkv_pieces[...] = jnp.zeros_like(qkv_pieces)
        out_pieces[...] = jnp.zeros_like(out_pieces)
        group = GROUP * HEAD
        for hh in (0, 1):
            qkv_pieces[2 * hh, :12] = qkv_ref[:, hh * group : hh * group + 512]
            for place_at, start, size in (
                (0, hh * group + 512, 256),
                (256, HEADS * HEAD + hh * HEAD, HEAD),
                (384, HEADS * HEAD + 256 + hh * HEAD, HEAD),
            ):
                qkv_pieces[2 * hh + 1, :12, place_at : place_at + size] = qkv_ref[:, start : start + size]
        for q in range(4):
            out_pieces[q, :12] = out_ref[:, q * 384 : (q + 1) * 384]
        for n in range(3):
            part = (gate_up_ref[n] if n < 2 else down_ref[...]).astype(F32)
            none = jnp.zeros((48, 64), F32)
            left = jnp.concatenate([part, none], axis=1)
            right = jnp.concatenate([none, part], axis=1)
            ff_ref[n] = jnp.where(jnp.broadcast_to(core, (48, PADDED)) == 1, right, left).astype(BF)

    greet(
        ring_others() + uly_others() + [(blk_of(1 - y, z, x), (uly + 2) % 4)]
        + row_to[0] + row_to[1] + row_from + out_to + out_from,
        prepare,
    )

    deliver = Deliver()
    piece_send, piece_recv, row_send, row_recv = take(4)
    for q in range(4):
        deliver.send(qkv_pieces.at[q], qkv_in.at[uly], piece_send.at[q], piece_recv.at[uly], (blk, q))
    for q in range(4):
        deliver.send(out_pieces.at[q], out_in.at[uly], piece_send.at[4 + q], piece_recv.at[4 + uly], out_to[q])
    for s in (0, 1):
        for hh in (0, 1):
            deliver.send(
                tokens_ref.at[s], rows.at[upper, core], row_send.at[s * 2 + hh],
                row_recv.at[upper * 2 + core], row_to[s][hh],
            )

    wide = PADDED // 2
    gathered = (gate_all, up_all, down_all)
    ff_send, ff_recv, y_send, y_recv, y_local = take(5)
    other_blk = blk_of(1 - y, z, x)

    def ff_part(n, half):
        return ff_ref.at[n, :, pl.ds(pl.multiple_of(half * wide, 128), wide)]

    picked = lax.broadcasted_iota(jnp.int32, (48, 64), 1)
    picked = jnp.where(picked % 16 < 12, picked // 16 * 12 + picked % 16, -1)
    picked = jnp.where(picked == lax.broadcasted_iota(jnp.int32, (48, 64), 0), 1.0, 0.0).astype(BF)
    for u in range(4):
        wait_arrival(qkv_in.at[u], piece_recv.at[u])
    qkv_part[...] = dot(picked, qkv_in[...].reshape(64, 512)).astype(BF)
    wq = Gather(
        lambda s: qkv_part.at[:, pl.ds(256 * s, 256)],
        lambda s, item: wq_all.at[
            core, pl.ds(pl.multiple_of(item * 48, 16), 48), pl.ds(256 * s, 256)
        ],
        *take(3),
    )
    wq.start()
    for u in range(4):
        wait_arrival(out_in.at[u], piece_recv.at[4 + u])
    out_part[...] = dot(picked, out_in[...].reshape(64, 384)).astype(BF)
    y_copies = []
    for n, ref in enumerate(gathered):
        copy = remote(ff_part(n, 1 - y), ref.at[blk], y_send.at[n], y_recv.at[n], (other_blk, uly))
        copy.start()
        y_copies.append(copy)
        copy = pltpu.make_async_copy(ff_part(n, y), ref.at[blk], y_local.at[n])
        copy.start()
        y_copies.append(copy)
    for s in (0, 1):
        deliver.send(
            cot_ref.at[s], cot_in.at[core], row_send.at[4 + s], row_recv.at[4 + core], (home, upper * 2 + s)
        )

    def out_columns(item, s):
        start = ((item % 2) * 2 + core) * 384
        return pl.ds(pl.multiple_of(start + 128 * s, 128), 128 + 128 * s)

    wo = Gather(
        lambda s: out_part.at[:, pl.ds(128 * s, 128 + 128 * s)],
        lambda s, item: wo_all.at[pl.ds(pl.multiple_of((item // 2) * 48, 16), 48), out_columns(item, s)],
        *take(3),
    )
    own_ff, other_ff = (
        [
            Ring(
                ff_part(n, y) if k == 0 else ref.at[other_blk],
                lambda item, ref=ref: ref.at[item],
                y if k == 0 else 1 - y,
                y if k == 0 else 1 - y,
                (1, 3, 1 + 2 * k)[n],
                ff_send.at[k, n], ff_recv.at[k, n],
            )
            for n, ref in enumerate(gathered)
        ]
        for k in (0, 1)
    )
    rings = own_ff + other_ff
    wq.second()
    wq.third()
    wq.fourth()
    for ring in own_ff:
        ring.start()
    for n in range(3):
        y_copies[2 * n].wait_recv()
    for ring in other_ff:
        ring.start()

    for slot, at in ((0, blk), (1, 63 - blk)):
        row = lax.broadcasted_iota(jnp.int32, (CHUNK, HEAD), 0) + at * CHUNK
        angle = row.astype(F32) * freq_ref[...]
        first = lax.broadcasted_iota(jnp.int32, (CHUNK, HEAD), 1) < HEAD // 2
        sine = jnp.sin(angle)
        cos_ref[slot * CHUNK : (slot + 1) * CHUNK, :] = jnp.cos(angle)
        sin_ref[slot * CHUNK : (slot + 1) * CHUNK, :] = jnp.where(first, -sine, sine)
        row = lax.broadcasted_iota(jnp.int32, (8, ROWS), 1) % CHUNK + at * CHUNK
        limit_ref[slot] = jnp.minimum(row, length - 1)
    group = GROUP * HEAD
    group_at = pl.ds(pl.multiple_of(h * group, 128), group)
    head_at = pl.ds(pl.multiple_of(h * HEAD, 128), HEAD)
    ao_ref[...] = a_ref[3, :, group_at]
    b_qkv_ref[...] = jnp.zeros_like(b_qkv_ref)
    b_qkv_ref[:16, :group] = b_ref[0, :, group_at]
    b_qkv_ref[16:32, group : group + HEAD] = bkv_ref[0, :, head_at]
    b_qkv_ref[32:, group + HEAD :] = bkv_ref[1, :, head_at]
    a_qkv = a_ref[:3].reshape(48, D)
    bo_ref = b_ref.at[1]

    def bias(n):
        at = h * GROUP + n if n < GROUP else HEADS + 2 * (n - GROUP) + h
        return bias_ref[pl.ds(at, 1), :]

    for n in range(4):
        wait_arrival(rows.at[n // 2, n % 2], row_recv.at[n])
        value = rows[n // 2, n % 2].astype(F32)
        at = slice(n * 64, (n + 1) * 64)
        rows_out[at, :] = rows[n // 2, n % 2]
        normed_ref[at, :] = (value * norm_scale(value) * norm_in_ref[...]).astype(BF)
    latent = dot_nt(normed_ref[...], a_qkv)
    adapted = dot(latent.astype(BF), b_qkv_ref[...])
    wq.last()
    pair_send, pair_recv = take(2)

    def pair_copy(ref, n):
        return remote(ref, ref, pair_send.at[n], pair_recv.at[n], sibling)

    pair_copy(wq_all.at[core], 0).start()
    wo.start()
    pair_copy(wq_all.at[core], 0).wait_send()
    pair_copy(wq_all.at[1 - core], 0).wait_recv()

    cos_table, sine_table = cos_ref[...], sin_ref[...]

    def turn(head):
        return head * cos_table + pltpu.roll(head, HEAD // 2, 1) * sine_table

    def query(n, head):
        q_ref[:, n * HEAD : (n + 1) * HEAD] = (turn(head + bias(n)) * (HEAD ** (-0.5) * LOG2E)).astype(BF)

    pairs = dot(normed_ref[...], wq_all[1, :, 256:]) + adapted[:, 768:]
    for n, head in ((0, turn(pairs[:, :HEAD] + bias(6))), (1, pairs[:, HEAD:] + bias(7))):
        at = slice(n * HEAD, (n + 1) * HEAD)
        kv_part[0, :, at] = head[:CHUNK].astype(BF)
        kv_part[1, :, at] = head[CHUNK:].astype(BF)
    kv = Gather(
        lambda s: kv_part.at[s],
        lambda s, item: kv_all.at[item if s == 0 else 63 - item],
        *take(3),
    )
    kv.start()
    heads = dot(normed_ref[...], wq_all[1, :, :256]) + adapted[:, 512:768]
    for n in (4, 5):
        query(n, heads[:, (n - 4) * HEAD : (n - 3) * HEAD])
    kv.second()
    for ring in rings:
        ring.second()
    wo.second()
    heads = dot(normed_ref[...], wq_all[0]) + adapted[:, :512]
    for n in range(4):
        query(n, heads[:, n * HEAD : (n + 1) * HEAD])
    kv.third()
    for ring in rings:
        ring.third()
    wo.third()
    kv.fourth()
    wo.fourth()

    for half in (0, 1):
        wait_arrival(cot_in.at[half], row_recv.at[4 + half])
        start = ((1 - h) * blk + h * (63 - blk)) * CHUNK + half * 64
        at = lax.broadcasted_iota(jnp.int32, (64, D), 0) + start
        cot_own[half * 64 : (half + 1) * 64, :] = jnp.where(
            at < length, cot_in[half].astype(F32), 0.0
        ).astype(BF)
    cot_spread = Spread(cot_own, cot_all, *take(3))
    cot_spread.start()
    kv.last()
    for e in (0, 1, 3, 2):
        for ring in rings:
            ring.spread(e)
    (out_sem,) = take(1)
    copies = []

    def keep(*pairs):
        for src, dst in pairs:
            copies.append(pltpu.make_async_copy(src, dst, out_sem.at[len(copies)]))
            copies[-1].start()

    keep(
        (kv_all, kv_out), (wq_all, wq_out), (q_ref, q_out), (rows_out, rows_hbm), (normed_ref, normed_out),
        (cot_own, cot_out), (limit_ref, limit_out), (cos_ref, cos_out), (sin_ref, sin_out),
        (b_qkv_ref, b_qkv_out), (ao_ref, ao_out),
    )
    wo.last()

    def wo_columns(c, n):
        return wo_all.at[:, pl.ds(pl.multiple_of((2 * n + c) * 384, 128), 384)]

    for n in (0, 1):
        pair_copy(wo_columns(core, n), 1 + n).start()
    args = (q_ref, kv_all, limit_ref, mixed_ref, lse_ref, acc_ref, stat_ref)
    beside = {
        3: lambda: [ring.fourth(0) for ring in rings] + [cot_spread.second()],
        5: lambda: [ring.fourth(1) for ring in rings],
        6: lambda: [ring.fourth(3) for ring in rings] + [cot_spread.third()],
        7: lambda: [ring.fourth(2) for ring in rings],
    }
    for slot, at in ((0, blk), (1, 63 - blk)):
        for part in range(4):
            forward_slot(slot, at, part, *args)
            if slot * 4 + part in beside:
                beside[slot * 4 + part]()
    for n in (0, 1):
        pair_copy(wo_columns(core, n), 1 + n).wait_send()
        pair_copy(wo_columns(1 - core, n), 1 + n).wait_recv()
    keep((wo_all, wo_out), (mixed_ref, mixed_out), (lse_ref, lse_out))

    def project(slot):
        mixed = mixed_ref[pl.ds(pl.multiple_of(slot * CHUNK, CHUNK), CHUNK), :]
        lifted = dot(dot_nt(mixed, ao_ref[...]).astype(BF), bo_ref[...])
        return dot(mixed, wo_all[...]) + lifted

    (cross_sem,) = take(1)
    cross_out[...] = project(1 - h).astype(BF)
    cross = remote(cross_out, cross_in, cross_sem.at[0], cross_sem.at[1], uly_others()[0])
    cross.start()
    mine = project(h) + rows_out[pl.ds(pl.multiple_of(h * CHUNK, CHUNK), CHUNK), :].astype(F32)
    cross.wait()
    residual = mine + cross_in[...].astype(F32)
    resid_ref[...] = residual
    keep((resid_ref, resid_out))
    nf_own[...] = (residual * norm_scale(residual) * norm_ff_ref[...]).astype(BF)
    nf_spread = Spread(nf_own, nf_all, *take(3))
    nf_spread.start()
    nf_spread.second()
    nf_spread.third()
    nf_spread.last()
    cot_spread.last()
    for ring in rings:
        ring.last()
    for n in range(3):
        y_copies[2 * n].wait_send()
        y_copies[2 * n + 1].wait()
    deliver.end()
    for copy in copies:
        copy.wait()


def forward(*args):
    weight = jax.ShapeDtypeStruct((32, 48, FF_COLS), BF)
    group = GROUP * HEAD
    dma = pltpu.SemaphoreType.DMA
    spread = jax.ShapeDtypeStruct((2, 4, CHUNK, D), BF)
    return pl.pallas_call(
        forward_kernel,
        out_shape=(
            jax.ShapeDtypeStruct((2 * CHUNK, group), BF),
            jax.ShapeDtypeStruct((2 * CHUNK, group), BF),
            jax.ShapeDtypeStruct((2, 8, ROWS), F32),
            jax.ShapeDtypeStruct((CHUNKS, CHUNK, 2 * HEAD), BF),
            jax.ShapeDtypeStruct((2, D, 512), BF),
            jax.ShapeDtypeStruct((D // 2, D), BF),
            weight, weight, weight,
            jax.ShapeDtypeStruct((2 * CHUNK, D), BF),
            jax.ShapeDtypeStruct((2 * CHUNK, D), BF),
            jax.ShapeDtypeStruct((CHUNK, D), F32),
            jax.ShapeDtypeStruct((CHUNK, D), BF),
            spread, spread,
            jax.ShapeDtypeStruct((2, 8, ROWS), jnp.int32),
            jax.ShapeDtypeStruct((2 * CHUNK, HEAD), F32),
            jax.ShapeDtypeStruct((2 * CHUNK, HEAD), F32),
            jax.ShapeDtypeStruct((48, 1024), BF),
            jax.ShapeDtypeStruct((16, group), BF),
        ),
        in_specs=[ANY] * 2 + [pl.BlockSpec(memory_space=pltpu.SMEM)] + [IN_VMEM] * 11,
        out_specs=(ANY,) * 20,
        scratch_shapes=[
            pltpu.VMEM((2 * CHUNK, group), BF),
            pltpu.VMEM((2 * CHUNK, group), BF),
            pltpu.VMEM((2, 8, ROWS), F32),
            pltpu.VMEM((2 * CHUNK, D), BF),
            pltpu.VMEM((2 * CHUNK, D), BF),
            pltpu.VMEM((CHUNK, D), F32),
            pltpu.VMEM((CHUNK, D), BF),
            pltpu.VMEM((2, 8, ROWS), jnp.int32),
            pltpu.VMEM((2 * CHUNK, HEAD), F32),
            pltpu.VMEM((2 * CHUNK, HEAD), F32),
            pltpu.VMEM((48, 1024), BF),
            pltpu.VMEM((16, group), BF),
            pltpu.VMEM((CHUNKS, CHUNK, 2 * HEAD), BF),
            pltpu.VMEM((2, D, 512), BF),
            pltpu.VMEM((D // 2, D), BF),
            pltpu.VMEM((2, 2, 64, D), BF),
            pltpu.VMEM((2, 64, D), BF),
            pltpu.VMEM((2, CHUNK, 2 * HEAD), BF),
            pltpu.VMEM((HEAD, ROWS), F32),
            pltpu.VMEM((2, 8, ROWS), F32),
            pltpu.VMEM((4, 16, 512), BF),
            pltpu.VMEM((4, 16, 384), BF),
            pltpu.VMEM((48, 512), BF),
            pltpu.VMEM((48, 384), BF),
            pltpu.VMEM((CHUNK, D), BF),
            pltpu.VMEM((CHUNK, D), BF),
            pltpu.VMEM((CHUNK, D), BF),
            pltpu.VMEM((4, 16, 512), BF),
            pltpu.VMEM((4, 16, 384), BF),
            pltpu.VMEM((3, 48, PADDED), BF),
            dma((8,)), dma((8,)), dma((6,)), dma((6,)),
            dma((2, 3, Ring.sends)), dma((2, 3, 16)), dma((3,)), dma((3,)), dma((3,)),
        ]
        + GATHER_SEMS()
        + GATHER_SEMS()
        + [dma((3,)), dma((3,))]
        + GATHER_SEMS()
        + SPREAD_SEMS
        + [dma((15,)), dma((2,))]
        + SPREAD_SEMS,
        compiler_params=pltpu.CompilerParams(
            collective_id=1, has_side_effects=True, vmem_limit_bytes=48 * 2**20
        ),
        name="forward",
    )(*args)


class Collect:
    @staticmethod
    def scratch():
        piece, half = (CHUNK, D), (CHUNK // 2, D)
        return [
            pltpu.VMEM((4,) + piece, BF),
            pltpu.VMEM((4,) + piece, BF),
            pltpu.VMEM((2,) + half, BF),
            pltpu.VMEM((2,) + piece, BF),
            pltpu.VMEM(piece, BF),
            pltpu.VMEM((2,) + piece, BF),
            pltpu.SemaphoreType.DMA((8,)),
            pltpu.SemaphoreType.DMA((8,)),
            pltpu.SemaphoreType.DMA,
        ]

    scratches = 9

    def __init__(self, src, scratch):
        self.src = src
        (
            self.mine, self.pair, self.halves, self.last_in, self.far, self.near,
            self.send_sem, self.recv_sem, self.local_sem,
        ) = scratch
        self.w = ring_at()
        self.core = lax.axis_index("uly") % 2
        self.sent = []

    def send(self, src, dst, recv, device):
        copy = remote(src, dst, self.send_sem.at[recv], self.recv_sem.at[recv], device)
        copy.start()
        self.sent.append(copy)

    def start(self):
        self.local = pltpu.make_async_copy(self.src.at[self.core], self.mine, self.local_sem)
        self.local.start()
        for d in (2, 1, 3, 0):
            at = (self.w + d) % 4
            self.send(self.src.at[1 - self.core, at], self.pair.at[at], d, uly_others()[1])

    def both(self, d):
        at = (self.w + d) % 4
        wait_arrival(self.pair.at[at], self.recv_sem.at[d])
        return self.mine[at].astype(F32) + self.pair[at].astype(F32)

    def second(self):
        half = CHUNK // 2
        self.local.wait()
        self.far[...] = self.both(2).astype(BF)
        self.send(self.far.at[pl.ds(0, half)], self.halves.at[0], 4, ring_place((self.w + 1) % 4))
        self.send(self.far.at[pl.ds(half, half)], self.halves.at[1], 5, ring_place((self.w + 3) % 4))

    def third(self):
        half = CHUNK // 2
        for k, d in ((0, 1), (1, 3)):
            total = self.both(d)
            wait_arrival(self.halves.at[k], self.recv_sem.at[4 + k])
            rows = slice(k * half, (k + 1) * half)
            other = slice((1 - k) * half, (2 - k) * half)
            self.near[k, rows] = (total[rows] + self.halves[k].astype(F32)).astype(BF)
            self.near[k, other] = total[other].astype(BF)
            self.send(self.near.at[k], self.last_in.at[k], 6 + k, ring_place((self.w + d) % 4))

    def fourth(self):
        total = self.both(0)
        for k in (0, 1):
            wait_arrival(self.last_in.at[k], self.recv_sem.at[6 + k])
            total += self.last_in[k].astype(F32)
        for copy in self.sent:
            copy.wait_send()
        return total


def ff_kernel(
    set_ref, x_hbm, cot_hbm, gate_hbm, up_hbm, down_hbm, a_wide, a_down, b_wide, b_ff,
    grad_out, down_out, cols_out, wide_out,
    cols_ref, wide_ref, x_ref, cot_ref, gate_w, up_w, down_w, a_ff, b_cols, a_cols, b_out, hidden_ref, grad_gate, grad_up,
    out_buf, sems, out_sems,
):
    y, z, x, blk, uly = place()
    core = uly % 2
    first = (35 * uly) // 2 * 128 + y * FF_COLS
    columns = pl.ds(pl.multiple_of(first, 128), FF_COLS)
    pairs = [(down_hbm, down_w), (cot_hbm, cot_ref), (x_hbm, x_ref), (gate_hbm, gate_w), (up_hbm, up_w)]
    for s in (0, 1):
        chosen = set_ref[s]
        for n in (0, 1):
            pairs.append((a_wide.at[4 + n, chosen], a_ff.at[s, pl.ds(16 * n, 16)]))
            pairs.append((b_ff.at[n, chosen, :, columns], b_cols.at[s, n]))
        pairs.append((a_down.at[chosen, :, columns], a_cols.at[s]))
        pairs.append((b_wide.at[2, chosen], b_out.at[s]))
    copies = [pltpu.make_async_copy(src, dst, sems.at[n]) for n, (src, dst) in enumerate(pairs)]
    for copy in copies[5:] + copies[:5]:
        copy.start()
    for copy in copies[5:]:
        copy.wait()
    at = lax.broadcasted_iota(jnp.int32, (16, FF_COLS), 1) + (y * FF_COLS - 64 * core)
    inside = jnp.logical_and(at >= 0, at < FF // 4)

    def keep(v):
        return jnp.where(inside, v.astype(F32), 0.0).astype(BF)

    for s in (0, 1):
        a_cols[s] = keep(a_cols[s])
        for n in (0, 1):
            b_cols[s, n] = keep(b_cols[s, n])
    cols_ref[...] = jnp.zeros_like(cols_ref)
    here = pl.ds(pl.multiple_of(y * FF_COLS, 128), FF_COLS)
    copies[0].wait()
    copies[1].wait()

    def flat(ref, s):
        return ref[s].reshape(4 * CHUNK, D)

    out_copies = []
    for s in (0, 1):
        cot = flat(cot_ref, s)
        latent_cot = dot_nt(cot, b_out[s])
        grad_hidden = dot(cot, down_w[...]) + dot(latent_cot.astype(BF), a_cols[s])
        if s == 0:
            for copy in copies[2:5]:
                copy.wait()
        rows = flat(x_ref, s)
        latent = dot_nt(rows, a_ff[s])
        low = latent.astype(BF)
        gate = dot(rows, gate_w[...]) + dot(low[:, :16], b_cols[s, 0])
        sigmoid = jax.nn.sigmoid(gate)
        silu = gate * sigmoid
        grad_up[...] = (grad_hidden * silu).astype(BF)
        slope = grad_hidden * (sigmoid * (1.0 + gate * (1.0 - sigmoid)))
        up = dot(rows, up_w[...]) + dot(low[:, 16:], b_cols[s, 1])
        grad_gate[...] = (slope * up).astype(BF)
        hidden_ref[...] = (silu * up).astype(BF)
        back_gate = dot_nt(grad_gate[...], b_cols[s, 0])
        back_up = dot_nt(grad_up[...], b_cols[s, 1])
        grads = (
            dot_nt(grad_gate[...], gate_w[...])
            + dot_nt(grad_up[...], up_w[...])
            + dot(back_gate.astype(BF), a_ff[s, :16])
            + dot(back_up.astype(BF), a_ff[s, 16:])
        )
        out_buf[0, s] = grads.astype(BF).reshape(4, CHUNK, D)
        copy = pltpu.make_async_copy(out_buf.at[0, s], grad_out.at[s], out_sems.at[0, s])
        copy.start()
        out_copies.append(copy)
        latent_down = dot_nt(hidden_ref[...], a_cols[s])
        down = dot_nt(hidden_ref[...], down_w[...]) + dot(latent_down.astype(BF), b_out[s])
        out_buf[1, s] = down.astype(BF).reshape(4, CHUNK, D)
        copy = pltpu.make_async_copy(out_buf.at[1, s], down_out.at[s], out_sems.at[1, s])
        copy.start()
        out_copies.append(copy)

        def put(ref, n, value, at=slice(None)):
            ref[(2 * n + s) * 16 : (2 * n + s + 1) * 16, at] = value.astype(BF)

        def turned(value):
            return value.T.astype(BF)

        put(cols_ref, 0, dot(turned(latent_cot), hidden_ref[...]), here)
        put(cols_ref, 1, dot(turned(latent[:, :16]), grad_gate[...]), here)
        put(cols_ref, 2, dot(turned(latent[:, 16:]), grad_up[...]), here)
        put(wide_ref, 0, dot(turned(back_gate), rows))
        put(wide_ref, 1, dot(turned(back_up), rows))
        put(wide_ref, 2, dot(turned(latent_down), cot))
    for n, (src, dst) in enumerate(((cols_ref, cols_out), (wide_ref, wide_out))):
        copy = pltpu.make_async_copy(src, dst, out_sems.at[2, n])
        copy.start()
        out_copies.append(copy)
    for copy in out_copies:
        copy.wait()


def feed_forward(set_index, x, cot, gate_w, up_w, down_w, a_wide, a_down, b_wide, b_ff):
    spread = jax.ShapeDtypeStruct((2, 4, CHUNK, D), BF)
    weight = pltpu.VMEM((D, FF_COLS), BF)
    rows = pltpu.VMEM((4 * CHUNK, FF_COLS), BF)
    return pl.pallas_call(
        ff_kernel,
        out_shape=(
            spread, spread,
            jax.ShapeDtypeStruct((96, PADDED), BF),
            jax.ShapeDtypeStruct((96, D), BF),
        ),
        in_specs=[pl.BlockSpec(memory_space=pltpu.SMEM)] + [ANY] * 9,
        out_specs=(ANY,) * 4,
        scratch_shapes=[
            pltpu.VMEM((96, PADDED), BF), pltpu.VMEM((96, D), BF),
            pltpu.VMEM((2, 4, CHUNK, D), BF), pltpu.VMEM((2, 4, CHUNK, D), BF),
            weight, weight, weight,
            pltpu.VMEM((2, 32, D), BF), pltpu.VMEM((2, 2, 16, FF_COLS), BF),
            pltpu.VMEM((2, 16, FF_COLS), BF), pltpu.VMEM((2, 16, D), BF),
            rows, rows, rows,
            pltpu.VMEM((2, 2, 4, CHUNK, D), BF),
            pltpu.SemaphoreType.DMA((17,)), pltpu.SemaphoreType.DMA((3, 2)),
        ],
        compiler_params=pltpu.CompilerParams(vmem_limit_bytes=60 * 2**20),
        name="feed_forward",
    )(set_index, x, cot, gate_w, up_w, down_w, a_wide, a_down, b_wide, b_ff)


def backward_slot(
    slot, chunk, part, q_ref, kv_ref, limit_ref, mixed_ref, grad_ref, lse_ref, dq_ref, dkv_ref, acc_ref
):
    turned = head_columns(q_ref, slot)
    rows = head_rows(q_ref, slot)
    grad_turned = head_columns(grad_ref, slot)
    grad_rows = head_rows(grad_ref, slot)
    mixed_turned = head_columns(mixed_ref, slot)
    row_dot = jnp.sum(
        grad_turned.astype(F32) * mixed_turned.astype(F32), axis=0, keepdims=True
    )
    limit = limit_ref[slot, 0:1, :]
    lse = lse_ref[slot, 0:1, :]
    if part == 0:
        acc_ref[...] = jnp.zeros_like(acc_ref)

    def step(n, carry):
        keys, values = key_block(kv_ref, n)
        scores = jnp.where(key_places(n) <= limit, dot(keys, turned), -1e30)
        probs = jnp.exp2(scores - lse)
        grad_probs = dot(values, grad_turned)
        grad_scores = (probs * (grad_probs - row_dot)).astype(BF)
        acc_ref[...] += dot(keys.T, grad_scores)
        at = pl.ds(pl.multiple_of(n * KEYS, KEYS), KEYS)
        dkv_ref[at, :HEAD] += dot(grad_scores, rows)
        dkv_ref[at, HEAD:] += dot(probs.astype(BF), grad_rows)
        return carry

    blocks = chunk // STEP + 1
    lax.fori_loop(blocks * part // 4, blocks * (part + 1) // 4, step, 0)
    if part == 3:
        for n in range(GROUP):
            dq_ref[slot * CHUNK : (slot + 1) * CHUNK, n * HEAD : (n + 1) * HEAD] = (
                acc_ref[:, n * CHUNK : (n + 1) * CHUNK].T * HEAD ** (-0.5)
            )


class Reduce:
    sends = 28

    @staticmethod
    def scratch(shape):
        return [
            pltpu.VMEM((2, 3, 2, 4) + shape, BF),
            pltpu.VMEM((2, 3, 2) + shape, BF),
            pltpu.VMEM((2,) + shape, BF),
            pltpu.VMEM((2, 4, 2) + shape, BF),
            pltpu.VMEM((2, 2) + shape, BF),
            pltpu.SemaphoreType.DMA((2, Reduce.sends)),
            pltpu.SemaphoreType.DMA((2, Reduce.sends)),
        ]

    def __init__(self, part, index, scratch):
        self.part, self.index = part, index
        self.buf_q, self.buf_p, self.buf_y, self.sum_p, self.sum_y, self.send_sem, self.recv_sem = scratch
        self.y, self.z, self.x, self.blk, self.uly = place()
        self.pq = ((self.x, self.z), (self.z, self.x))
        self.flying = []

    def at(self, half, y, p, q):
        return blk_of(y, q, p) if half == 0 else blk_of(y, p, q)

    def send(self, src, dst, half, n, y, p, q):
        copy = pltpu.make_async_remote_copy(
            src_ref=src, dst_ref=dst,
            send_sem=self.send_sem.at[half, n], recv_sem=self.recv_sem.at[half, n],
            device_id=(self.at(half, y, p, q), self.uly), device_id_type=MESH,
        )
        copy.start()
        self.flying.append(copy)

    def land(self):
        for copy in self.flying:
            copy.wait()
        self.flying = []

    def first(self):
        for d in (2, 1, 3):
            for half in (0, 1):
                p, q = self.pq[half]
                to = (q + d) % 4
                for y in (0, 1):
                    for pp in range(4):
                        self.send(
                            self.part.at[self.index(half, self.at(half, y, pp, to))],
                            self.buf_q.at[half, d - 1, y, pp],
                            half, (d - 1) * 8 + y * 4 + pp, self.y, p, to,
                        )

    def second(self):
        self.land()
        for d in (2, 1, 3, 0):
            for half in (0, 1):
                p, q = self.pq[half]
                to = (p + d) % 4
                for y in (0, 1):
                    total = self.part[self.index(half, self.at(half, y, to, q))].astype(F32)
                    for n in range(3):
                        total += self.buf_q[half, n, y, to].astype(F32)
                    self.sum_p[half, d, y] = total.astype(BF)
                if d > 0:
                    self.send(
                        self.sum_p.at[half, d], self.buf_p.at[half, d - 1], half, 23 + d, self.y, to, q
                    )

    def third(self):
        self.land()
        for k in (1, 0):
            for half in (0, 1):
                p, q = self.pq[half]
                y = self.y if k == 0 else 1 - self.y
                total = self.sum_p[half, 0, y].astype(F32)
                for n in range(3):
                    total += self.buf_p[half, n, y].astype(F32)
                self.sum_y[half, k] = total.astype(BF)
                if k == 1:
                    self.send(self.sum_y.at[half, 1], self.buf_y.at[half], half, 27, 1 - self.y, p, q)

    def fourth(self):
        self.land()
        return [self.sum_y[half, 0].astype(F32) + self.buf_y[half].astype(F32) for half in (0, 1)]


def reduce_others():
    y, z, x, blk, uly = place()
    return (
        [(blk_of(1 - y, z, x), uly)]
        + [(blk_of(y, z, (x + d) % 4), uly) for d in (1, 2, 3)]
        + [(blk_of(y, (z + d) % 4, x), uly) for d in (1, 2, 3)]
    )


UNIT = (16, 128)


class Total:
    @staticmethod
    def scratch(kept, summed):
        shape = (kept + summed,) + UNIT
        return (
            [pltpu.VMEM((64,) + shape, BF)]
            + Reduce.scratch(shape)
            + [
                pltpu.VMEM((2,) + shape, BF),
                pltpu.VMEM((3, 2) + shape, BF),
                pltpu.VMEM((2, 4 * kept + summed) + UNIT, BF),
                pltpu.SemaphoreType.DMA((3,)),
                pltpu.SemaphoreType.DMA((3,)),
                pltpu.SemaphoreType.DMA((1, Gather.sends)),
                pltpu.SemaphoreType.DMA((1, 32)),
                pltpu.SemaphoreType.DMA((1,)),
                pltpu.SemaphoreType.DMA,
                pltpu.SemaphoreType.DMA,
            ]
        )

    scratches = 18

    @staticmethod
    def shape(kept, summed):
        return jax.ShapeDtypeStruct((2, 32, 4 * kept + summed) + UNIT, BF)

    def __init__(self, kept, summed, all_ref, scratch):
        self.kept, self.summed, self.all_ref = kept, summed, all_ref
        self.part = scratch[0]
        self.reduce = Reduce(self.part, lambda half, item: half * 32 + item, scratch[1:8])
        self.own, self.buf, self.full, self.send_sem, self.recv_sem = scratch[8:13]
        self.pair_send, self.pair_recv = scratch[16:18]
        self.y, self.z, self.x, self.blk, self.uly = place()
        self.core = self.uly % 2
        self.gather = Gather(
            lambda s: self.full.at[self.core],
            lambda s, item: self.all_ref.at[self.core, item],
            *scratch[13:16],
            orders=(self.core,),
        )

    def pack(self, values, first, per, at):
        for n, value in enumerate(values, first):
            self.part[n // per, at + n % per] = value.astype(BF)

    def pack_kept(self, values, first=0):
        self.pack(values, first, self.kept, 0)

    def pack_summed(self, values, first=0):
        self.pack(values, first, self.summed, self.kept)

    def clear(self, kept, summed):
        nothing = jnp.zeros(UNIT, BF)
        self.pack_kept([nothing] * (64 * self.kept - kept), kept)
        self.pack_summed([nothing] * (64 * self.summed - summed), summed)

    def across(self):
        for half, total in enumerate(self.reduce.fourth()):
            self.own[half] = total.astype(BF)
        self.copies = []
        for n, other in enumerate(uly_others()):
            copy = pltpu.make_async_remote_copy(
                src_ref=self.own, dst_ref=self.buf.at[n],
                send_sem=self.send_sem.at[n], recv_sem=self.recv_sem.at[n],
                device_id=other, device_id_type=MESH,
            )
            copy.start()
            self.copies.append(copy)

    def join(self):
        for copy in self.copies:
            copy.wait()
        kept = self.kept
        terms = [self.own] + [self.buf.at[n] for n in range(3)]
        who = [self.uly] + [other[1] for other in uly_others()]
        for half in (0, 1):
            for term, uly in zip(terms, who):
                self.full[half, pl.ds(uly * kept, kept)] = term[half, :kept]
            if self.summed:
                self.full[half, 4 * kept :] = sum(
                    term[half, kept:].astype(F32) for term in terms
                ).astype(BF)
        self.gather.start()

    def hand(self):
        self.gather.last()
        self.pair(self.core).start()

    def pair(self, core):
        return pltpu.make_async_remote_copy(
            src_ref=self.all_ref.at[core], dst_ref=self.all_ref.at[core],
            send_sem=self.pair_send, recv_sem=self.pair_recv,
            device_id=uly_others()[1], device_id_type=MESH,
        )

    def end(self):
        self.pair(self.core).wait_send()
        self.pair(1 - self.core).wait_recv()

    def steps(self):
        return [
            self.reduce.first, self.reduce.second, self.reduce.third, self.across, self.join,
            self.gather.second, self.gather.third, self.gather.fourth, self.hand, self.end,
        ]


def units(value):
    rows, columns = value.shape
    return [
        value[n * 16 : (n + 1) * 16, t * 128 : (t + 1) * 128]
        for n in range(rows // 16) for t in range(columns // 128)
    ]


FF_KEPT, FF_SUMMED, QKV_KEPT = 2, 2, 1
COL_TILES = PADDED // 128
D_TILES = D // 128
DKV_SCRATCH = 7


def backward_kernel(
    grad_part_ref, down_part_ref, norm_ff_ref, norm_in_ref, a_qkv_ref, bo_ref,
    cols_hbm, ff_hbm, resid_hbm, cot_hbm, ao_hbm, mixed_hbm, wo_hbm, kv_hbm, q_hbm, limit_hbm, lse_hbm,
    wq_hbm, rows_hbm, normed_hbm, b_qkv_hbm, cos_hbm, sin_hbm,
    result_ref, input_grad_ref, ff_all, qkv_all,
    cols_ref, ff_ref, resid_ref, cot_ref, ao_ref, mixed_ref, wo_ref, kv_ref, q_ref, limit_ref, lse_ref,
    wq_ref, rows_ref, normed_ref, b_qkv_ref, cos_ref, sin_ref, dkv_ref, acc_ref, part, dq_ref, grad_ref, grad_attn, grad_resid, grad_qkv,
    cross_out, cross_in, home_out, home_in, copy_sem, cross_sem, home_send, home_recv,
    *scratch,
):
    y, z, x, blk, uly = place()
    core, h = uly % 2, uly // 2
    scratch = list(scratch)

    def take(count):
        got = scratch[:count]
        del scratch[:count]
        return got

    chunk = 2 * blk + h
    upper = chunk // 32
    home = (1 - upper) * chunk + upper * (63 - chunk)
    home_from = [(home, upper * 2 + s) for s in (0, 1)]
    own_chunk = (1 - h) * blk + h * (63 - blk)
    home_to = [(own_chunk // 2, (own_chunk % 2) * 2 + half) for half in (0, 1)]
    greet(
        reduce_others() + uly_others() + [(blk_of(1 - y, z, x), (uly + 2) % 4)] + home_from + home_to
    )
    copies = [
        pltpu.make_async_copy(src, dst, copy_sem.at[n])
        for n, (src, dst) in enumerate(
            (
                (cols_hbm, cols_ref), (ff_hbm, ff_ref), (resid_hbm, resid_ref), (cot_hbm, cot_ref),
                (ao_hbm, ao_ref), (mixed_hbm, mixed_ref), (wo_hbm, wo_ref), (kv_hbm, kv_ref),
                (q_hbm, q_ref), (limit_hbm, limit_ref), (lse_hbm, lse_ref), (wq_hbm, wq_ref),
                (rows_hbm, rows_ref), (normed_hbm, normed_ref), (b_qkv_hbm, b_qkv_ref),
                (cos_hbm, cos_ref), (sin_hbm, sin_ref),
            )
        )
    ]
    collect_grad = Collect(grad_part_ref, take(Collect.scratches))
    collect_out = Collect(down_part_ref, take(Collect.scratches))
    reduce = Reduce(
        part, lambda half, item: item if half == 0 else 63 - item, take(DKV_SCRATCH)
    )
    ff_total = Total(FF_KEPT, FF_SUMMED, ff_all, take(Total.scratches))
    qkv_total = Total(QKV_KEPT, 0, qkv_all, take(Total.scratches))
    deliver = Deliver()

    def send_home(n, value):
        home_out[n] = value.astype(BF)
        for half in (0, 1):
            deliver.send(
                home_out.at[n, pl.ds(half * 64, 64)], home_in.at[n, core],
                home_send.at[n, half], home_recv.at[n, core], home_to[half],
            )

    def arrived_home(n):
        for s in (0, 1):
            wait_arrival(home_in.at[n, s], home_recv.at[n, s])
        return home_in[n].astype(F32)

    def ready(first, last):
        for copy in copies[first:last]:
            copy.wait()

    collect_grad.start()
    for copy in copies:
        copy.start()
    ready(0, 2)
    ff_total.pack_kept(units(cols_ref))
    ff_total.pack_summed(units(ff_ref))
    at_o = 6 * COL_TILES
    ff_total.clear(at_o + D_TILES // 2 + D_TILES, 6 * D_TILES)
    qkv_total.clear(3 * D_TILES + D_TILES // 2 + 2, 0)
    collect_grad.second()
    collect_grad.third()
    ready(2, 7)
    residual = resid_ref[...]
    total = collect_grad.fourth()
    value = cot_ref[...].astype(F32) + norm_back(residual, norm_scale(residual), norm_ff_ref[...], total)
    grad_resid[...] = value
    own_rows = pl.ds(pl.multiple_of(h * CHUNK, CHUNK), CHUNK)
    other_rows = pl.ds(pl.multiple_of((1 - h) * CHUNK, CHUNK), CHUNK)
    grad_attn[own_rows, :] = value.astype(BF)
    partner = uly_others()[0]
    cross = remote(
        grad_attn.at[own_rows], grad_attn.at[own_rows], cross_sem.at[0], cross_sem.at[1], partner
    )
    cross.start()
    collect_out.start()
    dkv_ref[...] = jnp.zeros_like(dkv_ref)
    latent_o = dot_nt(ao_ref[...], mixed_ref[...]).astype(BF)
    cross.wait_send()
    wait_arrival(grad_attn.at[other_rows], cross_sem.at[1])
    back_o = dot_nt(grad_attn[...], bo_ref[...]).astype(BF)
    grad_ref[...] = (dot_nt(grad_attn[...], wo_ref[...]) + dot(back_o, ao_ref[...])).astype(BF)
    back_o = dot_nt(bo_ref[...], grad_attn[...]).astype(BF)
    ff_total.pack_kept(
        units(dot(back_o, mixed_ref[...])) + units(dot(latent_o, grad_attn[...])), at_o
    )

    ready(7, 11)
    steps = ff_total.steps()
    steps.pop(0)()
    more = [collect_out.second, collect_out.third]
    args = (q_ref, kv_ref, limit_ref, mixed_ref, grad_ref, lse_ref, dq_ref, dkv_ref, acc_ref)
    for slot, at in ((0, blk), (1, 63 - blk)):
        for part_of in range(4):
            backward_slot(slot, at, part_of, *args)
            if more:
                more.pop(0)()
            steps.pop(0)()

    def pack(n, carry):
        rows = dkv_ref[pl.ds(pl.multiple_of(n * CHUNK, CHUNK), CHUNK), :]
        part[n] = jnp.concatenate([rows[:, :HEAD] * LN2, rows[:, HEAD:]], axis=1).astype(BF)
        return carry

    lax.fori_loop(0, CHUNKS, pack, 0)
    reduce.first()
    ready(11, 17)
    send_home(0, resid_ref[...] + collect_out.fourth())
    while steps:
        steps.pop(0)()
    cos_table, sine_table = cos_ref[...], sin_ref[...]

    def turn_back(value, rows=slice(None)):
        return value * cos_table[rows] - pltpu.roll(value, HEAD // 2, 1) * sine_table[rows]

    for n in range(GROUP):
        at = slice(n * HEAD, (n + 1) * HEAD)
        grad_qkv[:, at] = turn_back(dq_ref[:, at]).astype(BF)
    latent_qkv = dot_nt(a_qkv_ref[...], normed_ref[...]).astype(BF)
    reduce.second()
    reduce.third()
    group = GROUP * HEAD
    for half, value in enumerate(reduce.fourth()):
        rows = slice(half * CHUNK, (half + 1) * CHUNK)
        grad_qkv[rows, group : group + HEAD] = turn_back(value[:, :HEAD], rows).astype(BF)
        grad_qkv[rows, group + HEAD :] = value[:, HEAD:].astype(BF)

    def project_back(rows):
        grads = grad_qkv[rows, :]
        lifted = dot(dot_nt(grads, b_qkv_ref[...]).astype(BF), a_qkv_ref[...])
        return dot_nt(grads[:, :512], wq_ref[0]) + dot_nt(grads[:, 512:], wq_ref[1]) + lifted

    cross_out[...] = project_back(other_rows).astype(BF)
    cross = remote(cross_out, cross_in, cross_sem.at[2], cross_sem.at[3], partner)
    cross.start()
    back_qkv = dot_nt(b_qkv_ref[...], grad_qkv[...]).astype(BF)
    grad_b = dot(latent_qkv, grad_qkv[...])
    qkv_total.pack_kept(
        units(dot(back_qkv, normed_ref[...]))
        + units(grad_b[:16, :group])
        + units(grad_b[16:32, group : group + HEAD])
        + units(grad_b[32:, group + HEAD :])
    )
    steps = qkv_total.steps()
    steps.pop(0)()
    mine = project_back(own_rows)
    steps.pop(0)()
    cross.wait()
    mine = mine + cross_in[...].astype(F32)
    tokens = rows_ref[own_rows, :].astype(F32)
    send_home(1, grad_resid[...] + norm_back(tokens, norm_scale(tokens), norm_in_ref[...], mine))
    while steps:
        steps.pop(0)()
    result_ref[...] = arrived_home(0).astype(BF)
    input_grad_ref[...] = arrived_home(1)
    deliver.end()


def backward(*args):
    dma = pltpu.SemaphoreType.DMA
    group = GROUP * HEAD
    return pl.pallas_call(
        backward_kernel,
        out_shape=(
            jax.ShapeDtypeStruct((2, CHUNK // 2, D), BF),
            jax.ShapeDtypeStruct((2, CHUNK // 2, D), F32),
            Total.shape(FF_KEPT, FF_SUMMED),
            Total.shape(QKV_KEPT, 0),
        ),
        in_specs=[ANY] * 2 + [IN_VMEM] * 4 + [ANY] * 17,
        out_specs=(IN_VMEM, IN_VMEM, ANY, ANY),
        scratch_shapes=[
            pltpu.VMEM((96, PADDED), BF),
            pltpu.VMEM((96, D), BF),
            pltpu.VMEM((CHUNK, D), F32),
            pltpu.VMEM((CHUNK, D), BF),
            pltpu.VMEM((16, group), BF),
            pltpu.VMEM((2 * CHUNK, group), BF),
            pltpu.VMEM((D // 2, D), BF),
            pltpu.VMEM((CHUNKS, CHUNK, 2 * HEAD), BF),
            pltpu.VMEM((2 * CHUNK, group), BF),
            pltpu.VMEM((2, 8, ROWS), jnp.int32),
            pltpu.VMEM((2, 8, ROWS), F32),
            pltpu.VMEM((2, D, 512), BF),
            pltpu.VMEM((2 * CHUNK, D), BF),
            pltpu.VMEM((2 * CHUNK, D), BF),
            pltpu.VMEM((48, 1024), BF),
            pltpu.VMEM((2 * CHUNK, HEAD), F32),
            pltpu.VMEM((2 * CHUNK, HEAD), F32),
            pltpu.VMEM((CHUNKS * CHUNK, 2 * HEAD), F32),
            pltpu.VMEM((HEAD, ROWS), F32),
            pltpu.VMEM((CHUNKS, CHUNK, 2 * HEAD), BF),
            pltpu.VMEM((2 * CHUNK, group), F32),
            pltpu.VMEM((2 * CHUNK, group), BF),
            pltpu.VMEM((2 * CHUNK, D), BF),
            pltpu.VMEM((CHUNK, D), F32),
            pltpu.VMEM((2 * CHUNK, 1024), BF),
            pltpu.VMEM((CHUNK, D), BF),
            pltpu.VMEM((CHUNK, D), BF),
            pltpu.VMEM((2, CHUNK, D), BF),
            pltpu.VMEM((2, 2, CHUNK // 2, D), BF),
            dma((17,)), dma((4,)), dma((2, 2)), dma((2, 2)),
        ]
        + Collect.scratch() * 2
        + Reduce.scratch((CHUNK, 2 * HEAD))
        + Total.scratch(FF_KEPT, FF_SUMMED)
        + Total.scratch(QKV_KEPT, 0),
        compiler_params=pltpu.CompilerParams(
            collective_id=2, has_side_effects=True, vmem_limit_bytes=60 * 2**20
        ),
        name="backward",
    )(*args)


def fold_kernel(pick_ref, ff_ref, qkv_ref, a_wide, a_down, b_wide, b_kv, b_ff):
    c = pl.program_id(0)

    def kept(ref, per, n, u):
        return ref[n // per // 32, n // per % 32, u * per + n % per].astype(F32)

    def ff_kept(n, u):
        return kept(ff_ref, FF_KEPT, n, u)

    def qkv_kept(n, u):
        return kept(qkv_ref, QKV_KEPT, n, u)

    def summed(n):
        item = n // FF_SUMMED
        return ff_ref[item // 32, item % 32, 4 * FF_KEPT + n % FF_SUMMED].astype(F32)

    def put(ref, at, tile, value):
        ref[at + (slice(None), slice(tile * 128, (tile + 1) * 128))] = (
            pick_ref[c, 0] * value(0) + pick_ref[c, 1] * value(1)
        )

    for n in range(3):
        for t in range(D_TILES):
            put(a_wide, (n, 0), t, lambda s: qkv_kept(n * D_TILES + t, s) + qkv_kept(n * D_TILES + t, 2 + s))
    at_o = 6 * COL_TILES
    half = D_TILES // 2
    for t in range(D_TILES):
        h, part = t // half, t % half
        put(a_wide, (3, 0), t, lambda s: ff_kept(at_o + part, 2 * h + s))
        put(b_wide, (0, 0), t, lambda s: qkv_kept(3 * D_TILES + part, 2 * h + s))
        put(
            b_wide, (1, 0), t,
            lambda s: ff_kept(at_o + half + t, s) + ff_kept(at_o + half + t, 2 + s),
        )
        for n, (ref, at) in enumerate(((a_wide, (4, 0)), (a_wide, (5, 0)), (b_wide, (2, 0)))):
            put(ref, at, t, lambda s: summed((2 * n + s) * D_TILES + t))
    for n in (0, 1):
        for h in (0, 1):
            put(b_kv, (n, 0), h, lambda s: qkv_kept(3 * D_TILES + half + n, 2 * h + s))
    for n, (ref, at) in enumerate(((a_down, (0,)), (b_ff, (0, 0)), (b_ff, (1, 0)))):
        for t in range(FF // 128):
            where = [
                (u, t - start) for u, start in enumerate((0, 17, 35, 52)) if 0 <= t - start < COL_TILES
            ]
            put(
                ref, at, t,
                lambda s: sum(ff_kept((2 * n + s) * COL_TILES + tile, u) for u, tile in where),
            )


def fold(pick, ff_all, qkv_all):
    def whole(v):
        return pl.BlockSpec(v.shape, lambda c: (0,) * v.ndim)

    def by_set(lead, columns):
        shape = lead + (1, 16, columns)
        return pl.BlockSpec(shape, lambda c: (0,) * len(lead) + (c, 0, 0))

    def out(lead, columns):
        return jax.ShapeDtypeStruct(lead + (SETS, 16, columns), F32)

    outs = (((6,), D), ((), FF), ((3,), D), ((2,), 2 * HEAD), ((2,), FF))
    return pl.pallas_call(
        fold_kernel,
        grid=(SETS,),
        out_shape=tuple(out(*o) for o in outs),
        in_specs=[pl.BlockSpec(memory_space=pltpu.SMEM), whole(ff_all), whole(qkv_all)],
        out_specs=tuple(by_set(*o) for o in outs),
        compiler_params=pltpu.CompilerParams(vmem_limit_bytes=40 * 2**20),
        name="fold",
    )(pick, ff_all, qkv_all)


def norm_scale(hidden):
    return lax.rsqrt(jnp.mean(hidden * hidden, axis=-1, keepdims=True) + EPS)


def norm_back(hidden, scaled, gain_vec, upstream):
    normed = hidden * scaled
    weighted = upstream * gain_vec
    return scaled * (weighted - normed * jnp.mean(weighted * normed, axis=-1, keepdims=True))


def body(
    tokens, cotangent, lengths, set_index, norm_in, norm_ff, qkv_bias, w_qkv, w_out, w_gate_up, w_down,
    a_wide, a_down, b_wide, b_kv, b_ff,
):
    own_set = set_index[lax.axis_index("uly") % 2]

    def chosen(table):
        return lax.dynamic_index_in_dim(table, own_set, 1, keepdims=False)

    a_own, b_own = chosen(a_wide[:4]), chosen(b_wide[:2])
    frequencies = np.float64(THETA) ** (-np.arange(0, HEAD, 2, dtype=np.float64) / HEAD)
    frequencies = np.concatenate([frequencies, frequencies])[None].astype(np.float32)
    (
        q, mixed, lse, kv_all, qkv_w, out_w, gate_w, up_w, down_w, rows, normed, residual, grad_out,
        gathered, grad_gathered, limit, cos_table, sine_table, b_qkv, ao,
    ) = forward(
        tokens, cotangent, lengths, w_qkv, w_out, w_gate_up, w_down.T, norm_in[None], norm_ff[None],
        qkv_bias.reshape(16, HEAD), frequencies, a_own, b_own, chosen(b_kv),
    )
    gate_w, up_w, down_w = (w.reshape(D, FF_COLS) for w in (gate_w, up_w, down_w))
    grad_part, down_part, cols, ff_wide = feed_forward(
        set_index, gathered, grad_gathered, gate_w, up_w, down_w, a_wide, a_down, b_wide, b_ff
    )
    result, input_grad, ff_all, qkv_all = backward(
        grad_part, down_part, norm_ff[None], norm_in[None], a_own[:3].reshape(48, D), b_own[1],
        cols, ff_wide, residual, grad_out, ao, mixed, out_w, kv_all, q, limit, lse,
        qkv_w, rows, normed, b_qkv, cos_table, sine_table,
    )
    pick = (jnp.arange(SETS, dtype=jnp.int32)[:, None] == set_index[None, :]).astype(F32)
    return (result, input_grad) + tuple(fold(pick, ff_all, qkv_all))


def solution(mesh):
    spread = P(None, ("blk", "uly"), None)
    in_specs = (
        spread, spread, P(), P(), P(), P(), P(),
        P(("blk", "uly"), None), P(("blk", "uly"), None), P(None, "blk", "uly"), P("uly", "blk"),
        P(), P(), P(), P(), P(),
    )
    out_specs = (spread, spread, P(), P(), P(), P(), P())
    return jax.shard_map(body, mesh=mesh, in_specs=in_specs, out_specs=out_specs, check_vma=False)
```

```python
import functools

import jax
import jax.numpy as jnp
import numpy as np
from jax import lax
from jax.experimental import pallas as pl
from jax.experimental.pallas import tpu as pltpu
from jax.sharding import PartitionSpec as P

HEADS = 12
KV_HEADS = 2
HEAD = 128
GROUP = HEADS // KV_HEADS
FF = 8960
SETS = 8
D = 1536
CHUNK = 128
CHUNKS = 64
PADDED = 2304
EPS = 1e-06
THETA = 1000000.0
LOG2E = 1.4426950408889634
LN2 = 0.6931471805599453
MESH = pl.DeviceIdType.MESH
BF = jnp.bfloat16
F32 = jnp.float32
ANY = pl.BlockSpec(memory_space=pltpu.HBM)
IN_VMEM = pl.BlockSpec(memory_space=pltpu.VMEM)


def blk_of(y, z, x):
    return y * 16 + z * 4 + x


def place():
    blk = lax.axis_index("blk")
    return blk // 16, (blk // 4) % 4, blk % 4, blk, lax.axis_index("uly")


def ring_others():
    y, z, x, blk, uly = place()
    return [
        (blk_of(1 - y, z, x), uly),
        (blk_of(y, z, (x + 1) % 4), uly),
        (blk_of(y, z, (x + 3) % 4), uly),
        (blk_of(y, (z + 1) % 4, x), uly),
        (blk_of(y, (z + 3) % 4, x), uly),
    ]


def greet(others, meanwhile=None):
    barrier = pltpu.get_barrier_semaphore()
    for other in others:
        pl.semaphore_signal(barrier, inc=1, device_id=other, device_id_type=MESH)
    if meanwhile is not None:
        meanwhile()
    pl.semaphore_wait(barrier, len(others))


class Gather:
    sends = 31

    def __init__(self, src, dst, send_sem, recv_sem, local_sem, orders=(0, 1)):
        self.src, self.dst, self.orders = src, dst, orders
        self.streams = range(len(orders))
        self.send_sem, self.recv_sem, self.local_sem = send_sem, recv_sem, local_sem
        self.y, self.z, self.x, self.blk, self.uly = place()
        self.count = [0] * len(orders)
        self.sent = []
        self.local = []

    def at(self, stream, y, p, q):
        order = self.orders[stream]
        return blk_of(y, order * p + (1 - order) * q, order * q + (1 - order) * p)

    def pq(self, stream):
        order = self.orders[stream]
        return (
            order * self.z + (1 - order) * self.x,
            order * self.x + (1 - order) * self.z,
        )

    def send(self, stream, item, target, src=None):
        copy = pltpu.make_async_remote_copy(
            src_ref=self.dst(stream, item) if src is None else src,
            dst_ref=self.dst(stream, item),
            send_sem=self.send_sem.at[stream, self.count[stream]],
            recv_sem=self.recv_sem.at[stream, item],
            device_id=(target, self.uly),
            device_id_type=MESH,
        )
        self.count[stream] += 1
        copy.start()
        self.sent.append(copy)

    def wait(self, stream, item):
        ref = self.dst(stream, item)
        pltpu.make_async_remote_copy(
            src_ref=ref,
            dst_ref=ref,
            send_sem=self.send_sem.at[stream, 0],
            recv_sem=self.recv_sem.at[stream, item],
            device_id=(self.blk, self.uly),
            device_id_type=MESH,
        ).wait_recv()

    def start(self):
        for s in self.streams:
            p, q = self.pq(s)
            self.send(s, self.blk, self.at(s, 1 - self.y, p, q), self.src(s))
        for s in self.streams:
            p, q = self.pq(s)
            for d in (1, 3):
                self.send(s, self.blk, self.at(s, self.y, (p + d) % 4, q), self.src(s))
            copy = pltpu.make_async_copy(self.src(s), self.dst(s, self.blk), self.local_sem.at[s])
            copy.start()
            self.local.append(copy)

    def second(self):
        for s in self.streams:
            p, q = self.pq(s)
            item = self.at(s, 1 - self.y, p, q)
            self.wait(s, item)
            for d in (1, 3):
                self.send(s, item, self.at(s, self.y, (p + d) % 4, q))
            for d in (1, 3):
                onward = self.at(s, self.y, p, (q + d) % 4)
                self.send(s, self.blk, onward, self.src(s))
                self.send(s, item, onward)

    def spread(self, s, item):
        p, q = self.pq(s)
        for d in (1, 3):
            self.send(s, item, self.at(s, self.y, p, (q + d) % 4))

    def third(self):
        for k, y in enumerate((self.y, 1 - self.y)):
            for s in self.streams:
                p, q = self.pq(s)
                for d in (3, 1):
                    item = self.at(s, y, (p + d) % 4, q)
                    self.wait(s, item)
                    if (d == 3) == (k == 0):
                        self.send(s, item, self.at(s, self.y, (p + 4 - d) % 4, q))
                    self.spread(s, item)
        for y in (self.y, 1 - self.y):
            for s in self.streams:
                p, q = self.pq(s)
                item = self.at(s, y, (p + 2) % 4, q)
                self.wait(s, item)
                self.spread(s, item)

    def fourth(self):
        for e in (0, 1, 3, 2):
            for k, y in enumerate((self.y, 1 - self.y)):
                for s in self.streams:
                    p, q = self.pq(s)
                    for d in (3, 1):
                        item = self.at(s, y, (p + e) % 4, (q + d) % 4)
                        self.wait(s, item)
                        if (d == 3) == (k == 0):
                            self.send(s, item, self.at(s, self.y, p, (q + 4 - d) % 4))

    def last(self):
        for e in (0, 1, 3, 2):
            for y in (self.y, 1 - self.y):
                for s in self.streams:
                    p, q = self.pq(s)
                    self.wait(s, self.at(s, y, (p + e) % 4, (q + 2) % 4))
        for copy in self.local:
            copy.wait()
        for copy in self.sent:
            copy.wait_send()


GATHER_SEMS = lambda *lead: [
    pltpu.SemaphoreType.DMA(lead + (2, Gather.sends)),
    pltpu.SemaphoreType.DMA(lead + (2, 32)),
    pltpu.SemaphoreType.DMA(lead + (2,)),
]


KEYS = 1024
KEYS_BACK = 512
ROWS = GROUP * CHUNK


def head_columns(ref, slot):
    return jnp.concatenate(
        [
            ref[slot * CHUNK : (slot + 1) * CHUNK, n * HEAD : (n + 1) * HEAD].T
            for n in range(GROUP)
        ],
        axis=1,
    )


def head_rows(ref, slot):
    return jnp.concatenate(
        [
            ref[slot * CHUNK : (slot + 1) * CHUNK, n * HEAD : (n + 1) * HEAD]
            for n in range(GROUP)
        ],
        axis=0,
    )


def key_block(kv_ref, step, keys):
    count = keys // CHUNK
    rows = kv_ref[pl.ds(step * count, count)].reshape(keys, 2 * HEAD)
    return rows[:, :HEAD], rows[:, HEAD:]


def dot(a, b):
    return jnp.dot(a, b, preferred_element_type=F32)


def key_places(step, keys):
    return lax.broadcasted_iota(jnp.int32, (keys, ROWS), 0) + step * keys


def dot_nt(a, b):
    return lax.dot_general(a, b, (((1,), (1,)), ((), ())), preferred_element_type=F32)


def forward_slot(slot, chunk, part, q_ref, kv_ref, limit_ref, mixed_ref, lse_ref, acc_ref, stat_ref):
    turned = head_columns(q_ref, slot)
    limit = limit_ref[slot, 0:1, :]
    if part == 0:
        acc_ref[...] = jnp.zeros_like(acc_ref)
        stat_ref[0] = jnp.full(stat_ref.shape[1:], -1e30, F32)
        stat_ref[1] = jnp.zeros(stat_ref.shape[1:], F32)

    def step(n, carry):
        top, total = carry
        keys, values = key_block(kv_ref, n, KEYS)
        scores = jnp.where(key_places(n, KEYS) <= limit, dot(keys, turned), -1e30)
        new_top = jnp.maximum(top, jnp.max(scores, axis=0, keepdims=True))
        fade = jnp.exp2(top - new_top)
        probs = jnp.exp2(scores - new_top)
        total = total * fade + jnp.sum(probs, axis=0, keepdims=True)
        acc_ref[...] = acc_ref[...] * fade + dot(values.T, probs.astype(BF))
        return new_top, total

    blocks = chunk * CHUNK // KEYS + 1
    top, total = lax.fori_loop(
        blocks * part // 4, blocks * (part + 1) // 4, step, (stat_ref[0, 0:1, :], stat_ref[1, 0:1, :])
    )
    if part < 3:
        stat_ref[0, 0:1, :] = top
        stat_ref[1, 0:1, :] = total
        return
    out = acc_ref[...] / total
    for n in range(GROUP):
        mixed_ref[slot * CHUNK : (slot + 1) * CHUNK, n * HEAD : (n + 1) * HEAD] = out[
            :, n * CHUNK : (n + 1) * CHUNK
        ].T.astype(BF)
    lse_ref[slot] = jnp.broadcast_to(top + jnp.log2(total), (8, ROWS))


def uly_others():
    y, z, x, blk, uly = place()
    return [(blk, (uly + 2) % 4), (blk, uly + 1 - 2 * (uly % 2)), (blk, 3 - uly)]


def ring_place(w):
    y, z, x, blk, uly = place()
    return (blk_of(w % 2, z, x), (w // 2) * 2 + uly % 2)


def ring_at():
    y, z, x, blk, uly = place()
    return (uly // 2) * 2 + y


def wait_arrival(ref, sem):
    pltpu.make_async_copy(ref, ref, sem).wait()


def remote(src, dst, send, recv, device):
    return pltpu.make_async_remote_copy(
        src_ref=src, dst_ref=dst, send_sem=send, recv_sem=recv, device_id=device, device_id_type=MESH
    )


class Deliver:
    def __init__(self):
        self.sent = []

    def send(self, src, dst, send, recv, device):
        y, z, x, blk, uly = place()
        here = jnp.logical_and(device[0] == blk, device[1] == uly)

        @pl.when(here)
        def _():
            pltpu.make_async_copy(src, dst, recv).start()

        @pl.when(jnp.logical_not(here))
        def _():
            remote(src, dst, send, recv, device).start()

        self.sent.append((here, src, dst, send, recv, device))

    def end(self):
        for here, *copy in self.sent:

            @pl.when(jnp.logical_not(here))
            def _():
                remote(*copy).wait_send()


class Ring:
    sends = 15

    def __init__(self, src, dst, y, order, way, send_sem, recv_sem):
        self.src, self.dst, self.y, self.order, self.way = src, dst, y, order, way
        self.send_sem, self.recv_sem = send_sem, recv_sem
        self.own_y, self.z, self.x, self.blk, self.uly = place()
        self.p = order * self.z + (1 - order) * self.x
        self.q = order * self.x + (1 - order) * self.z
        self.sent = []

    def at(self, y, p, q):
        order = self.order
        return blk_of(y, order * p + (1 - order) * q, order * q + (1 - order) * p)

    def index(self, p, q):
        return self.at(0, p, q)

    def send(self, p, q, dp, dq, src=None):
        ref = self.dst(self.at(self.y, p, q))
        target = self.at(self.own_y, (self.p + dp) % 4, (self.q + dq) % 4)
        copy = remote(
            ref if src is None else src, ref, self.send_sem.at[len(self.sent)],
            self.recv_sem.at[self.index(p, q)], (target, self.uly),
        )
        copy.start()
        self.sent.append(copy)

    def wait(self, p, q):
        wait_arrival(self.dst(self.at(self.y, p, q)), self.recv_sem.at[self.index(p, q)])

    def start(self):
        for d in (1, 3):
            self.send(self.p, self.q, d, 0, self.src)

    def second(self):
        for d in (4 - self.way, self.way):
            p = (self.p + d) % 4
            self.wait(p, self.q)
            if d == 4 - self.way:
                self.send(p, self.q, self.way, 0)

    def third(self):
        self.wait((self.p + 2) % 4, self.q)

    def spread(self, e):
        p = (self.p + e) % 4
        for d in (1, 3):
            self.send(p, self.q, 0, d, self.src if e == 0 else None)

    def fourth(self, e):
        p = (self.p + e) % 4
        for d in (4 - self.way, self.way):
            q = (self.q + d) % 4
            self.wait(p, q)
            if d == 4 - self.way:
                self.send(p, q, 0, self.way)

    def last(self):
        for e in (0, 1, 3, 2):
            self.wait((self.p + e) % 4, (self.q + 2) % 4)
        for copy in self.sent:
            copy.wait_send()


class Spread:
    def __init__(self, own, all_ref, send_sem, recv_sem, local_sem):
        self.own, self.all_ref = own, all_ref
        self.send_sem, self.recv_sem, self.local_sem = send_sem, recv_sem, local_sem
        self.w = ring_at()
        self.core = lax.axis_index("uly") % 2
        self.sibling = uly_others()[1]
        self.sent = []

    def piece(self, d, rows=slice(None), core=None):
        core = self.core if core is None else core
        ref = self.all_ref.at[core, (self.w + d) % 4]
        return ref if rows == slice(None) else ref.at[pl.ds(rows.start, rows.stop - rows.start)]

    def send(self, src, dst, recv, device):
        copy = remote(src, dst, self.send_sem.at[len(self.sent)], self.recv_sem.at[recv], device)
        copy.start()
        self.sent.append(copy)

    def pair(self, d, src=None):
        self.send(self.piece(d) if src is None else src, self.piece(d), 4 + d, self.sibling)

    def start(self):
        self.local = pltpu.make_async_copy(self.own, self.piece(0), self.local_sem)
        self.local.start()
        self.send(self.own, self.piece(0), 0, ring_place((self.w + 1) % 4))
        self.send(self.own, self.piece(0), 1, ring_place((self.w + 3) % 4))
        self.pair(0, self.own)

    def second(self):
        half = CHUNK // 2
        wait_arrival(self.piece(3), self.recv_sem.at[0])
        low = self.piece(3, slice(0, half))
        self.send(low, low, 2, ring_place((self.w + 1) % 4))
        self.pair(3)
        wait_arrival(self.piece(1), self.recv_sem.at[1])
        high = self.piece(1, slice(half, CHUNK))
        self.send(high, high, 3, ring_place((self.w + 3) % 4))
        self.pair(1)

    def third(self):
        half = CHUNK // 2
        wait_arrival(self.piece(2, slice(0, half)), self.recv_sem.at[2])
        wait_arrival(self.piece(2, slice(half, CHUNK)), self.recv_sem.at[3])
        self.pair(2)

    def last(self):
        for d in range(4):
            wait_arrival(self.piece(d, core=1 - self.core), self.recv_sem.at[4 + d])
        for copy in self.sent:
            copy.wait_send()
        self.local.wait()


SPREAD_SEMS = [pltpu.SemaphoreType.DMA((8,)), pltpu.SemaphoreType.DMA((8,)), pltpu.SemaphoreType.DMA]
FF_COLS = PADDED // 2


def forward_kernel(
    tokens_ref, cot_ref, length_ref, qkv_ref, out_ref, gate_up_ref, down_ref, norm_in_ref, norm_ff_ref,
    bias_ref, freq_ref, a_ref, b_ref, bkv_ref,
    q_out, mixed_out, lse_out, kv_out, wq_out, wo_out, gate_all, up_all, down_all, rows_hbm, normed_out,
    resid_out, cot_out, nf_out, cot_all, limit_out, cos_out, sin_out, b_qkv_out, ao_out,
    q_ref, mixed_ref, lse_ref, rows_out, normed_ref, resid_ref, cot_own, limit_ref, cos_ref, sin_ref,
    b_qkv_ref, ao_ref, kv_all, wq_all, wo_all, rows, cot_in, kv_part, acc_ref, stat_ref, qkv_in, out_in, qkv_part, out_part,
    nf_own, cross_out, cross_in, qkv_pieces, out_pieces, ff_ref,
    *sems,
):
    y, z, x, blk, uly = place()
    core, h = uly % 2, uly // 2
    sems = list(sems)

    def take(count):
        got = sems[:count]
        del sems[:count]
        return got

    chunk = 2 * blk + h
    upper = chunk // 32
    home = (1 - upper) * chunk + upper * (63 - chunk)
    row_to = [[(home, hh * 2 + s) for hh in (0, 1)] for s in (0, 1)]
    row_from = [(c // 2, (c % 2) * 2 + half) for c in (blk, 63 - blk) for half in (0, 1)]
    out_to = [(2 * (blk % 16) + q // 2, (blk // 16) * 2 + q % 2) for q in range(4)]
    out_from = [(16 * h + blk // 2, u) for u in range(4)]
    sibling = uly_others()[1]
    length = length_ref[0] * (1 - core) + length_ref[1] * core

    def prepare():
        qkv_pieces[...] = jnp.zeros_like(qkv_pieces)
        out_pieces[...] = jnp.zeros_like(out_pieces)
        group = GROUP * HEAD
        for hh in (0, 1):
            qkv_pieces[2 * hh, :12] = qkv_ref[:, hh * group : hh * group + 512]
            for place_at, start, size in (
                (0, hh * group + 512, 256),
                (256, HEADS * HEAD + hh * HEAD, HEAD),
                (384, HEADS * HEAD + 256 + hh * HEAD, HEAD),
            ):
                qkv_pieces[2 * hh + 1, :12, place_at : place_at + size] = qkv_ref[:, start : start + size]
        for q in range(4):
            out_pieces[q, :12] = out_ref[:, q * 384 : (q + 1) * 384]
        for n in range(3):
            part = (gate_up_ref[n] if n < 2 else down_ref[...]).astype(F32)
            none = jnp.zeros((48, 64), F32)
            left = jnp.concatenate([part, none], axis=1)
            right = jnp.concatenate([none, part], axis=1)
            ff_ref[n] = jnp.where(jnp.broadcast_to(core, (48, PADDED)) == 1, right, left).astype(BF)

    greet(
        ring_others() + uly_others() + [(blk_of(1 - y, z, x), (uly + 2) % 4)]
        + row_to[0] + row_to[1] + row_from + out_to + out_from,
        prepare,
    )

    deliver = Deliver()
    piece_send, piece_recv, row_send, row_recv = take(4)
    for q in range(4):
        deliver.send(qkv_pieces.at[q], qkv_in.at[uly], piece_send.at[q], piece_recv.at[uly], (blk, q))
    for q in range(4):
        deliver.send(out_pieces.at[q], out_in.at[uly], piece_send.at[4 + q], piece_recv.at[4 + uly], out_to[q])
    for s in (0, 1):
        for hh in (0, 1):
            deliver.send(
                tokens_ref.at[s], rows.at[upper, core], row_send.at[s * 2 + hh],
                row_recv.at[upper * 2 + core], row_to[s][hh],
            )

    wide = PADDED // 2
    gathered = (gate_all, up_all, down_all)
    ff_send, ff_recv, y_send, y_recv, y_local = take(5)
    other_blk = blk_of(1 - y, z, x)

    def ff_part(n, half):
        return ff_ref.at[n, :, pl.ds(pl.multiple_of(half * wide, 128), wide)]

    picked = lax.broadcasted_iota(jnp.int32, (48, 64), 1)
    picked = jnp.where(picked % 16 < 12, picked // 16 * 12 + picked % 16, -1)
    picked = jnp.where(picked == lax.broadcasted_iota(jnp.int32, (48, 64), 0), 1.0, 0.0).astype(BF)
    for u in range(4):
        wait_arrival(qkv_in.at[u], piece_recv.at[u])
    qkv_part[...] = dot(picked, qkv_in[...].reshape(64, 512)).astype(BF)
    wq = Gather(
        lambda s: qkv_part.at[:, pl.ds(256 * s, 256)],
        lambda s, item: wq_all.at[
            core, pl.ds(pl.multiple_of(item * 48, 16), 48), pl.ds(256 * s, 256)
        ],
        *take(3),
    )
    wq.start()
    for u in range(4):
        wait_arrival(out_in.at[u], piece_recv.at[4 + u])
    out_part[...] = dot(picked, out_in[...].reshape(64, 384)).astype(BF)
    y_copies = []
    for n, ref in enumerate(gathered):
        copy = remote(ff_part(n, 1 - y), ref.at[blk], y_send.at[n], y_recv.at[n], (other_blk, uly))
        copy.start()
        y_copies.append(copy)
        copy = pltpu.make_async_copy(ff_part(n, y), ref.at[blk], y_local.at[n])
        copy.start()
        y_copies.append(copy)
    for s in (0, 1):
        deliver.send(
            cot_ref.at[s], cot_in.at[core], row_send.at[4 + s], row_recv.at[4 + core], (home, upper * 2 + s)
        )

    def out_columns(item, s):
        start = ((item % 2) * 2 + core) * 384
        return pl.ds(pl.multiple_of(start + 128 * s, 128), 128 + 128 * s)

    wo = Gather(
        lambda s: out_part.at[:, pl.ds(128 * s, 128 + 128 * s)],
        lambda s, item: wo_all.at[pl.ds(pl.multiple_of((item // 2) * 48, 16), 48), out_columns(item, s)],
        *take(3),
    )
    own_ff, other_ff = (
        [
            Ring(
                ff_part(n, y) if k == 0 else ref.at[other_blk],
                lambda item, ref=ref: ref.at[item],
                y if k == 0 else 1 - y,
                y if k == 0 else 1 - y,
                (1, 3, 1 + 2 * k)[n],
                ff_send.at[k, n], ff_recv.at[k, n],
            )
            for n, ref in enumerate(gathered)
        ]
        for k in (0, 1)
    )
    rings = own_ff + other_ff
    wq.second()
    wq.third()
    wq.fourth()
    for ring in own_ff:
        ring.start()
    for n in range(3):
        y_copies[2 * n].wait_recv()
    for ring in other_ff:
        ring.start()

    for slot, at in ((0, blk), (1, 63 - blk)):
        row = lax.broadcasted_iota(jnp.int32, (CHUNK, HEAD), 0) + at * CHUNK
        angle = row.astype(F32) * freq_ref[...]
        first = lax.broadcasted_iota(jnp.int32, (CHUNK, HEAD), 1) < HEAD // 2
        sine = jnp.sin(angle)
        cos_ref[slot * CHUNK : (slot + 1) * CHUNK, :] = jnp.cos(angle)
        sin_ref[slot * CHUNK : (slot + 1) * CHUNK, :] = jnp.where(first, -sine, sine)
        row = lax.broadcasted_iota(jnp.int32, (8, ROWS), 1) % CHUNK + at * CHUNK
        limit_ref[slot] = jnp.minimum(row, length - 1)
    group = GROUP * HEAD
    group_at = pl.ds(pl.multiple_of(h * group, 128), group)
    head_at = pl.ds(pl.multiple_of(h * HEAD, 128), HEAD)
    ao_ref[...] = a_ref[3, :, group_at]
    b_qkv_ref[...] = jnp.zeros_like(b_qkv_ref)
    b_qkv_ref[:16, :group] = b_ref[0, :, group_at]
    b_qkv_ref[16:32, group : group + HEAD] = bkv_ref[0, :, head_at]
    b_qkv_ref[32:, group + HEAD :] = bkv_ref[1, :, head_at]
    a_qkv = a_ref[:3].reshape(48, D)
    bo_ref = b_ref.at[1]

    def bias(n):
        at = h * GROUP + n if n < GROUP else HEADS + 2 * (n - GROUP) + h
        return bias_ref[pl.ds(at, 1), :]

    for n in range(4):
        wait_arrival(rows.at[n // 2, n % 2], row_recv.at[n])
        value = rows[n // 2, n % 2].astype(F32)
        at = slice(n * 64, (n + 1) * 64)
        rows_out[at, :] = rows[n // 2, n % 2]
        normed_ref[at, :] = (value * norm_scale(value) * norm_in_ref[...]).astype(BF)
    latent = dot_nt(normed_ref[...], a_qkv)
    adapted = dot(latent.astype(BF), b_qkv_ref[...])
    wq.last()
    pair_send, pair_recv = take(2)

    def pair_copy(ref, n):
        return remote(ref, ref, pair_send.at[n], pair_recv.at[n], sibling)

    pair_copy(wq_all.at[core], 0).start()
    wo.start()
    pair_copy(wq_all.at[core], 0).wait_send()
    pair_copy(wq_all.at[1 - core], 0).wait_recv()

    cos_table, sine_table = cos_ref[...], sin_ref[...]

    def turn(head):
        return head * cos_table + pltpu.roll(head, HEAD // 2, 1) * sine_table

    def query(n, head):
        q_ref[:, n * HEAD : (n + 1) * HEAD] = (turn(head + bias(n)) * (HEAD ** (-0.5) * LOG2E)).astype(BF)

    pairs = dot(normed_ref[...], wq_all[1, :, 256:]) + adapted[:, 768:]
    for n, head in ((0, turn(pairs[:, :HEAD] + bias(6))), (1, pairs[:, HEAD:] + bias(7))):
        at = slice(n * HEAD, (n + 1) * HEAD)
        kv_part[0, :, at] = head[:CHUNK].astype(BF)
        kv_part[1, :, at] = head[CHUNK:].astype(BF)
    kv = Gather(
        lambda s: kv_part.at[s],
        lambda s, item: kv_all.at[item if s == 0 else 63 - item],
        *take(3),
    )
    kv.start()
    heads = dot(normed_ref[...], wq_all[1, :, :256]) + adapted[:, 512:768]
    for n in (4, 5):
        query(n, heads[:, (n - 4) * HEAD : (n - 3) * HEAD])
    kv.second()
    for ring in rings:
        ring.second()
    wo.second()
    heads = dot(normed_ref[...], wq_all[0]) + adapted[:, :512]
    for n in range(4):
        query(n, heads[:, n * HEAD : (n + 1) * HEAD])
    kv.third()
    for ring in rings:
        ring.third()
    wo.third()
    kv.fourth()
    wo.fourth()

    for half in (0, 1):
        wait_arrival(cot_in.at[half], row_recv.at[4 + half])
        start = ((1 - h) * blk + h * (63 - blk)) * CHUNK + half * 64
        at = lax.broadcasted_iota(jnp.int32, (64, D), 0) + start
        cot_own[half * 64 : (half + 1) * 64, :] = jnp.where(
            at < length, cot_in[half].astype(F32), 0.0
        ).astype(BF)
    cot_spread = Spread(cot_own, cot_all, *take(3))
    cot_spread.start()
    kv.last()
    for e in (0, 1, 3, 2):
        for ring in rings:
            ring.spread(e)
    (out_sem,) = take(1)
    copies = []

    def keep(*pairs):
        for src, dst in pairs:
            copies.append(pltpu.make_async_copy(src, dst, out_sem.at[len(copies)]))
            copies[-1].start()

    keep(
        (kv_all, kv_out), (wq_all, wq_out), (q_ref, q_out), (rows_out, rows_hbm), (normed_ref, normed_out),
        (cot_own, cot_out), (limit_ref, limit_out), (cos_ref, cos_out), (sin_ref, sin_out),
        (b_qkv_ref, b_qkv_out), (ao_ref, ao_out),
    )
    wo.last()

    def wo_columns(c, n):
        return wo_all.at[:, pl.ds(pl.multiple_of((2 * n + c) * 384, 128), 384)]

    for n in (0, 1):
        pair_copy(wo_columns(core, n), 1 + n).start()
    args = (q_ref, kv_all, limit_ref, mixed_ref, lse_ref, acc_ref, stat_ref)
    beside = {
        3: lambda: [ring.fourth(0) for ring in rings] + [cot_spread.second()],
        5: lambda: [ring.fourth(1) for ring in rings],
        6: lambda: [ring.fourth(3) for ring in rings] + [cot_spread.third()],
        7: lambda: [ring.fourth(2) for ring in rings],
    }
    for slot, at in ((0, blk), (1, 63 - blk)):
        for part in range(4):
            forward_slot(slot, at, part, *args)
            if slot * 4 + part in beside:
                beside[slot * 4 + part]()
    for n in (0, 1):
        pair_copy(wo_columns(core, n), 1 + n).wait_send()
        pair_copy(wo_columns(1 - core, n), 1 + n).wait_recv()
    keep((wo_all, wo_out), (mixed_ref, mixed_out), (lse_ref, lse_out))

    def project(slot):
        mixed = mixed_ref[pl.ds(pl.multiple_of(slot * CHUNK, CHUNK), CHUNK), :]
        lifted = dot(dot_nt(mixed, ao_ref[...]).astype(BF), bo_ref[...])
        return dot(mixed, wo_all[...]) + lifted

    (cross_sem,) = take(1)
    cross_out[...] = project(1 - h).astype(BF)
    cross = remote(cross_out, cross_in, cross_sem.at[0], cross_sem.at[1], uly_others()[0])
    cross.start()
    mine = project(h) + rows_out[pl.ds(pl.multiple_of(h * CHUNK, CHUNK), CHUNK), :].astype(F32)
    cross.wait()
    residual = mine + cross_in[...].astype(F32)
    resid_ref[...] = residual
    keep((resid_ref, resid_out))
    nf_own[...] = (residual * norm_scale(residual) * norm_ff_ref[...]).astype(BF)
    keep((nf_own, nf_out))
    cot_spread.last()
    for ring in rings:
        ring.last()
    for n in range(3):
        y_copies[2 * n].wait_send()
        y_copies[2 * n + 1].wait()
    deliver.end()
    for copy in copies:
        copy.wait()


def forward(*args):
    weight = jax.ShapeDtypeStruct((32, 48, FF_COLS), BF)
    group = GROUP * HEAD
    dma = pltpu.SemaphoreType.DMA
    spread = jax.ShapeDtypeStruct((2, 4, CHUNK, D), BF)
    return pl.pallas_call(
        forward_kernel,
        out_shape=(
            jax.ShapeDtypeStruct((2 * CHUNK, group), BF),
            jax.ShapeDtypeStruct((2 * CHUNK, group), BF),
            jax.ShapeDtypeStruct((2, 8, ROWS), F32),
            jax.ShapeDtypeStruct((CHUNKS, CHUNK, 2 * HEAD), BF),
            jax.ShapeDtypeStruct((2, D, 512), BF),
            jax.ShapeDtypeStruct((D // 2, D), BF),
            weight, weight, weight,
            jax.ShapeDtypeStruct((2 * CHUNK, D), BF),
            jax.ShapeDtypeStruct((2 * CHUNK, D), BF),
            jax.ShapeDtypeStruct((CHUNK, D), F32),
            jax.ShapeDtypeStruct((CHUNK, D), BF),
            jax.ShapeDtypeStruct((CHUNK, D), BF),
            spread,
            jax.ShapeDtypeStruct((2, 8, ROWS), jnp.int32),
            jax.ShapeDtypeStruct((2 * CHUNK, HEAD), F32),
            jax.ShapeDtypeStruct((2 * CHUNK, HEAD), F32),
            jax.ShapeDtypeStruct((48, 1024), BF),
            jax.ShapeDtypeStruct((16, group), BF),
        ),
        in_specs=[ANY] * 2 + [pl.BlockSpec(memory_space=pltpu.SMEM)] + [IN_VMEM] * 11,
        out_specs=(ANY,) * 20,
        scratch_shapes=[
            pltpu.VMEM((2 * CHUNK, group), BF),
            pltpu.VMEM((2 * CHUNK, group), BF),
            pltpu.VMEM((2, 8, ROWS), F32),
            pltpu.VMEM((2 * CHUNK, D), BF),
            pltpu.VMEM((2 * CHUNK, D), BF),
            pltpu.VMEM((CHUNK, D), F32),
            pltpu.VMEM((CHUNK, D), BF),
            pltpu.VMEM((2, 8, ROWS), jnp.int32),
            pltpu.VMEM((2 * CHUNK, HEAD), F32),
            pltpu.VMEM((2 * CHUNK, HEAD), F32),
            pltpu.VMEM((48, 1024), BF),
            pltpu.VMEM((16, group), BF),
            pltpu.VMEM((CHUNKS, CHUNK, 2 * HEAD), BF),
            pltpu.VMEM((2, D, 512), BF),
            pltpu.VMEM((D // 2, D), BF),
            pltpu.VMEM((2, 2, 64, D), BF),
            pltpu.VMEM((2, 64, D), BF),
            pltpu.VMEM((2, CHUNK, 2 * HEAD), BF),
            pltpu.VMEM((HEAD, ROWS), F32),
            pltpu.VMEM((2, 8, ROWS), F32),
            pltpu.VMEM((4, 16, 512), BF),
            pltpu.VMEM((4, 16, 384), BF),
            pltpu.VMEM((48, 512), BF),
            pltpu.VMEM((48, 384), BF),
            pltpu.VMEM((CHUNK, D), BF),
            pltpu.VMEM((CHUNK, D), BF),
            pltpu.VMEM((CHUNK, D), BF),
            pltpu.VMEM((4, 16, 512), BF),
            pltpu.VMEM((4, 16, 384), BF),
            pltpu.VMEM((3, 48, PADDED), BF),
            dma((8,)), dma((8,)), dma((6,)), dma((6,)),
            dma((2, 3, Ring.sends)), dma((2, 3, 16)), dma((3,)), dma((3,)), dma((3,)),
        ]
        + GATHER_SEMS()
        + GATHER_SEMS()
        + [dma((3,)), dma((3,))]
        + GATHER_SEMS()
        + SPREAD_SEMS
        + [dma((16,)), dma((2,))],
        compiler_params=pltpu.CompilerParams(
            collective_id=1, has_side_effects=True, vmem_limit_bytes=48 * 2**20
        ),
        name="forward",
    )(*args)


class RingSum:
    @staticmethod
    def scratch():
        piece, half = (CHUNK, D), (CHUNK // 2, D)
        return [
            pltpu.VMEM((2,) + half, BF),
            pltpu.VMEM((2,) + piece, BF),
            pltpu.VMEM(piece, BF),
            pltpu.VMEM((2,) + piece, BF),
            pltpu.SemaphoreType.DMA((4,)),
            pltpu.SemaphoreType.DMA((4,)),
        ]

    scratches = 6

    def __init__(self, term, scratch):
        self.term = term
        self.halves, self.last_in, self.far, self.near, self.send_sem, self.recv_sem = scratch
        self.w = ring_at()
        self.sent = []

    def send(self, src, dst, recv, d):
        copy = remote(
            src, dst, self.send_sem.at[recv], self.recv_sem.at[recv], ring_place((self.w + d) % 4)
        )
        copy.start()
        self.sent.append(copy)

    def first(self):
        half = CHUNK // 2
        self.far[...] = self.term(2).astype(BF)
        self.send(self.far.at[pl.ds(0, half)], self.halves.at[0], 0, 1)
        self.send(self.far.at[pl.ds(half, half)], self.halves.at[1], 1, 3)

    def second(self):
        half = CHUNK // 2
        for k, d in ((0, 1), (1, 3)):
            total = self.term(d)
            wait_arrival(self.halves.at[k], self.recv_sem.at[k])
            rows = slice(k * half, (k + 1) * half)
            other = slice((1 - k) * half, (2 - k) * half)
            self.near[k, rows] = (total[rows] + self.halves[k].astype(F32)).astype(BF)
            self.near[k, other] = total[other].astype(BF)
            self.send(self.near.at[k], self.last_in.at[k], 2 + k, d)

    def third(self):
        total = self.term(0)
        for k in (0, 1):
            wait_arrival(self.last_in.at[k], self.recv_sem.at[2 + k])
            total += self.last_in[k].astype(F32)
        for copy in self.sent:
            copy.wait_send()
        return total


def pick_kernel(
    set_ref, a_wide, a_down, b_wide, b_kv, b_ff, a_own, b_own, b_pair, a_ff, b_cols, a_cols, b_out, sems
):
    y, z, x, blk, uly = place()
    own = set_ref[uly % 2]
    first = (35 * uly) // 2 * 128 + y * FF_COLS
    columns = pl.ds(pl.multiple_of(first, 128), FF_COLS)
    pairs = [(a_wide.at[n, own], a_own.at[n]) for n in range(4)]
    pairs += [(b_wide.at[n, own], b_own.at[n]) for n in (0, 1)]
    pairs += [(b_kv.at[n, own], b_pair.at[n]) for n in (0, 1)]
    for s in (0, 1):
        chosen = set_ref[s]
        for n in (0, 1):
            pairs.append((a_wide.at[4 + n, chosen], a_ff.at[s, pl.ds(16 * n, 16)]))
            pairs.append((b_ff.at[n, chosen, :, columns], b_cols.at[s, n]))
        pairs.append((a_down.at[chosen, :, columns], a_cols.at[s]))
        pairs.append((b_wide.at[2, chosen], b_out.at[s]))
    copies = [pltpu.make_async_copy(src, dst, sems.at[n]) for n, (src, dst) in enumerate(pairs)]
    for copy in copies:
        copy.start()
    for copy in copies:
        copy.wait()


def pick(*args):
    def out(*shape):
        return jax.ShapeDtypeStruct(shape, BF)

    return pl.pallas_call(
        pick_kernel,
        out_shape=(
            out(4, 16, D), out(2, 16, D), out(2, 16, 2 * HEAD), out(2, 32, D), out(2, 2, 16, FF_COLS),
            out(2, 16, FF_COLS), out(2, 16, D),
        ),
        in_specs=[pl.BlockSpec(memory_space=pltpu.SMEM)] + [ANY] * 5,
        out_specs=(IN_VMEM,) * 7,
        scratch_shapes=[pltpu.SemaphoreType.DMA((20,))],
        name="pick",
    )(*args)


def ff_kernel(
    own_hbm, cot_hbm, gate_hbm, up_hbm, down_hbm, a_ff, b_cols_ref, a_cols_ref, b_out,
    grad_out, down_out, cols_out, wide_out,
    cols_ref, wide_ref, x_ref, cot_ref, gate_w, up_w, down_w, b_cols, a_cols, hidden_ref, grad_gate, grad_up,
    grad_hidden, own_ref, terms, pair, total_ref, down_sum, sems, out_sems, pair_send, pair_recv, *scratch,
):
    y, z, x, blk, uly = place()
    core = uly % 2
    scratch = list(scratch)

    def take(count):
        got = scratch[:count]
        del scratch[:count]
        return got

    pairs = (
        (own_hbm, own_ref), (down_hbm, down_w), (cot_hbm, cot_ref), (gate_hbm, gate_w), (up_hbm, up_w),
    )
    copies = [pltpu.make_async_copy(src, dst, sems.at[n]) for n, (src, dst) in enumerate(pairs)]
    for copy in copies:
        copy.start()
    at = lax.broadcasted_iota(jnp.int32, (16, FF_COLS), 1) + (y * FF_COLS - 64 * core)
    inside = jnp.logical_and(at >= 0, at < FF // 4)

    def keep(v):
        return jnp.where(inside, v.astype(F32), 0.0).astype(BF)

    def prepare():
        for s in (0, 1):
            a_cols[s] = keep(a_cols_ref[s])
            for n in (0, 1):
                b_cols[s, n] = keep(b_cols_ref[s, n])
        cols_ref[...] = jnp.zeros_like(cols_ref)

    sibling = uly_others()[1]
    greet([sibling, (blk_of(1 - y, z, x), uly), (blk_of(1 - y, z, x), (uly + 2) % 4)], prepare)
    here = pl.ds(pl.multiple_of(y * FF_COLS, 128), FF_COLS)
    copies[0].wait()
    spread = Spread(own_ref, x_ref, *take(3))
    spread.start()

    def flat(ref, s):
        return ref[s].reshape(4 * CHUNK, D)

    order = (1 - core, core)
    copies[1].wait()
    copies[2].wait()
    latent_cots = []
    for k, s in enumerate(order):
        cot = flat(cot_ref, s)
        latent_cots.append(dot_nt(cot, b_out[s]))
        grad_hidden[k] = dot(cot, down_w[...]) + dot(latent_cots[k].astype(BF), a_cols[s])
        (spread.second, spread.third)[k]()
    copies[3].wait()
    copies[4].wait()
    spread.last()

    def pair_copy(n, d):
        at = (ring_at() + d) % 4
        return remote(
            terms.at[n, 0, at], pair.at[n, at], pair_send.at[n, d], pair_recv.at[n, d], sibling
        )

    def term(n, d):
        at = (ring_at() + d) % 4
        wait_arrival(pair.at[n, at], pair_recv.at[n, d])
        return terms[n, 1, at].astype(F32) + pair[n, at].astype(F32)

    ring = RingSum(lambda d: term(0, d), take(RingSum.scratches))
    for k, s in enumerate(order):
        rows = flat(x_ref, s)
        latent = dot_nt(rows, a_ff[s])
        low = latent.astype(BF)
        gate = dot(rows, gate_w[...]) + dot(low[:, :16], b_cols[s, 0])
        sigmoid = jax.nn.sigmoid(gate)
        silu = gate * sigmoid
        grad_up[...] = (grad_hidden[k] * silu).astype(BF)
        slope = grad_hidden[k] * (sigmoid * (1.0 + gate * (1.0 - sigmoid)))
        up = dot(rows, up_w[...]) + dot(low[:, 16:], b_cols[s, 1])
        grad_gate[...] = (slope * up).astype(BF)
        hidden_ref[...] = (silu * up).astype(BF)
        back_gate = dot_nt(grad_gate[...], b_cols[s, 0])
        back_up = dot_nt(grad_up[...], b_cols[s, 1])
        grads = (
            dot_nt(grad_gate[...], gate_w[...])
            + dot_nt(grad_up[...], up_w[...])
            + dot(back_gate.astype(BF), a_ff[s, :16])
            + dot(back_up.astype(BF), a_ff[s, 16:])
        )
        terms[0, k] = grads.astype(BF).reshape(4, CHUNK, D)
        if k == 0:
            for d in (2, 1, 3, 0):
                pair_copy(0, d).start()
        else:
            ring.first()
        latent_down = dot_nt(hidden_ref[...], a_cols[s])
        down = dot_nt(hidden_ref[...], down_w[...]) + dot(latent_down.astype(BF), b_out[s])
        terms[1, k] = down.astype(BF).reshape(4, CHUNK, D)
        if k == 0:
            for d in (2, 1, 3, 0):
                pair_copy(1, d).start()
        else:
            ring.second()

        def put(ref, n, value, at=slice(None)):
            ref[pl.ds(pl.multiple_of((2 * n + s) * 16, 16), 16), at] = value.astype(BF)

        def turned(value):
            return value.T.astype(BF)

        put(cols_ref, 0, dot(turned(latent_cots[k]), hidden_ref[...]), here)
        put(cols_ref, 1, dot(turned(latent[:, :16]), grad_gate[...]), here)
        put(cols_ref, 2, dot(turned(latent[:, 16:]), grad_up[...]), here)
        put(wide_ref, 0, dot(turned(back_gate), rows))
        put(wide_ref, 1, dot(turned(back_up), rows))
        put(wide_ref, 2, dot(turned(latent_down), flat(cot_ref, s)))
    outs = [
        pltpu.make_async_copy(src, dst, out_sems.at[n])
        for n, (src, dst) in enumerate(
            ((cols_ref, cols_out), (wide_ref, wide_out), (down_sum, down_out), (total_ref, grad_out))
        )
    ]
    outs[0].start()
    outs[1].start()
    for d in range(4):
        down_sum[(ring_at() + d) % 4] = term(1, d).astype(BF)
    outs[2].start()
    total_ref[...] = ring.third()
    outs[3].start()
    for n in (0, 1):
        for d in range(4):
            pair_copy(n, d).wait_send()
    for copy in outs:
        copy.wait()


def feed_forward(*args):
    dma = pltpu.SemaphoreType.DMA
    weight = pltpu.VMEM((D, FF_COLS), BF)
    rows = pltpu.VMEM((4 * CHUNK, FF_COLS), BF)
    pieces = (4, CHUNK, D)
    return pl.pallas_call(
        ff_kernel,
        out_shape=(
            jax.ShapeDtypeStruct((CHUNK, D), F32),
            jax.ShapeDtypeStruct(pieces, BF),
            jax.ShapeDtypeStruct((96, PADDED), BF),
            jax.ShapeDtypeStruct((96, D), BF),
        ),
        in_specs=[ANY] * 5 + [IN_VMEM] * 4,
        out_specs=(ANY,) * 4,
        scratch_shapes=[
            pltpu.VMEM((96, PADDED), BF), pltpu.VMEM((96, D), BF),
            pltpu.VMEM((2,) + pieces, BF), pltpu.VMEM((2,) + pieces, BF),
            weight, weight, weight,
            pltpu.VMEM((2, 2, 16, FF_COLS), BF), pltpu.VMEM((2, 16, FF_COLS), BF),
            rows, rows, rows,
            pltpu.VMEM((2, 4 * CHUNK, FF_COLS), F32),
            pltpu.VMEM((CHUNK, D), BF),
            pltpu.VMEM((2, 2) + pieces, BF), pltpu.VMEM((2,) + pieces, BF),
            pltpu.VMEM((CHUNK, D), F32), pltpu.VMEM(pieces, BF),
            dma((5,)), dma((4,)), dma((2, 4)), dma((2, 4)),
        ]
        + SPREAD_SEMS
        + RingSum.scratch(),
        compiler_params=pltpu.CompilerParams(
            collective_id=4, has_side_effects=True, vmem_limit_bytes=62 * 2**20
        ),
        name="feed_forward",
    )(*args)


def backward_blocks(
    slot, first, last, q_ref, kv_ref, limit_ref, mixed_ref, grad_ref, lse_ref, dkv_ref, acc_ref
):
    turned = head_columns(q_ref, slot)
    rows = head_rows(q_ref, slot)
    grad_turned = head_columns(grad_ref, slot)
    grad_rows = head_rows(grad_ref, slot)
    mixed_turned = head_columns(mixed_ref, slot)
    row_dot = jnp.sum(
        grad_turned.astype(F32) * mixed_turned.astype(F32), axis=0, keepdims=True
    )
    limit = limit_ref[slot, 0:1, :]
    lse = lse_ref[slot, 0:1, :]

    def step(n, carry):
        keys, values = key_block(kv_ref, n, KEYS_BACK)
        scores = jnp.where(key_places(n, KEYS_BACK) <= limit, dot(keys, turned), -1e30)
        probs = jnp.exp2(scores - lse)
        grad_probs = dot(values, grad_turned)
        grad_scores = (probs * (grad_probs - row_dot)).astype(BF)
        acc_ref[slot] += dot(keys.T, grad_scores)
        at = pl.ds(pl.multiple_of(n * KEYS_BACK, KEYS_BACK), KEYS_BACK)
        dkv_ref[at, :HEAD] += dot(grad_scores, rows)
        dkv_ref[at, HEAD:] += dot(probs.astype(BF), grad_rows)
        return carry

    lax.fori_loop(first, last, step, 0)


class Reduce:
    @staticmethod
    def scratch(shape):
        return [
            pltpu.VMEM((2, 3, 2, 4) + shape, BF),
            pltpu.VMEM((2, 3, 2) + shape, BF),
            pltpu.VMEM((2,) + shape, BF),
            pltpu.VMEM((2, 4, 2) + shape, BF),
            pltpu.VMEM((2, 2) + shape, BF),
            pltpu.SemaphoreType.DMA((2, 10)),
            pltpu.SemaphoreType.DMA((2, 10)),
        ]

    scratches = 7

    def __init__(self, part, scratch):
        self.part = part
        self.buf_q, self.buf_p, self.buf_y, self.sum_p, self.sum_y, self.send_sem, self.recv_sem = scratch
        self.y, self.z, self.x, self.blk, self.uly = place()
        self.pq = ((self.x, self.z), (self.z, self.x))
        self.flying = []

    def send(self, src, dst, half, n, y, p, q):
        target = blk_of(y, q, p) if half == 0 else blk_of(y, p, q)
        copy = remote(
            src, dst, self.send_sem.at[half, n], self.recv_sem.at[half, n], (target, self.uly)
        )
        copy.start()
        self.flying.append(copy)

    def land(self):
        for copy in self.flying:
            copy.wait()
        self.flying = []

    def first(self):
        for d in (2, 1, 3):
            for half in (0, 1):
                p, q = self.pq[half]
                to = (q + d) % 4
                for y in (0, 1):
                    src = self.part.at[0, y, to] if half == 0 else self.part.at[1, y, :, to]
                    self.send(
                        src, self.buf_q.at[half, d - 1, y], half, (d - 1) * 2 + y, self.y, p, to
                    )

    def second(self):
        self.land()
        for d in (2, 1, 3, 0):
            for half in (0, 1):
                p, q = self.pq[half]
                to = (p + d) % 4
                for y in (0, 1):
                    own = self.part[0, y, q, to] if half == 0 else self.part[1, y, to, q]
                    total = own.astype(F32)
                    for n in range(3):
                        total += self.buf_q[half, n, y, to].astype(F32)
                    self.sum_p[half, d, y] = total.astype(BF)
                if d > 0:
                    self.send(
                        self.sum_p.at[half, d], self.buf_p.at[half, d - 1], half, 5 + d, self.y, to, q
                    )

    def third(self):
        self.land()
        for k in (1, 0):
            for half in (0, 1):
                p, q = self.pq[half]
                y = self.y if k == 0 else 1 - self.y
                total = self.sum_p[half, 0, y].astype(F32)
                for n in range(3):
                    total += self.buf_p[half, n, y].astype(F32)
                self.sum_y[half, k] = total.astype(BF)
                if k == 1:
                    self.send(self.sum_y.at[half, 1], self.buf_y.at[half], half, 9, 1 - self.y, p, q)

    def fourth(self):
        self.land()
        return [self.sum_y[half, 0].astype(F32) + self.buf_y[half].astype(F32) for half in (0, 1)]


class Shed:
    @staticmethod
    def scratch(shape):
        return [
            pltpu.VMEM((2, 4) + shape, BF),
            pltpu.VMEM((2, 4) + shape, BF),
            pltpu.VMEM((2, 2, 4) + shape, BF),
            pltpu.VMEM((4, 2) + shape, BF),
            pltpu.VMEM((3, 2) + shape, BF),
            pltpu.VMEM((2,) + shape, BF),
            pltpu.VMEM(shape, BF),
            pltpu.SemaphoreType.DMA((10,)),
            pltpu.SemaphoreType.DMA((10,)),
        ]

    scratches = 9

    def __init__(self, part, half, rows, order, scratch):
        self.part, self.half, self.rows, self.order = part, half, rows, order
        (
            self.buf_far, self.sum_mid, self.buf_in, self.sum_p, self.buf_p, self.sum_y, self.buf_y,
            self.send_sem, self.recv_sem,
        ) = scratch
        self.y, self.z, self.x, self.blk, self.uly = place()
        self.p, self.q = (self.x, self.z) if order == 0 else (self.z, self.x)
        self.flying = []

    def line(self, y, q):
        rows = pl.ds(*self.rows)
        if self.order == 0:
            return self.part.at[self.half, y, q, :, rows]
        return self.part.at[self.half, y, :, q, rows]

    def value(self, y, q, p):
        start, size = self.rows
        z, x = (q, p) if self.order == 0 else (p, q)
        return self.part[self.half, y, z, x, start : start + size].astype(F32)

    def send(self, src, dst, n, y, p, q):
        target = blk_of(y, q, p) if self.order == 0 else blk_of(y, p, q)
        copy = remote(src, dst, self.send_sem.at[n], self.recv_sem.at[n], (target, self.uly))
        copy.start()
        self.flying.append(copy)

    def land(self):
        for copy in self.flying:
            copy.wait()
        self.flying = []

    def first(self):
        for y, d in ((0, 1), (1, 3)):
            to = (self.q + d) % 4
            self.send(self.line(y, (self.q + 2) % 4), self.buf_far.at[y], y, self.y, self.p, to)
        for y, d in ((1, 1), (0, 3)):
            to = (self.q + d) % 4
            self.send(self.line(y, to), self.buf_in.at[d // 2, y], 2 + d // 2, self.y, self.p, to)

    def second(self):
        direct = self.flying[2:]
        self.flying = self.flying[:2]
        self.land()
        for y, d in ((0, 1), (1, 3)):
            to = (self.q + d) % 4
            for p in range(4):
                total = self.value(y, to, p) + self.buf_far[y, p].astype(F32)
                self.sum_mid[y, p] = total.astype(BF)
            self.send(self.sum_mid.at[y], self.buf_in.at[d // 2, y], 4 + y, self.y, self.p, to)
        self.flying += direct

    def third(self):
        self.land()
        for d in (2, 1, 3, 0):
            to = (self.p + d) % 4
            for y in (0, 1):
                total = self.value(y, self.q, to)
                for n in (0, 1):
                    total += self.buf_in[n, y, to].astype(F32)
                self.sum_p[d, y] = total.astype(BF)
            if d > 0:
                self.send(self.sum_p.at[d], self.buf_p.at[d - 1], 5 + d, self.y, to, self.q)

    def fourth(self):
        self.land()
        for k in (1, 0):
            y = self.y if k == 0 else 1 - self.y
            total = self.sum_p[0, y].astype(F32)
            for n in range(3):
                total += self.buf_p[n, y].astype(F32)
            self.sum_y[k] = total.astype(BF)
            if k == 1:
                self.send(self.sum_y.at[1], self.buf_y, 9, 1 - self.y, self.p, self.q)

    def last(self):
        self.land()
        return self.sum_y[0].astype(F32) + self.buf_y[...].astype(F32)


def reduce_others():
    y, z, x, blk, uly = place()
    return (
        [(blk_of(1 - y, z, x), uly)]
        + [(blk_of(y, z, (x + d) % 4), uly) for d in (1, 2, 3)]
        + [(blk_of(y, (z + d) % 4, x), uly) for d in (1, 2, 3)]
    )


UNIT = (16, 128)


class Total:
    @staticmethod
    def scratch(kept, summed):
        shape = (kept + summed,) + UNIT
        return (
            [pltpu.VMEM((2, 2, 4, 4) + shape, BF)]
            + Reduce.scratch(shape)
            + [
                pltpu.VMEM((2,) + shape, BF),
                pltpu.VMEM((3, 2) + shape, BF),
                pltpu.VMEM((2, 4 * kept + summed) + UNIT, BF),
                pltpu.SemaphoreType.DMA((3,)),
                pltpu.SemaphoreType.DMA((3,)),
                pltpu.SemaphoreType.DMA((13,)),
                pltpu.SemaphoreType.DMA((13,)),
                pltpu.SemaphoreType.DMA,
                pltpu.SemaphoreType.DMA,
                pltpu.SemaphoreType.DMA,
            ]
        )

    scratches = 18

    @staticmethod
    def shape(kept, summed):
        return jax.ShapeDtypeStruct((2, 2, 4, 4, 4 * kept + summed) + UNIT, BF)

    def __init__(self, kept, summed, all_ref, scratch):
        self.kept, self.summed, self.all_ref = kept, summed, all_ref
        self.part = scratch[0]
        self.reduce = Reduce(self.part, scratch[1:8])
        self.own, self.buf, self.full, self.send_sem, self.recv_sem = scratch[8:13]
        self.all_send, self.all_recv, self.local_sem, self.pair_send, self.pair_recv = scratch[13:18]
        self.y, self.z, self.x, self.blk, self.uly = place()
        self.core = self.uly % 2
        self.flying = []

    def pack(self, values, first, per, at):
        for n, value in enumerate(values, first):
            item = n // per
            self.part[item // 32, item // 16 % 2, item // 4 % 4, item % 4, at + n % per] = value.astype(BF)

    def pack_kept(self, values, first=0):
        self.pack(values, first, self.kept, 0)

    def pack_summed(self, values, first=0):
        self.pack(values, first, self.summed, self.kept)

    def clear(self, kept, summed):
        nothing = jnp.zeros(UNIT, BF)
        self.pack_kept([nothing] * (64 * self.kept - kept), kept)
        self.pack_summed([nothing] * (64 * self.summed - summed), summed)

    def across(self):
        for half, total in enumerate(self.reduce.fourth()):
            self.own[half] = total.astype(BF)
        self.copies = []
        for n, other in enumerate(uly_others()):
            copy = remote(self.own, self.buf.at[n], self.send_sem.at[n], self.recv_sem.at[n], other)
            copy.start()
            self.copies.append(copy)

    def send(self, src, dst, n, y, z, x):
        copy = remote(src, dst, self.all_send.at[n], self.all_recv.at[n], (blk_of(y, z, x), self.uly))
        copy.start()
        self.flying.append(copy)

    def item(self, y, x=None):
        ref = self.all_ref.at[self.core, y, self.z]
        return ref if x is None else ref.at[x]

    def along_x(self, y, src, first):
        for d in (1, 2, 3):
            self.send(src, self.item(y, self.x), first + d, self.y, self.z, (self.x + d) % 4)

    def join(self):
        for copy in self.copies:
            copy.wait()
        kept = self.kept
        terms = [self.own] + [self.buf.at[n] for n in range(3)]
        who = [self.uly] + [other[1] for other in uly_others()]
        for half in (0, 1):
            for term, uly in zip(terms, who):
                self.full[half, pl.ds(uly * kept, kept)] = term[half, :kept]
            if self.summed:
                self.full[half, 4 * kept :] = sum(
                    term[half, kept:].astype(F32) for term in terms
                ).astype(BF)
        own = self.full.at[self.core]
        self.send(own, self.item(self.y, self.x), 0, 1 - self.y, self.z, self.x)
        self.along_x(self.y, own, 0)
        self.local = pltpu.make_async_copy(own, self.item(self.y, self.x), self.local_sem)
        self.local.start()

    def onward(self):
        other = self.item(1 - self.y, self.x)
        wait_arrival(other, self.all_recv.at[0])
        self.along_x(1 - self.y, other, 3)

    def spread(self):
        self.local.wait()
        for k, y in enumerate((self.y, 1 - self.y)):
            for d in (1, 2, 3):
                wait_arrival(self.item(y, (self.x + 4 - d) % 4), self.all_recv.at[3 * k + d])
            for d in (1, 2, 3):
                self.send(
                    self.item(y), self.item(y), 6 + 3 * k + d, self.y, (self.z + d) % 4, self.x
                )

    def hand(self):
        for k, y in enumerate((self.y, 1 - self.y)):
            for d in (1, 2, 3):
                wait_arrival(
                    self.all_ref.at[self.core, y, (self.z + 4 - d) % 4], self.all_recv.at[6 + 3 * k + d]
                )
        self.pair(self.core).start()

    def pair(self, core):
        return remote(
            self.all_ref.at[core], self.all_ref.at[core], self.pair_send, self.pair_recv, uly_others()[1]
        )

    def end(self):
        for copy in self.flying:
            copy.wait_send()
        self.pair(self.core).wait_send()
        wait_arrival(self.all_ref.at[1 - self.core], self.pair_recv)

    def steps(self):
        return [
            self.reduce.first, self.reduce.second, self.reduce.third, self.across, self.join,
            self.onward, self.spread, self.hand, self.end,
        ]


def units(value):
    rows, columns = value.shape
    return [
        value[n * 16 : (n + 1) * 16, t * 128 : (t + 1) * 128]
        for n in range(rows // 16) for t in range(columns // 128)
    ]


FF_KEPT, FF_SUMMED, QKV_KEPT = 2, 2, 1
COL_TILES = PADDED // 128
D_TILES = D // 128
DKV_ROWS = CHUNK // 2
DKV_STREAMS = 2


def backward_kernel(
    norm_ff_ref, norm_in_ref, a_qkv_ref, bo_ref, total_hbm, down_hbm, cols_hbm, ff_hbm, resid_hbm, cot_hbm, ao_hbm, mixed_hbm, wo_hbm, kv_hbm, q_hbm, limit_hbm, lse_hbm,
    wq_hbm, rows_hbm, normed_hbm, b_qkv_hbm, cos_hbm, sin_hbm,
    result_ref, input_grad_ref, ff_all, qkv_all,
    total_ref, down_ref, cols_ref, ff_ref, resid_ref, cot_ref, ao_ref, mixed_ref, wo_ref, kv_ref, q_ref, limit_ref,
    lse_ref, wq_ref, rows_ref, normed_ref, b_qkv_ref, cos_ref, sin_ref, dkv_ref, acc_ref, part, dq_ref, grad_ref, grad_attn, grad_resid, grad_qkv,
    cross_out, cross_in, home_out, home_in, copy_sem, cross_sem, home_send, home_recv,
    *scratch,
):
    y, z, x, blk, uly = place()
    core, h = uly % 2, uly // 2
    scratch = list(scratch)

    def take(count):
        got = scratch[:count]
        del scratch[:count]
        return got

    chunk = 2 * blk + h
    upper = chunk // 32
    home = (1 - upper) * chunk + upper * (63 - chunk)
    home_from = [(home, upper * 2 + s) for s in (0, 1)]
    own_chunk = (1 - h) * blk + h * (63 - blk)
    home_to = [(own_chunk // 2, (own_chunk % 2) * 2 + half) for half in (0, 1)]
    copies = [
        pltpu.make_async_copy(src, dst, copy_sem.at[n])
        for n, (src, dst) in enumerate(
            (
                (total_hbm, total_ref), (resid_hbm, resid_ref), (cot_hbm, cot_ref), (cols_hbm, cols_ref),
                (ff_hbm, ff_ref), (down_hbm, down_ref), (ao_hbm, ao_ref), (mixed_hbm, mixed_ref),
                (wo_hbm, wo_ref), (kv_hbm, kv_ref),
                (q_hbm, q_ref), (limit_hbm, limit_ref), (lse_hbm, lse_ref), (wq_hbm, wq_ref),
                (rows_hbm, rows_ref), (normed_hbm, normed_ref), (b_qkv_hbm, b_qkv_ref),
                (cos_hbm, cos_ref), (sin_hbm, sin_ref),
            )
        )
    ]
    for copy in copies:
        copy.start()
    greet(
        reduce_others() + uly_others() + [(blk_of(1 - y, z, x), (uly + 2) % 4)] + home_from + home_to
    )
    collect_out = RingSum(
        lambda d: down_ref[(ring_at() + d) % 4].astype(F32), take(RingSum.scratches)
    )
    low, high = (
        [
            Shed(part, half, (n * DKV_ROWS, DKV_ROWS), n, take(Shed.scratches))
            for n in range(DKV_STREAMS)
        ]
        for half in (0, 1)
    )
    ff_total = Total(FF_KEPT, FF_SUMMED, ff_all, take(Total.scratches))
    qkv_total = Total(QKV_KEPT, 0, qkv_all, take(Total.scratches))
    deliver = Deliver()

    def send_home(n, value):
        home_out[n] = value.astype(BF)
        for half in (0, 1):
            deliver.send(
                home_out.at[n, pl.ds(half * 64, 64)], home_in.at[n, core],
                home_send.at[n, half], home_recv.at[n, core], home_to[half],
            )

    def arrived_home(n):
        for s in (0, 1):
            wait_arrival(home_in.at[n, s], home_recv.at[n, s])
        return home_in[n].astype(F32)

    def ready(first, last):
        for copy in copies[first:last]:
            copy.wait()

    ready(0, 3)
    residual = resid_ref[...]
    value = cot_ref[...].astype(F32) + norm_back(
        residual, norm_scale(residual), norm_ff_ref[...], total_ref[...]
    )
    grad_resid[...] = value
    own_rows = pl.ds(pl.multiple_of(h * CHUNK, CHUNK), CHUNK)
    other_rows = pl.ds(pl.multiple_of((1 - h) * CHUNK, CHUNK), CHUNK)
    grad_attn[own_rows, :] = value.astype(BF)
    partner = uly_others()[0]
    cross = remote(
        grad_attn.at[own_rows], grad_attn.at[own_rows], cross_sem.at[0], cross_sem.at[1], partner
    )
    cross.start()
    ready(3, 9)
    ff_total.pack_kept(units(cols_ref))
    ff_total.pack_summed(units(ff_ref))
    at_o = 6 * COL_TILES
    ff_total.clear(at_o + D_TILES // 2 + D_TILES, 6 * D_TILES)
    qkv_total.clear(3 * D_TILES + D_TILES // 2 + 2, 0)
    dkv_ref[...] = jnp.zeros_like(dkv_ref)
    acc_ref[...] = jnp.zeros_like(acc_ref)
    latent_o = dot_nt(ao_ref[...], mixed_ref[...]).astype(BF)
    cross.wait_send()
    wait_arrival(grad_attn.at[other_rows], cross_sem.at[1])
    back_o = dot_nt(grad_attn[...], bo_ref[...]).astype(BF)
    grad_ref[...] = (dot_nt(grad_attn[...], wo_ref[...]) + dot(back_o, ao_ref[...])).astype(BF)
    back_o = dot_nt(bo_ref[...], grad_attn[...]).astype(BF)
    ff_total.pack_kept(
        units(dot(back_o, mixed_ref[...])) + units(dot(latent_o, grad_attn[...])), at_o
    )

    ready(9, 13)
    steps = ff_total.steps()

    def beside(*more):
        for step in more:
            step()
        if steps:
            steps.pop(0)()

    def pack(half):
        def one(n, carry):
            chunk = n if half == 0 else 63 - n
            rows = dkv_ref[pl.ds(pl.multiple_of(chunk * CHUNK, CHUNK), CHUNK), :]
            both = jnp.concatenate([rows[:, :HEAD] * LN2, rows[:, HEAD:]], axis=1)
            part[half, n // 16, n // 4 % 4, n % 4] = both.astype(BF)
            return carry

        lax.fori_loop(0, 32, one, 0)

    def shed(streams, name):
        def run():
            for stream in streams:
                getattr(stream, name)()

        return run

    args = (q_ref, kv_ref, limit_ref, mixed_ref, grad_ref, lse_ref, dkv_ref, acc_ref)
    step = KEYS_BACK // CHUNK
    middle = 32 // step
    beside()
    backward_blocks(1, middle, (63 - blk) // step + 1, *args)
    pack(1)
    beside(shed(high, "first"))
    names = ["second", "third", "fourth"]
    extra = [collect_out.first, collect_out.second]
    for n in range(0, middle, 2):
        backward_blocks(1, n, n + 2, *args)
        more = [shed(high, names.pop(0))] if names else []
        more += [extra.pop(0)] if extra else []
        beside(*more)
    blocks = blk // step + 1
    backward_blocks(0, 0, blocks // 2, *args)
    beside()
    backward_blocks(0, blocks // 2, blocks, *args)
    pack(0)
    for stream in low:
        stream.first()
    beside()
    for slot in (0, 1):
        for n in range(GROUP):
            dq_ref[slot * CHUNK : (slot + 1) * CHUNK, n * HEAD : (n + 1) * HEAD] = (
                acc_ref[slot, :, n * CHUNK : (n + 1) * CHUNK].T * HEAD ** (-0.5)
            )
    ready(13, 19)
    for stream in low:
        stream.second()
    cos_table, sine_table = cos_ref[...], sin_ref[...]

    def turn_back(value, rows=slice(None)):
        return value * cos_table[rows] - pltpu.roll(value, HEAD // 2, 1) * sine_table[rows]

    for n in range(GROUP):
        at = slice(n * HEAD, (n + 1) * HEAD)
        grad_qkv[:, at] = turn_back(dq_ref[:, at]).astype(BF)
    group = GROUP * HEAD

    def key_value(half, streams):
        for n, stream in enumerate(streams):
            rows = slice(half * CHUNK + n * DKV_ROWS, half * CHUNK + (n + 1) * DKV_ROWS)
            value = stream.last()
            grad_qkv[rows, group : group + HEAD] = turn_back(value[:, :HEAD], rows).astype(BF)
            grad_qkv[rows, group + HEAD :] = value[:, HEAD:].astype(BF)

    key_value(1, high)
    for stream in low:
        stream.third()
    send_home(0, resid_ref[...] + collect_out.third())
    latent_qkv = dot_nt(a_qkv_ref[...], normed_ref[...]).astype(BF)
    for stream in low:
        stream.fourth()
    while steps:
        steps.pop(0)()
    key_value(0, low)

    def project_back(rows):
        grads = grad_qkv[rows, :]
        lifted = dot(dot_nt(grads, b_qkv_ref[...]).astype(BF), a_qkv_ref[...])
        return dot_nt(grads[:, :512], wq_ref[0]) + dot_nt(grads[:, 512:], wq_ref[1]) + lifted

    cross_out[...] = project_back(other_rows).astype(BF)
    cross = remote(cross_out, cross_in, cross_sem.at[2], cross_sem.at[3], partner)
    cross.start()
    back_qkv = dot_nt(b_qkv_ref[...], grad_qkv[...]).astype(BF)
    grad_b = dot(latent_qkv, grad_qkv[...])
    qkv_total.pack_kept(
        units(dot(back_qkv, normed_ref[...]))
        + units(grad_b[:16, :group])
        + units(grad_b[16:32, group : group + HEAD])
        + units(grad_b[32:, group + HEAD :])
    )
    steps = qkv_total.steps()
    steps.pop(0)()
    mine = project_back(own_rows)
    steps.pop(0)()
    cross.wait()
    mine = mine + cross_in[...].astype(F32)
    tokens = rows_ref[own_rows, :].astype(F32)
    send_home(1, grad_resid[...] + norm_back(tokens, norm_scale(tokens), norm_in_ref[...], mine))
    while steps:
        steps.pop(0)()
    result_ref[...] = arrived_home(0).astype(BF)
    input_grad_ref[...] = arrived_home(1)
    deliver.end()


def backward(*args):
    dma = pltpu.SemaphoreType.DMA
    group = GROUP * HEAD
    return pl.pallas_call(
        backward_kernel,
        out_shape=(
            jax.ShapeDtypeStruct((2, CHUNK // 2, D), BF),
            jax.ShapeDtypeStruct((2, CHUNK // 2, D), F32),
            Total.shape(FF_KEPT, FF_SUMMED),
            Total.shape(QKV_KEPT, 0),
        ),
        in_specs=[IN_VMEM] * 4 + [ANY] * 19,
        out_specs=(IN_VMEM, IN_VMEM, ANY, ANY),
        scratch_shapes=[
            pltpu.VMEM((CHUNK, D), F32),
            pltpu.VMEM((4, CHUNK, D), BF),
            pltpu.VMEM((96, PADDED), BF),
            pltpu.VMEM((96, D), BF),
            pltpu.VMEM((CHUNK, D), F32),
            pltpu.VMEM((CHUNK, D), BF),
            pltpu.VMEM((16, group), BF),
            pltpu.VMEM((2 * CHUNK, group), BF),
            pltpu.VMEM((D // 2, D), BF),
            pltpu.VMEM((CHUNKS, CHUNK, 2 * HEAD), BF),
            pltpu.VMEM((2 * CHUNK, group), BF),
            pltpu.VMEM((2, 8, ROWS), jnp.int32),
            pltpu.VMEM((2, 8, ROWS), F32),
            pltpu.VMEM((2, D, 512), BF),
            pltpu.VMEM((2 * CHUNK, D), BF),
            pltpu.VMEM((2 * CHUNK, D), BF),
            pltpu.VMEM((48, 1024), BF),
            pltpu.VMEM((2 * CHUNK, HEAD), F32),
            pltpu.VMEM((2 * CHUNK, HEAD), F32),
            pltpu.VMEM((CHUNKS * CHUNK, 2 * HEAD), F32),
            pltpu.VMEM((2, HEAD, ROWS), F32),
            pltpu.VMEM((2, 2, 4, 4, CHUNK, 2 * HEAD), BF),
            pltpu.VMEM((2 * CHUNK, group), F32),
            pltpu.VMEM((2 * CHUNK, group), BF),
            pltpu.VMEM((2 * CHUNK, D), BF),
            pltpu.VMEM((CHUNK, D), F32),
            pltpu.VMEM((2 * CHUNK, 1024), BF),
            pltpu.VMEM((CHUNK, D), BF),
            pltpu.VMEM((CHUNK, D), BF),
            pltpu.VMEM((2, CHUNK, D), BF),
            pltpu.VMEM((2, 2, CHUNK // 2, D), BF),
            dma((19,)), dma((4,)), dma((2, 2)), dma((2, 2)),
        ]
        + RingSum.scratch()
        + Shed.scratch((DKV_ROWS, 2 * HEAD)) * (2 * DKV_STREAMS)
        + Total.scratch(FF_KEPT, FF_SUMMED)
        + Total.scratch(QKV_KEPT, 0),
        compiler_params=pltpu.CompilerParams(
            collective_id=2, has_side_effects=True, vmem_limit_bytes=60 * 2**20
        ),
        name="backward",
    )(*args)


def fold_kernel(pick_ref, ff_ref, qkv_ref, a_wide, a_down, b_wide, b_kv, b_ff):
    c = pl.program_id(0)

    def kept(ref, per, n, u):
        item = n // per
        return ref[item // 32, item // 16 % 2, item // 4 % 4, item % 4, u * per + n % per].astype(F32)

    def ff_kept(n, u):
        return kept(ff_ref, FF_KEPT, n, u)

    def qkv_kept(n, u):
        return kept(qkv_ref, QKV_KEPT, n, u)

    def summed(n):
        item = n // FF_SUMMED
        return ff_ref[
            item // 32, item // 16 % 2, item // 4 % 4, item % 4, 4 * FF_KEPT + n % FF_SUMMED
        ].astype(F32)

    def put(ref, at, tile, value):
        ref[at + (slice(None), slice(tile * 128, (tile + 1) * 128))] = (
            pick_ref[c, 0] * value(0) + pick_ref[c, 1] * value(1)
        )

    for n in range(3):
        for t in range(D_TILES):
            put(a_wide, (n, 0), t, lambda s: qkv_kept(n * D_TILES + t, s) + qkv_kept(n * D_TILES + t, 2 + s))
    at_o = 6 * COL_TILES
    half = D_TILES // 2
    for t in range(D_TILES):
        h, part = t // half, t % half
        put(a_wide, (3, 0), t, lambda s: ff_kept(at_o + part, 2 * h + s))
        put(b_wide, (0, 0), t, lambda s: qkv_kept(3 * D_TILES + part, 2 * h + s))
        put(
            b_wide, (1, 0), t,
            lambda s: ff_kept(at_o + half + t, s) + ff_kept(at_o + half + t, 2 + s),
        )
        for n, (ref, at) in enumerate(((a_wide, (4, 0)), (a_wide, (5, 0)), (b_wide, (2, 0)))):
            put(ref, at, t, lambda s: summed((2 * n + s) * D_TILES + t))
    for n in (0, 1):
        for h in (0, 1):
            put(b_kv, (n, 0), h, lambda s: qkv_kept(3 * D_TILES + half + n, 2 * h + s))
    for n, (ref, at) in enumerate(((a_down, (0,)), (b_ff, (0, 0)), (b_ff, (1, 0)))):
        for t in range(FF // 128):
            where = [
                (u, t - start) for u, start in enumerate((0, 17, 35, 52)) if 0 <= t - start < COL_TILES
            ]
            put(
                ref, at, t,
                lambda s: sum(ff_kept((2 * n + s) * COL_TILES + tile, u) for u, tile in where),
            )


def fold(pick, ff_all, qkv_all):
    def whole(v):
        return pl.BlockSpec(v.shape, lambda c: (0,) * v.ndim)

    def by_set(lead, columns):
        shape = lead + (1, 16, columns)
        return pl.BlockSpec(shape, lambda c: (0,) * len(lead) + (c, 0, 0))

    def out(lead, columns):
        return jax.ShapeDtypeStruct(lead + (SETS, 16, columns), F32)

    outs = (((6,), D), ((), FF), ((3,), D), ((2,), 2 * HEAD), ((2,), FF))
    return pl.pallas_call(
        fold_kernel,
        grid=(SETS,),
        out_shape=tuple(out(*o) for o in outs),
        in_specs=[pl.BlockSpec(memory_space=pltpu.SMEM), whole(ff_all), whole(qkv_all)],
        out_specs=tuple(by_set(*o) for o in outs),
        compiler_params=pltpu.CompilerParams(vmem_limit_bytes=40 * 2**20),
        name="fold",
    )(pick, ff_all, qkv_all)


def norm_scale(hidden):
    return lax.rsqrt(jnp.mean(hidden * hidden, axis=-1, keepdims=True) + EPS)


def norm_back(hidden, scaled, gain_vec, upstream):
    normed = hidden * scaled
    weighted = upstream * gain_vec
    return scaled * (weighted - normed * jnp.mean(weighted * normed, axis=-1, keepdims=True))


def body(
    tokens, cotangent, lengths, set_index, norm_in, norm_ff, qkv_bias, w_qkv, w_out, w_gate_up, w_down,
    a_wide, a_down, b_wide, b_kv, b_ff,
):
    a_own, b_own, b_pair, a_ff, b_cols, a_cols, b_out = pick(set_index, a_wide, a_down, b_wide, b_kv, b_ff)
    frequencies = np.float64(THETA) ** (-np.arange(0, HEAD, 2, dtype=np.float64) / HEAD)
    frequencies = np.concatenate([frequencies, frequencies])[None].astype(np.float32)
    (
        q, mixed, lse, kv_all, qkv_w, out_w, gate_w, up_w, down_w, rows, normed, residual, grad_out,
        normed_ff, grad_gathered, limit, cos_table, sine_table, b_qkv, ao,
    ) = forward(
        tokens, cotangent, lengths, w_qkv, w_out, w_gate_up, w_down.T, norm_in[None], norm_ff[None],
        qkv_bias.reshape(16, HEAD), frequencies, a_own, b_own, b_pair,
    )
    gate_w, up_w, down_w = (w.reshape(D, FF_COLS) for w in (gate_w, up_w, down_w))
    grad_normed_ff, down_sum, cols, ff_wide = feed_forward(
        normed_ff, grad_gathered, gate_w, up_w, down_w, a_ff, b_cols, a_cols, b_out
    )
    result, input_grad, ff_all, qkv_all = backward(
        norm_ff[None], norm_in[None], a_own[:3].reshape(48, D), b_own[1],
        grad_normed_ff, down_sum, cols, ff_wide, residual, grad_out, ao, mixed, out_w, kv_all, q, limit, lse,
        qkv_w, rows, normed, b_qkv, cos_table, sine_table,
    )
    share = (jnp.arange(SETS, dtype=jnp.int32)[:, None] == set_index[None, :]).astype(F32)
    return (result, input_grad) + tuple(fold(share, ff_all, qkv_all))


def solution(mesh):
    spread = P(None, ("blk", "uly"), None)
    in_specs = (
        spread, spread, P(), P(), P(), P(), P(),
        P(("blk", "uly"), None), P(("blk", "uly"), None), P(None, "blk", "uly"), P("uly", "blk"),
        P(), P(), P(), P(), P(),
    )
    out_specs = (spread, spread, P(), P(), P(), P(), P())
    return jax.shard_map(body, mesh=mesh, in_specs=in_specs, out_specs=out_specs, check_vma=False)
```

```python
import functools

import jax
import jax.numpy as jnp
import numpy as np
from jax import lax
from jax.experimental import pallas as pl
from jax.experimental.pallas import tpu as pltpu
from jax.sharding import PartitionSpec as P

HEADS = 12
KV_HEADS = 2
HEAD = 128
GROUP = HEADS // KV_HEADS
FF = 8960
SETS = 8
D = 1536
CHUNK = 128
CHUNKS = 64
PADDED = 2304
EPS = 1e-06
THETA = 1000000.0
LOG2E = 1.4426950408889634
LN2 = 0.6931471805599453
MESH = pl.DeviceIdType.MESH
BF = jnp.bfloat16
F32 = jnp.float32
ANY = pl.BlockSpec(memory_space=pltpu.HBM)
IN_VMEM = pl.BlockSpec(memory_space=pltpu.VMEM)
HELD = pltpu.HBM


def blk_of(y, z, x):
    return y * 16 + z * 4 + x


def low_chunk(blk):
    return (1 - blk // 16) * 2 * blk + blk // 16 * (63 - 2 * blk)


def place():
    blk = lax.axis_index("blk")
    return blk // 16, (blk // 4) % 4, blk % 4, blk, lax.axis_index("uly")


def ring_others():
    y, z, x, blk, uly = place()
    return [
        (blk_of(1 - y, z, x), uly),
        (blk_of(y, z, (x + 1) % 4), uly),
        (blk_of(y, z, (x + 3) % 4), uly),
        (blk_of(y, (z + 1) % 4, x), uly),
        (blk_of(y, (z + 3) % 4, x), uly),
    ]


def greet(others, meanwhile=None):
    barrier = pltpu.get_barrier_semaphore()
    for other in others:
        pl.semaphore_signal(barrier, inc=1, device_id=other, device_id_type=MESH)
    if meanwhile is not None:
        meanwhile()
    pl.semaphore_wait(barrier, len(others))


class Gather:
    sends = 31

    def __init__(self, src, dst, send_sem, recv_sem, local_sem, orders=(0, 1)):
        self.src, self.dst, self.orders = src, dst, orders
        self.streams = range(len(orders))
        self.send_sem, self.recv_sem, self.local_sem = send_sem, recv_sem, local_sem
        self.y, self.z, self.x, self.blk, self.uly = place()
        self.count = [0] * len(orders)
        self.sent = []
        self.local = []

    def at(self, stream, y, p, q):
        order = self.orders[stream]
        return blk_of(y, order * p + (1 - order) * q, order * q + (1 - order) * p)

    def pq(self, stream):
        order = self.orders[stream]
        return (
            order * self.z + (1 - order) * self.x,
            order * self.x + (1 - order) * self.z,
        )

    def send(self, stream, item, target, src=None):
        copy = pltpu.make_async_remote_copy(
            src_ref=self.dst(stream, item) if src is None else src,
            dst_ref=self.dst(stream, item),
            send_sem=self.send_sem.at[stream, self.count[stream]],
            recv_sem=self.recv_sem.at[stream, item],
            device_id=(target, self.uly),
            device_id_type=MESH,
        )
        self.count[stream] += 1
        copy.start()
        self.sent.append(copy)

    def wait(self, stream, item):
        ref = self.dst(stream, item)
        pltpu.make_async_remote_copy(
            src_ref=ref,
            dst_ref=ref,
            send_sem=self.send_sem.at[stream, 0],
            recv_sem=self.recv_sem.at[stream, item],
            device_id=(self.blk, self.uly),
            device_id_type=MESH,
        ).wait_recv()

    def start(self):
        for s in self.streams:
            p, q = self.pq(s)
            self.send(s, self.blk, self.at(s, 1 - self.y, p, q), self.src(s))
        for s in self.streams:
            p, q = self.pq(s)
            for d in (1, 3):
                self.send(s, self.blk, self.at(s, self.y, (p + d) % 4, q), self.src(s))
            copy = pltpu.make_async_copy(self.src(s), self.dst(s, self.blk), self.local_sem.at[s])
            copy.start()
            self.local.append(copy)

    def second(self):
        for s in self.streams:
            p, q = self.pq(s)
            item = self.at(s, 1 - self.y, p, q)
            self.wait(s, item)
            for d in (1, 3):
                self.send(s, item, self.at(s, self.y, (p + d) % 4, q))
            for d in (1, 3):
                onward = self.at(s, self.y, p, (q + d) % 4)
                self.send(s, self.blk, onward, self.src(s))
                self.send(s, item, onward)

    def spread(self, s, item):
        p, q = self.pq(s)
        for d in (1, 3):
            self.send(s, item, self.at(s, self.y, p, (q + d) % 4))

    def third(self):
        for k, y in enumerate((self.y, 1 - self.y)):
            for s in self.streams:
                p, q = self.pq(s)
                for d in (3, 1):
                    item = self.at(s, y, (p + d) % 4, q)
                    self.wait(s, item)
                    if (d == 3) == (k == 0):
                        self.send(s, item, self.at(s, self.y, (p + 4 - d) % 4, q))
                    self.spread(s, item)
        for y in (self.y, 1 - self.y):
            for s in self.streams:
                p, q = self.pq(s)
                item = self.at(s, y, (p + 2) % 4, q)
                self.wait(s, item)
                self.spread(s, item)

    def fourth(self):
        for e in (0, 1, 3, 2):
            for k, y in enumerate((self.y, 1 - self.y)):
                for s in self.streams:
                    p, q = self.pq(s)
                    for d in (3, 1):
                        item = self.at(s, y, (p + e) % 4, (q + d) % 4)
                        self.wait(s, item)
                        if (d == 3) == (k == 0):
                            self.send(s, item, self.at(s, self.y, p, (q + 4 - d) % 4))

    def last(self):
        for e in (0, 1, 3, 2):
            for y in (self.y, 1 - self.y):
                for s in self.streams:
                    p, q = self.pq(s)
                    self.wait(s, self.at(s, y, (p + e) % 4, (q + 2) % 4))
        for copy in self.local:
            copy.wait()
        for copy in self.sent:
            copy.wait_send()


GATHER_SEMS = lambda *lead: [
    pltpu.SemaphoreType.DMA(lead + (2, Gather.sends)),
    pltpu.SemaphoreType.DMA(lead + (2, 32)),
    pltpu.SemaphoreType.DMA(lead + (2,)),
]


KEYS = 1024
KEYS_BACK = 512
ROWS = GROUP * CHUNK


def head_columns(ref, slot):
    return jnp.concatenate(
        [
            ref[slot * CHUNK : (slot + 1) * CHUNK, n * HEAD : (n + 1) * HEAD].T
            for n in range(GROUP)
        ],
        axis=1,
    )


def head_rows(ref, slot):
    return jnp.concatenate(
        [
            ref[slot * CHUNK : (slot + 1) * CHUNK, n * HEAD : (n + 1) * HEAD]
            for n in range(GROUP)
        ],
        axis=0,
    )


def key_block(kv_ref, step, keys):
    count = keys // CHUNK
    rows = kv_ref[pl.ds(step * count, count)].reshape(keys, 2 * HEAD)
    return rows[:, :HEAD], rows[:, HEAD:]


def dot(a, b):
    return jnp.dot(a, b, preferred_element_type=F32)


def key_places(step, keys):
    return lax.broadcasted_iota(jnp.int32, (keys, ROWS), 0) + step * keys


def dot_nt(a, b):
    return lax.dot_general(a, b, (((1,), (1,)), ((), ())), preferred_element_type=F32)


def forward_blocks(slot, first, last, turned_ref, kv_ref, limit_ref, acc_ref, stat_ref):
    turned = turned_ref[slot]
    limit = limit_ref[slot, 0:1, :]

    def step(n, carry):
        top, total = carry
        keys, values = key_block(kv_ref, n, KEYS)
        scores = jnp.where(key_places(n, KEYS) <= limit, dot(keys, turned), -1e30)
        new_top = jnp.maximum(top, jnp.max(scores, axis=0, keepdims=True))
        fade = jnp.exp2(top - new_top)
        probs = jnp.exp2(scores - new_top)
        total = total * fade + jnp.sum(probs, axis=0, keepdims=True)
        acc_ref[slot] = acc_ref[slot] * fade + dot(values.T, probs.astype(BF))
        return new_top, total

    top, total = lax.fori_loop(
        first, last, step, (stat_ref[slot, 0, 0:1, :], stat_ref[slot, 1, 0:1, :])
    )
    stat_ref[slot, 0, 0:1, :] = top
    stat_ref[slot, 1, 0:1, :] = total


def forward_end(slot, mixed_ref, lse_ref, acc_ref, stat_ref):
    top, total = stat_ref[slot, 0, 0:1, :], stat_ref[slot, 1, 0:1, :]
    out = acc_ref[slot] / total
    for n in range(GROUP):
        mixed_ref[slot * CHUNK : (slot + 1) * CHUNK, n * HEAD : (n + 1) * HEAD] = out[
            :, n * CHUNK : (n + 1) * CHUNK
        ].T.astype(BF)
    lse_ref[slot] = jnp.broadcast_to(top + jnp.log2(total), (8, ROWS))


def uly_others():
    y, z, x, blk, uly = place()
    return [(blk, (uly + 2) % 4), (blk, uly + 1 - 2 * (uly % 2)), (blk, 3 - uly)]


def ring_place(w):
    y, z, x, blk, uly = place()
    return (blk_of(w % 2, z, x), (w // 2) * 2 + uly % 2)


def ring_at():
    y, z, x, blk, uly = place()
    return (uly // 2) * 2 + y


def wait_arrival(ref, sem):
    pltpu.make_async_copy(ref, ref, sem).wait()


def remote(src, dst, send, recv, device):
    return pltpu.make_async_remote_copy(
        src_ref=src, dst_ref=dst, send_sem=send, recv_sem=recv, device_id=device, device_id_type=MESH
    )


class Deliver:
    def __init__(self):
        self.sent = []

    def send(self, src, dst, send, recv, device):
        y, z, x, blk, uly = place()
        here = jnp.logical_and(device[0] == blk, device[1] == uly)

        @pl.when(here)
        def _():
            pltpu.make_async_copy(src, dst, recv).start()

        @pl.when(jnp.logical_not(here))
        def _():
            remote(src, dst, send, recv, device).start()

        self.sent.append((here, src, dst, send, recv, device))

    def end(self):
        for here, *copy in self.sent:

            @pl.when(jnp.logical_not(here))
            def _():
                remote(*copy).wait_send()


class Ring:
    sends = 15

    def __init__(self, src, dst, y, order, way, send_sem, recv_sem):
        self.src, self.dst, self.y, self.order, self.way = src, dst, y, order, way
        self.send_sem, self.recv_sem = send_sem, recv_sem
        self.own_y, self.z, self.x, self.blk, self.uly = place()
        self.p = order * self.z + (1 - order) * self.x
        self.q = order * self.x + (1 - order) * self.z
        self.sent = []

    def at(self, y, p, q):
        order = self.order
        return blk_of(y, order * p + (1 - order) * q, order * q + (1 - order) * p)

    def index(self, p, q):
        return self.at(0, p, q)

    def send(self, p, q, dp, dq, src=None):
        ref = self.dst(self.at(self.y, p, q))
        target = self.at(self.own_y, (self.p + dp) % 4, (self.q + dq) % 4)
        copy = remote(
            ref if src is None else src, ref, self.send_sem.at[len(self.sent)],
            self.recv_sem.at[self.index(p, q)], (target, self.uly),
        )
        copy.start()
        self.sent.append(copy)

    def wait(self, p, q):
        wait_arrival(self.dst(self.at(self.y, p, q)), self.recv_sem.at[self.index(p, q)])

    def start(self):
        for d in (1, 3):
            self.send(self.p, self.q, d, 0, self.src)

    def second(self):
        for d in (4 - self.way, self.way):
            p = (self.p + d) % 4
            self.wait(p, self.q)
            if d == 4 - self.way:
                self.send(p, self.q, self.way, 0)

    def third(self):
        self.wait((self.p + 2) % 4, self.q)

    def spread(self, e):
        p = (self.p + e) % 4
        for d in (1, 3):
            self.send(p, self.q, 0, d, self.src if e == 0 else None)

    def fourth(self, e):
        p = (self.p + e) % 4
        for d in (4 - self.way, self.way):
            q = (self.q + d) % 4
            self.wait(p, q)
            if d == 4 - self.way:
                self.send(p, q, 0, self.way)

    def last(self):
        for e in (0, 1, 3, 2):
            self.wait((self.p + e) % 4, (self.q + 2) % 4)
        for copy in self.sent:
            copy.wait_send()


class Spread:
    def __init__(self, own, all_ref, send_sem, recv_sem, local_sem):
        self.own, self.all_ref = own, all_ref
        self.send_sem, self.recv_sem, self.local_sem = send_sem, recv_sem, local_sem
        self.w = ring_at()
        self.core = lax.axis_index("uly") % 2
        self.sibling = uly_others()[1]
        self.sent = []

    def piece(self, d, rows=slice(None), core=None):
        core = self.core if core is None else core
        ref = self.all_ref.at[core, (self.w + d) % 4]
        return ref if rows == slice(None) else ref.at[pl.ds(rows.start, rows.stop - rows.start)]

    def send(self, src, dst, recv, device):
        copy = remote(src, dst, self.send_sem.at[len(self.sent)], self.recv_sem.at[recv], device)
        copy.start()
        self.sent.append(copy)

    def pair(self, d, src=None):
        self.send(self.piece(d) if src is None else src, self.piece(d), 4 + d, self.sibling)

    def start(self):
        self.local = pltpu.make_async_copy(self.own, self.piece(0), self.local_sem)
        self.local.start()
        self.send(self.own, self.piece(0), 0, ring_place((self.w + 1) % 4))
        self.send(self.own, self.piece(0), 1, ring_place((self.w + 3) % 4))
        self.pair(0, self.own)

    def second(self):
        half = CHUNK // 2
        wait_arrival(self.piece(3), self.recv_sem.at[0])
        low = self.piece(3, slice(0, half))
        self.send(low, low, 2, ring_place((self.w + 1) % 4))
        self.pair(3)
        wait_arrival(self.piece(1), self.recv_sem.at[1])
        high = self.piece(1, slice(half, CHUNK))
        self.send(high, high, 3, ring_place((self.w + 3) % 4))
        self.pair(1)

    def third(self):
        half = CHUNK // 2
        wait_arrival(self.piece(2, slice(0, half)), self.recv_sem.at[2])
        wait_arrival(self.piece(2, slice(half, CHUNK)), self.recv_sem.at[3])
        self.pair(2)

    def last(self):
        for d in range(4):
            wait_arrival(self.piece(d, core=1 - self.core), self.recv_sem.at[4 + d])
        for copy in self.sent:
            copy.wait_send()
        self.local.wait()


SPREAD_SEMS = [pltpu.SemaphoreType.DMA((8,)), pltpu.SemaphoreType.DMA((8,)), pltpu.SemaphoreType.DMA]
FF_COLS = PADDED // 2


def forward_kernel(
    tokens_ref, cot_ref, length_ref, qkv_ref, out_ref, gate_up_ref, down_ref, norm_in_ref, norm_ff_ref,
    bias_ref, freq_ref, a_hbm, b_hbm, bkv_hbm,
    q_out, mixed_out, lse_out, kv_out, wq_out, wo_out, gate_all, up_all, down_all, rows_hbm, normed_out,
    resid_out, cot_out, nf_out, cot_all, limit_out, cos_out, sin_out, b_qkv_out, ao_out,
    q_ref, mixed_ref, lse_ref, rows_out, normed_ref, resid_ref, cot_own, limit_ref, cos_ref, sin_ref,
    b_qkv_ref, ao_ref, a_ref, b_ref, bkv_ref, turned_ref, kv_all, wq_all, wo_all, rows, cot_in, kv_part, acc_ref, stat_ref, qkv_in, out_in, qkv_part, out_part,
    nf_own, cross_out, cross_in, qkv_pieces, out_pieces, ff_ref,
    *sems,
):
    y, z, x, blk, uly = place()
    core, h = uly % 2, uly // 2
    sems = list(sems)

    def take(count):
        got = sems[:count]
        del sems[:count]
        return got

    chunk = 2 * blk + h
    upper = chunk // 32
    home = (1 - h) * blk + h * (31 - blk)
    row_to = [[(home, hh * 2 + s) for hh in (0, 1)] for s in (0, 1)]
    row_from = [(b, hh * 2 + half) for b, hh in ((blk, 0), (31 - blk, 1)) for half in (0, 1)]
    lower = low_chunk(blk)
    out_to = [(2 * (blk % 16) + q // 2, (blk // 16) * 2 + q % 2) for q in range(4)]
    out_from = [(16 * h + blk // 2, u) for u in range(4)]
    sibling = uly_others()[1]
    length = length_ref[0] * (1 - core) + length_ref[1] * core
    set_sem = sems.pop()
    set_copies = [
        pltpu.make_async_copy(src, dst, set_sem.at[n])
        for n, (src, dst) in enumerate(((a_hbm, a_ref), (b_hbm, b_ref), (bkv_hbm, bkv_ref)))
    ]
    for copy in set_copies:
        copy.start()

    def prepare():
        qkv_pieces[...] = jnp.zeros_like(qkv_pieces)
        out_pieces[...] = jnp.zeros_like(out_pieces)
        group = GROUP * HEAD
        for hh in (0, 1):
            qkv_pieces[2 * hh, :12] = qkv_ref[:, hh * group : hh * group + 512]
            for place_at, start, size in (
                (0, hh * group + 512, 256),
                (256, HEADS * HEAD + hh * HEAD, HEAD),
                (384, HEADS * HEAD + 256 + hh * HEAD, HEAD),
            ):
                qkv_pieces[2 * hh + 1, :12, place_at : place_at + size] = qkv_ref[:, start : start + size]
        for q in range(4):
            out_pieces[q, :12] = out_ref[:, q * 384 : (q + 1) * 384]
        for n in range(3):
            part = (gate_up_ref[n] if n < 2 else down_ref[...]).astype(F32)
            none = jnp.zeros((48, 64), F32)
            left = jnp.concatenate([part, none], axis=1)
            right = jnp.concatenate([none, part], axis=1)
            ff_ref[n] = jnp.where(jnp.broadcast_to(core, (48, PADDED)) == 1, right, left).astype(BF)

    greet(
        ring_others() + uly_others() + [(blk_of(1 - y, z, x), (uly + 2) % 4)]
        + row_to[0] + row_to[1] + row_from + out_to + out_from,
        prepare,
    )

    deliver = Deliver()
    piece_send, piece_recv, row_send, row_recv = take(4)
    for q in range(4):
        deliver.send(qkv_pieces.at[q], qkv_in.at[uly], piece_send.at[q], piece_recv.at[uly], (blk, q))
    for q in range(4):
        deliver.send(out_pieces.at[q], out_in.at[uly], piece_send.at[4 + q], piece_recv.at[4 + uly], out_to[q])
    for s in (0, 1):
        for hh in (0, 1):
            deliver.send(
                tokens_ref.at[s], rows.at[upper, core], row_send.at[s * 2 + hh],
                row_recv.at[upper * 2 + core], row_to[s][hh],
            )

    wide = PADDED // 2
    gathered = (gate_all, up_all, down_all)
    ff_send, ff_recv, y_send, y_recv, y_local = take(5)
    other_blk = blk_of(1 - y, z, x)

    def ff_part(n, half):
        return ff_ref.at[n, :, pl.ds(pl.multiple_of(half * wide, 128), wide)]

    picked = lax.broadcasted_iota(jnp.int32, (48, 64), 1)
    picked = jnp.where(picked % 16 < 12, picked // 16 * 12 + picked % 16, -1)
    picked = jnp.where(picked == lax.broadcasted_iota(jnp.int32, (48, 64), 0), 1.0, 0.0).astype(BF)
    for u in range(4):
        wait_arrival(qkv_in.at[u], piece_recv.at[u])
    qkv_part[...] = dot(picked, qkv_in[...].reshape(64, 512)).astype(BF)
    wq = Gather(
        lambda s: qkv_part.at[:, pl.ds(256 * s, 256)],
        lambda s, item: wq_all.at[
            core, pl.ds(pl.multiple_of(item * 48, 16), 48), pl.ds(256 * s, 256)
        ],
        *take(3),
    )
    wq.start()
    for u in range(4):
        wait_arrival(out_in.at[u], piece_recv.at[4 + u])
    out_part[...] = dot(picked, out_in[...].reshape(64, 384)).astype(BF)
    y_copies = []
    for n, ref in enumerate(gathered):
        copy = remote(ff_part(n, 1 - y), ref.at[blk], y_send.at[n], y_recv.at[n], (other_blk, uly))
        copy.start()
        y_copies.append(copy)
        copy = pltpu.make_async_copy(ff_part(n, y), ref.at[blk], y_local.at[n])
        copy.start()
        y_copies.append(copy)
    for s in (0, 1):
        deliver.send(
            cot_ref.at[s], cot_in.at[core], row_send.at[4 + s], row_recv.at[4 + core], (home, upper * 2 + s)
        )

    def out_columns(item, s):
        start = ((item % 2) * 2 + core) * 384
        return pl.ds(pl.multiple_of(start + 128 * s, 128), 128 + 128 * s)

    wo = Gather(
        lambda s: out_part.at[:, pl.ds(128 * s, 128 + 128 * s)],
        lambda s, item: wo_all.at[pl.ds(pl.multiple_of((item // 2) * 48, 16), 48), out_columns(item, s)],
        *take(3),
    )
    own_ff, other_ff = (
        [
            Ring(
                ff_part(n, y) if k == 0 else ref.at[other_blk],
                lambda item, ref=ref: ref.at[item],
                y if k == 0 else 1 - y,
                y if k == 0 else 1 - y,
                (1, 3, 1 + 2 * k)[n],
                ff_send.at[k, n], ff_recv.at[k, n],
            )
            for n, ref in enumerate(gathered)
        ]
        for k in (0, 1)
    )
    rings = own_ff + other_ff
    def tables(slot):
        at = lower if slot == 0 else 63 - lower
        row = lax.broadcasted_iota(jnp.int32, (CHUNK, HEAD), 0) + at * CHUNK
        angle = row.astype(F32) * freq_ref[...]
        first = lax.broadcasted_iota(jnp.int32, (CHUNK, HEAD), 1) < HEAD // 2
        sine = jnp.sin(angle)
        cos_ref[slot * CHUNK : (slot + 1) * CHUNK, :] = jnp.cos(angle)
        sin_ref[slot * CHUNK : (slot + 1) * CHUNK, :] = jnp.where(first, -sine, sine)
        row = lax.broadcasted_iota(jnp.int32, (8, ROWS), 1) % CHUNK + at * CHUNK
        limit_ref[slot] = jnp.minimum(row, length - 1)

    stat_ref[:, 0] = jnp.full((2, 8, ROWS), -1e30, F32)
    stat_ref[:, 1] = jnp.zeros((2, 8, ROWS), F32)
    acc_ref[...] = jnp.zeros_like(acc_ref)
    for copy in set_copies:
        copy.wait()
    group = GROUP * HEAD
    group_at = pl.ds(pl.multiple_of(h * group, 128), group)
    head_at = pl.ds(pl.multiple_of(h * HEAD, 128), HEAD)
    ao_ref[...] = a_ref[3, :, group_at]
    b_qkv_ref[...] = jnp.zeros_like(b_qkv_ref)
    b_qkv_ref[:16, :group] = b_ref[0, :, group_at]
    b_qkv_ref[16:32, group : group + HEAD] = bkv_ref[0, :, head_at]
    b_qkv_ref[32:, group + HEAD :] = bkv_ref[1, :, head_at]
    a_qkv = a_ref[:3].reshape(48, D)
    bo_ref = b_ref.at[1]

    def bias(n):
        at = h * GROUP + n if n < GROUP else HEADS + 2 * (n - GROUP) + h
        return bias_ref[pl.ds(at, 1), :]

    wq.second()
    tables(0)
    wq.third()
    tables(1)
    wq.fourth()
    for ring in own_ff:
        ring.start()
    for n in range(3):
        y_copies[2 * n].wait_recv()
    for ring in other_ff:
        ring.start()
    for ring in rings:
        ring.spread(0)

    for n in range(4):
        wait_arrival(rows.at[n // 2, n % 2], row_recv.at[n])
        value = rows[n // 2, n % 2].astype(F32)
        at = slice(n * 64, (n + 1) * 64)
        rows_out[at, :] = rows[n // 2, n % 2]
        normed_ref[at, :] = (value * norm_scale(value) * norm_in_ref[...]).astype(BF)
    latent = dot_nt(normed_ref[...], a_qkv)
    adapted = dot(latent.astype(BF), b_qkv_ref[...])
    wq.last()
    pair_send, pair_recv = take(2)

    def pair_copy(ref, n):
        return remote(ref, ref, pair_send.at[n], pair_recv.at[n], sibling)

    pair_copy(wq_all.at[core], 0).start()
    wo.start()
    pair_copy(wq_all.at[core], 0).wait_send()
    pair_copy(wq_all.at[1 - core], 0).wait_recv()

    cos_table, sine_table = cos_ref[...], sin_ref[...]

    def turn(head):
        return head * cos_table + pltpu.roll(head, HEAD // 2, 1) * sine_table

    def query(n, head):
        q_ref[:, n * HEAD : (n + 1) * HEAD] = (turn(head + bias(n)) * (HEAD ** (-0.5) * LOG2E)).astype(BF)

    pairs = dot(normed_ref[...], wq_all[1, :, 256:]) + adapted[:, 768:]
    for n, head in ((0, turn(pairs[:, :HEAD] + bias(6))), (1, pairs[:, HEAD:] + bias(7))):
        at = slice(n * HEAD, (n + 1) * HEAD)
        kv_part[0, :, at] = head[:CHUNK].astype(BF)
        kv_part[1, :, at] = head[CHUNK:].astype(BF)
    kv = Gather(
        lambda s: kv_part.at[s],
        lambda s, item: kv_all.at[low_chunk(item) if s == 0 else 63 - low_chunk(item)],
        *take(3),
    )
    kv.start()
    heads = dot(normed_ref[...], wq_all[1, :, :256]) + adapted[:, 512:768]
    for n in (4, 5):
        query(n, heads[:, (n - 4) * HEAD : (n - 3) * HEAD])
    kv.second()
    for ring in rings:
        ring.second()
    wo.second()
    heads = dot(normed_ref[...], wq_all[0]) + adapted[:, :512]
    for n in range(4):
        query(n, heads[:, n * HEAD : (n + 1) * HEAD])
    kv.third()
    for ring in rings:
        ring.third()
    wo.third()
    kv.fourth()
    wo.fourth()

    for half in (0, 1):
        wait_arrival(cot_in.at[half], row_recv.at[4 + half])
        start = ((1 - h) * lower + h * (63 - lower)) * CHUNK + half * 64
        at = lax.broadcasted_iota(jnp.int32, (64, D), 0) + start
        cot_own[half * 64 : (half + 1) * 64, :] = jnp.where(
            at < length, cot_in[half].astype(F32), 0.0
        ).astype(BF)
    cot_spread = Spread(cot_own, cot_all, *take(3))
    cot_spread.start()
    kv.last()
    for e in (1, 3, 2):
        for ring in rings:
            ring.spread(e)
    (out_sem,) = take(1)
    copies = []

    def keep(*pairs):
        for src, dst in pairs:
            copies.append(pltpu.make_async_copy(src, dst, out_sem.at[len(copies)]))
            copies[-1].start()

    keep(
        (kv_all, kv_out), (wq_all, wq_out), (q_ref, q_out), (rows_out, rows_hbm), (normed_ref, normed_out),
        (cot_own, cot_out), (limit_ref, limit_out), (cos_ref, cos_out), (sin_ref, sin_out),
        (b_qkv_ref, b_qkv_out), (ao_ref, ao_out),
    )
    wo.last()

    def wo_columns(c, n):
        return wo_all.at[:, pl.ds(pl.multiple_of((2 * n + c) * 384, 128), 384)]

    for n in (0, 1):
        pair_copy(wo_columns(core, n), 1 + n).start()
    for slot in (0, 1):
        turned_ref[slot] = head_columns(q_ref, slot)
    args = (turned_ref, kv_all, limit_ref, acc_ref, stat_ref)

    def end(slot):
        forward_end(slot, mixed_ref, lse_ref, acc_ref, stat_ref)

    blocks = KEYS // CHUNK
    middle = CHUNKS // 2 // blocks
    forward_blocks(0, 0, lower // blocks + 1, *args)
    forward_blocks(1, middle, (63 - lower) // blocks + 1, *args)
    end(0)
    for ring in rings:
        ring.fourth(0)
    cot_spread.second()
    forward_blocks(1, 0, middle // 2, *args)
    for ring in rings:
        ring.fourth(1)
    cot_spread.third()
    forward_blocks(1, middle // 2, middle, *args)
    end(1)
    for n in (0, 1):
        pair_copy(wo_columns(core, n), 1 + n).wait_send()
        pair_copy(wo_columns(1 - core, n), 1 + n).wait_recv()
    keep((wo_all, wo_out), (mixed_ref, mixed_out), (lse_ref, lse_out))

    def project(slot):
        mixed = mixed_ref[pl.ds(pl.multiple_of(slot * CHUNK, CHUNK), CHUNK), :]
        lifted = dot(dot_nt(mixed, ao_ref[...]).astype(BF), bo_ref[...])
        return dot(mixed, wo_all[...]) + lifted

    (cross_sem,) = take(1)
    cross_out[...] = project(1 - h).astype(BF)
    cross = remote(cross_out, cross_in, cross_sem.at[0], cross_sem.at[1], uly_others()[0])
    cross.start()
    for ring in rings:
        ring.fourth(3)
    mine = project(h) + rows_out[pl.ds(pl.multiple_of(h * CHUNK, CHUNK), CHUNK), :].astype(F32)
    for ring in rings:
        ring.fourth(2)
    cross.wait()
    residual = mine + cross_in[...].astype(F32)
    resid_ref[...] = residual
    keep((resid_ref, resid_out))
    nf_own[...] = (residual * norm_scale(residual) * norm_ff_ref[...]).astype(BF)
    keep((nf_own, nf_out))
    cot_spread.last()
    for ring in rings:
        ring.last()
    for n in range(3):
        y_copies[2 * n].wait_send()
        y_copies[2 * n + 1].wait()
    deliver.end()
    for copy in copies:
        copy.wait()


def forward(*args):
    weight = HELD((32, 48, FF_COLS), BF)
    group = GROUP * HEAD
    dma = pltpu.SemaphoreType.DMA
    spread = HELD((2, 4, CHUNK, D), BF)
    return pl.pallas_call(
        forward_kernel,
        out_shape=(
            HELD((2 * CHUNK, group), BF),
            HELD((2 * CHUNK, group), BF),
            HELD((2, 8, ROWS), F32),
            HELD((CHUNKS, CHUNK, 2 * HEAD), BF),
            HELD((2, D, 512), BF),
            HELD((D // 2, D), BF),
            weight, weight, weight,
            HELD((2 * CHUNK, D), BF),
            HELD((2 * CHUNK, D), BF),
            HELD((CHUNK, D), F32),
            HELD((CHUNK, D), BF),
            HELD((CHUNK, D), BF),
            spread,
            HELD((2, 8, ROWS), jnp.int32),
            HELD((2 * CHUNK, HEAD), F32),
            HELD((2 * CHUNK, HEAD), F32),
            HELD((48, 1024), BF),
            HELD((16, group), BF),
        ),
        in_specs=[ANY] * 2 + [pl.BlockSpec(memory_space=pltpu.SMEM)] + [IN_VMEM] * 8 + [ANY] * 3,
        out_specs=(ANY,) * 20,
        scratch_shapes=[
            pltpu.VMEM((2 * CHUNK, group), BF),
            pltpu.VMEM((2 * CHUNK, group), BF),
            pltpu.VMEM((2, 8, ROWS), F32),
            pltpu.VMEM((2 * CHUNK, D), BF),
            pltpu.VMEM((2 * CHUNK, D), BF),
            pltpu.VMEM((CHUNK, D), F32),
            pltpu.VMEM((CHUNK, D), BF),
            pltpu.VMEM((2, 8, ROWS), jnp.int32),
            pltpu.VMEM((2 * CHUNK, HEAD), F32),
            pltpu.VMEM((2 * CHUNK, HEAD), F32),
            pltpu.VMEM((48, 1024), BF),
            pltpu.VMEM((16, group), BF),
            pltpu.VMEM((4, 16, D), BF),
            pltpu.VMEM((2, 16, D), BF),
            pltpu.VMEM((2, 16, 2 * HEAD), BF),
            pltpu.VMEM((2, HEAD, ROWS), BF),
            pltpu.VMEM((CHUNKS, CHUNK, 2 * HEAD), BF),
            pltpu.VMEM((2, D, 512), BF),
            pltpu.VMEM((D // 2, D), BF),
            pltpu.VMEM((2, 2, 64, D), BF),
            pltpu.VMEM((2, 64, D), BF),
            pltpu.VMEM((2, CHUNK, 2 * HEAD), BF),
            pltpu.VMEM((2, HEAD, ROWS), F32),
            pltpu.VMEM((2, 2, 8, ROWS), F32),
            pltpu.VMEM((4, 16, 512), BF),
            pltpu.VMEM((4, 16, 384), BF),
            pltpu.VMEM((48, 512), BF),
            pltpu.VMEM((48, 384), BF),
            pltpu.VMEM((CHUNK, D), BF),
            pltpu.VMEM((CHUNK, D), BF),
            pltpu.VMEM((CHUNK, D), BF),
            pltpu.VMEM((4, 16, 512), BF),
            pltpu.VMEM((4, 16, 384), BF),
            pltpu.VMEM((3, 48, PADDED), BF),
            dma((8,)), dma((8,)), dma((6,)), dma((6,)),
            dma((2, 3, Ring.sends)), dma((2, 3, 16)), dma((3,)), dma((3,)), dma((3,)),
        ]
        + GATHER_SEMS()
        + GATHER_SEMS()
        + [dma((3,)), dma((3,))]
        + GATHER_SEMS()
        + SPREAD_SEMS
        + [dma((16,)), dma((2,)), dma((3,))],
        compiler_params=pltpu.CompilerParams(
            collective_id=1, has_side_effects=True, vmem_limit_bytes=48 * 2**20
        ),
        name="forward",
    )(*args)


class RingSum:
    @staticmethod
    def scratch():
        piece, half = (CHUNK, D), (CHUNK // 2, D)
        return [
            pltpu.VMEM((2,) + half, BF),
            pltpu.VMEM((2,) + piece, BF),
            pltpu.VMEM(piece, BF),
            pltpu.VMEM((2,) + piece, BF),
            pltpu.SemaphoreType.DMA((4,)),
            pltpu.SemaphoreType.DMA((4,)),
        ]

    scratches = 6

    def __init__(self, term, scratch):
        self.term = term
        self.halves, self.last_in, self.far, self.near, self.send_sem, self.recv_sem = scratch
        self.w = ring_at()
        self.sent = []

    def send(self, src, dst, recv, d):
        copy = remote(
            src, dst, self.send_sem.at[recv], self.recv_sem.at[recv], ring_place((self.w + d) % 4)
        )
        copy.start()
        self.sent.append(copy)

    def first(self):
        half = CHUNK // 2
        self.far[...] = self.term(2).astype(BF)
        self.send(self.far.at[pl.ds(0, half)], self.halves.at[0], 0, 1)
        self.send(self.far.at[pl.ds(half, half)], self.halves.at[1], 1, 3)

    def second(self):
        half = CHUNK // 2
        for k, d in ((0, 1), (1, 3)):
            total = self.term(d)
            wait_arrival(self.halves.at[k], self.recv_sem.at[k])
            rows = slice(k * half, (k + 1) * half)
            other = slice((1 - k) * half, (2 - k) * half)
            self.near[k, rows] = (total[rows] + self.halves[k].astype(F32)).astype(BF)
            self.near[k, other] = total[other].astype(BF)
            self.send(self.near.at[k], self.last_in.at[k], 2 + k, d)

    def third(self):
        total = self.term(0)
        for k in (0, 1):
            wait_arrival(self.last_in.at[k], self.recv_sem.at[2 + k])
            total += self.last_in[k].astype(F32)
        for copy in self.sent:
            copy.wait_send()
        return total


def pick_kernel(
    set_ref, a_wide, a_down, b_wide, b_kv, b_ff, a_own, b_own, b_pair, a_ff, b_cols, a_cols, b_out, sems
):
    y, z, x, blk, uly = place()
    own = set_ref[uly % 2]
    first = (35 * uly) // 2 * 128 + y * FF_COLS
    columns = pl.ds(pl.multiple_of(first, 128), FF_COLS)
    pairs = [(a_wide.at[n, own], a_own.at[n]) for n in range(4)]
    pairs += [(b_wide.at[n, own], b_own.at[n]) for n in (0, 1)]
    pairs += [(b_kv.at[n, own], b_pair.at[n]) for n in (0, 1)]
    for s in (0, 1):
        chosen = set_ref[s]
        for n in (0, 1):
            pairs.append((a_wide.at[4 + n, chosen], a_ff.at[s, pl.ds(16 * n, 16)]))
            pairs.append((b_ff.at[n, chosen, :, columns], b_cols.at[s, n]))
        pairs.append((a_down.at[chosen, :, columns], a_cols.at[s]))
        pairs.append((b_wide.at[2, chosen], b_out.at[s]))
    copies = [pltpu.make_async_copy(src, dst, sems.at[n]) for n, (src, dst) in enumerate(pairs)]
    for copy in copies:
        copy.start()
    for copy in copies:
        copy.wait()


def pick(*args):
    def out(*shape):
        return jax.ShapeDtypeStruct(shape, BF)

    return pl.pallas_call(
        pick_kernel,
        out_shape=(
            out(4, 16, D), out(2, 16, D), out(2, 16, 2 * HEAD), out(2, 32, D), out(2, 2, 16, FF_COLS),
            out(2, 16, FF_COLS), out(2, 16, D),
        ),
        in_specs=[pl.BlockSpec(memory_space=pltpu.SMEM)] + [ANY] * 5,
        out_specs=(IN_VMEM,) * 7,
        scratch_shapes=[pltpu.SemaphoreType.DMA((20,))],
        name="pick",
    )(*args)


def ff_kernel(
    own_hbm, cot_hbm, gate_hbm, up_hbm, down_hbm, a_ff, b_cols_ref, a_cols_ref, b_out,
    grad_out, down_out, cols_out, wide_out,
    cols_ref, wide_ref, x_ref, cot_ref, gate_w, up_w, down_w, b_cols, a_cols, hidden_ref, grad_gate, grad_up,
    grad_hidden, own_ref, terms, pair, total_ref, down_sum, sems, out_sems, pair_send, pair_recv, *scratch,
):
    y, z, x, blk, uly = place()
    core = uly % 2
    scratch = list(scratch)

    def take(count):
        got = scratch[:count]
        del scratch[:count]
        return got

    pairs = (
        (own_hbm, own_ref), (down_hbm, down_w), (cot_hbm, cot_ref), (gate_hbm, gate_w), (up_hbm, up_w),
    )
    copies = [pltpu.make_async_copy(src, dst, sems.at[n]) for n, (src, dst) in enumerate(pairs)]
    for copy in copies:
        copy.start()
    at = lax.broadcasted_iota(jnp.int32, (16, FF_COLS), 1) + (y * FF_COLS - 64 * core)
    inside = jnp.logical_and(at >= 0, at < FF // 4)

    def keep(v):
        return jnp.where(inside, v.astype(F32), 0.0).astype(BF)

    def prepare():
        for s in (0, 1):
            a_cols[s] = keep(a_cols_ref[s])
            for n in (0, 1):
                b_cols[s, n] = keep(b_cols_ref[s, n])
        cols_ref[...] = jnp.zeros_like(cols_ref)

    sibling = uly_others()[1]
    greet([sibling, (blk_of(1 - y, z, x), uly), (blk_of(1 - y, z, x), (uly + 2) % 4)], prepare)
    here = pl.ds(pl.multiple_of(y * FF_COLS, 128), FF_COLS)
    copies[0].wait()
    spread = Spread(own_ref, x_ref, *take(3))
    spread.start()

    def flat(ref, s):
        return ref[s].reshape(4 * CHUNK, D)

    order = (1 - core, core)
    copies[1].wait()
    copies[2].wait()
    latent_cots = []
    for k, s in enumerate(order):
        cot = flat(cot_ref, s)
        latent_cots.append(dot_nt(cot, b_out[s]))
        grad_hidden[k] = dot(cot, down_w[...]) + dot(latent_cots[k].astype(BF), a_cols[s])
        (spread.second, spread.third)[k]()
    copies[3].wait()
    copies[4].wait()
    spread.last()

    def pair_copy(n, d):
        at = (ring_at() + d) % 4
        return remote(
            terms.at[n, 0, at], pair.at[n, at], pair_send.at[n, d], pair_recv.at[n, d], sibling
        )

    def term(n, d):
        at = (ring_at() + d) % 4
        wait_arrival(pair.at[n, at], pair_recv.at[n, d])
        return terms[n, 1, at].astype(F32) + pair[n, at].astype(F32)

    ring = RingSum(lambda d: term(0, d), take(RingSum.scratches))
    for k, s in enumerate(order):
        rows = flat(x_ref, s)
        latent = dot_nt(rows, a_ff[s])
        low = latent.astype(BF)
        gate = dot(rows, gate_w[...]) + dot(low[:, :16], b_cols[s, 0])
        sigmoid = jax.nn.sigmoid(gate)
        silu = gate * sigmoid
        grad_up[...] = (grad_hidden[k] * silu).astype(BF)
        slope = grad_hidden[k] * (sigmoid * (1.0 + gate * (1.0 - sigmoid)))
        up = dot(rows, up_w[...]) + dot(low[:, 16:], b_cols[s, 1])
        grad_gate[...] = (slope * up).astype(BF)
        hidden_ref[...] = (silu * up).astype(BF)
        back_gate = dot_nt(grad_gate[...], b_cols[s, 0])
        back_up = dot_nt(grad_up[...], b_cols[s, 1])
        grads = (
            dot_nt(grad_gate[...], gate_w[...])
            + dot_nt(grad_up[...], up_w[...])
            + dot(back_gate.astype(BF), a_ff[s, :16])
            + dot(back_up.astype(BF), a_ff[s, 16:])
        )
        terms[0, k] = grads.astype(BF).reshape(4, CHUNK, D)
        if k == 0:
            for d in (2, 1, 3, 0):
                pair_copy(0, d).start()
        else:
            ring.first()
        latent_down = dot_nt(hidden_ref[...], a_cols[s])
        down = dot_nt(hidden_ref[...], down_w[...]) + dot(latent_down.astype(BF), b_out[s])
        terms[1, k] = down.astype(BF).reshape(4, CHUNK, D)
        if k == 0:
            for d in (2, 1, 3, 0):
                pair_copy(1, d).start()
        else:
            ring.second()

        def put(ref, n, value, at=slice(None)):
            ref[pl.ds(pl.multiple_of((2 * n + s) * 16, 16), 16), at] = value.astype(BF)

        def turned(value):
            return value.T.astype(BF)

        put(cols_ref, 0, dot(turned(latent_cots[k]), hidden_ref[...]), here)
        put(cols_ref, 1, dot(turned(latent[:, :16]), grad_gate[...]), here)
        put(cols_ref, 2, dot(turned(latent[:, 16:]), grad_up[...]), here)
        put(wide_ref, 0, dot(turned(back_gate), rows))
        put(wide_ref, 1, dot(turned(back_up), rows))
        put(wide_ref, 2, dot(turned(latent_down), flat(cot_ref, s)))
    outs = [
        pltpu.make_async_copy(src, dst, out_sems.at[n])
        for n, (src, dst) in enumerate(
            ((cols_ref, cols_out), (wide_ref, wide_out), (down_sum, down_out), (total_ref, grad_out))
        )
    ]
    outs[0].start()
    outs[1].start()
    for d in range(4):
        down_sum[(ring_at() + d) % 4] = term(1, d).astype(BF)
    outs[2].start()
    total_ref[...] = ring.third()
    outs[3].start()
    for n in (0, 1):
        for d in range(4):
            pair_copy(n, d).wait_send()
    for copy in outs:
        copy.wait()


def feed_forward(*args):
    dma = pltpu.SemaphoreType.DMA
    weight = pltpu.VMEM((D, FF_COLS), BF)
    rows = pltpu.VMEM((4 * CHUNK, FF_COLS), BF)
    pieces = (4, CHUNK, D)
    return pl.pallas_call(
        ff_kernel,
        out_shape=(
            HELD((CHUNK, D), F32),
            HELD(pieces, BF),
            HELD((96, PADDED), BF),
            HELD((96, D), BF),
        ),
        in_specs=[ANY] * 5 + [IN_VMEM] * 4,
        out_specs=(ANY,) * 4,
        scratch_shapes=[
            pltpu.VMEM((96, PADDED), BF), pltpu.VMEM((96, D), BF),
            pltpu.VMEM((2,) + pieces, BF), pltpu.VMEM((2,) + pieces, BF),
            weight, weight, weight,
            pltpu.VMEM((2, 2, 16, FF_COLS), BF), pltpu.VMEM((2, 16, FF_COLS), BF),
            rows, rows, rows,
            pltpu.VMEM((2, 4 * CHUNK, FF_COLS), F32),
            pltpu.VMEM((CHUNK, D), BF),
            pltpu.VMEM((2, 2) + pieces, BF), pltpu.VMEM((2,) + pieces, BF),
            pltpu.VMEM((CHUNK, D), F32), pltpu.VMEM(pieces, BF),
            dma((5,)), dma((4,)), dma((2, 4)), dma((2, 4)),
        ]
        + SPREAD_SEMS
        + RingSum.scratch(),
        compiler_params=pltpu.CompilerParams(
            collective_id=4, has_side_effects=True, vmem_limit_bytes=62 * 2**20
        ),
        name="feed_forward",
    )(*args)


def backward_blocks(slot, first, last, turned_ref, rows_ref, dot_ref, kv_ref, limit_ref, lse_ref, dkv_ref, acc_ref):
    limit = limit_ref[slot, 0:1, :]
    lse = lse_ref[slot, 0:1, :]
    row_dot = dot_ref[slot, 0:1, :]

    def step(n, carry):
        keys, values = key_block(kv_ref, n, KEYS_BACK)
        scores = jnp.where(key_places(n, KEYS_BACK) <= limit, dot(keys, turned_ref[0, slot]), -1e30)
        probs = jnp.exp2(scores - lse)
        grad_probs = dot(values, turned_ref[1, slot])
        grad_scores = (probs * (grad_probs - row_dot)).astype(BF)
        acc_ref[slot] += dot(keys.T, grad_scores)
        at = pl.ds(pl.multiple_of(n * KEYS_BACK, KEYS_BACK), KEYS_BACK)
        dkv_ref[at, :HEAD] += dot(grad_scores, rows_ref[0, slot])
        dkv_ref[at, HEAD:] += dot(probs.astype(BF), rows_ref[1, slot])
        return carry

    lax.fori_loop(first, last, step, 0)


class Reduce:
    @staticmethod
    def scratch(shape):
        return [
            pltpu.VMEM((2, 3, 2, 4) + shape, BF),
            pltpu.VMEM((2, 3, 2) + shape, BF),
            pltpu.VMEM((2,) + shape, BF),
            pltpu.VMEM((2, 4, 2) + shape, BF),
            pltpu.VMEM((2, 2) + shape, BF),
            pltpu.SemaphoreType.DMA((2, 10)),
            pltpu.SemaphoreType.DMA((2, 10)),
        ]

    scratches = 7

    def __init__(self, part, scratch):
        self.part = part
        self.buf_q, self.buf_p, self.buf_y, self.sum_p, self.sum_y, self.send_sem, self.recv_sem = scratch
        self.y, self.z, self.x, self.blk, self.uly = place()
        self.pq = ((self.x, self.z), (self.z, self.x))
        self.flying = []

    def send(self, src, dst, half, n, y, p, q):
        target = blk_of(y, q, p) if half == 0 else blk_of(y, p, q)
        copy = remote(
            src, dst, self.send_sem.at[half, n], self.recv_sem.at[half, n], (target, self.uly)
        )
        copy.start()
        self.flying.append(copy)

    def land(self):
        for copy in self.flying:
            copy.wait()
        self.flying = []

    def first(self):
        for d in (2, 1, 3):
            for half in (0, 1):
                p, q = self.pq[half]
                to = (q + d) % 4
                for y in (0, 1):
                    src = self.part.at[0, y, to] if half == 0 else self.part.at[1, y, :, to]
                    self.send(
                        src, self.buf_q.at[half, d - 1, y], half, (d - 1) * 2 + y, self.y, p, to
                    )

    def second(self):
        self.land()
        for d in (2, 1, 3, 0):
            for half in (0, 1):
                p, q = self.pq[half]
                to = (p + d) % 4
                for y in (0, 1):
                    own = self.part[0, y, q, to] if half == 0 else self.part[1, y, to, q]
                    total = own.astype(F32)
                    for n in range(3):
                        total += self.buf_q[half, n, y, to].astype(F32)
                    self.sum_p[half, d, y] = total.astype(BF)
                if d > 0:
                    self.send(
                        self.sum_p.at[half, d], self.buf_p.at[half, d - 1], half, 5 + d, self.y, to, q
                    )

    def third(self):
        self.land()
        for k in (1, 0):
            for half in (0, 1):
                p, q = self.pq[half]
                y = self.y if k == 0 else 1 - self.y
                total = self.sum_p[half, 0, y].astype(F32)
                for n in range(3):
                    total += self.buf_p[half, n, y].astype(F32)
                self.sum_y[half, k] = total.astype(BF)
                if k == 1:
                    self.send(self.sum_y.at[half, 1], self.buf_y.at[half], half, 9, 1 - self.y, p, q)

    def fourth(self):
        self.land()
        return [self.sum_y[half, 0].astype(F32) + self.buf_y[half].astype(F32) for half in (0, 1)]


class Shed:
    @staticmethod
    def scratch(shape):
        return [
            pltpu.VMEM((2, 4) + shape, BF),
            pltpu.VMEM((2, 4) + shape, BF),
            pltpu.VMEM((2, 2, 4) + shape, BF),
            pltpu.VMEM((4, 2) + shape, BF),
            pltpu.VMEM((3, 2) + shape, BF),
            pltpu.VMEM((2,) + shape, BF),
            pltpu.VMEM(shape, BF),
            pltpu.SemaphoreType.DMA((10,)),
            pltpu.SemaphoreType.DMA((10,)),
        ]

    scratches = 9

    def __init__(self, part, half, rows, order, scratch):
        self.part, self.half, self.rows, self.order = part, half, rows, order
        (
            self.buf_far, self.sum_mid, self.buf_in, self.sum_p, self.buf_p, self.sum_y, self.buf_y,
            self.send_sem, self.recv_sem,
        ) = scratch
        self.y, self.z, self.x, self.blk, self.uly = place()
        self.p, self.q = (self.x, self.z) if order == 0 else (self.z, self.x)
        self.flying = []

    def line(self, y, q):
        rows = pl.ds(*self.rows)
        if self.order == 0:
            return self.part.at[self.half, y, q, :, rows]
        return self.part.at[self.half, y, :, q, rows]

    def value(self, y, q, p):
        start, size = self.rows
        z, x = (q, p) if self.order == 0 else (p, q)
        return self.part[self.half, y, z, x, start : start + size].astype(F32)

    def send(self, src, dst, n, y, p, q):
        target = blk_of(y, q, p) if self.order == 0 else blk_of(y, p, q)
        copy = remote(src, dst, self.send_sem.at[n], self.recv_sem.at[n], (target, self.uly))
        copy.start()
        self.flying.append(copy)

    def land(self):
        for copy in self.flying:
            copy.wait()
        self.flying = []

    def first(self):
        for y, d in ((0, 1), (1, 3)):
            to = (self.q + d) % 4
            self.send(self.line(y, (self.q + 2) % 4), self.buf_far.at[y], y, self.y, self.p, to)
        for y, d in ((1, 1), (0, 3)):
            to = (self.q + d) % 4
            self.send(self.line(y, to), self.buf_in.at[d // 2, y], 2 + d // 2, self.y, self.p, to)

    def second(self):
        direct = self.flying[2:]
        self.flying = self.flying[:2]
        self.land()
        for y, d in ((0, 1), (1, 3)):
            to = (self.q + d) % 4
            for p in range(4):
                total = self.value(y, to, p) + self.buf_far[y, p].astype(F32)
                self.sum_mid[y, p] = total.astype(BF)
            self.send(self.sum_mid.at[y], self.buf_in.at[d // 2, y], 4 + y, self.y, self.p, to)
        self.flying += direct

    def third(self):
        self.land()
        for d in (2, 1, 3, 0):
            to = (self.p + d) % 4
            for y in (0, 1):
                total = self.value(y, self.q, to)
                for n in (0, 1):
                    total += self.buf_in[n, y, to].astype(F32)
                self.sum_p[d, y] = total.astype(BF)
            if d > 0:
                self.send(self.sum_p.at[d], self.buf_p.at[d - 1], 5 + d, self.y, to, self.q)

    def fourth(self):
        self.land()
        for k in (1, 0):
            y = self.y if k == 0 else 1 - self.y
            total = self.sum_p[0, y].astype(F32)
            for n in range(3):
                total += self.buf_p[n, y].astype(F32)
            self.sum_y[k] = total.astype(BF)
            if k == 1:
                self.send(self.sum_y.at[1], self.buf_y, 9, 1 - self.y, self.p, self.q)

    def last(self):
        self.land()
        return self.sum_y[0].astype(F32) + self.buf_y[...].astype(F32)


def reduce_others():
    y, z, x, blk, uly = place()
    return (
        [(blk_of(1 - y, z, x), uly)]
        + [(blk_of(y, z, (x + d) % 4), uly) for d in (1, 2, 3)]
        + [(blk_of(y, (z + d) % 4, x), uly) for d in (1, 2, 3)]
    )


UNIT = (16, 128)


class Total:
    @staticmethod
    def scratch(kept, summed):
        shape = (kept + summed,) + UNIT
        return (
            [pltpu.VMEM((2, 2, 4, 4) + shape, BF)]
            + Reduce.scratch(shape)
            + [
                pltpu.VMEM((2,) + shape, BF),
                pltpu.VMEM((3, 2) + shape, BF),
                pltpu.VMEM((2, 4 * kept + summed) + UNIT, BF),
                pltpu.SemaphoreType.DMA((3,)),
                pltpu.SemaphoreType.DMA((3,)),
                pltpu.SemaphoreType.DMA((31,)),
                pltpu.SemaphoreType.DMA((31,)),
                pltpu.SemaphoreType.DMA,
                pltpu.SemaphoreType.DMA,
                pltpu.SemaphoreType.DMA,
            ]
        )

    scratches = 18

    @staticmethod
    def shape(kept, summed):
        return HELD((2, 2, 4, 4, 4 * kept + summed) + UNIT, BF)

    def __init__(self, kept, summed, all_ref, scratch):
        self.kept, self.summed, self.all_ref = kept, summed, all_ref
        self.part = scratch[0]
        self.reduce = Reduce(self.part, scratch[1:8])
        self.own, self.buf, self.full, self.send_sem, self.recv_sem = scratch[8:13]
        self.all_send, self.all_recv, self.local_sem, self.pair_send, self.pair_recv = scratch[13:18]
        self.y, self.z, self.x, self.blk, self.uly = place()
        self.core = self.uly % 2
        self.flying = []

    def pack(self, values, first, per, at):
        for n, value in enumerate(values, first):
            item = n // per
            self.part[item // 32, item // 16 % 2, item // 4 % 4, item % 4, at + n % per] = value.astype(BF)

    def pack_kept(self, values, first=0):
        self.pack(values, first, self.kept, 0)

    def pack_summed(self, values, first=0):
        self.pack(values, first, self.summed, self.kept)

    def clear(self, kept, summed):
        nothing = jnp.zeros(UNIT, BF)
        self.pack_kept([nothing] * (64 * self.kept - kept), kept)
        self.pack_summed([nothing] * (64 * self.summed - summed), summed)

    def across(self):
        for half, total in enumerate(self.reduce.fourth()):
            self.own[half] = total.astype(BF)
        self.copies = []
        for n, other in enumerate(uly_others()):
            copy = remote(self.own, self.buf.at[n], self.send_sem.at[n], self.recv_sem.at[n], other)
            copy.start()
            self.copies.append(copy)

    def send(self, src, dst, n, y, z, x):
        copy = remote(src, dst, self.all_send.at[n], self.all_recv.at[n], (blk_of(y, z, x), self.uly))
        copy.start()
        self.flying.append(copy)

    def item(self, y, d=0, e=0):
        dz, dx = self.core * d + (1 - self.core) * e, self.core * e + (1 - self.core) * d
        return self.all_ref.at[self.core, y, (self.z + dz) % 4, (self.x + dx) % 4]

    def along(self, y, src, n, d, e):
        dz, dx = self.core * d + (1 - self.core) * e, self.core * e + (1 - self.core) * d
        self.send(src[0], src[1], n, self.y, (self.z + dz) % 4, (self.x + dx) % 4)

    def along_first(self, y, src, first):
        for d in (1, 2, 3):
            self.along(y, (src, self.item(y)), first + d, d, 0)

    def join(self):
        for copy in self.copies:
            copy.wait()
        kept = self.kept
        terms = [self.own] + [self.buf.at[n] for n in range(3)]
        who = [self.uly] + [other[1] for other in uly_others()]
        for half in (0, 1):
            for term, uly in zip(terms, who):
                self.full[half, pl.ds(uly * kept, kept)] = term[half, :kept]
            if self.summed:
                self.full[half, 4 * kept :] = sum(
                    term[half, kept:].astype(F32) for term in terms
                ).astype(BF)
        own = self.full.at[self.core]
        self.send(own, self.item(self.y), 0, 1 - self.y, self.z, self.x)
        self.along_first(self.y, own, 0)
        self.local = pltpu.make_async_copy(own, self.item(self.y), self.local_sem)
        self.local.start()

    def onward(self):
        other = self.item(1 - self.y)
        wait_arrival(other, self.all_recv.at[0])
        self.along_first(1 - self.y, other, 3)

    def spread(self):
        self.local.wait()
        for k, y in enumerate((self.y, 1 - self.y)):
            for d in range(4):
                if d > 0:
                    wait_arrival(self.item(y, 4 - d), self.all_recv.at[3 * k + d])
                for e in (1, 2, 3):
                    ref = self.item(y, (4 - d) % 4)
                    self.along(y, (ref, ref), 7 + k * 12 + d * 3 + e - 1, 0, e)

    def hand(self):
        for k, y in enumerate((self.y, 1 - self.y)):
            for d in range(4):
                for e in (1, 2, 3):
                    wait_arrival(
                        self.item(y, (4 - d) % 4, 4 - e), self.all_recv.at[7 + k * 12 + d * 3 + e - 1]
                    )
        self.pair(self.core).start()

    def pair(self, core):
        return remote(
            self.all_ref.at[core], self.all_ref.at[core], self.pair_send, self.pair_recv, uly_others()[1]
        )

    def end(self):
        for copy in self.flying:
            copy.wait_send()
        self.pair(self.core).wait_send()
        wait_arrival(self.all_ref.at[1 - self.core], self.pair_recv)

    def steps(self):
        return [
            self.reduce.first, self.reduce.second, self.reduce.third, self.across, self.join,
            self.onward, self.spread, self.hand, self.end,
        ]


def units(value):
    rows, columns = value.shape
    return [
        value[n * 16 : (n + 1) * 16, t * 128 : (t + 1) * 128]
        for n in range(rows // 16) for t in range(columns // 128)
    ]


FF_KEPT, FF_SUMMED, QKV_KEPT = 2, 2, 1
COL_TILES = PADDED // 128
D_TILES = D // 128
DKV_ROWS = CHUNK // 2
DKV_STREAMS = 2


def backward_kernel(
    norm_ff_ref, norm_in_ref, a_qkv_ref, bo_ref, total_hbm, down_hbm, cols_hbm, ff_hbm, resid_hbm, cot_hbm, ao_hbm, mixed_hbm, wo_hbm, kv_hbm, q_hbm, limit_hbm, lse_hbm,
    wq_hbm, rows_hbm, normed_hbm, b_qkv_hbm, cos_hbm, sin_hbm,
    result_ref, input_grad_ref, ff_all, qkv_all,
    total_ref, down_ref, cols_ref, ff_ref, resid_ref, cot_ref, ao_ref, mixed_ref, wo_ref, kv_ref, q_ref, limit_ref,
    lse_ref, wq_ref, rows_ref, normed_ref, b_qkv_ref, cos_ref, sin_ref, dkv_ref, acc_ref, part, dq_ref, grad_ref, grad_attn, grad_resid, grad_qkv,
    cross_out, cross_in, home_out, home_in, turned_ref, by_rows_ref, dot_ref, copy_sem, cross_sem, home_send,
    home_recv, *scratch,
):
    y, z, x, blk, uly = place()
    core, h = uly % 2, uly // 2
    scratch = list(scratch)

    def take(count):
        got = scratch[:count]
        del scratch[:count]
        return got

    chunk = 2 * blk + h
    upper = chunk // 32
    home = (1 - h) * blk + h * (31 - blk)
    home_from = [(home, upper * 2 + s) for s in (0, 1)]
    lower = low_chunk(blk)
    own_chunk = (1 - h) * lower + h * (63 - lower)
    home_to = [(own_chunk // 2, (own_chunk % 2) * 2 + half) for half in (0, 1)]
    copies = [
        pltpu.make_async_copy(src, dst, copy_sem.at[n])
        for n, (src, dst) in enumerate(
            (
                (total_hbm, total_ref), (resid_hbm, resid_ref), (cot_hbm, cot_ref), (cols_hbm, cols_ref),
                (ff_hbm, ff_ref), (down_hbm, down_ref), (ao_hbm, ao_ref), (mixed_hbm, mixed_ref),
                (wo_hbm, wo_ref), (kv_hbm, kv_ref),
                (q_hbm, q_ref), (limit_hbm, limit_ref), (lse_hbm, lse_ref), (wq_hbm, wq_ref),
                (rows_hbm, rows_ref), (normed_hbm, normed_ref), (b_qkv_hbm, b_qkv_ref),
                (cos_hbm, cos_ref), (sin_hbm, sin_ref),
            )
        )
    ]
    for copy in copies:
        copy.start()
    greet(
        reduce_others() + uly_others() + [(blk_of(1 - y, z, x), (uly + 2) % 4)] + home_from + home_to
    )
    collect_out = RingSum(
        lambda d: down_ref[(ring_at() + d) % 4].astype(F32), take(RingSum.scratches)
    )
    low, high = (
        [
            Shed(part, half, (n * DKV_ROWS, DKV_ROWS), n, take(Shed.scratches))
            for n in range(DKV_STREAMS)
        ]
        for half in (0, 1)
    )
    ff_total = Total(FF_KEPT, FF_SUMMED, ff_all, take(Total.scratches))
    qkv_total = Total(QKV_KEPT, 0, qkv_all, take(Total.scratches))
    deliver = Deliver()

    def send_home(n, value):
        home_out[n] = value.astype(BF)
        for half in (0, 1):
            deliver.send(
                home_out.at[n, pl.ds(half * 64, 64)], home_in.at[n, core],
                home_send.at[n, half], home_recv.at[n, core], home_to[half],
            )

    def arrived_home(n):
        for s in (0, 1):
            wait_arrival(home_in.at[n, s], home_recv.at[n, s])
        return home_in[n].astype(F32)

    def ready(first, last):
        for copy in copies[first:last]:
            copy.wait()

    ready(0, 3)
    residual = resid_ref[...]
    value = cot_ref[...].astype(F32) + norm_back(
        residual, norm_scale(residual), norm_ff_ref[...], total_ref[...]
    )
    grad_resid[...] = value
    own_rows = pl.ds(pl.multiple_of(h * CHUNK, CHUNK), CHUNK)
    other_rows = pl.ds(pl.multiple_of((1 - h) * CHUNK, CHUNK), CHUNK)
    grad_attn[own_rows, :] = value.astype(BF)
    partner = uly_others()[0]
    cross = remote(
        grad_attn.at[own_rows], grad_attn.at[own_rows], cross_sem.at[0], cross_sem.at[1], partner
    )
    cross.start()
    ready(3, 9)
    ff_total.pack_kept(units(cols_ref))
    ff_total.pack_summed(units(ff_ref))
    at_o = 6 * COL_TILES
    ff_total.clear(at_o + D_TILES // 2 + D_TILES, 6 * D_TILES)
    qkv_total.clear(3 * D_TILES + D_TILES // 2 + 2, 0)
    dkv_ref[...] = jnp.zeros_like(dkv_ref)
    acc_ref[...] = jnp.zeros_like(acc_ref)
    latent_o = dot_nt(ao_ref[...], mixed_ref[...]).astype(BF)
    cross.wait_send()
    wait_arrival(grad_attn.at[other_rows], cross_sem.at[1])
    back_o = dot_nt(grad_attn[...], bo_ref[...]).astype(BF)
    grad_ref[...] = (dot_nt(grad_attn[...], wo_ref[...]) + dot(back_o, ao_ref[...])).astype(BF)
    back_o = dot_nt(bo_ref[...], grad_attn[...]).astype(BF)
    ff_total.pack_kept(
        units(dot(back_o, mixed_ref[...])) + units(dot(latent_o, grad_attn[...])), at_o
    )

    ready(9, 13)
    steps = ff_total.steps()

    def beside(*more):
        for step in more:
            step()
        if steps:
            steps.pop(0)()

    def pack(half):
        def one(n, carry):
            chunk = low_chunk(n) if half == 0 else 63 - low_chunk(n)
            rows = dkv_ref[pl.ds(pl.multiple_of(chunk * CHUNK, CHUNK), CHUNK), :]
            both = jnp.concatenate([rows[:, :HEAD] * LN2, rows[:, HEAD:]], axis=1)
            part[half, n // 16, n // 4 % 4, n % 4] = both.astype(BF)
            return carry

        lax.fori_loop(0, 32, one, 0)

    def shed(streams, name):
        def run():
            for stream in streams:
                getattr(stream, name)()

        return run

    args = (turned_ref, by_rows_ref, dot_ref, kv_ref, limit_ref, lse_ref, dkv_ref, acc_ref)
    step = KEYS_BACK // CHUNK
    middle = CHUNKS // 2 // step
    beside()
    for slot in (0, 1):
        for n, ref in enumerate((q_ref, grad_ref)):
            turned_ref[n, slot] = head_columns(ref, slot)
            by_rows_ref[n, slot] = head_rows(ref, slot)
        row_dot = turned_ref[1, slot].astype(F32) * head_columns(mixed_ref, slot).astype(F32)
        dot_ref[slot] = jnp.broadcast_to(jnp.sum(row_dot, axis=0, keepdims=True), (8, ROWS))
    backward_blocks(1, middle, (63 - lower) // step + 1, *args)
    backward_blocks(0, 0, lower // step + 1, *args)
    pack(1)
    beside(shed(high, "first"))
    names = ["second", "third", "fourth"]
    extra = [collect_out.first, collect_out.second]
    for n in range(0, middle, 2):
        backward_blocks(1, n, n + 2, *args)
        more = [shed(high, names.pop(0))] if names else []
        more += [extra.pop(0)] if extra else []
        beside(*more)
    pack(0)
    for stream in low:
        stream.first()
    for slot in (0, 1):
        for n in range(GROUP):
            dq_ref[slot * CHUNK : (slot + 1) * CHUNK, n * HEAD : (n + 1) * HEAD] = (
                acc_ref[slot, :, n * CHUNK : (n + 1) * CHUNK].T * HEAD ** (-0.5)
            )
    ready(13, 19)
    for stream in low:
        stream.second()
    beside()
    cos_table, sine_table = cos_ref[...], sin_ref[...]

    def turn_back(value, rows=slice(None)):
        return value * cos_table[rows] - pltpu.roll(value, HEAD // 2, 1) * sine_table[rows]

    for n in range(GROUP):
        at = slice(n * HEAD, (n + 1) * HEAD)
        grad_qkv[:, at] = turn_back(dq_ref[:, at]).astype(BF)
    group = GROUP * HEAD

    def key_value(half, streams):
        for n, stream in enumerate(streams):
            rows = slice(half * CHUNK + n * DKV_ROWS, half * CHUNK + (n + 1) * DKV_ROWS)
            value = stream.last()
            grad_qkv[rows, group : group + HEAD] = turn_back(value[:, :HEAD], rows).astype(BF)
            grad_qkv[rows, group + HEAD :] = value[:, HEAD:].astype(BF)

    key_value(1, high)
    for stream in low:
        stream.third()
    send_home(0, resid_ref[...] + collect_out.third())
    latent_qkv = dot_nt(a_qkv_ref[...], normed_ref[...]).astype(BF)
    for stream in low:
        stream.fourth()
    key_value(0, low)

    def project_back(rows):
        grads = grad_qkv[rows, :]
        lifted = dot(dot_nt(grads, b_qkv_ref[...]).astype(BF), a_qkv_ref[...])
        return dot_nt(grads[:, :512], wq_ref[0]) + dot_nt(grads[:, 512:], wq_ref[1]) + lifted

    cross_out[...] = project_back(other_rows).astype(BF)
    cross = remote(cross_out, cross_in, cross_sem.at[2], cross_sem.at[3], partner)
    cross.start()
    back_qkv = dot_nt(b_qkv_ref[...], grad_qkv[...]).astype(BF)
    grad_b = dot(latent_qkv, grad_qkv[...])
    qkv_total.pack_kept(
        units(dot(back_qkv, normed_ref[...]))
        + units(grad_b[:16, :group])
        + units(grad_b[16:32, group : group + HEAD])
        + units(grad_b[32:, group + HEAD :])
    )
    last_steps = qkv_total.steps()
    last_steps.pop(0)()
    mine = project_back(own_rows)
    last_steps.pop(0)()
    beside()
    cross.wait()
    mine = mine + cross_in[...].astype(F32)
    tokens = rows_ref[own_rows, :].astype(F32)
    send_home(1, grad_resid[...] + norm_back(tokens, norm_scale(tokens), norm_in_ref[...], mine))
    for step in last_steps + steps:
        step()
    result_ref[...] = arrived_home(0).astype(BF)
    input_grad_ref[...] = arrived_home(1).astype(BF)
    deliver.end()


def backward(*args):
    dma = pltpu.SemaphoreType.DMA
    group = GROUP * HEAD
    return pl.pallas_call(
        backward_kernel,
        out_shape=(
            jax.ShapeDtypeStruct((2, CHUNK // 2, D), BF),
            jax.ShapeDtypeStruct((2, CHUNK // 2, D), BF),
            Total.shape(FF_KEPT, FF_SUMMED),
            Total.shape(QKV_KEPT, 0),
        ),
        in_specs=[IN_VMEM] * 4 + [ANY] * 19,
        out_specs=(IN_VMEM, IN_VMEM, ANY, ANY),
        scratch_shapes=[
            pltpu.VMEM((CHUNK, D), F32),
            pltpu.VMEM((4, CHUNK, D), BF),
            pltpu.VMEM((96, PADDED), BF),
            pltpu.VMEM((96, D), BF),
            pltpu.VMEM((CHUNK, D), F32),
            pltpu.VMEM((CHUNK, D), BF),
            pltpu.VMEM((16, group), BF),
            pltpu.VMEM((2 * CHUNK, group), BF),
            pltpu.VMEM((D // 2, D), BF),
            pltpu.VMEM((CHUNKS, CHUNK, 2 * HEAD), BF),
            pltpu.VMEM((2 * CHUNK, group), BF),
            pltpu.VMEM((2, 8, ROWS), jnp.int32),
            pltpu.VMEM((2, 8, ROWS), F32),
            pltpu.VMEM((2, D, 512), BF),
            pltpu.VMEM((2 * CHUNK, D), BF),
            pltpu.VMEM((2 * CHUNK, D), BF),
            pltpu.VMEM((48, 1024), BF),
            pltpu.VMEM((2 * CHUNK, HEAD), F32),
            pltpu.VMEM((2 * CHUNK, HEAD), F32),
            pltpu.VMEM((CHUNKS * CHUNK, 2 * HEAD), F32),
            pltpu.VMEM((2, HEAD, ROWS), F32),
            pltpu.VMEM((2, 2, 4, 4, CHUNK, 2 * HEAD), BF),
            pltpu.VMEM((2 * CHUNK, group), F32),
            pltpu.VMEM((2 * CHUNK, group), BF),
            pltpu.VMEM((2 * CHUNK, D), BF),
            pltpu.VMEM((CHUNK, D), F32),
            pltpu.VMEM((2 * CHUNK, 1024), BF),
            pltpu.VMEM((CHUNK, D), BF),
            pltpu.VMEM((CHUNK, D), BF),
            pltpu.VMEM((2, CHUNK, D), BF),
            pltpu.VMEM((2, 2, CHUNK // 2, D), BF),
            pltpu.VMEM((2, 2, HEAD, ROWS), BF),
            pltpu.VMEM((2, 2, ROWS, HEAD), BF),
            pltpu.VMEM((2, 8, ROWS), F32),
            dma((19,)), dma((4,)), dma((2, 2)), dma((2, 2)),
        ]
        + RingSum.scratch()
        + Shed.scratch((DKV_ROWS, 2 * HEAD)) * (2 * DKV_STREAMS)
        + Total.scratch(FF_KEPT, FF_SUMMED)
        + Total.scratch(QKV_KEPT, 0),
        compiler_params=pltpu.CompilerParams(
            collective_id=2, has_side_effects=True, vmem_limit_bytes=60 * 2**20
        ),
        name="backward",
    )(*args)


def fold_kernel(
    pick_ref, result_in, grad_in, ff_hbm, qkv_hbm, result_ref, input_grad_ref, a_wide, a_down, b_wide, b_kv, b_ff,
    ff_ref, qkv_ref, sems,
):
    c = pl.program_id(0)

    @pl.when(c == 0)
    def _():
        copies = [
            pltpu.make_async_copy(src, dst, sems.at[n])
            for n, (src, dst) in enumerate(((ff_hbm, ff_ref), (qkv_hbm, qkv_ref)))
        ]
        for copy in copies:
            copy.start()
        result_ref[...] = result_in[...]
        input_grad_ref[...] = grad_in[...].astype(F32)
        for copy in copies:
            copy.wait()

    def kept(ref, per, n, u):
        item = n // per
        return ref[item // 32, item // 16 % 2, item // 4 % 4, item % 4, u * per + n % per].astype(F32)

    def ff_kept(n, u):
        return kept(ff_ref, FF_KEPT, n, u)

    def qkv_kept(n, u):
        return kept(qkv_ref, QKV_KEPT, n, u)

    def summed(n):
        item = n // FF_SUMMED
        return ff_ref[
            item // 32, item // 16 % 2, item // 4 % 4, item % 4, 4 * FF_KEPT + n % FF_SUMMED
        ].astype(F32)

    def put(ref, at, tile, value):
        ref[at + (slice(None), slice(tile * 128, (tile + 1) * 128))] = (
            pick_ref[c, 0] * value(0) + pick_ref[c, 1] * value(1)
        )

    for n in range(3):
        for t in range(D_TILES):
            put(a_wide, (n, 0), t, lambda s: qkv_kept(n * D_TILES + t, s) + qkv_kept(n * D_TILES + t, 2 + s))
    at_o = 6 * COL_TILES
    half = D_TILES // 2
    for t in range(D_TILES):
        h, part = t // half, t % half
        put(a_wide, (3, 0), t, lambda s: ff_kept(at_o + part, 2 * h + s))
        put(b_wide, (0, 0), t, lambda s: qkv_kept(3 * D_TILES + part, 2 * h + s))
        put(
            b_wide, (1, 0), t,
            lambda s: ff_kept(at_o + half + t, s) + ff_kept(at_o + half + t, 2 + s),
        )
        for n, (ref, at) in enumerate(((a_wide, (4, 0)), (a_wide, (5, 0)), (b_wide, (2, 0)))):
            put(ref, at, t, lambda s: summed((2 * n + s) * D_TILES + t))
    for n in (0, 1):
        for h in (0, 1):
            put(b_kv, (n, 0), h, lambda s: qkv_kept(3 * D_TILES + half + n, 2 * h + s))
    for n, (ref, at) in enumerate(((a_down, (0,)), (b_ff, (0, 0)), (b_ff, (1, 0)))):
        for t in range(FF // 128):
            where = [
                (u, t - start) for u, start in enumerate((0, 17, 35, 52)) if 0 <= t - start < COL_TILES
            ]
            put(
                ref, at, t,
                lambda s: sum(ff_kept((2 * n + s) * COL_TILES + tile, u) for u, tile in where),
            )


def fold(share, result, input_grad, ff_all, qkv_all):
    rows = pl.BlockSpec(result.shape, lambda c: (0, 0, 0))

    def by_set(lead, columns):
        shape = lead + (1, 16, columns)
        return pl.BlockSpec(shape, lambda c: (0,) * len(lead) + (c, 0, 0))

    def out(lead, columns):
        return jax.ShapeDtypeStruct(lead + (SETS, 16, columns), F32)

    outs = (((6,), D), ((), FF), ((3,), D), ((2,), 2 * HEAD), ((2,), FF))
    return pl.pallas_call(
        fold_kernel,
        grid=(SETS,),
        out_shape=(
            jax.ShapeDtypeStruct(result.shape, BF),
            jax.ShapeDtypeStruct(result.shape, F32),
        )
        + tuple(out(*o) for o in outs),
        in_specs=[pl.BlockSpec(memory_space=pltpu.SMEM), rows, rows, ANY, ANY],
        out_specs=(rows, rows) + tuple(by_set(*o) for o in outs),
        scratch_shapes=[
            pltpu.VMEM(ff_all.shape, BF), pltpu.VMEM(qkv_all.shape, BF), pltpu.SemaphoreType.DMA((2,))
        ],
        compiler_params=pltpu.CompilerParams(vmem_limit_bytes=40 * 2**20),
        name="fold",
    )(share, result, input_grad, ff_all, qkv_all)


def norm_scale(hidden):
    return lax.rsqrt(jnp.mean(hidden * hidden, axis=-1, keepdims=True) + EPS)


def norm_back(hidden, scaled, gain_vec, upstream):
    normed = hidden * scaled
    weighted = upstream * gain_vec
    return scaled * (weighted - normed * jnp.mean(weighted * normed, axis=-1, keepdims=True))


def body(
    tokens, cotangent, lengths, set_index, norm_in, norm_ff, qkv_bias, w_qkv, w_out, w_gate_up, w_down,
    a_wide, a_down, b_wide, b_kv, b_ff,
):
    a_own, b_own, b_pair, a_ff, b_cols, a_cols, b_out = pick(set_index, a_wide, a_down, b_wide, b_kv, b_ff)
    frequencies = np.float64(THETA) ** (-np.arange(0, HEAD, 2, dtype=np.float64) / HEAD)
    frequencies = np.concatenate([frequencies, frequencies])[None].astype(np.float32)
    (
        q, mixed, lse, kv_all, qkv_w, out_w, gate_w, up_w, down_w, rows, normed, residual, grad_out,
        normed_ff, grad_gathered, limit, cos_table, sine_table, b_qkv, ao,
    ) = forward(
        tokens, cotangent, lengths, w_qkv, w_out, w_gate_up, w_down.T, norm_in[None], norm_ff[None],
        qkv_bias.reshape(16, HEAD), frequencies, a_own, b_own, b_pair,
    )
    gate_w, up_w, down_w = (w.reshape(D, FF_COLS) for w in (gate_w, up_w, down_w))
    grad_normed_ff, down_sum, cols, ff_wide = feed_forward(
        normed_ff, grad_gathered, gate_w, up_w, down_w, a_ff, b_cols, a_cols, b_out
    )
    result, input_grad, ff_all, qkv_all = backward(
        norm_ff[None], norm_in[None], a_own[:3].reshape(48, D), b_own[1],
        grad_normed_ff, down_sum, cols, ff_wide, residual, grad_out, ao, mixed, out_w, kv_all, q, limit, lse,
        qkv_w, rows, normed, b_qkv, cos_table, sine_table,
    )
    share = (jnp.arange(SETS, dtype=jnp.int32)[:, None] == set_index[None, :]).astype(F32)
    return tuple(fold(share, result, input_grad, ff_all, qkv_all))


def solution(mesh):
    spread = P(None, ("blk", "uly"), None)
    in_specs = (
        spread, spread, P(), P(), P(), P(), P(),
        P(("blk", "uly"), None), P(("blk", "uly"), None), P(None, "blk", "uly"), P("uly", "blk"),
        P(), P(), P(), P(), P(),
    )
    out_specs = (spread, spread, P(), P(), P(), P(), P())
    return jax.shard_map(body, mesh=mesh, in_specs=in_specs, out_specs=out_specs, check_vma=False)
```

```python
import functools

import jax
import jax.numpy as jnp
import numpy as np
from jax import lax
from jax.experimental import pallas as pl
from jax.experimental.pallas import tpu as pltpu
from jax.sharding import PartitionSpec as P

HEADS = 12
KV_HEADS = 2
HEAD = 128
GROUP = HEADS // KV_HEADS
FF = 8960
SETS = 8
D = 1536
CHUNK = 128
CHUNKS = 64
PADDED = 2304
EPS = 1e-06
THETA = 1000000.0
LOG2E = 1.4426950408889634
LN2 = 0.6931471805599453
MESH = pl.DeviceIdType.MESH
BF = jnp.bfloat16
F32 = jnp.float32
ANY = pl.BlockSpec(memory_space=pltpu.HBM)
IN_VMEM = pl.BlockSpec(memory_space=pltpu.VMEM)
HELD = pltpu.HBM


def blk_of(y, z, x):
    return y * 16 + z * 4 + x


def low_chunk(blk):
    return (1 - blk // 16) * 2 * blk + blk // 16 * (63 - 2 * blk)


def place():
    blk = lax.axis_index("blk")
    return blk // 16, (blk // 4) % 4, blk % 4, blk, lax.axis_index("uly")


def ring_others():
    y, z, x, blk, uly = place()
    return [
        (blk_of(1 - y, z, x), uly),
        (blk_of(y, z, (x + 1) % 4), uly),
        (blk_of(y, z, (x + 3) % 4), uly),
        (blk_of(y, (z + 1) % 4, x), uly),
        (blk_of(y, (z + 3) % 4, x), uly),
    ]


def choose(number, value):
    chosen = value(0)
    for c in range(1, SETS):
        chosen = jnp.where(number == c, value(c), chosen)
    return chosen


def gain(ref, first):
    return jnp.concatenate([ref[n : n + 1, :] for n in range(first, first + D // 128)], axis=1)


def greet(others, meanwhile=None):
    barrier = pltpu.get_barrier_semaphore()
    for other in others:
        pl.semaphore_signal(barrier, inc=1, device_id=other, device_id_type=MESH)
    if meanwhile is not None:
        meanwhile()
    pl.semaphore_wait(barrier, len(others))


class Gather:
    sends = 31

    def __init__(self, src, dst, send_sem, recv_sem, local_sem, orders=(0, 1)):
        self.src, self.dst, self.orders = src, dst, orders
        self.streams = range(len(orders))
        self.send_sem, self.recv_sem, self.local_sem = send_sem, recv_sem, local_sem
        self.y, self.z, self.x, self.blk, self.uly = place()
        self.count = [0] * len(orders)
        self.sent = []
        self.local = []

    def at(self, stream, y, p, q):
        order = self.orders[stream]
        return blk_of(y, order * p + (1 - order) * q, order * q + (1 - order) * p)

    def pq(self, stream):
        order = self.orders[stream]
        return (
            order * self.z + (1 - order) * self.x,
            order * self.x + (1 - order) * self.z,
        )

    def send(self, stream, item, target, src=None):
        copy = pltpu.make_async_remote_copy(
            src_ref=self.dst(stream, item) if src is None else src,
            dst_ref=self.dst(stream, item),
            send_sem=self.send_sem.at[stream, self.count[stream]],
            recv_sem=self.recv_sem.at[stream, item],
            device_id=(target, self.uly),
            device_id_type=MESH,
        )
        self.count[stream] += 1
        copy.start()
        self.sent.append(copy)

    def wait(self, stream, item):
        ref = self.dst(stream, item)
        pltpu.make_async_remote_copy(
            src_ref=ref,
            dst_ref=ref,
            send_sem=self.send_sem.at[stream, 0],
            recv_sem=self.recv_sem.at[stream, item],
            device_id=(self.blk, self.uly),
            device_id_type=MESH,
        ).wait_recv()

    def start(self):
        for s in self.streams:
            p, q = self.pq(s)
            self.send(s, self.blk, self.at(s, 1 - self.y, p, q), self.src(s))
        for s in self.streams:
            p, q = self.pq(s)
            for d in (1, 3):
                self.send(s, self.blk, self.at(s, self.y, (p + d) % 4, q), self.src(s))
            copy = pltpu.make_async_copy(self.src(s), self.dst(s, self.blk), self.local_sem.at[s])
            copy.start()
            self.local.append(copy)

    def second(self):
        for s in self.streams:
            p, q = self.pq(s)
            item = self.at(s, 1 - self.y, p, q)
            self.wait(s, item)
            for d in (1, 3):
                self.send(s, item, self.at(s, self.y, (p + d) % 4, q))
            for d in (1, 3):
                onward = self.at(s, self.y, p, (q + d) % 4)
                self.send(s, self.blk, onward, self.src(s))
                self.send(s, item, onward)

    def spread(self, s, item):
        p, q = self.pq(s)
        for d in (1, 3):
            self.send(s, item, self.at(s, self.y, p, (q + d) % 4))

    def third(self):
        for k, y in enumerate((self.y, 1 - self.y)):
            for s in self.streams:
                p, q = self.pq(s)
                for d in (3, 1):
                    item = self.at(s, y, (p + d) % 4, q)
                    self.wait(s, item)
                    if (d == 3) == (k == 0):
                        self.send(s, item, self.at(s, self.y, (p + 4 - d) % 4, q))
                    self.spread(s, item)
        for y in (self.y, 1 - self.y):
            for s in self.streams:
                p, q = self.pq(s)
                item = self.at(s, y, (p + 2) % 4, q)
                self.wait(s, item)
                self.spread(s, item)

    def fourth(self):
        for e in (0, 1, 3, 2):
            for k, y in enumerate((self.y, 1 - self.y)):
                for s in self.streams:
                    p, q = self.pq(s)
                    for d in (3, 1):
                        item = self.at(s, y, (p + e) % 4, (q + d) % 4)
                        self.wait(s, item)
                        if (d == 3) == (k == 0):
                            self.send(s, item, self.at(s, self.y, p, (q + 4 - d) % 4))

    def last(self):
        for e in (0, 1, 3, 2):
            for y in (self.y, 1 - self.y):
                for s in self.streams:
                    p, q = self.pq(s)
                    self.wait(s, self.at(s, y, (p + e) % 4, (q + 2) % 4))
        for copy in self.local:
            copy.wait()
        for copy in self.sent:
            copy.wait_send()


GATHER_SEMS = lambda *lead: [
    pltpu.SemaphoreType.DMA(lead + (2, Gather.sends)),
    pltpu.SemaphoreType.DMA(lead + (2, 32)),
    pltpu.SemaphoreType.DMA(lead + (2,)),
]


KEYS = 1024
KEYS_BACK = 512
ROWS = GROUP * CHUNK


def head_columns(ref, slot):
    return jnp.concatenate(
        [
            ref[slot * CHUNK : (slot + 1) * CHUNK, n * HEAD : (n + 1) * HEAD].T
            for n in range(GROUP)
        ],
        axis=1,
    )


def head_rows(ref, slot):
    return jnp.concatenate(
        [
            ref[slot * CHUNK : (slot + 1) * CHUNK, n * HEAD : (n + 1) * HEAD]
            for n in range(GROUP)
        ],
        axis=0,
    )


def key_block(kv_ref, step, keys):
    count = keys // CHUNK
    rows = kv_ref[pl.ds(step * count, count)].reshape(keys, 2 * HEAD)
    return rows[:, :HEAD], rows[:, HEAD:]


def dot(a, b):
    return jnp.dot(a, b, preferred_element_type=F32)


def key_places(step, keys):
    return lax.broadcasted_iota(jnp.int32, (keys, ROWS), 0) + step * keys


def dot_nt(a, b):
    return lax.dot_general(a, b, (((1,), (1,)), ((), ())), preferred_element_type=F32)


def forward_blocks(slot, first, last, turned_ref, kv_ref, limit_ref, acc_ref, stat_ref):
    turned = turned_ref[slot]
    limit = limit_ref[slot, 0:1, :]

    def step(n, carry):
        top, total = carry
        keys, values = key_block(kv_ref, n, KEYS)
        scores = jnp.where(key_places(n, KEYS) <= limit, dot(keys, turned), -1e30)
        new_top = jnp.maximum(top, jnp.max(scores, axis=0, keepdims=True))
        fade = jnp.exp2(top - new_top)
        probs = jnp.exp2(scores - new_top)
        total = total * fade + jnp.sum(probs, axis=0, keepdims=True)
        acc_ref[slot] = acc_ref[slot] * fade + dot(values.T, probs.astype(BF))
        return new_top, total

    top, total = lax.fori_loop(
        first, last, step, (stat_ref[slot, 0, 0:1, :], stat_ref[slot, 1, 0:1, :])
    )
    stat_ref[slot, 0, 0:1, :] = top
    stat_ref[slot, 1, 0:1, :] = total


def forward_end(slot, mixed_ref, lse_ref, acc_ref, stat_ref):
    top, total = stat_ref[slot, 0, 0:1, :], stat_ref[slot, 1, 0:1, :]
    out = acc_ref[slot] / total
    for n in range(GROUP):
        mixed_ref[slot * CHUNK : (slot + 1) * CHUNK, n * HEAD : (n + 1) * HEAD] = out[
            :, n * CHUNK : (n + 1) * CHUNK
        ].T.astype(BF)
    lse_ref[slot] = jnp.broadcast_to(top + jnp.log2(total), (8, ROWS))


def uly_others():
    y, z, x, blk, uly = place()
    return [(blk, (uly + 2) % 4), (blk, uly + 1 - 2 * (uly % 2)), (blk, 3 - uly)]


def ring_place(w):
    y, z, x, blk, uly = place()
    return (blk_of(w % 2, z, x), (w // 2) * 2 + uly % 2)


def ring_at():
    y, z, x, blk, uly = place()
    return (uly // 2) * 2 + y


def wait_arrival(ref, sem):
    pltpu.make_async_copy(ref, ref, sem).wait()


def remote(src, dst, send, recv, device):
    return pltpu.make_async_remote_copy(
        src_ref=src, dst_ref=dst, send_sem=send, recv_sem=recv, device_id=device, device_id_type=MESH
    )


class Deliver:
    def __init__(self):
        self.sent = []

    def send(self, src, dst, send, recv, device):
        y, z, x, blk, uly = place()
        here = jnp.logical_and(device[0] == blk, device[1] == uly)

        @pl.when(here)
        def _():
            pltpu.make_async_copy(src, dst, recv).start()

        @pl.when(jnp.logical_not(here))
        def _():
            remote(src, dst, send, recv, device).start()

        self.sent.append((here, src, dst, send, recv, device))

    def end(self):
        for here, *copy in self.sent:

            @pl.when(jnp.logical_not(here))
            def _():
                remote(*copy).wait_send()


class Ring:
    sends = 15

    def __init__(self, src, dst, y, order, way, send_sem, recv_sem):
        self.src, self.dst, self.y, self.order, self.way = src, dst, y, order, way
        self.send_sem, self.recv_sem = send_sem, recv_sem
        self.own_y, self.z, self.x, self.blk, self.uly = place()
        self.p = order * self.z + (1 - order) * self.x
        self.q = order * self.x + (1 - order) * self.z
        self.sent = []

    def at(self, y, p, q):
        order = self.order
        return blk_of(y, order * p + (1 - order) * q, order * q + (1 - order) * p)

    def index(self, p, q):
        return self.at(0, p, q)

    def send(self, p, q, dp, dq, src=None):
        ref = self.dst(self.at(self.y, p, q))
        target = self.at(self.own_y, (self.p + dp) % 4, (self.q + dq) % 4)
        copy = remote(
            ref if src is None else src, ref, self.send_sem.at[len(self.sent)],
            self.recv_sem.at[self.index(p, q)], (target, self.uly),
        )
        copy.start()
        self.sent.append(copy)

    def wait(self, p, q):
        wait_arrival(self.dst(self.at(self.y, p, q)), self.recv_sem.at[self.index(p, q)])

    def start(self):
        for d in (1, 3):
            self.send(self.p, self.q, d, 0, self.src)

    def second(self):
        for d in (4 - self.way, self.way):
            p = (self.p + d) % 4
            self.wait(p, self.q)
            if d == 4 - self.way:
                self.send(p, self.q, self.way, 0)

    def third(self):
        self.wait((self.p + 2) % 4, self.q)

    def spread(self, e):
        p = (self.p + e) % 4
        for d in (1, 3):
            self.send(p, self.q, 0, d, self.src if e == 0 else None)

    def fourth(self, e):
        p = (self.p + e) % 4
        for d in (4 - self.way, self.way):
            q = (self.q + d) % 4
            self.wait(p, q)
            if d == 4 - self.way:
                self.send(p, q, 0, self.way)

    def last(self):
        for e in (0, 1, 3, 2):
            self.wait((self.p + e) % 4, (self.q + 2) % 4)
        for copy in self.sent:
            copy.wait_send()


class Spread:
    def __init__(self, own, all_ref, send_sem, recv_sem, local_sem):
        self.own, self.all_ref = own, all_ref
        self.send_sem, self.recv_sem, self.local_sem = send_sem, recv_sem, local_sem
        self.w = ring_at()
        self.core = lax.axis_index("uly") % 2
        self.sibling = uly_others()[1]
        self.sent = []

    def piece(self, d, rows=slice(None), core=None):
        core = self.core if core is None else core
        ref = self.all_ref.at[core, (self.w + d) % 4]
        return ref if rows == slice(None) else ref.at[pl.ds(rows.start, rows.stop - rows.start)]

    def send(self, src, dst, recv, device):
        copy = remote(src, dst, self.send_sem.at[len(self.sent)], self.recv_sem.at[recv], device)
        copy.start()
        self.sent.append(copy)

    def pair(self, d, src=None):
        self.send(self.piece(d) if src is None else src, self.piece(d), 4 + d, self.sibling)

    def start(self):
        self.local = pltpu.make_async_copy(self.own, self.piece(0), self.local_sem)
        self.local.start()
        self.send(self.own, self.piece(0), 0, ring_place((self.w + 1) % 4))
        self.send(self.own, self.piece(0), 1, ring_place((self.w + 3) % 4))
        self.pair(0, self.own)

    def second(self):
        half = CHUNK // 2
        wait_arrival(self.piece(3), self.recv_sem.at[0])
        low = self.piece(3, slice(0, half))
        self.send(low, low, 2, ring_place((self.w + 1) % 4))
        self.pair(3)
        wait_arrival(self.piece(1), self.recv_sem.at[1])
        high = self.piece(1, slice(half, CHUNK))
        self.send(high, high, 3, ring_place((self.w + 3) % 4))
        self.pair(1)

    def third(self):
        half = CHUNK // 2
        wait_arrival(self.piece(2, slice(0, half)), self.recv_sem.at[2])
        wait_arrival(self.piece(2, slice(half, CHUNK)), self.recv_sem.at[3])
        self.pair(2)

    def last(self):
        for d in range(4):
            wait_arrival(self.piece(d, core=1 - self.core), self.recv_sem.at[4 + d])
        for copy in self.sent:
            copy.wait_send()
        self.local.wait()


SPREAD_SEMS = [pltpu.SemaphoreType.DMA((8,)), pltpu.SemaphoreType.DMA((8,)), pltpu.SemaphoreType.DMA]
FF_COLS = PADDED // 2


def forward_kernel(
    tokens_ref, cot_ref, length_hbm, set_hbm, qkv_hbm, w_out_hbm, gate_up_hbm, down_hbm, gains_hbm, freq_hbm,
    a_hbm, b_hbm, bkv_hbm,
    q_out, mixed_out, lse_out, kv_out, wq_out, wo_out, gate_all, up_all, down_all, rows_hbm, normed_out,
    resid_out, cot_out, nf_out, cot_all, limit_out, cos_out, sin_out, b_qkv_out, ao_out, a_out, bo_out,
    q_ref, mixed_ref, lse_ref, rows_out, normed_ref, resid_ref, cot_own, limit_ref, cos_ref, sin_ref,
    b_qkv_ref, ao_ref, a_ref, b_ref, bkv_ref, a_sets, b_sets, bkv_sets, turned_ref,
    length_ref, set_ref, qkv_ref, out_ref, gate_up_ref, down_ref, gains_ref, freq_ref, kv_all, wq_all, wo_all, rows, cot_in, kv_part, acc_ref, stat_ref, qkv_in, out_in, qkv_part, out_part,
    nf_own, cross_out, cross_in, qkv_pieces, out_pieces, ff_ref,
    *sems,
):
    y, z, x, blk, uly = place()
    core, h = uly % 2, uly // 2
    sems = list(sems)

    def take(count):
        got = sems[:count]
        del sems[:count]
        return got

    chunk = 2 * blk + h
    upper = chunk // 32
    home = (1 - h) * blk + h * (31 - blk)
    row_to = [[(home, hh * 2 + s) for hh in (0, 1)] for s in (0, 1)]
    row_from = [(b, hh * 2 + half) for b, hh in ((blk, 0), (31 - blk, 1)) for half in (0, 1)]
    lower = low_chunk(blk)
    out_to = [(2 * (blk % 16) + q // 2, (blk // 16) * 2 + q % 2) for q in range(4)]
    out_from = [(16 * h + blk // 2, u) for u in range(4)]
    sibling = uly_others()[1]
    set_sem = sems.pop()
    in_sem = sems.pop()
    in_copies = [
        pltpu.make_async_copy(src, dst, in_sem.at[n])
        for n, (src, dst) in enumerate(
            (
                (qkv_hbm, qkv_ref), (w_out_hbm, out_ref), (gate_up_hbm, gate_up_ref), (down_hbm, down_ref),
                (length_hbm, length_ref), (set_hbm, set_ref), (gains_hbm, gains_ref), (freq_hbm, freq_ref),
            )
        )
    ]
    for copy in in_copies:
        copy.start()
    set_copies = [
        pltpu.make_async_copy(src, dst, set_sem.at[n])
        for n, (src, dst) in enumerate(
            ((a_hbm.at[pl.ds(0, 4)], a_sets), (b_hbm.at[pl.ds(0, 2)], b_sets), (bkv_hbm, bkv_sets))
        )
    ]
    for copy in set_copies:
        copy.start()

    def prepare():
        qkv_pieces[...] = jnp.zeros_like(qkv_pieces)
        out_pieces[...] = jnp.zeros_like(out_pieces)
        for copy in in_copies:
            copy.wait()
        group = GROUP * HEAD
        for hh in (0, 1):
            qkv_pieces[2 * hh, :12] = qkv_ref[:, hh * group : hh * group + 512]
            for place_at, start, size in (
                (0, hh * group + 512, 256),
                (256, HEADS * HEAD + hh * HEAD, HEAD),
                (384, HEADS * HEAD + 256 + hh * HEAD, HEAD),
            ):
                qkv_pieces[2 * hh + 1, :12, place_at : place_at + size] = qkv_ref[:, start : start + size]
        for q in range(4):
            out_pieces[q, :12] = out_ref[:, q * 384 : (q + 1) * 384]
        for n in range(3):
            part = (gate_up_ref[n] if n < 2 else down_ref[...]).astype(F32)
            none = jnp.zeros((48, 64), F32)
            left = jnp.concatenate([part, none], axis=1)
            right = jnp.concatenate([none, part], axis=1)
            ff_ref[n] = jnp.where(jnp.broadcast_to(core, (48, PADDED)) == 1, right, left).astype(BF)

    greet(
        ring_others() + uly_others() + [(blk_of(1 - y, z, x), (uly + 2) % 4)]
        + row_to[0] + row_to[1] + row_from + out_to + out_from,
        prepare,
    )

    length = length_ref[0] * (1 - core) + length_ref[1] * core

    deliver = Deliver()
    piece_send, piece_recv, row_send, row_recv = take(4)
    for q in range(4):
        deliver.send(qkv_pieces.at[q], qkv_in.at[uly], piece_send.at[q], piece_recv.at[uly], (blk, q))
    for q in range(4):
        deliver.send(out_pieces.at[q], out_in.at[uly], piece_send.at[4 + q], piece_recv.at[4 + uly], out_to[q])
    for s in (0, 1):
        for hh in (0, 1):
            deliver.send(
                tokens_ref.at[s], rows.at[upper, core], row_send.at[s * 2 + hh],
                row_recv.at[upper * 2 + core], row_to[s][hh],
            )

    wide = PADDED // 2
    gathered = (gate_all, up_all, down_all)
    ff_send, ff_recv, y_send, y_recv, y_local = take(5)
    other_blk = blk_of(1 - y, z, x)

    def ff_part(n, half):
        return ff_ref.at[n, :, pl.ds(pl.multiple_of(half * wide, 128), wide)]

    y_copies = []
    for n, ref in enumerate(gathered):
        copy = remote(ff_part(n, 1 - y), ref.at[blk], y_send.at[n], y_recv.at[n], (other_blk, uly))
        copy.start()
        y_copies.append(copy)
        copy = pltpu.make_async_copy(ff_part(n, y), ref.at[blk], y_local.at[n])
        copy.start()
        y_copies.append(copy)
    own_ff, other_ff = (
        [
            Ring(
                ff_part(n, y) if k == 0 else ref.at[other_blk],
                lambda item, ref=ref: ref.at[item],
                y if k == 0 else 1 - y,
                y if k == 0 else 1 - y,
                (1, 3, 1 + 2 * k)[n],
                ff_send.at[k, n], ff_recv.at[k, n],
            )
            for n, ref in enumerate(gathered)
        ]
        for k in (0, 1)
    )
    for ring in own_ff:
        ring.start()

    picked = lax.broadcasted_iota(jnp.int32, (48, 64), 1)
    picked = jnp.where(picked % 16 < 12, picked // 16 * 12 + picked % 16, -1)
    picked = jnp.where(picked == lax.broadcasted_iota(jnp.int32, (48, 64), 0), 1.0, 0.0).astype(BF)
    for u in range(4):
        wait_arrival(qkv_in.at[u], piece_recv.at[u])
    qkv_part[...] = dot(picked, qkv_in[...].reshape(64, 512)).astype(BF)
    wq = Gather(
        lambda s: qkv_part.at[:, pl.ds(256 * s, 256)],
        lambda s, item: wq_all.at[
            core, pl.ds(pl.multiple_of(item * 48, 16), 48), pl.ds(256 * s, 256)
        ],
        *take(3),
    )
    wq.start()
    for u in range(4):
        wait_arrival(out_in.at[u], piece_recv.at[4 + u])
    out_part[...] = dot(picked, out_in[...].reshape(64, 384)).astype(BF)
    for s in (0, 1):
        deliver.send(
            cot_ref.at[s], cot_in.at[core], row_send.at[4 + s], row_recv.at[4 + core], (home, upper * 2 + s)
        )

    def out_columns(item, s):
        start = ((item % 2) * 2 + core) * 384
        return pl.ds(pl.multiple_of(start + 128 * s, 128), 128 + 128 * s)

    wo = Gather(
        lambda s: out_part.at[:, pl.ds(128 * s, 128 + 128 * s)],
        lambda s, item: wo_all.at[pl.ds(pl.multiple_of((item // 2) * 48, 16), 48), out_columns(item, s)],
        *take(3),
    )
    rings = own_ff + other_ff
    def tables(slot):
        at = lower if slot == 0 else 63 - lower
        row = lax.broadcasted_iota(jnp.int32, (CHUNK, HEAD), 0) + at * CHUNK
        angle = row.astype(F32) * freq_ref[...]
        first = lax.broadcasted_iota(jnp.int32, (CHUNK, HEAD), 1) < HEAD // 2
        sine = jnp.sin(angle)
        cos_ref[slot * CHUNK : (slot + 1) * CHUNK, :] = jnp.cos(angle)
        sin_ref[slot * CHUNK : (slot + 1) * CHUNK, :] = jnp.where(first, -sine, sine)
        row = lax.broadcasted_iota(jnp.int32, (8, ROWS), 1) % CHUNK + at * CHUNK
        limit_ref[slot] = jnp.minimum(row, length - 1)

    stat_ref[:, 0] = jnp.full((2, 8, ROWS), -1e30, F32)
    stat_ref[:, 1] = jnp.zeros((2, 8, ROWS), F32)
    acc_ref[...] = jnp.zeros_like(acc_ref)
    own_set = set_ref[0] * (1 - core) + set_ref[1] * core
    for copy in set_copies:
        copy.wait()
    for sets, ref in ((a_sets, a_ref), (b_sets, b_ref), (bkv_sets, bkv_ref)):
        for n in range(ref.shape[0]):
            ref[n] = choose(own_set, lambda c: sets[n, c])
    group = GROUP * HEAD
    group_at = pl.ds(pl.multiple_of(h * group, 128), group)
    head_at = pl.ds(pl.multiple_of(h * HEAD, 128), HEAD)
    ao_ref[...] = a_ref[3, :, group_at]
    b_qkv_ref[...] = jnp.zeros_like(b_qkv_ref)
    b_qkv_ref[:16, :group] = b_ref[0, :, group_at]
    b_qkv_ref[16:32, group : group + HEAD] = bkv_ref[0, :, head_at]
    b_qkv_ref[32:, group + HEAD :] = bkv_ref[1, :, head_at]
    a_qkv = a_ref[:3].reshape(48, D)
    bo_ref = b_ref.at[1]

    def bias(n):
        at = h * GROUP + n if n < GROUP else HEADS + 2 * (n - GROUP) + h
        return gains_ref[pl.ds(2 * D_TILES + at, 1), :]

    wq.second()
    tables(0)
    wq.third()
    tables(1)
    wq.fourth()
    for n in range(3):
        y_copies[2 * n].wait_recv()
    for ring in other_ff:
        ring.start()
    for ring in rings:
        ring.spread(0)

    for n in range(4):
        wait_arrival(rows.at[n // 2, n % 2], row_recv.at[n])
        value = rows[n // 2, n % 2].astype(F32)
        at = slice(n * 64, (n + 1) * 64)
        rows_out[at, :] = rows[n // 2, n % 2]
        normed_ref[at, :] = (value * norm_scale(value) * gain(gains_ref, 0)).astype(BF)
    latent = dot_nt(normed_ref[...], a_qkv)
    adapted = dot(latent.astype(BF), b_qkv_ref[...])
    wq.last()
    pair_send, pair_recv = take(2)

    def pair_copy(ref, n):
        return remote(ref, ref, pair_send.at[n], pair_recv.at[n], sibling)

    pair_copy(wq_all.at[core], 0).start()
    wo.start()
    pair_copy(wq_all.at[core], 0).wait_send()
    pair_copy(wq_all.at[1 - core], 0).wait_recv()

    cos_table, sine_table = cos_ref[...], sin_ref[...]

    def turn(head):
        return head * cos_table + pltpu.roll(head, HEAD // 2, 1) * sine_table

    def query(n, head):
        q_ref[:, n * HEAD : (n + 1) * HEAD] = (turn(head + bias(n)) * (HEAD ** (-0.5) * LOG2E)).astype(BF)

    pairs = dot(normed_ref[...], wq_all[1, :, 256:]) + adapted[:, 768:]
    for n, head in ((0, turn(pairs[:, :HEAD] + bias(6))), (1, pairs[:, HEAD:] + bias(7))):
        at = slice(n * HEAD, (n + 1) * HEAD)
        kv_part[0, :, at] = head[:CHUNK].astype(BF)
        kv_part[1, :, at] = head[CHUNK:].astype(BF)
    kv = Gather(
        lambda s: kv_part.at[s],
        lambda s, item: kv_all.at[low_chunk(item) if s == 0 else 63 - low_chunk(item)],
        *take(3),
    )
    kv.start()
    heads = dot(normed_ref[...], wq_all[1, :, :256]) + adapted[:, 512:768]
    for n in (4, 5):
        query(n, heads[:, (n - 4) * HEAD : (n - 3) * HEAD])
    kv.second()
    for ring in rings:
        ring.second()
    wo.second()
    heads = dot(normed_ref[...], wq_all[0]) + adapted[:, :512]
    for n in range(4):
        query(n, heads[:, n * HEAD : (n + 1) * HEAD])
    kv.third()
    for ring in rings:
        ring.third()
    wo.third()
    kv.fourth()
    wo.fourth()

    for half in (0, 1):
        wait_arrival(cot_in.at[half], row_recv.at[4 + half])
        start = ((1 - h) * lower + h * (63 - lower)) * CHUNK + half * 64
        at = lax.broadcasted_iota(jnp.int32, (64, D), 0) + start
        cot_own[half * 64 : (half + 1) * 64, :] = jnp.where(
            at < length, cot_in[half].astype(F32), 0.0
        ).astype(BF)
    cot_spread = Spread(cot_own, cot_all, *take(3))
    cot_spread.start()
    kv.last()
    for e in (1, 3, 2):
        for ring in rings:
            ring.spread(e)
    (out_sem,) = take(1)
    copies = []

    def keep(*pairs):
        for src, dst in pairs:
            copies.append(pltpu.make_async_copy(src, dst, out_sem.at[len(copies)]))
            copies[-1].start()

    keep(
        (kv_all, kv_out), (wq_all, wq_out), (q_ref, q_out), (rows_out, rows_hbm), (normed_ref, normed_out),
        (cot_own, cot_out), (limit_ref, limit_out), (cos_ref, cos_out), (sin_ref, sin_out),
        (b_qkv_ref, b_qkv_out), (ao_ref, ao_out), (a_ref.at[pl.ds(0, 3)], a_out), (b_ref.at[1], bo_out),
    )
    wo.last()

    def wo_columns(c, n):
        return wo_all.at[:, pl.ds(pl.multiple_of((2 * n + c) * 384, 128), 384)]

    for n in (0, 1):
        pair_copy(wo_columns(core, n), 1 + n).start()
    for slot in (0, 1):
        turned_ref[slot] = head_columns(q_ref, slot)
    args = (turned_ref, kv_all, limit_ref, acc_ref, stat_ref)

    def end(slot):
        forward_end(slot, mixed_ref, lse_ref, acc_ref, stat_ref)

    blocks = KEYS // CHUNK
    middle = CHUNKS // 2 // blocks
    forward_blocks(0, 0, lower // blocks + 1, *args)
    forward_blocks(1, middle, (63 - lower) // blocks + 1, *args)
    end(0)
    for ring in rings:
        ring.fourth(0)
    cot_spread.second()
    forward_blocks(1, 0, middle // 2, *args)
    for ring in rings:
        ring.fourth(1)
    cot_spread.third()
    forward_blocks(1, middle // 2, middle, *args)
    end(1)
    for n in (0, 1):
        pair_copy(wo_columns(core, n), 1 + n).wait_send()
        pair_copy(wo_columns(1 - core, n), 1 + n).wait_recv()
    keep((wo_all, wo_out), (mixed_ref, mixed_out), (lse_ref, lse_out))

    def project(slot):
        mixed = mixed_ref[pl.ds(pl.multiple_of(slot * CHUNK, CHUNK), CHUNK), :]
        lifted = dot(dot_nt(mixed, ao_ref[...]).astype(BF), bo_ref[...])
        return dot(mixed, wo_all[...]) + lifted

    (cross_sem,) = take(1)
    cross_out[...] = project(1 - h).astype(BF)
    cross = remote(cross_out, cross_in, cross_sem.at[0], cross_sem.at[1], uly_others()[0])
    cross.start()
    for ring in rings:
        ring.fourth(3)
    mine = project(h) + rows_out[pl.ds(pl.multiple_of(h * CHUNK, CHUNK), CHUNK), :].astype(F32)
    for ring in rings:
        ring.fourth(2)
    cross.wait()
    residual = mine + cross_in[...].astype(F32)
    resid_ref[...] = residual
    keep((resid_ref, resid_out))
    nf_own[...] = (residual * norm_scale(residual) * gain(gains_ref, D_TILES)).astype(BF)
    keep((nf_own, nf_out))
    cot_spread.last()
    for ring in rings:
        ring.last()
    for n in range(3):
        y_copies[2 * n].wait_send()
        y_copies[2 * n + 1].wait()
    deliver.end()
    for copy in copies:
        copy.wait()


def forward(*args):
    weight = HELD((32, 48, FF_COLS), BF)
    group = GROUP * HEAD
    dma = pltpu.SemaphoreType.DMA
    spread = HELD((2, 4, CHUNK, D), BF)
    return pl.pallas_call(
        forward_kernel,
        out_shape=(
            HELD((2 * CHUNK, group), BF),
            HELD((2 * CHUNK, group), BF),
            HELD((2, 8, ROWS), F32),
            HELD((CHUNKS, CHUNK, 2 * HEAD), BF),
            HELD((2, D, 512), BF),
            HELD((D // 2, D), BF),
            weight, weight, weight,
            HELD((2 * CHUNK, D), BF),
            HELD((2 * CHUNK, D), BF),
            HELD((CHUNK, D), F32),
            HELD((CHUNK, D), BF),
            HELD((CHUNK, D), BF),
            spread,
            HELD((2, 8, ROWS), jnp.int32),
            HELD((2 * CHUNK, HEAD), F32),
            HELD((2 * CHUNK, HEAD), F32),
            HELD((48, 1024), BF),
            HELD((16, group), BF),
            HELD((3, 16, D), BF),
            HELD((16, D), BF),
        ),
        in_specs=[ANY] * 13,
        out_specs=(ANY,) * 22,
        scratch_shapes=[
            pltpu.VMEM((2 * CHUNK, group), BF),
            pltpu.VMEM((2 * CHUNK, group), BF),
            pltpu.VMEM((2, 8, ROWS), F32),
            pltpu.VMEM((2 * CHUNK, D), BF),
            pltpu.VMEM((2 * CHUNK, D), BF),
            pltpu.VMEM((CHUNK, D), F32),
            pltpu.VMEM((CHUNK, D), BF),
            pltpu.VMEM((2, 8, ROWS), jnp.int32),
            pltpu.VMEM((2 * CHUNK, HEAD), F32),
            pltpu.VMEM((2 * CHUNK, HEAD), F32),
            pltpu.VMEM((48, 1024), BF),
            pltpu.VMEM((16, group), BF),
            pltpu.VMEM((4, 16, D), BF),
            pltpu.VMEM((2, 16, D), BF),
            pltpu.VMEM((2, 16, 2 * HEAD), BF),
            pltpu.VMEM((4, SETS, 16, D), BF),
            pltpu.VMEM((2, SETS, 16, D), BF),
            pltpu.VMEM((2, SETS, 16, 2 * HEAD), BF),
            pltpu.VMEM((2, HEAD, ROWS), BF),
            pltpu.SMEM((2,), jnp.int32),
            pltpu.SMEM((2,), jnp.int32),
            pltpu.VMEM((12, 2048), BF),
            pltpu.VMEM((12, D), BF),
            pltpu.VMEM((2, 48, FF // 4), BF),
            pltpu.VMEM((48, FF // 4), BF),
            pltpu.VMEM((40, 128), F32),
            pltpu.VMEM((1, 128), F32),
            pltpu.VMEM((CHUNKS, CHUNK, 2 * HEAD), BF),
            pltpu.VMEM((2, D, 512), BF),
            pltpu.VMEM((D // 2, D), BF),
            pltpu.VMEM((2, 2, 64, D), BF),
            pltpu.VMEM((2, 64, D), BF),
            pltpu.VMEM((2, CHUNK, 2 * HEAD), BF),
            pltpu.VMEM((2, HEAD, ROWS), F32),
            pltpu.VMEM((2, 2, 8, ROWS), F32),
            pltpu.VMEM((4, 16, 512), BF),
            pltpu.VMEM((4, 16, 384), BF),
            pltpu.VMEM((48, 512), BF),
            pltpu.VMEM((48, 384), BF),
            pltpu.VMEM((CHUNK, D), BF),
            pltpu.VMEM((CHUNK, D), BF),
            pltpu.VMEM((CHUNK, D), BF),
            pltpu.VMEM((4, 16, 512), BF),
            pltpu.VMEM((4, 16, 384), BF),
            pltpu.VMEM((3, 48, PADDED), BF),
            dma((8,)), dma((8,)), dma((6,)), dma((6,)),
            dma((2, 3, Ring.sends)), dma((2, 3, 16)), dma((3,)), dma((3,)), dma((3,)),
        ]
        + GATHER_SEMS()
        + GATHER_SEMS()
        + [dma((3,)), dma((3,))]
        + GATHER_SEMS()
        + SPREAD_SEMS
        + [dma((18,)), dma((2,)), dma((8,)), dma((3,))],
        compiler_params=pltpu.CompilerParams(
            collective_id=1, has_side_effects=True, vmem_limit_bytes=48 * 2**20
        ),
        name="forward",
    )(*args)


class RingSum:
    @staticmethod
    def scratch():
        piece, half = (CHUNK, D), (CHUNK // 2, D)
        return [
            pltpu.VMEM((2,) + half, BF),
            pltpu.VMEM((2,) + piece, BF),
            pltpu.VMEM(piece, BF),
            pltpu.VMEM((2,) + piece, BF),
            pltpu.SemaphoreType.DMA((4,)),
            pltpu.SemaphoreType.DMA((4,)),
        ]

    scratches = 6

    def __init__(self, term, scratch):
        self.term = term
        self.halves, self.last_in, self.far, self.near, self.send_sem, self.recv_sem = scratch
        self.w = ring_at()
        self.sent = []

    def send(self, src, dst, recv, d):
        copy = remote(
            src, dst, self.send_sem.at[recv], self.recv_sem.at[recv], ring_place((self.w + d) % 4)
        )
        copy.start()
        self.sent.append(copy)

    def first(self):
        half = CHUNK // 2
        self.far[...] = self.term(2).astype(BF)
        self.send(self.far.at[pl.ds(0, half)], self.halves.at[0], 0, 1)
        self.send(self.far.at[pl.ds(half, half)], self.halves.at[1], 1, 3)

    def second(self):
        half = CHUNK // 2
        for k, d in ((0, 1), (1, 3)):
            total = self.term(d)
            wait_arrival(self.halves.at[k], self.recv_sem.at[k])
            rows = slice(k * half, (k + 1) * half)
            other = slice((1 - k) * half, (2 - k) * half)
            self.near[k, rows] = (total[rows] + self.halves[k].astype(F32)).astype(BF)
            self.near[k, other] = total[other].astype(BF)
            self.send(self.near.at[k], self.last_in.at[k], 2 + k, d)

    def third(self):
        total = self.term(0)
        for k in (0, 1):
            wait_arrival(self.last_in.at[k], self.recv_sem.at[2 + k])
            total += self.last_in[k].astype(F32)
        for copy in self.sent:
            copy.wait_send()
        return total


def ff_kernel(
    set_ref, own_hbm, cot_hbm, gate_hbm, up_hbm, down_hbm, a_wide, a_down, b_wide, b_ff,
    grad_out, down_out, cols_out, wide_out,
    cols_ref, wide_ref, x_ref, cot_ref, gate_w, up_w, down_w, b_cols, a_cols, hidden_ref, grad_gate, grad_up,
    grad_hidden, own_ref, terms, pair, total_ref, down_sum, a_ff, b_out, wide_sets, down_sets, out_sets,
    ff_sets, sems, out_sems, pair_send, pair_recv, *scratch,
):
    y, z, x, blk, uly = place()
    core = uly % 2
    scratch = list(scratch)

    def take(count):
        got = scratch[:count]
        del scratch[:count]
        return got

    first = (35 * uly) // 2 * 128 + y * FF_COLS
    columns = pl.ds(pl.multiple_of(first, 128), FF_COLS)
    pairs = (
        (own_hbm, own_ref), (down_hbm, down_w), (cot_hbm, cot_ref), (gate_hbm, gate_w), (up_hbm, up_w),
        (a_wide.at[pl.ds(4, 2)], wide_sets), (a_down.at[:, :, columns], down_sets), (b_wide.at[2], out_sets),
        (b_ff.at[:, :, :, columns], ff_sets),
    )
    copies = [pltpu.make_async_copy(src, dst, sems.at[n]) for n, (src, dst) in enumerate(pairs)]
    for copy in copies[:1] + copies[5:] + copies[1:5]:
        copy.start()
    at = lax.broadcasted_iota(jnp.int32, (16, FF_COLS), 1) + (y * FF_COLS - 64 * core)
    inside = jnp.logical_and(at >= 0, at < FF // 4)

    def keep(v):
        return jnp.where(inside, v.astype(F32), 0.0).astype(BF)

    def prepare():
        for copy in copies[5:]:
            copy.wait()
        for s in (0, 1):
            number = set_ref[s]
            a_cols[s] = keep(choose(number, lambda c: down_sets[c]))
            b_out[s] = choose(number, lambda c: out_sets[c])
            for n in (0, 1):
                b_cols[s, n] = keep(choose(number, lambda c: ff_sets[n, c]))
                a_ff[s, 16 * n : 16 * n + 16] = choose(number, lambda c: wide_sets[n, c])
        cols_ref[...] = jnp.zeros_like(cols_ref)

    sibling = uly_others()[1]
    greet([sibling, (blk_of(1 - y, z, x), uly), (blk_of(1 - y, z, x), (uly + 2) % 4)], prepare)
    here = pl.ds(pl.multiple_of(y * FF_COLS, 128), FF_COLS)
    copies[0].wait()
    spread = Spread(own_ref, x_ref, *take(3))
    spread.start()

    def flat(ref, s):
        return ref[s].reshape(4 * CHUNK, D)

    order = (1 - core, core)
    copies[1].wait()
    copies[2].wait()
    latent_cots = []
    for k, s in enumerate(order):
        cot = flat(cot_ref, s)
        latent_cots.append(dot_nt(cot, b_out[s]))
        grad_hidden[k] = dot(cot, down_w[...]) + dot(latent_cots[k].astype(BF), a_cols[s])
        (spread.second, spread.third)[k]()
    copies[3].wait()
    copies[4].wait()
    spread.last()

    def pair_copy(n, d):
        at = (ring_at() + d) % 4
        return remote(
            terms.at[n, 0, at], pair.at[n, at], pair_send.at[n, d], pair_recv.at[n, d], sibling
        )

    def term(n, d):
        at = (ring_at() + d) % 4
        wait_arrival(pair.at[n, at], pair_recv.at[n, d])
        return terms[n, 1, at].astype(F32) + pair[n, at].astype(F32)

    ring = RingSum(lambda d: term(0, d), take(RingSum.scratches))
    for k, s in enumerate(order):
        rows = flat(x_ref, s)
        latent = dot_nt(rows, a_ff[s])
        low = latent.astype(BF)
        gate = dot(rows, gate_w[...]) + dot(low[:, :16], b_cols[s, 0])
        sigmoid = jax.nn.sigmoid(gate)
        silu = gate * sigmoid
        grad_up[...] = (grad_hidden[k] * silu).astype(BF)
        slope = grad_hidden[k] * (sigmoid * (1.0 + gate * (1.0 - sigmoid)))
        up = dot(rows, up_w[...]) + dot(low[:, 16:], b_cols[s, 1])
        grad_gate[...] = (slope * up).astype(BF)
        hidden_ref[...] = (silu * up).astype(BF)
        back_gate = dot_nt(grad_gate[...], b_cols[s, 0])
        back_up = dot_nt(grad_up[...], b_cols[s, 1])
        grads = (
            dot_nt(grad_gate[...], gate_w[...])
            + dot_nt(grad_up[...], up_w[...])
            + dot(back_gate.astype(BF), a_ff[s, :16])
            + dot(back_up.astype(BF), a_ff[s, 16:])
        )
        terms[0, k] = grads.astype(BF).reshape(4, CHUNK, D)
        if k == 0:
            for d in (2, 1, 3, 0):
                pair_copy(0, d).start()
        else:
            ring.first()
        latent_down = dot_nt(hidden_ref[...], a_cols[s])
        down = dot_nt(hidden_ref[...], down_w[...]) + dot(latent_down.astype(BF), b_out[s])
        terms[1, k] = down.astype(BF).reshape(4, CHUNK, D)
        if k == 0:
            for d in (2, 1, 3, 0):
                pair_copy(1, d).start()
        else:
            ring.second()

        def put(ref, n, value, at=slice(None)):
            ref[pl.ds(pl.multiple_of((2 * n + s) * 16, 16), 16), at] = value.astype(BF)

        def turned(value):
            return value.T.astype(BF)

        put(cols_ref, 0, dot(turned(latent_cots[k]), hidden_ref[...]), here)
        put(cols_ref, 1, dot(turned(latent[:, :16]), grad_gate[...]), here)
        put(cols_ref, 2, dot(turned(latent[:, 16:]), grad_up[...]), here)
        put(wide_ref, 0, dot(turned(back_gate), rows))
        put(wide_ref, 1, dot(turned(back_up), rows))
        put(wide_ref, 2, dot(turned(latent_down), flat(cot_ref, s)))
    outs = [
        pltpu.make_async_copy(src, dst, out_sems.at[n])
        for n, (src, dst) in enumerate(
            ((cols_ref, cols_out), (wide_ref, wide_out), (down_sum, down_out), (total_ref, grad_out))
        )
    ]
    outs[0].start()
    outs[1].start()
    for d in range(4):
        down_sum[(ring_at() + d) % 4] = term(1, d).astype(BF)
    outs[2].start()
    total_ref[...] = ring.third()
    outs[3].start()
    for n in (0, 1):
        for d in range(4):
            pair_copy(n, d).wait_send()
    for copy in outs:
        copy.wait()


def feed_forward(*args):
    dma = pltpu.SemaphoreType.DMA
    weight = pltpu.VMEM((D, FF_COLS), BF)
    rows = pltpu.VMEM((4 * CHUNK, FF_COLS), BF)
    pieces = (4, CHUNK, D)
    return pl.pallas_call(
        ff_kernel,
        out_shape=(
            HELD((CHUNK, D), F32),
            HELD(pieces, BF),
            HELD((96, PADDED), BF),
            HELD((96, D), BF),
        ),
        in_specs=[pl.BlockSpec(memory_space=pltpu.SMEM)] + [ANY] * 9,
        out_specs=(ANY,) * 4,
        scratch_shapes=[
            pltpu.VMEM((96, PADDED), BF), pltpu.VMEM((96, D), BF),
            pltpu.VMEM((2,) + pieces, BF), pltpu.VMEM((2,) + pieces, BF),
            weight, weight, weight,
            pltpu.VMEM((2, 2, 16, FF_COLS), BF), pltpu.VMEM((2, 16, FF_COLS), BF),
            rows, rows, rows,
            pltpu.VMEM((2, 4 * CHUNK, FF_COLS), F32),
            pltpu.VMEM((CHUNK, D), BF),
            pltpu.VMEM((2, 2) + pieces, BF), pltpu.VMEM((2,) + pieces, BF),
            pltpu.VMEM((CHUNK, D), F32), pltpu.VMEM(pieces, BF),
            pltpu.VMEM((2, 32, D), BF), pltpu.VMEM((2, 16, D), BF),
            pltpu.VMEM((2, SETS, 16, D), BF), pltpu.VMEM((SETS, 16, FF_COLS), BF),
            pltpu.VMEM((SETS, 16, D), BF), pltpu.VMEM((2, SETS, 16, FF_COLS), BF),
            dma((9,)), dma((4,)), dma((2, 4)), dma((2, 4)),
        ]
        + SPREAD_SEMS
        + RingSum.scratch(),
        compiler_params=pltpu.CompilerParams(
            collective_id=4, has_side_effects=True, vmem_limit_bytes=62 * 2**20
        ),
        name="feed_forward",
    )(*args)


def backward_blocks(slot, first, last, turned_ref, rows_ref, dot_ref, kv_ref, limit_ref, lse_ref, dkv_ref, acc_ref):
    limit = limit_ref[slot, 0:1, :]
    lse = lse_ref[slot, 0:1, :]
    row_dot = dot_ref[slot, 0:1, :]

    def step(n, carry):
        keys, values = key_block(kv_ref, n, KEYS_BACK)
        scores = jnp.where(key_places(n, KEYS_BACK) <= limit, dot(keys, turned_ref[0, slot]), -1e30)
        probs = jnp.exp2(scores - lse)
        grad_probs = dot(values, turned_ref[1, slot])
        grad_scores = (probs * (grad_probs - row_dot)).astype(BF)
        acc_ref[slot] += dot(keys.T, grad_scores)
        at = pl.ds(pl.multiple_of(n * KEYS_BACK, KEYS_BACK), KEYS_BACK)
        dkv_ref[at, :HEAD] += dot(grad_scores, rows_ref[0, slot])
        dkv_ref[at, HEAD:] += dot(probs.astype(BF), rows_ref[1, slot])
        return carry

    lax.fori_loop(first, last, step, 0)


class Reduce:
    @staticmethod
    def scratch(shape):
        return [
            pltpu.VMEM((2, 3, 2, 4) + shape, BF),
            pltpu.VMEM((2, 3, 2) + shape, BF),
            pltpu.VMEM((2,) + shape, BF),
            pltpu.VMEM((2, 4, 2) + shape, BF),
            pltpu.VMEM((2, 2) + shape, BF),
            pltpu.SemaphoreType.DMA((2, 10)),
            pltpu.SemaphoreType.DMA((2, 10)),
        ]

    scratches = 7

    def __init__(self, part, scratch):
        self.part = part
        self.buf_q, self.buf_p, self.buf_y, self.sum_p, self.sum_y, self.send_sem, self.recv_sem = scratch
        self.y, self.z, self.x, self.blk, self.uly = place()
        self.pq = ((self.x, self.z), (self.z, self.x))
        self.flying = []

    def send(self, src, dst, half, n, y, p, q):
        target = blk_of(y, q, p) if half == 0 else blk_of(y, p, q)
        copy = remote(
            src, dst, self.send_sem.at[half, n], self.recv_sem.at[half, n], (target, self.uly)
        )
        copy.start()
        self.flying.append(copy)

    def land(self):
        for copy in self.flying:
            copy.wait()
        self.flying = []

    def first(self):
        for d in (2, 1, 3):
            for half in (0, 1):
                p, q = self.pq[half]
                to = (q + d) % 4
                for y in (0, 1):
                    src = self.part.at[0, y, to] if half == 0 else self.part.at[1, y, :, to]
                    self.send(
                        src, self.buf_q.at[half, d - 1, y], half, (d - 1) * 2 + y, self.y, p, to
                    )

    def second(self):
        self.land()
        for d in (2, 1, 3, 0):
            for half in (0, 1):
                p, q = self.pq[half]
                to = (p + d) % 4
                for y in (0, 1):
                    own = self.part[0, y, q, to] if half == 0 else self.part[1, y, to, q]
                    total = own.astype(F32)
                    for n in range(3):
                        total += self.buf_q[half, n, y, to].astype(F32)
                    self.sum_p[half, d, y] = total.astype(BF)
                if d > 0:
                    self.send(
                        self.sum_p.at[half, d], self.buf_p.at[half, d - 1], half, 5 + d, self.y, to, q
                    )

    def third(self):
        self.land()
        for k in (1, 0):
            for half in (0, 1):
                p, q = self.pq[half]
                y = self.y if k == 0 else 1 - self.y
                total = self.sum_p[half, 0, y].astype(F32)
                for n in range(3):
                    total += self.buf_p[half, n, y].astype(F32)
                self.sum_y[half, k] = total.astype(BF)
                if k == 1:
                    self.send(self.sum_y.at[half, 1], self.buf_y.at[half], half, 9, 1 - self.y, p, q)

    def fourth(self):
        self.land()
        return [self.sum_y[half, 0].astype(F32) + self.buf_y[half].astype(F32) for half in (0, 1)]


class Shed:
    @staticmethod
    def scratch(shape):
        return [
            pltpu.VMEM((2, 4) + shape, BF),
            pltpu.VMEM((2, 4) + shape, BF),
            pltpu.VMEM((2, 2, 4) + shape, BF),
            pltpu.VMEM((4, 2) + shape, BF),
            pltpu.VMEM((3, 2) + shape, BF),
            pltpu.VMEM((2,) + shape, BF),
            pltpu.VMEM(shape, BF),
            pltpu.SemaphoreType.DMA((10,)),
            pltpu.SemaphoreType.DMA((10,)),
        ]

    scratches = 9

    def __init__(self, part, half, rows, order, scratch):
        self.part, self.half, self.rows, self.order = part, half, rows, order
        (
            self.buf_far, self.sum_mid, self.buf_in, self.sum_p, self.buf_p, self.sum_y, self.buf_y,
            self.send_sem, self.recv_sem,
        ) = scratch
        self.y, self.z, self.x, self.blk, self.uly = place()
        self.p, self.q = (self.x, self.z) if order == 0 else (self.z, self.x)
        self.flying = []

    def line(self, y, q):
        rows = pl.ds(*self.rows)
        if self.order == 0:
            return self.part.at[self.half, y, q, :, rows]
        return self.part.at[self.half, y, :, q, rows]

    def value(self, y, q, p):
        start, size = self.rows
        z, x = (q, p) if self.order == 0 else (p, q)
        return self.part[self.half, y, z, x, start : start + size].astype(F32)

    def send(self, src, dst, n, y, p, q):
        target = blk_of(y, q, p) if self.order == 0 else blk_of(y, p, q)
        copy = remote(src, dst, self.send_sem.at[n], self.recv_sem.at[n], (target, self.uly))
        copy.start()
        self.flying.append(copy)

    def land(self):
        for copy in self.flying:
            copy.wait()
        self.flying = []

    def first(self):
        for y, d in ((0, 1), (1, 3)):
            to = (self.q + d) % 4
            self.send(self.line(y, (self.q + 2) % 4), self.buf_far.at[y], y, self.y, self.p, to)
        for y, d in ((1, 1), (0, 3)):
            to = (self.q + d) % 4
            self.send(self.line(y, to), self.buf_in.at[d // 2, y], 2 + d // 2, self.y, self.p, to)

    def second(self):
        direct = self.flying[2:]
        self.flying = self.flying[:2]
        self.land()
        for y, d in ((0, 1), (1, 3)):
            to = (self.q + d) % 4
            for p in range(4):
                total = self.value(y, to, p) + self.buf_far[y, p].astype(F32)
                self.sum_mid[y, p] = total.astype(BF)
            self.send(self.sum_mid.at[y], self.buf_in.at[d // 2, y], 4 + y, self.y, self.p, to)
        self.flying += direct

    def third(self):
        self.land()
        for d in (2, 1, 3, 0):
            to = (self.p + d) % 4
            for y in (0, 1):
                total = self.value(y, self.q, to)
                for n in (0, 1):
                    total += self.buf_in[n, y, to].astype(F32)
                self.sum_p[d, y] = total.astype(BF)
            if d > 0:
                self.send(self.sum_p.at[d], self.buf_p.at[d - 1], 5 + d, self.y, to, self.q)

    def fourth(self):
        self.land()
        for k in (1, 0):
            y = self.y if k == 0 else 1 - self.y
            total = self.sum_p[0, y].astype(F32)
            for n in range(3):
                total += self.buf_p[n, y].astype(F32)
            self.sum_y[k] = total.astype(BF)
            if k == 1:
                self.send(self.sum_y.at[1], self.buf_y, 9, 1 - self.y, self.p, self.q)

    def last(self):
        self.land()
        return self.sum_y[0].astype(F32) + self.buf_y[...].astype(F32)


def reduce_others():
    y, z, x, blk, uly = place()
    return (
        [(blk_of(1 - y, z, x), uly)]
        + [(blk_of(y, z, (x + d) % 4), uly) for d in (1, 2, 3)]
        + [(blk_of(y, (z + d) % 4, x), uly) for d in (1, 2, 3)]
    )


UNIT = (16, 128)


class Total:
    @staticmethod
    def scratch(kept, summed):
        shape = (kept + summed,) + UNIT
        return (
            [pltpu.VMEM((2, 2, 4, 4) + shape, BF)]
            + Reduce.scratch(shape)
            + [
                pltpu.VMEM((2,) + shape, BF),
                pltpu.VMEM((3, 2) + shape, BF),
                pltpu.VMEM((2, 4 * kept + summed) + UNIT, BF),
                pltpu.SemaphoreType.DMA((3,)),
                pltpu.SemaphoreType.DMA((3,)),
                pltpu.SemaphoreType.DMA((31,)),
                pltpu.SemaphoreType.DMA((31,)),
                pltpu.SemaphoreType.DMA,
                pltpu.SemaphoreType.DMA,
                pltpu.SemaphoreType.DMA,
            ]
        )

    scratches = 18

    @staticmethod
    def shape(kept, summed):
        return HELD((2, 2, 4, 4, 4 * kept + summed) + UNIT, BF)

    def __init__(self, kept, summed, all_ref, scratch):
        self.kept, self.summed, self.all_ref = kept, summed, all_ref
        self.part = scratch[0]
        self.reduce = Reduce(self.part, scratch[1:8])
        self.own, self.buf, self.full, self.send_sem, self.recv_sem = scratch[8:13]
        self.all_send, self.all_recv, self.local_sem, self.pair_send, self.pair_recv = scratch[13:18]
        self.y, self.z, self.x, self.blk, self.uly = place()
        self.core = self.uly % 2
        self.flying = []

    def pack(self, values, first, per, at):
        for n, value in enumerate(values, first):
            item = n // per
            self.part[item // 32, item // 16 % 2, item // 4 % 4, item % 4, at + n % per] = value.astype(BF)

    def pack_kept(self, values, first=0):
        self.pack(values, first, self.kept, 0)

    def pack_summed(self, values, first=0):
        self.pack(values, first, self.summed, self.kept)

    def clear(self, kept, summed):
        nothing = jnp.zeros(UNIT, BF)
        self.pack_kept([nothing] * (64 * self.kept - kept), kept)
        self.pack_summed([nothing] * (64 * self.summed - summed), summed)

    def across(self):
        for half, total in enumerate(self.reduce.fourth()):
            self.own[half] = total.astype(BF)
        self.copies = []
        for n, other in enumerate(uly_others()):
            copy = remote(self.own, self.buf.at[n], self.send_sem.at[n], self.recv_sem.at[n], other)
            copy.start()
            self.copies.append(copy)

    def send(self, src, dst, n, y, z, x):
        copy = remote(src, dst, self.all_send.at[n], self.all_recv.at[n], (blk_of(y, z, x), self.uly))
        copy.start()
        self.flying.append(copy)

    def item(self, y, d=0, e=0):
        dz, dx = self.core * d + (1 - self.core) * e, self.core * e + (1 - self.core) * d
        return self.all_ref.at[self.core, y, (self.z + dz) % 4, (self.x + dx) % 4]

    def along(self, y, src, n, d, e):
        dz, dx = self.core * d + (1 - self.core) * e, self.core * e + (1 - self.core) * d
        self.send(src[0], src[1], n, self.y, (self.z + dz) % 4, (self.x + dx) % 4)

    def along_first(self, y, src, first):
        for d in (1, 2, 3):
            self.along(y, (src, self.item(y)), first + d, d, 0)

    def join(self):
        for copy in self.copies:
            copy.wait()
        kept = self.kept
        terms = [self.own] + [self.buf.at[n] for n in range(3)]
        who = [self.uly] + [other[1] for other in uly_others()]
        for half in (0, 1):
            for term, uly in zip(terms, who):
                self.full[half, pl.ds(uly * kept, kept)] = term[half, :kept]
            if self.summed:
                self.full[half, 4 * kept :] = sum(
                    term[half, kept:].astype(F32) for term in terms
                ).astype(BF)
        own = self.full.at[self.core]
        self.send(own, self.item(self.y), 0, 1 - self.y, self.z, self.x)
        self.along_first(self.y, own, 0)
        self.local = pltpu.make_async_copy(own, self.item(self.y), self.local_sem)
        self.local.start()

    def onward(self):
        other = self.item(1 - self.y)
        wait_arrival(other, self.all_recv.at[0])
        self.along_first(1 - self.y, other, 3)

    def spread(self):
        self.local.wait()
        for k, y in enumerate((self.y, 1 - self.y)):
            for d in range(4):
                if d > 0:
                    wait_arrival(self.item(y, 4 - d), self.all_recv.at[3 * k + d])
                for e in (1, 2, 3):
                    ref = self.item(y, (4 - d) % 4)
                    self.along(y, (ref, ref), 7 + k * 12 + d * 3 + e - 1, 0, e)

    def hand(self):
        for k, y in enumerate((self.y, 1 - self.y)):
            for d in range(4):
                for e in (1, 2, 3):
                    wait_arrival(
                        self.item(y, (4 - d) % 4, 4 - e), self.all_recv.at[7 + k * 12 + d * 3 + e - 1]
                    )
        self.pair(self.core).start()

    def pair(self, core):
        return remote(
            self.all_ref.at[core], self.all_ref.at[core], self.pair_send, self.pair_recv, uly_others()[1]
        )

    def end(self):
        for copy in self.flying:
            copy.wait_send()
        self.pair(self.core).wait_send()
        wait_arrival(self.all_ref.at[1 - self.core], self.pair_recv)

    def steps(self):
        return [
            self.reduce.first, self.reduce.second, self.reduce.third, self.across, self.join,
            self.onward, self.spread, self.hand, self.end,
        ]


def units(value):
    rows, columns = value.shape
    return [
        value[n * 16 : (n + 1) * 16, t * 128 : (t + 1) * 128]
        for n in range(rows // 16) for t in range(columns // 128)
    ]


FF_KEPT, FF_SUMMED, QKV_KEPT = 2, 2, 1
COL_TILES = PADDED // 128
D_TILES = D // 128
DKV_ROWS = CHUNK // 2
DKV_STREAMS = 2


def backward_kernel(
    gains_hbm, total_hbm, down_hbm, cols_hbm, ff_hbm, resid_hbm, cot_hbm, ao_hbm, mixed_hbm, wo_hbm, kv_hbm, q_hbm, limit_hbm, lse_hbm,
    wq_hbm, rows_hbm, normed_hbm, b_qkv_hbm, cos_hbm, sin_hbm, a_hbm, bo_hbm,
    result_ref, input_grad_ref, ff_all, qkv_all,
    gains_ref, total_ref, down_ref, cols_ref, ff_ref, resid_ref, cot_ref, ao_ref, mixed_ref, wo_ref, kv_ref, q_ref, limit_ref,
    lse_ref, wq_ref, rows_ref, normed_ref, b_qkv_ref, cos_ref, sin_ref, a_ref, bo_ref, dkv_ref, acc_ref, part, dq_ref, grad_ref, grad_attn, grad_resid, grad_qkv,
    cross_out, cross_in, home_out, home_in, turned_ref, by_rows_ref, dot_ref, copy_sem, cross_sem, home_send,
    home_recv, *scratch,
):
    y, z, x, blk, uly = place()
    core, h = uly % 2, uly // 2
    scratch = list(scratch)

    def take(count):
        got = scratch[:count]
        del scratch[:count]
        return got

    chunk = 2 * blk + h
    upper = chunk // 32
    home = (1 - h) * blk + h * (31 - blk)
    home_from = [(home, upper * 2 + s) for s in (0, 1)]
    lower = low_chunk(blk)
    own_chunk = (1 - h) * lower + h * (63 - lower)
    home_to = [(own_chunk // 2, (own_chunk % 2) * 2 + half) for half in (0, 1)]
    copies = [
        pltpu.make_async_copy(src, dst, copy_sem.at[n])
        for n, (src, dst) in enumerate(
            (
                (total_hbm, total_ref), (resid_hbm, resid_ref), (cot_hbm, cot_ref), (gains_hbm, gains_ref),
                (cols_hbm, cols_ref), (ff_hbm, ff_ref), (down_hbm, down_ref), (ao_hbm, ao_ref), (mixed_hbm, mixed_ref),
                (wo_hbm, wo_ref), (bo_hbm, bo_ref), (kv_hbm, kv_ref),
                (q_hbm, q_ref), (limit_hbm, limit_ref), (lse_hbm, lse_ref), (wq_hbm, wq_ref),
                (rows_hbm, rows_ref), (normed_hbm, normed_ref), (b_qkv_hbm, b_qkv_ref),
                (cos_hbm, cos_ref), (sin_hbm, sin_ref), (a_hbm, a_ref),
            )
        )
    ]
    for copy in copies:
        copy.start()
    greet(
        reduce_others() + uly_others() + [(blk_of(1 - y, z, x), (uly + 2) % 4)] + home_from + home_to
    )
    collect_out = RingSum(
        lambda d: down_ref[(ring_at() + d) % 4].astype(F32), take(RingSum.scratches)
    )
    low, high = (
        [
            Shed(part, half, (n * DKV_ROWS, DKV_ROWS), n, take(Shed.scratches))
            for n in range(DKV_STREAMS)
        ]
        for half in (0, 1)
    )
    ff_total = Total(FF_KEPT, FF_SUMMED, ff_all, take(Total.scratches))
    qkv_total = Total(QKV_KEPT, 0, qkv_all, take(Total.scratches))
    deliver = Deliver()

    def send_home(n, value):
        home_out[n] = value.astype(BF)
        for half in (0, 1):
            deliver.send(
                home_out.at[n, pl.ds(half * 64, 64)], home_in.at[n, core],
                home_send.at[n, half], home_recv.at[n, core], home_to[half],
            )

    def arrived_home(n):
        for s in (0, 1):
            wait_arrival(home_in.at[n, s], home_recv.at[n, s])
        return home_in[n].astype(F32)

    def ready(first, last):
        for copy in copies[first:last]:
            copy.wait()

    ready(0, 4)
    residual = resid_ref[...]
    value = cot_ref[...].astype(F32) + norm_back(
        residual, norm_scale(residual), gain(gains_ref, D_TILES), total_ref[...]
    )
    grad_resid[...] = value
    own_rows = pl.ds(pl.multiple_of(h * CHUNK, CHUNK), CHUNK)
    other_rows = pl.ds(pl.multiple_of((1 - h) * CHUNK, CHUNK), CHUNK)
    grad_attn[own_rows, :] = value.astype(BF)
    partner = uly_others()[0]
    cross = remote(
        grad_attn.at[own_rows], grad_attn.at[own_rows], cross_sem.at[0], cross_sem.at[1], partner
    )
    cross.start()
    ready(4, 11)
    ff_total.pack_kept(units(cols_ref))
    ff_total.pack_summed(units(ff_ref))
    ff_total.clear(6 * COL_TILES, 6 * D_TILES)
    steps = ff_total.steps()

    def beside(*more):
        for step in more:
            step()
        if steps:
            steps.pop(0)()

    beside()
    at_o = 3 * D_TILES + D_TILES // 2 + 2
    qkv_total.clear(at_o + D_TILES // 2 + D_TILES, 0)
    dkv_ref[...] = jnp.zeros_like(dkv_ref)
    acc_ref[...] = jnp.zeros_like(acc_ref)
    latent_o = dot_nt(ao_ref[...], mixed_ref[...]).astype(BF)
    cross.wait_send()
    wait_arrival(grad_attn.at[other_rows], cross_sem.at[1])
    back_o = dot_nt(grad_attn[...], bo_ref[...]).astype(BF)
    grad_ref[...] = (dot_nt(grad_attn[...], wo_ref[...]) + dot(back_o, ao_ref[...])).astype(BF)
    back_o = dot_nt(bo_ref[...], grad_attn[...]).astype(BF)
    qkv_total.pack_kept(
        units(dot(back_o, mixed_ref[...])) + units(dot(latent_o, grad_attn[...])), at_o
    )
    beside()

    ready(11, 15)
    def pack(half):
        def one(n, carry):
            chunk = low_chunk(n) if half == 0 else 63 - low_chunk(n)
            rows = dkv_ref[pl.ds(pl.multiple_of(chunk * CHUNK, CHUNK), CHUNK), :]
            both = jnp.concatenate([rows[:, :HEAD] * LN2, rows[:, HEAD:]], axis=1)
            part[half, n // 16, n // 4 % 4, n % 4] = both.astype(BF)
            return carry

        lax.fori_loop(0, 32, one, 0)

    def shed(streams, name):
        def run():
            for stream in streams:
                getattr(stream, name)()

        return run

    args = (turned_ref, by_rows_ref, dot_ref, kv_ref, limit_ref, lse_ref, dkv_ref, acc_ref)
    step = KEYS_BACK // CHUNK
    middle = CHUNKS // 2 // step
    beside()
    for slot in (0, 1):
        for n, ref in enumerate((q_ref, grad_ref)):
            turned_ref[n, slot] = head_columns(ref, slot)
            by_rows_ref[n, slot] = head_rows(ref, slot)
        row_dot = turned_ref[1, slot].astype(F32) * head_columns(mixed_ref, slot).astype(F32)
        dot_ref[slot] = jnp.broadcast_to(jnp.sum(row_dot, axis=0, keepdims=True), (8, ROWS))
    backward_blocks(1, middle, (63 - lower) // step + 1, *args)
    backward_blocks(0, 0, lower // step + 1, *args)
    pack(1)
    beside(shed(high, "first"))
    names = ["second", "third", "fourth"]
    extra = [collect_out.first, collect_out.second]
    for n in range(0, middle, 2):
        backward_blocks(1, n, n + 2, *args)
        more = [shed(high, names.pop(0))] if names else []
        more += [extra.pop(0)] if extra else []
        if n < middle - 2:
            beside(*more)
    pack(0)
    for stream in low:
        stream.first()
    for slot in (0, 1):
        for n in range(GROUP):
            dq_ref[slot * CHUNK : (slot + 1) * CHUNK, n * HEAD : (n + 1) * HEAD] = (
                acc_ref[slot, :, n * CHUNK : (n + 1) * CHUNK].T * HEAD ** (-0.5)
            )
    ready(15, 22)
    a_qkv = a_ref[...].reshape(48, D)
    for stream in low:
        stream.second()
    beside()
    cos_table, sine_table = cos_ref[...], sin_ref[...]

    def turn_back(value, rows=slice(None)):
        return value * cos_table[rows] - pltpu.roll(value, HEAD // 2, 1) * sine_table[rows]

    for n in range(GROUP):
        at = slice(n * HEAD, (n + 1) * HEAD)
        grad_qkv[:, at] = turn_back(dq_ref[:, at]).astype(BF)
    group = GROUP * HEAD

    def key_value(half, streams):
        for n, stream in enumerate(streams):
            rows = slice(half * CHUNK + n * DKV_ROWS, half * CHUNK + (n + 1) * DKV_ROWS)
            value = stream.last()
            grad_qkv[rows, group : group + HEAD] = turn_back(value[:, :HEAD], rows).astype(BF)
            grad_qkv[rows, group + HEAD :] = value[:, HEAD:].astype(BF)

    key_value(1, high)
    for stream in low:
        stream.third()
    send_home(0, resid_ref[...] + collect_out.third())
    latent_qkv = dot_nt(a_qkv, normed_ref[...]).astype(BF)
    for stream in low:
        stream.fourth()
    key_value(0, low)

    def project_back(rows):
        grads = grad_qkv[rows, :]
        lifted = dot(dot_nt(grads, b_qkv_ref[...]).astype(BF), a_qkv)
        return dot_nt(grads[:, :512], wq_ref[0]) + dot_nt(grads[:, 512:], wq_ref[1]) + lifted

    cross_out[...] = project_back(other_rows).astype(BF)
    cross = remote(cross_out, cross_in, cross_sem.at[2], cross_sem.at[3], partner)
    cross.start()
    back_qkv = dot_nt(b_qkv_ref[...], grad_qkv[...]).astype(BF)
    grad_b = dot(latent_qkv, grad_qkv[...])
    qkv_total.pack_kept(
        units(dot(back_qkv, normed_ref[...]))
        + units(grad_b[:16, :group])
        + units(grad_b[16:32, group : group + HEAD])
        + units(grad_b[32:, group + HEAD :])
    )
    last_steps = qkv_total.steps()
    last_steps.pop(0)()
    mine = project_back(own_rows)
    last_steps.pop(0)()
    beside()
    cross.wait()
    mine = mine + cross_in[...].astype(F32)
    tokens = rows_ref[own_rows, :].astype(F32)
    send_home(1, grad_resid[...] + norm_back(tokens, norm_scale(tokens), gain(gains_ref, 0), mine))
    for step in last_steps + steps:
        step()
    result_ref[...] = arrived_home(0).astype(BF)
    input_grad_ref[...] = arrived_home(1).astype(BF)
    deliver.end()


def backward(*args):
    dma = pltpu.SemaphoreType.DMA
    group = GROUP * HEAD
    return pl.pallas_call(
        backward_kernel,
        out_shape=(
            jax.ShapeDtypeStruct((2, CHUNK // 2, D), BF),
            jax.ShapeDtypeStruct((2, CHUNK // 2, D), BF),
            Total.shape(FF_KEPT, FF_SUMMED),
            Total.shape(QKV_KEPT, 0),
        ),
        in_specs=[ANY] * 22,
        out_specs=(IN_VMEM, IN_VMEM, ANY, ANY),
        scratch_shapes=[
            pltpu.VMEM((40, 128), F32),
            pltpu.VMEM((CHUNK, D), F32),
            pltpu.VMEM((4, CHUNK, D), BF),
            pltpu.VMEM((96, PADDED), BF),
            pltpu.VMEM((96, D), BF),
            pltpu.VMEM((CHUNK, D), F32),
            pltpu.VMEM((CHUNK, D), BF),
            pltpu.VMEM((16, group), BF),
            pltpu.VMEM((2 * CHUNK, group), BF),
            pltpu.VMEM((D // 2, D), BF),
            pltpu.VMEM((CHUNKS, CHUNK, 2 * HEAD), BF),
            pltpu.VMEM((2 * CHUNK, group), BF),
            pltpu.VMEM((2, 8, ROWS), jnp.int32),
            pltpu.VMEM((2, 8, ROWS), F32),
            pltpu.VMEM((2, D, 512), BF),
            pltpu.VMEM((2 * CHUNK, D), BF),
            pltpu.VMEM((2 * CHUNK, D), BF),
            pltpu.VMEM((48, 1024), BF),
            pltpu.VMEM((2 * CHUNK, HEAD), F32),
            pltpu.VMEM((2 * CHUNK, HEAD), F32),
            pltpu.VMEM((3, 16, D), BF),
            pltpu.VMEM((16, D), BF),
            pltpu.VMEM((CHUNKS * CHUNK, 2 * HEAD), F32),
            pltpu.VMEM((2, HEAD, ROWS), F32),
            pltpu.VMEM((2, 2, 4, 4, CHUNK, 2 * HEAD), BF),
            pltpu.VMEM((2 * CHUNK, group), F32),
            pltpu.VMEM((2 * CHUNK, group), BF),
            pltpu.VMEM((2 * CHUNK, D), BF),
            pltpu.VMEM((CHUNK, D), F32),
            pltpu.VMEM((2 * CHUNK, 1024), BF),
            pltpu.VMEM((CHUNK, D), BF),
            pltpu.VMEM((CHUNK, D), BF),
            pltpu.VMEM((2, CHUNK, D), BF),
            pltpu.VMEM((2, 2, CHUNK // 2, D), BF),
            pltpu.VMEM((2, 2, HEAD, ROWS), BF),
            pltpu.VMEM((2, 2, ROWS, HEAD), BF),
            pltpu.VMEM((2, 8, ROWS), F32),
            dma((22,)), dma((4,)), dma((2, 2)), dma((2, 2)),
        ]
        + RingSum.scratch()
        + Shed.scratch((DKV_ROWS, 2 * HEAD)) * (2 * DKV_STREAMS)
        + Total.scratch(FF_KEPT, FF_SUMMED)
        + Total.scratch(QKV_KEPT, 0),
        compiler_params=pltpu.CompilerParams(
            collective_id=2, has_side_effects=True, vmem_limit_bytes=60 * 2**20
        ),
        name="backward",
    )(*args)


def fold_kernel(
    set_ref, result_in, grad_in, ff_hbm, qkv_hbm, result_ref, input_grad_ref, a_wide, a_down, b_wide, b_kv, b_ff,
    ff_ref, qkv_ref, sems,
):
    c = pl.program_id(0)
    share = [jnp.where(set_ref[s] == c, 1.0, 0.0) for s in (0, 1)]

    @pl.when(c == 0)
    def _():
        copies = [
            pltpu.make_async_copy(src, dst, sems.at[n])
            for n, (src, dst) in enumerate(((ff_hbm, ff_ref), (qkv_hbm, qkv_ref)))
        ]
        for copy in copies:
            copy.start()
        result_ref[...] = result_in[...]
        input_grad_ref[...] = grad_in[...].astype(F32)
        for copy in copies:
            copy.wait()

    def kept(ref, per, n, u):
        item = n // per
        return ref[item // 32, item // 16 % 2, item // 4 % 4, item % 4, u * per + n % per].astype(F32)

    def ff_kept(n, u):
        return kept(ff_ref, FF_KEPT, n, u)

    def qkv_kept(n, u):
        return kept(qkv_ref, QKV_KEPT, n, u)

    def summed(n):
        item = n // FF_SUMMED
        return ff_ref[
            item // 32, item // 16 % 2, item // 4 % 4, item % 4, 4 * FF_KEPT + n % FF_SUMMED
        ].astype(F32)

    def put(ref, at, tile, value):
        ref[at + (slice(None), slice(tile * 128, (tile + 1) * 128))] = (
            share[0] * value(0) + share[1] * value(1)
        )

    for n in range(3):
        for t in range(D_TILES):
            put(a_wide, (n, 0), t, lambda s: qkv_kept(n * D_TILES + t, s) + qkv_kept(n * D_TILES + t, 2 + s))
    half = D_TILES // 2
    at_o = 3 * D_TILES + half + 2
    for t in range(D_TILES):
        h, part = t // half, t % half
        put(a_wide, (3, 0), t, lambda s: qkv_kept(at_o + part, 2 * h + s))
        put(b_wide, (0, 0), t, lambda s: qkv_kept(3 * D_TILES + part, 2 * h + s))
        put(
            b_wide, (1, 0), t,
            lambda s: qkv_kept(at_o + half + t, s) + qkv_kept(at_o + half + t, 2 + s),
        )
        for n, (ref, at) in enumerate(((a_wide, (4, 0)), (a_wide, (5, 0)), (b_wide, (2, 0)))):
            put(ref, at, t, lambda s: summed((2 * n + s) * D_TILES + t))
    for n in (0, 1):
        for h in (0, 1):
            put(b_kv, (n, 0), h, lambda s: qkv_kept(3 * D_TILES + half + n, 2 * h + s))
    for n, (ref, at) in enumerate(((a_down, (0,)), (b_ff, (0, 0)), (b_ff, (1, 0)))):
        for t in range(FF // 128):
            where = [
                (u, t - start) for u, start in enumerate((0, 17, 35, 52)) if 0 <= t - start < COL_TILES
            ]
            put(
                ref, at, t,
                lambda s: sum(ff_kept((2 * n + s) * COL_TILES + tile, u) for u, tile in where),
            )


def fold(set_index, result, input_grad, ff_all, qkv_all):
    rows = pl.BlockSpec(result.shape, lambda c: (0, 0, 0))

    def by_set(lead, columns):
        shape = lead + (1, 16, columns)
        return pl.BlockSpec(shape, lambda c: (0,) * len(lead) + (c, 0, 0))

    def out(lead, columns):
        return jax.ShapeDtypeStruct(lead + (SETS, 16, columns), F32)

    outs = (((6,), D), ((), FF), ((3,), D), ((2,), 2 * HEAD), ((2,), FF))
    return pl.pallas_call(
        fold_kernel,
        grid=(SETS,),
        out_shape=(
            jax.ShapeDtypeStruct(result.shape, BF),
            jax.ShapeDtypeStruct(result.shape, F32),
        )
        + tuple(out(*o) for o in outs),
        in_specs=[pl.BlockSpec(memory_space=pltpu.SMEM), rows, rows, ANY, ANY],
        out_specs=(rows, rows) + tuple(by_set(*o) for o in outs),
        scratch_shapes=[
            pltpu.VMEM(ff_all.shape, BF), pltpu.VMEM(qkv_all.shape, BF), pltpu.SemaphoreType.DMA((2,))
        ],
        compiler_params=pltpu.CompilerParams(vmem_limit_bytes=40 * 2**20),
        name="fold",
    )(set_index, result, input_grad, ff_all, qkv_all)


def norm_scale(hidden):
    return lax.rsqrt(jnp.mean(hidden * hidden, axis=-1, keepdims=True) + EPS)


def norm_back(hidden, scaled, gain_vec, upstream):
    normed = hidden * scaled
    weighted = upstream * gain_vec
    return scaled * (weighted - normed * jnp.mean(weighted * normed, axis=-1, keepdims=True))


def held(*arrays):
    return [pltpu.with_memory_space_constraint(v, pltpu.HBM) for v in arrays]


def body(
    tokens, cotangent, lengths, set_index, norm_in, norm_ff, qkv_bias, w_qkv, w_out, w_gate_up, w_down,
    a_wide, a_down, b_wide, b_kv, b_ff,
):
    frequencies = np.float64(THETA) ** (-np.arange(0, HEAD, 2, dtype=np.float64) / HEAD)
    frequencies = jnp.asarray(np.concatenate([frequencies, frequencies])[None].astype(np.float32))
    gains = jnp.concatenate([norm_in, norm_ff, qkv_bias]).reshape(40, 128)
    (
        q, mixed, lse, kv_all, qkv_w, out_w, gate_w, up_w, down_w, rows, normed, residual, grad_out,
        normed_ff, grad_gathered, limit, cos_table, sine_table, b_qkv, ao, a_own, bo,
    ) = forward(
        *held(
            tokens, cotangent, lengths, set_index, w_qkv, w_out, w_gate_up, w_down.T, gains, frequencies,
            a_wide, b_wide, b_kv,
        )
    )
    gate_w, up_w, down_w = (w.reshape(D, FF_COLS) for w in (gate_w, up_w, down_w))
    grad_normed_ff, down_sum, cols, ff_wide = feed_forward(
        set_index, normed_ff, grad_gathered, gate_w, up_w, down_w, *held(a_wide, a_down, b_wide, b_ff)
    )
    result, input_grad, ff_all, qkv_all = backward(
        gains,
        grad_normed_ff, down_sum, cols, ff_wide, residual, grad_out, ao, mixed, out_w, kv_all, q, limit, lse,
        qkv_w, rows, normed, b_qkv, cos_table, sine_table, a_own, bo,
    )
    return tuple(fold(set_index, *held(result, input_grad, ff_all, qkv_all)))


def solution(mesh):
    spread = P(None, ("blk", "uly"), None)
    in_specs = (
        spread, spread, P(), P(), P(), P(), P(),
        P(("blk", "uly"), None), P(("blk", "uly"), None), P(None, "blk", "uly"), P("uly", "blk"),
        P(), P(), P(), P(), P(),
    )
    out_specs = (spread, spread, P(), P(), P(), P(), P())
    return jax.shard_map(body, mesh=mesh, in_specs=in_specs, out_specs=out_specs, check_vma=False)
```

```python
import functools

import jax
import jax.numpy as jnp
import numpy as np
from jax import lax
from jax.experimental import pallas as pl
from jax.experimental.pallas import tpu as pltpu
from jax.sharding import PartitionSpec as P

HEADS = 12
KV_HEADS = 2
HEAD = 128
GROUP = HEADS // KV_HEADS
FF = 8960
SETS = 8
D = 1536
CHUNK = 128
CHUNKS = 64
PADDED = 2304
EPS = 1e-06
THETA = 1000000.0
LOG2E = 1.4426950408889634
LN2 = 0.6931471805599453
MESH = pl.DeviceIdType.MESH
BF = jnp.bfloat16
F32 = jnp.float32
ANY = pl.BlockSpec(memory_space=pltpu.HBM)
IN_VMEM = pl.BlockSpec(memory_space=pltpu.VMEM)
HELD = pltpu.HBM


def blk_of(y, z, x):
    return y * 16 + z * 4 + x


def low_chunk(blk):
    return (1 - blk // 16) * 2 * blk + blk // 16 * (63 - 2 * blk)


def place():
    blk = lax.axis_index("blk")
    return blk // 16, (blk // 4) % 4, blk % 4, blk, lax.axis_index("uly")


def ring_others():
    y, z, x, blk, uly = place()
    return [
        (blk_of(1 - y, z, x), uly),
        (blk_of(y, z, (x + 1) % 4), uly),
        (blk_of(y, z, (x + 3) % 4), uly),
        (blk_of(y, (z + 1) % 4, x), uly),
        (blk_of(y, (z + 3) % 4, x), uly),
    ]


def choose(number, value):
    chosen = value(0)
    for c in range(1, SETS):
        chosen = jnp.where(number == c, value(c), chosen)
    return chosen


def gain(ref, first):
    return jnp.concatenate([ref[n : n + 1, :] for n in range(first, first + D // 128)], axis=1)


def greet(others, meanwhile=None):
    barrier = pltpu.get_barrier_semaphore()
    for other in others:
        pl.semaphore_signal(barrier, inc=1, device_id=other, device_id_type=MESH)
    if meanwhile is not None:
        meanwhile()
    pl.semaphore_wait(barrier, len(others))


class Gather:
    sends = 31

    def __init__(self, src, dst, send_sem, recv_sem, local_sem, orders=(0, 1)):
        self.src, self.dst, self.orders = src, dst, orders
        self.streams = range(len(orders))
        self.send_sem, self.recv_sem, self.local_sem = send_sem, recv_sem, local_sem
        self.y, self.z, self.x, self.blk, self.uly = place()
        self.count = [0] * len(orders)
        self.sent = []
        self.local = []

    def at(self, stream, y, p, q):
        order = self.orders[stream]
        return blk_of(y, order * p + (1 - order) * q, order * q + (1 - order) * p)

    def pq(self, stream):
        order = self.orders[stream]
        return (
            order * self.z + (1 - order) * self.x,
            order * self.x + (1 - order) * self.z,
        )

    def send(self, stream, item, target, src=None):
        copy = pltpu.make_async_remote_copy(
            src_ref=self.dst(stream, item) if src is None else src,
            dst_ref=self.dst(stream, item),
            send_sem=self.send_sem.at[stream, self.count[stream]],
            recv_sem=self.recv_sem.at[stream, item],
            device_id=(target, self.uly),
            device_id_type=MESH,
        )
        self.count[stream] += 1
        copy.start()
        self.sent.append(copy)

    def wait(self, stream, item):
        ref = self.dst(stream, item)
        pltpu.make_async_remote_copy(
            src_ref=ref,
            dst_ref=ref,
            send_sem=self.send_sem.at[stream, 0],
            recv_sem=self.recv_sem.at[stream, item],
            device_id=(self.blk, self.uly),
            device_id_type=MESH,
        ).wait_recv()

    def start(self):
        for s in self.streams:
            p, q = self.pq(s)
            self.send(s, self.blk, self.at(s, 1 - self.y, p, q), self.src(s))
        for s in self.streams:
            p, q = self.pq(s)
            for d in (1, 3):
                self.send(s, self.blk, self.at(s, self.y, (p + d) % 4, q), self.src(s))
            copy = pltpu.make_async_copy(self.src(s), self.dst(s, self.blk), self.local_sem.at[s])
            copy.start()
            self.local.append(copy)

    def second(self):
        for s in self.streams:
            p, q = self.pq(s)
            item = self.at(s, 1 - self.y, p, q)
            self.wait(s, item)
            for d in (1, 3):
                self.send(s, item, self.at(s, self.y, (p + d) % 4, q))
            for d in (1, 3):
                onward = self.at(s, self.y, p, (q + d) % 4)
                self.send(s, self.blk, onward, self.src(s))
                self.send(s, item, onward)

    def spread(self, s, item):
        p, q = self.pq(s)
        for d in (1, 3):
            self.send(s, item, self.at(s, self.y, p, (q + d) % 4))

    def third(self):
        for k, y in enumerate((self.y, 1 - self.y)):
            for s in self.streams:
                p, q = self.pq(s)
                for d in (3, 1):
                    item = self.at(s, y, (p + d) % 4, q)
                    self.wait(s, item)
                    if (d == 3) == (k == 0):
                        self.send(s, item, self.at(s, self.y, (p + 4 - d) % 4, q))
                    self.spread(s, item)
        for y in (self.y, 1 - self.y):
            for s in self.streams:
                p, q = self.pq(s)
                item = self.at(s, y, (p + 2) % 4, q)
                self.wait(s, item)
                self.spread(s, item)

    def fourth(self):
        for e in (0, 1, 3, 2):
            for k, y in enumerate((self.y, 1 - self.y)):
                for s in self.streams:
                    p, q = self.pq(s)
                    for d in (3, 1):
                        item = self.at(s, y, (p + e) % 4, (q + d) % 4)
                        self.wait(s, item)
                        if (d == 3) == (k == 0):
                            self.send(s, item, self.at(s, self.y, p, (q + 4 - d) % 4))

    def last(self):
        for e in (0, 1, 3, 2):
            for y in (self.y, 1 - self.y):
                for s in self.streams:
                    p, q = self.pq(s)
                    self.wait(s, self.at(s, y, (p + e) % 4, (q + 2) % 4))
        for copy in self.local:
            copy.wait()
        for copy in self.sent:
            copy.wait_send()


GATHER_SEMS = lambda *lead: [
    pltpu.SemaphoreType.DMA(lead + (2, Gather.sends)),
    pltpu.SemaphoreType.DMA(lead + (2, 32)),
    pltpu.SemaphoreType.DMA(lead + (2,)),
]


KEYS = 1024
KEYS_BACK = 512
ROWS = GROUP * CHUNK


def head_columns(ref, slot):
    return jnp.concatenate(
        [
            ref[slot * CHUNK : (slot + 1) * CHUNK, n * HEAD : (n + 1) * HEAD].T
            for n in range(GROUP)
        ],
        axis=1,
    )


def head_rows(ref, slot):
    return jnp.concatenate(
        [
            ref[slot * CHUNK : (slot + 1) * CHUNK, n * HEAD : (n + 1) * HEAD]
            for n in range(GROUP)
        ],
        axis=0,
    )


def key_block(kv_ref, step, keys):
    count = keys // CHUNK
    rows = kv_ref[pl.ds(step * count, count)].reshape(keys, 2 * HEAD)
    return rows[:, :HEAD], rows[:, HEAD:]


def dot(a, b):
    return jnp.dot(a, b, preferred_element_type=F32)


def key_places(step, keys):
    return lax.broadcasted_iota(jnp.int32, (keys, ROWS), 0) + step * keys


def dot_nt(a, b):
    return lax.dot_general(a, b, (((1,), (1,)), ((), ())), preferred_element_type=F32)


def forward_blocks(slot, first, last, turned_ref, kv_ref, limit_ref, acc_ref, stat_ref):
    turned = turned_ref[slot]
    limit = limit_ref[slot, 0:1, :]

    def step(n, carry):
        top, total = carry
        keys, values = key_block(kv_ref, n, KEYS)
        scores = jnp.where(key_places(n, KEYS) <= limit, dot(keys, turned), -1e30)
        new_top = jnp.maximum(top, jnp.max(scores, axis=0, keepdims=True))
        fade = jnp.exp2(top - new_top)
        probs = jnp.exp2(scores - new_top)
        total = total * fade + jnp.sum(probs, axis=0, keepdims=True)
        acc_ref[slot] = acc_ref[slot] * fade + dot(values.T, probs.astype(BF))
        return new_top, total

    top, total = lax.fori_loop(
        first, last, step, (stat_ref[slot, 0, 0:1, :], stat_ref[slot, 1, 0:1, :])
    )
    stat_ref[slot, 0, 0:1, :] = top
    stat_ref[slot, 1, 0:1, :] = total


def forward_end(slot, mixed_ref, lse_ref, acc_ref, stat_ref):
    top, total = stat_ref[slot, 0, 0:1, :], stat_ref[slot, 1, 0:1, :]
    out = acc_ref[slot] / total
    for n in range(GROUP):
        mixed_ref[slot * CHUNK : (slot + 1) * CHUNK, n * HEAD : (n + 1) * HEAD] = out[
            :, n * CHUNK : (n + 1) * CHUNK
        ].T.astype(BF)
    lse_ref[slot] = jnp.broadcast_to(top + jnp.log2(total), (8, ROWS))


def uly_others():
    y, z, x, blk, uly = place()
    return [(blk, (uly + 2) % 4), (blk, uly + 1 - 2 * (uly % 2)), (blk, 3 - uly)]


def ring_place(w):
    y, z, x, blk, uly = place()
    return (blk_of(w % 2, z, x), (w // 2) * 2 + uly % 2)


def ring_at():
    y, z, x, blk, uly = place()
    return (uly // 2) * 2 + y


def wait_arrival(ref, sem):
    pltpu.make_async_copy(ref, ref, sem).wait()


def remote(src, dst, send, recv, device):
    return pltpu.make_async_remote_copy(
        src_ref=src, dst_ref=dst, send_sem=send, recv_sem=recv, device_id=device, device_id_type=MESH
    )


class Deliver:
    def __init__(self):
        self.sent = []

    def send(self, src, dst, send, recv, device):
        y, z, x, blk, uly = place()
        here = jnp.logical_and(device[0] == blk, device[1] == uly)

        @pl.when(here)
        def _():
            pltpu.make_async_copy(src, dst, recv).start()

        @pl.when(jnp.logical_not(here))
        def _():
            remote(src, dst, send, recv, device).start()

        self.sent.append((here, src, dst, send, recv, device))

    def end(self):
        for here, *copy in self.sent:

            @pl.when(jnp.logical_not(here))
            def _():
                remote(*copy).wait_send()


class Ring:
    sends = 15

    def __init__(self, src, dst, y, order, way, send_sem, recv_sem):
        self.src, self.dst, self.y, self.order, self.way = src, dst, y, order, way
        self.send_sem, self.recv_sem = send_sem, recv_sem
        self.own_y, self.z, self.x, self.blk, self.uly = place()
        self.p = order * self.z + (1 - order) * self.x
        self.q = order * self.x + (1 - order) * self.z
        self.sent = []

    def at(self, y, p, q):
        order = self.order
        return blk_of(y, order * p + (1 - order) * q, order * q + (1 - order) * p)

    def index(self, p, q):
        return self.at(0, p, q)

    def send(self, p, q, dp, dq, src=None):
        ref = self.dst(self.at(self.y, p, q))
        target = self.at(self.own_y, (self.p + dp) % 4, (self.q + dq) % 4)
        copy = remote(
            ref if src is None else src, ref, self.send_sem.at[len(self.sent)],
            self.recv_sem.at[self.index(p, q)], (target, self.uly),
        )
        copy.start()
        self.sent.append(copy)

    def wait(self, p, q):
        wait_arrival(self.dst(self.at(self.y, p, q)), self.recv_sem.at[self.index(p, q)])

    def start(self):
        for d in (1, 3):
            self.send(self.p, self.q, d, 0, self.src)

    def second(self):
        for d in (4 - self.way, self.way):
            p = (self.p + d) % 4
            self.wait(p, self.q)
            if d == 4 - self.way:
                self.send(p, self.q, self.way, 0)

    def third(self):
        self.wait((self.p + 2) % 4, self.q)

    def spread(self, e):
        p = (self.p + e) % 4
        for d in (1, 3):
            self.send(p, self.q, 0, d, self.src if e == 0 else None)

    def fourth(self, e):
        p = (self.p + e) % 4
        way = self.way if e % 2 == 0 else 4 - self.way
        for d in (4 - way, way):
            q = (self.q + d) % 4
            self.wait(p, q)
            if d == 4 - way:
                self.send(p, q, 0, way)

    def last(self):
        for e in (0, 1, 3, 2):
            self.wait((self.p + e) % 4, (self.q + 2) % 4)
        self.end()

    def end(self):
        for copy in self.sent:
            copy.wait_send()


class Spread:
    def __init__(self, own, all_ref, send_sem, recv_sem, local_sem):
        self.own, self.all_ref = own, all_ref
        self.send_sem, self.recv_sem, self.local_sem = send_sem, recv_sem, local_sem
        self.w = ring_at()
        self.core = lax.axis_index("uly") % 2
        self.sibling = uly_others()[1]
        self.sent = []

    def piece(self, d, rows=slice(None), core=None):
        core = self.core if core is None else core
        ref = self.all_ref.at[core, (self.w + d) % 4]
        return ref if rows == slice(None) else ref.at[pl.ds(rows.start, rows.stop - rows.start)]

    def send(self, src, dst, recv, device):
        copy = remote(src, dst, self.send_sem.at[len(self.sent)], self.recv_sem.at[recv], device)
        copy.start()
        self.sent.append(copy)

    def pair(self, d, src=None):
        self.send(self.piece(d) if src is None else src, self.piece(d), 4 + d, self.sibling)

    def start(self):
        self.local = pltpu.make_async_copy(self.own, self.piece(0), self.local_sem)
        self.local.start()
        self.send(self.own, self.piece(0), 0, ring_place((self.w + 1) % 4))
        self.send(self.own, self.piece(0), 1, ring_place((self.w + 3) % 4))
        self.pair(0, self.own)

    def second(self):
        half = CHUNK // 2
        wait_arrival(self.piece(3), self.recv_sem.at[0])
        low = self.piece(3, slice(0, half))
        self.send(low, low, 2, ring_place((self.w + 1) % 4))
        self.pair(3)
        wait_arrival(self.piece(1), self.recv_sem.at[1])
        high = self.piece(1, slice(half, CHUNK))
        self.send(high, high, 3, ring_place((self.w + 3) % 4))
        self.pair(1)

    def third(self):
        half = CHUNK // 2
        wait_arrival(self.piece(2, slice(0, half)), self.recv_sem.at[2])
        wait_arrival(self.piece(2, slice(half, CHUNK)), self.recv_sem.at[3])
        self.pair(2)

    def last(self):
        for d in range(4):
            wait_arrival(self.piece(d, core=1 - self.core), self.recv_sem.at[4 + d])
        for copy in self.sent:
            copy.wait_send()
        self.local.wait()


SPREAD_SEMS = [pltpu.SemaphoreType.DMA((8,)), pltpu.SemaphoreType.DMA((8,)), pltpu.SemaphoreType.DMA]
FF_COLS = PADDED // 2


def forward_kernel(
    tokens_ref, cot_ref, length_hbm, set_hbm, qkv_hbm, w_out_hbm, gate_up_hbm, down_hbm, gains_hbm, freq_hbm,
    a_hbm, b_hbm, bkv_hbm,
    q_out, mixed_out, lse_out, kv_out, wq_out, wo_out, gate_all, up_all, down_all, rows_hbm, normed_out,
    resid_out, cot_out, nf_out, cot_all, limit_out, cos_out, sin_out, b_qkv_out, ao_out, a_out, bo_out,
    q_ref, mixed_ref, lse_ref, rows_out, normed_ref, resid_ref, cot_own, limit_ref, cos_ref, sin_ref,
    b_qkv_ref, ao_ref, a_ref, b_ref, bkv_ref, a_sets, b_sets, bkv_sets, turned_ref,
    length_ref, set_ref, qkv_ref, out_ref, gate_up_ref, down_ref, gains_ref, freq_ref, kv_all, wq_all, wo_all, rows, cot_in, kv_part, acc_ref, stat_ref, qkv_in, out_in, qkv_part, out_part,
    nf_own, cross_out, cross_in, qkv_pieces, out_pieces, ff_ref,
    *sems,
):
    y, z, x, blk, uly = place()
    core, h = uly % 2, uly // 2
    sems = list(sems)

    def take(count):
        got = sems[:count]
        del sems[:count]
        return got

    chunk = 2 * blk + h
    upper = chunk // 32
    home = (1 - h) * blk + h * (31 - blk)
    row_to = [[(home, hh * 2 + s) for hh in (0, 1)] for s in (0, 1)]
    row_from = [(b, hh * 2 + half) for b, hh in ((blk, 0), (31 - blk, 1)) for half in (0, 1)]
    lower = low_chunk(blk)
    out_to = [(2 * (blk % 16) + q // 2, (blk // 16) * 2 + q % 2) for q in range(4)]
    out_from = [(16 * h + blk // 2, u) for u in range(4)]
    sibling = uly_others()[1]
    set_sem = sems.pop()
    in_sem = sems.pop()
    in_copies = [
        pltpu.make_async_copy(src, dst, in_sem.at[n])
        for n, (src, dst) in enumerate(
            (
                (qkv_hbm, qkv_ref), (w_out_hbm, out_ref), (gate_up_hbm, gate_up_ref), (down_hbm, down_ref),
                (length_hbm, length_ref), (set_hbm, set_ref), (gains_hbm, gains_ref), (freq_hbm, freq_ref),
            )
        )
    ]
    for copy in in_copies:
        copy.start()
    set_copies = [
        pltpu.make_async_copy(src, dst, set_sem.at[n])
        for n, (src, dst) in enumerate(
            ((a_hbm.at[pl.ds(0, 4)], a_sets), (b_hbm.at[pl.ds(0, 2)], b_sets), (bkv_hbm, bkv_sets))
        )
    ]
    for copy in set_copies:
        copy.start()

    def prepare():
        qkv_pieces[...] = jnp.zeros_like(qkv_pieces)
        out_pieces[...] = jnp.zeros_like(out_pieces)
        for copy in in_copies:
            copy.wait()
        group = GROUP * HEAD
        for hh in (0, 1):
            qkv_pieces[2 * hh, :12] = qkv_ref[:, hh * group : hh * group + 512]
            for place_at, start, size in (
                (0, hh * group + 512, 256),
                (256, HEADS * HEAD + hh * HEAD, HEAD),
                (384, HEADS * HEAD + 256 + hh * HEAD, HEAD),
            ):
                qkv_pieces[2 * hh + 1, :12, place_at : place_at + size] = qkv_ref[:, start : start + size]
        for q in range(4):
            out_pieces[q, :12] = out_ref[:, q * 384 : (q + 1) * 384]
        for n in range(3):
            part = (gate_up_ref[n] if n < 2 else down_ref[...]).astype(F32)
            none = jnp.zeros((48, 64), F32)
            left = jnp.concatenate([part, none], axis=1)
            right = jnp.concatenate([none, part], axis=1)
            ff_ref[n] = jnp.where(jnp.broadcast_to(core, (48, PADDED)) == 1, right, left).astype(BF)

    greet(
        ring_others() + uly_others() + [(blk_of(1 - y, z, x), (uly + 2) % 4)]
        + row_to[0] + row_to[1] + row_from + out_to + out_from,
        prepare,
    )

    length = length_ref[0] * (1 - core) + length_ref[1] * core

    deliver = Deliver()
    piece_send, piece_recv, row_send, row_recv = take(4)
    for q in range(4):
        deliver.send(qkv_pieces.at[q], qkv_in.at[uly], piece_send.at[q], piece_recv.at[uly], (blk, q))
    for q in range(4):
        deliver.send(out_pieces.at[q], out_in.at[uly], piece_send.at[4 + q], piece_recv.at[4 + uly], out_to[q])
    for s in (0, 1):
        for hh in (0, 1):
            deliver.send(
                tokens_ref.at[s], rows.at[upper, core], row_send.at[s * 2 + hh],
                row_recv.at[upper * 2 + core], row_to[s][hh],
            )

    wide = PADDED // 2
    gathered = (gate_all, up_all, down_all)
    ff_send, ff_recv, y_send, y_recv, y_local = take(5)
    other_blk = blk_of(1 - y, z, x)

    def ff_part(n, half):
        return ff_ref.at[n, :, pl.ds(pl.multiple_of(half * wide, 128), wide)]

    y_copies = []
    for n, ref in enumerate(gathered):
        copy = remote(ff_part(n, 1 - y), ref.at[blk], y_send.at[n], y_recv.at[n], (other_blk, uly))
        copy.start()
        y_copies.append(copy)
        copy = pltpu.make_async_copy(ff_part(n, y), ref.at[blk], y_local.at[n])
        copy.start()
        y_copies.append(copy)
    own_ff, other_ff = (
        [
            Ring(
                ff_part(n, y) if k == 0 else ref.at[other_blk],
                lambda item, ref=ref: ref.at[item],
                y if k == 0 else 1 - y,
                y if k == 0 else 1 - y,
                (1, 3, 1 + 2 * k)[n],
                ff_send.at[k, n], ff_recv.at[k, n],
            )
            for n, ref in enumerate(gathered)
        ]
        for k in (0, 1)
    )
    for ring in own_ff:
        ring.start()

    picked = lax.broadcasted_iota(jnp.int32, (48, 64), 1)
    picked = jnp.where(picked % 16 < 12, picked // 16 * 12 + picked % 16, -1)
    picked = jnp.where(picked == lax.broadcasted_iota(jnp.int32, (48, 64), 0), 1.0, 0.0).astype(BF)
    for u in range(4):
        wait_arrival(qkv_in.at[u], piece_recv.at[u])
    qkv_part[...] = dot(picked, qkv_in[...].reshape(64, 512)).astype(BF)
    wq = Gather(
        lambda s: qkv_part.at[:, pl.ds(256 * s, 256)],
        lambda s, item: wq_all.at[
            core, pl.ds(pl.multiple_of(item * 48, 16), 48), pl.ds(256 * s, 256)
        ],
        *take(3),
    )
    wq.start()
    for u in range(4):
        wait_arrival(out_in.at[u], piece_recv.at[4 + u])
    out_part[...] = dot(picked, out_in[...].reshape(64, 384)).astype(BF)
    for s in (0, 1):
        deliver.send(
            cot_ref.at[s], cot_in.at[core], row_send.at[4 + s], row_recv.at[4 + core], (home, upper * 2 + s)
        )

    def out_columns(item, s):
        start = ((item % 2) * 2 + core) * 384
        return pl.ds(pl.multiple_of(start + 128 * s, 128), 128 + 128 * s)

    wo = Gather(
        lambda s: out_part.at[:, pl.ds(128 * s, 128 + 128 * s)],
        lambda s, item: wo_all.at[pl.ds(pl.multiple_of((item // 2) * 48, 16), 48), out_columns(item, s)],
        *take(3),
    )
    rings = own_ff + other_ff
    whole = [ring for n, ring in enumerate(rings) if n % 3 != 1]
    def tables(slot):
        at = lower if slot == 0 else 63 - lower
        row = lax.broadcasted_iota(jnp.int32, (CHUNK, HEAD), 0) + at * CHUNK
        angle = row.astype(F32) * freq_ref[...]
        first = lax.broadcasted_iota(jnp.int32, (CHUNK, HEAD), 1) < HEAD // 2
        sine = jnp.sin(angle)
        cos_ref[slot * CHUNK : (slot + 1) * CHUNK, :] = jnp.cos(angle)
        sin_ref[slot * CHUNK : (slot + 1) * CHUNK, :] = jnp.where(first, -sine, sine)
        row = lax.broadcasted_iota(jnp.int32, (8, ROWS), 1) % CHUNK + at * CHUNK
        limit_ref[slot] = jnp.minimum(row, length - 1)

    stat_ref[:, 0] = jnp.full((2, 8, ROWS), -1e30, F32)
    stat_ref[:, 1] = jnp.zeros((2, 8, ROWS), F32)
    acc_ref[...] = jnp.zeros_like(acc_ref)
    own_set = set_ref[0] * (1 - core) + set_ref[1] * core
    for copy in set_copies:
        copy.wait()
    for sets, ref in ((a_sets, a_ref), (b_sets, b_ref), (bkv_sets, bkv_ref)):
        for n in range(ref.shape[0]):
            ref[n] = choose(own_set, lambda c: sets[n, c])
    group = GROUP * HEAD
    group_at = pl.ds(pl.multiple_of(h * group, 128), group)
    head_at = pl.ds(pl.multiple_of(h * HEAD, 128), HEAD)
    ao_ref[...] = a_ref[3, :, group_at]
    b_qkv_ref[...] = jnp.zeros_like(b_qkv_ref)
    b_qkv_ref[:16, :group] = b_ref[0, :, group_at]
    b_qkv_ref[16:32, group : group + HEAD] = bkv_ref[0, :, head_at]
    b_qkv_ref[32:, group + HEAD :] = bkv_ref[1, :, head_at]
    a_qkv = a_ref[:3].reshape(48, D)
    bo_ref = b_ref.at[1]

    def bias(n):
        at = h * GROUP + n if n < GROUP else HEADS + 2 * (n - GROUP) + h
        return gains_ref[pl.ds(2 * D_TILES + at, 1), :]

    wq.second()
    tables(0)
    wq.third()
    tables(1)
    wq.fourth()
    for n in range(3):
        y_copies[2 * n].wait_recv()
    for ring in other_ff:
        ring.start()
    for ring in whole:
        ring.spread(0)

    for n in range(4):
        wait_arrival(rows.at[n // 2, n % 2], row_recv.at[n])
        value = rows[n // 2, n % 2].astype(F32)
        at = slice(n * 64, (n + 1) * 64)
        rows_out[at, :] = rows[n // 2, n % 2]
        normed_ref[at, :] = (value * norm_scale(value) * gain(gains_ref, 0)).astype(BF)
    latent = dot_nt(normed_ref[...], a_qkv)
    adapted = dot(latent.astype(BF), b_qkv_ref[...])
    wq.last()
    pair_send, pair_recv = take(2)

    def pair_copy(ref, n):
        return remote(ref, ref, pair_send.at[n], pair_recv.at[n], sibling)

    pair_copy(wq_all.at[core], 0).start()
    wo.start()
    pair_copy(wq_all.at[core], 0).wait_send()
    pair_copy(wq_all.at[1 - core], 0).wait_recv()

    cos_table, sine_table = cos_ref[...], sin_ref[...]

    def turn(head):
        return head * cos_table + pltpu.roll(head, HEAD // 2, 1) * sine_table

    def query(n, head):
        q_ref[:, n * HEAD : (n + 1) * HEAD] = (turn(head + bias(n)) * (HEAD ** (-0.5) * LOG2E)).astype(BF)

    pairs = dot(normed_ref[...], wq_all[1, :, 256:]) + adapted[:, 768:]
    for n, head in ((0, turn(pairs[:, :HEAD] + bias(6))), (1, pairs[:, HEAD:] + bias(7))):
        at = slice(n * HEAD, (n + 1) * HEAD)
        kv_part[0, :, at] = head[:CHUNK].astype(BF)
        kv_part[1, :, at] = head[CHUNK:].astype(BF)
    kv = Gather(
        lambda s: kv_part.at[s],
        lambda s, item: kv_all.at[low_chunk(item) if s == 0 else 63 - low_chunk(item)],
        *take(3),
    )
    kv.start()
    heads = dot(normed_ref[...], wq_all[1, :, :256]) + adapted[:, 512:768]
    for n in (4, 5):
        query(n, heads[:, (n - 4) * HEAD : (n - 3) * HEAD])
    kv.second()
    for ring in rings:
        ring.second()
    wo.second()
    heads = dot(normed_ref[...], wq_all[0]) + adapted[:, :512]
    for n in range(4):
        query(n, heads[:, n * HEAD : (n + 1) * HEAD])
    kv.third()
    for ring in rings:
        ring.third()
    wo.third()
    kv.fourth()
    wo.fourth()

    for half in (0, 1):
        wait_arrival(cot_in.at[half], row_recv.at[4 + half])
        start = ((1 - h) * lower + h * (63 - lower)) * CHUNK + half * 64
        at = lax.broadcasted_iota(jnp.int32, (64, D), 0) + start
        cot_own[half * 64 : (half + 1) * 64, :] = jnp.where(
            at < length, cot_in[half].astype(F32), 0.0
        ).astype(BF)
    cot_spread = Spread(cot_own, cot_all, *take(3))
    cot_spread.start()
    kv.last()
    for e in (1, 3, 2):
        for ring in whole:
            ring.spread(e)
    (out_sem,) = take(1)
    copies = []

    def keep(*pairs):
        for src, dst in pairs:
            copies.append(pltpu.make_async_copy(src, dst, out_sem.at[len(copies)]))
            copies[-1].start()

    keep(
        (kv_all, kv_out), (wq_all, wq_out), (q_ref, q_out), (rows_out, rows_hbm), (normed_ref, normed_out),
        (cot_own, cot_out), (limit_ref, limit_out), (cos_ref, cos_out), (sin_ref, sin_out),
        (b_qkv_ref, b_qkv_out), (ao_ref, ao_out), (a_ref.at[pl.ds(0, 3)], a_out), (b_ref.at[1], bo_out),
    )
    wo.last()

    def wo_columns(c, n):
        return wo_all.at[:, pl.ds(pl.multiple_of((2 * n + c) * 384, 128), 384)]

    for n in (0, 1):
        pair_copy(wo_columns(core, n), 1 + n).start()
    for slot in (0, 1):
        turned_ref[slot] = head_columns(q_ref, slot)
    args = (turned_ref, kv_all, limit_ref, acc_ref, stat_ref)

    def end(slot):
        forward_end(slot, mixed_ref, lse_ref, acc_ref, stat_ref)

    blocks = KEYS // CHUNK
    middle = CHUNKS // 2 // blocks
    forward_blocks(0, 0, lower // blocks + 1, *args)
    forward_blocks(1, middle, (63 - lower) // blocks + 1, *args)
    end(0)
    for ring in whole:
        ring.fourth(0)
    cot_spread.second()
    forward_blocks(1, 0, middle // 2, *args)
    for ring in whole:
        ring.fourth(1)
    cot_spread.third()
    forward_blocks(1, middle // 2, middle, *args)
    end(1)
    for n in (0, 1):
        pair_copy(wo_columns(core, n), 1 + n).wait_send()
        pair_copy(wo_columns(1 - core, n), 1 + n).wait_recv()
    keep((wo_all, wo_out), (mixed_ref, mixed_out), (lse_ref, lse_out))

    def project(slot):
        mixed = mixed_ref[pl.ds(pl.multiple_of(slot * CHUNK, CHUNK), CHUNK), :]
        lifted = dot(dot_nt(mixed, ao_ref[...]).astype(BF), bo_ref[...])
        return dot(mixed, wo_all[...]) + lifted

    (cross_sem,) = take(1)
    cross_out[...] = project(1 - h).astype(BF)
    cross = remote(cross_out, cross_in, cross_sem.at[0], cross_sem.at[1], uly_others()[0])
    cross.start()
    for ring in whole:
        ring.fourth(3)
    mine = project(h) + rows_out[pl.ds(pl.multiple_of(h * CHUNK, CHUNK), CHUNK), :].astype(F32)
    for ring in whole:
        ring.fourth(2)
    cross.wait()
    residual = mine + cross_in[...].astype(F32)
    resid_ref[...] = residual
    keep((resid_ref, resid_out))
    nf_own[...] = (residual * norm_scale(residual) * gain(gains_ref, D_TILES)).astype(BF)
    keep((nf_own, nf_out))
    cot_spread.last()
    for ring in whole:
        ring.last()
    for ring in (own_ff[1], other_ff[1]):
        ring.end()
    for n in range(3):
        y_copies[2 * n].wait_send()
        y_copies[2 * n + 1].wait()
    deliver.end()
    for copy in copies:
        copy.wait()


def forward(*args):
    weight = HELD((32, 48, FF_COLS), BF)
    group = GROUP * HEAD
    dma = pltpu.SemaphoreType.DMA
    spread = HELD((2, 4, CHUNK, D), BF)
    return pl.pallas_call(
        forward_kernel,
        out_shape=(
            HELD((2 * CHUNK, group), BF),
            HELD((2 * CHUNK, group), BF),
            HELD((2, 8, ROWS), F32),
            HELD((CHUNKS, CHUNK, 2 * HEAD), BF),
            HELD((2, D, 512), BF),
            HELD((D // 2, D), BF),
            weight, weight, weight,
            HELD((2 * CHUNK, D), BF),
            HELD((2 * CHUNK, D), BF),
            HELD((CHUNK, D), F32),
            HELD((CHUNK, D), BF),
            HELD((CHUNK, D), BF),
            spread,
            HELD((2, 8, ROWS), jnp.int32),
            HELD((2 * CHUNK, HEAD), F32),
            HELD((2 * CHUNK, HEAD), F32),
            HELD((48, 1024), BF),
            HELD((16, group), BF),
            HELD((3, 16, D), BF),
            HELD((16, D), BF),
        ),
        in_specs=[ANY] * 13,
        out_specs=(ANY,) * 22,
        scratch_shapes=[
            pltpu.VMEM((2 * CHUNK, group), BF),
            pltpu.VMEM((2 * CHUNK, group), BF),
            pltpu.VMEM((2, 8, ROWS), F32),
            pltpu.VMEM((2 * CHUNK, D), BF),
            pltpu.VMEM((2 * CHUNK, D), BF),
            pltpu.VMEM((CHUNK, D), F32),
            pltpu.VMEM((CHUNK, D), BF),
            pltpu.VMEM((2, 8, ROWS), jnp.int32),
            pltpu.VMEM((2 * CHUNK, HEAD), F32),
            pltpu.VMEM((2 * CHUNK, HEAD), F32),
            pltpu.VMEM((48, 1024), BF),
            pltpu.VMEM((16, group), BF),
            pltpu.VMEM((4, 16, D), BF),
            pltpu.VMEM((2, 16, D), BF),
            pltpu.VMEM((2, 16, 2 * HEAD), BF),
            pltpu.VMEM((4, SETS, 16, D), BF),
            pltpu.VMEM((2, SETS, 16, D), BF),
            pltpu.VMEM((2, SETS, 16, 2 * HEAD), BF),
            pltpu.VMEM((2, HEAD, ROWS), BF),
            pltpu.SMEM((2,), jnp.int32),
            pltpu.SMEM((2,), jnp.int32),
            pltpu.VMEM((12, 2048), BF),
            pltpu.VMEM((12, D), BF),
            pltpu.VMEM((2, 48, FF // 4), BF),
            pltpu.VMEM((48, FF // 4), BF),
            pltpu.VMEM((40, 128), F32),
            pltpu.VMEM((1, 128), F32),
            pltpu.VMEM((CHUNKS, CHUNK, 2 * HEAD), BF),
            pltpu.VMEM((2, D, 512), BF),
            pltpu.VMEM((D // 2, D), BF),
            pltpu.VMEM((2, 2, 64, D), BF),
            pltpu.VMEM((2, 64, D), BF),
            pltpu.VMEM((2, CHUNK, 2 * HEAD), BF),
            pltpu.VMEM((2, HEAD, ROWS), F32),
            pltpu.VMEM((2, 2, 8, ROWS), F32),
            pltpu.VMEM((4, 16, 512), BF),
            pltpu.VMEM((4, 16, 384), BF),
            pltpu.VMEM((48, 512), BF),
            pltpu.VMEM((48, 384), BF),
            pltpu.VMEM((CHUNK, D), BF),
            pltpu.VMEM((CHUNK, D), BF),
            pltpu.VMEM((CHUNK, D), BF),
            pltpu.VMEM((4, 16, 512), BF),
            pltpu.VMEM((4, 16, 384), BF),
            pltpu.VMEM((3, 48, PADDED), BF),
            dma((8,)), dma((8,)), dma((6,)), dma((6,)),
            dma((2, 3, Ring.sends)), dma((2, 3, 16)), dma((3,)), dma((3,)), dma((3,)),
        ]
        + GATHER_SEMS()
        + GATHER_SEMS()
        + [dma((3,)), dma((3,))]
        + GATHER_SEMS()
        + SPREAD_SEMS
        + [dma((18,)), dma((2,)), dma((8,)), dma((3,))],
        compiler_params=pltpu.CompilerParams(
            collective_id=1, has_side_effects=True, vmem_limit_bytes=48 * 2**20
        ),
        name="forward",
    )(*args)


class RingSum:
    @staticmethod
    def scratch():
        piece, half = (CHUNK, D), (CHUNK // 2, D)
        return [
            pltpu.VMEM((2,) + half, BF),
            pltpu.VMEM((2,) + piece, BF),
            pltpu.VMEM(piece, BF),
            pltpu.VMEM((2,) + piece, BF),
            pltpu.SemaphoreType.DMA((4,)),
            pltpu.SemaphoreType.DMA((4,)),
        ]

    scratches = 6

    def __init__(self, term, scratch):
        self.term = term
        self.halves, self.last_in, self.far, self.near, self.send_sem, self.recv_sem = scratch
        self.w = ring_at()
        self.sent = []

    def send(self, src, dst, recv, d):
        copy = remote(
            src, dst, self.send_sem.at[recv], self.recv_sem.at[recv], ring_place((self.w + d) % 4)
        )
        copy.start()
        self.sent.append(copy)

    def first(self):
        half = CHUNK // 2
        self.far[...] = self.term(2).astype(BF)
        self.send(self.far.at[pl.ds(0, half)], self.halves.at[0], 0, 1)
        self.send(self.far.at[pl.ds(half, half)], self.halves.at[1], 1, 3)

    def second(self):
        half = CHUNK // 2
        for k, d in ((0, 1), (1, 3)):
            total = self.term(d)
            wait_arrival(self.halves.at[k], self.recv_sem.at[k])
            rows = slice(k * half, (k + 1) * half)
            other = slice((1 - k) * half, (2 - k) * half)
            self.near[k, rows] = (total[rows] + self.halves[k].astype(F32)).astype(BF)
            self.near[k, other] = total[other].astype(BF)
            self.send(self.near.at[k], self.last_in.at[k], 2 + k, d)

    def third(self):
        total = self.term(0)
        for k in (0, 1):
            wait_arrival(self.last_in.at[k], self.recv_sem.at[2 + k])
            total += self.last_in[k].astype(F32)
        for copy in self.sent:
            copy.wait_send()
        return total


def ff_kernel(
    set_ref, own_hbm, cot_hbm, gate_hbm, up_hbm, down_hbm, a_wide, a_down, b_wide, b_ff,
    grad_out, down_out, cols_out, wide_out,
    cols_ref, wide_ref, x_ref, cot_ref, gate_w, up_w, down_w, b_cols, a_cols, hidden_ref, grad_gate, grad_up,
    grad_hidden, own_ref, terms, pair, total_ref, down_sum, a_ff, b_out, wide_sets, down_sets, out_sets,
    ff_sets, sems, out_sems, pair_send, pair_recv, *scratch,
):
    y, z, x, blk, uly = place()
    core = uly % 2
    scratch = list(scratch)

    def take(count):
        got = scratch[:count]
        del scratch[:count]
        return got

    first = (35 * uly) // 2 * 128 + y * FF_COLS
    columns = pl.ds(pl.multiple_of(first, 128), FF_COLS)
    pairs = (
        (own_hbm, own_ref), (down_hbm, down_w), (cot_hbm, cot_ref), (gate_hbm, gate_w),
        (a_wide.at[pl.ds(4, 2)], wide_sets), (a_down.at[:, :, columns], down_sets), (b_wide.at[2], out_sets),
        (b_ff.at[:, :, :, columns], ff_sets),
    )
    copies = [pltpu.make_async_copy(src, dst, sems.at[n]) for n, (src, dst) in enumerate(pairs)]
    for copy in copies[:1] + copies[4:] + copies[1:4]:
        copy.start()
    other_blk = blk_of(1 - y, z, x)
    up_send, up_recv, up_sem = take(3)
    rings = [
        Ring(
            up_w.at[b], lambda item: up_w.at[item], yy, yy, 1 + 2 * k, up_send.at[k], up_recv.at[k]
        )
        for k, (yy, b) in enumerate(((y, blk), (1 - y, other_blk)))
    ]
    lines = []
    for k, ring in enumerate(rings):
        for d in range(4):
            item = ring.at(ring.y, (ring.p + d) % 4, ring.q)
            lines.append(pltpu.make_async_copy(up_hbm.at[item], up_w.at[item], up_sem.at[k, d]))
            lines[-1].start()
    at = lax.broadcasted_iota(jnp.int32, (16, FF_COLS), 1) + (y * FF_COLS - 64 * core)
    inside = jnp.logical_and(at >= 0, at < FF // 4)

    def keep(v):
        return jnp.where(inside, v.astype(F32), 0.0).astype(BF)

    def prepare():
        for copy in copies[4:]:
            copy.wait()
        for s in (0, 1):
            number = set_ref[s]
            a_cols[s] = keep(choose(number, lambda c: down_sets[c]))
            b_out[s] = choose(number, lambda c: out_sets[c])
            for n in (0, 1):
                b_cols[s, n] = keep(choose(number, lambda c: ff_sets[n, c]))
                a_ff[s, 16 * n : 16 * n + 16] = choose(number, lambda c: wide_sets[n, c])
        cols_ref[...] = jnp.zeros_like(cols_ref)

    sibling = uly_others()[1]
    greet([sibling, (other_blk, (uly + 2) % 4)] + ring_others(), prepare)
    here = pl.ds(pl.multiple_of(y * FF_COLS, 128), FF_COLS)
    copies[0].wait()
    spread = Spread(own_ref, x_ref, *take(3))
    spread.start()
    for copy in lines:
        copy.wait()
    for e in (0, 1, 3, 2):
        for ring in rings:
            ring.spread(e)

    def flat(ref, s):
        return ref[s].reshape(4 * CHUNK, D)

    order = (1 - core, core)
    copies[1].wait()
    copies[2].wait()
    latent_cots = []
    for k, s in enumerate(order):
        cot = flat(cot_ref, s)
        latent_cots.append(dot_nt(cot, b_out[s]))
        grad_hidden[k] = dot(cot, down_w[...]) + dot(latent_cots[k].astype(BF), a_cols[s])
        (spread.second, spread.third)[k]()
        for ring in rings:
            ring.fourth(k)
    copies[3].wait()
    for e in (3, 2):
        for ring in rings:
            ring.fourth(e)
    spread.last()

    def pair_copy(n, d):
        at = (ring_at() + d) % 4
        return remote(
            terms.at[n, 0, at], pair.at[n, at], pair_send.at[n, d], pair_recv.at[n, d], sibling
        )

    def term(n, d):
        at = (ring_at() + d) % 4
        wait_arrival(pair.at[n, at], pair_recv.at[n, d])
        return terms[n, 1, at].astype(F32) + pair[n, at].astype(F32)

    ring = RingSum(lambda d: term(0, d), take(RingSum.scratches))

    def up_weight():
        return up_w[...].reshape(D, FF_COLS)

    for k, s in enumerate(order):
        rows = flat(x_ref, s)
        latent = dot_nt(rows, a_ff[s])
        low = latent.astype(BF)
        gate = dot(rows, gate_w[...]) + dot(low[:, :16], b_cols[s, 0])
        sigmoid = jax.nn.sigmoid(gate)
        silu = gate * sigmoid
        grad_up[...] = (grad_hidden[k] * silu).astype(BF)
        slope = grad_hidden[k] * (sigmoid * (1.0 + gate * (1.0 - sigmoid)))
        if k == 0:
            for up_ring in rings:
                up_ring.last()
        up = dot(rows, up_weight()) + dot(low[:, 16:], b_cols[s, 1])
        grad_gate[...] = (slope * up).astype(BF)
        hidden_ref[...] = (silu * up).astype(BF)
        back_gate = dot_nt(grad_gate[...], b_cols[s, 0])
        back_up = dot_nt(grad_up[...], b_cols[s, 1])
        grads = (
            dot_nt(grad_gate[...], gate_w[...])
            + dot_nt(grad_up[...], up_weight())
            + dot(back_gate.astype(BF), a_ff[s, :16])
            + dot(back_up.astype(BF), a_ff[s, 16:])
        )
        terms[0, k] = grads.astype(BF).reshape(4, CHUNK, D)
        if k == 0:
            for d in (2, 1, 3, 0):
                pair_copy(0, d).start()
        else:
            ring.first()
        latent_down = dot_nt(hidden_ref[...], a_cols[s])
        down = dot_nt(hidden_ref[...], down_w[...]) + dot(latent_down.astype(BF), b_out[s])
        terms[1, k] = down.astype(BF).reshape(4, CHUNK, D)
        if k == 0:
            for d in (2, 1, 3, 0):
                pair_copy(1, d).start()
        else:
            ring.second()

        def put(ref, n, value, at=slice(None)):
            ref[pl.ds(pl.multiple_of((2 * n + s) * 16, 16), 16), at] = value.astype(BF)

        def turned(value):
            return value.T.astype(BF)

        put(cols_ref, 0, dot(turned(latent_cots[k]), hidden_ref[...]), here)
        put(cols_ref, 1, dot(turned(latent[:, :16]), grad_gate[...]), here)
        put(cols_ref, 2, dot(turned(latent[:, 16:]), grad_up[...]), here)
        put(wide_ref, 0, dot(turned(back_gate), rows))
        put(wide_ref, 1, dot(turned(back_up), rows))
        put(wide_ref, 2, dot(turned(latent_down), flat(cot_ref, s)))
    outs = [
        pltpu.make_async_copy(src, dst, out_sems.at[n])
        for n, (src, dst) in enumerate(
            ((cols_ref, cols_out), (wide_ref, wide_out), (down_sum, down_out), (total_ref, grad_out))
        )
    ]
    outs[0].start()
    outs[1].start()
    for d in range(4):
        down_sum[(ring_at() + d) % 4] = term(1, d).astype(BF)
    outs[2].start()
    total_ref[...] = ring.third()
    outs[3].start()
    for n in (0, 1):
        for d in range(4):
            pair_copy(n, d).wait_send()
    for copy in outs:
        copy.wait()


def feed_forward(*args):
    dma = pltpu.SemaphoreType.DMA
    weight = pltpu.VMEM((D, FF_COLS), BF)
    rows = pltpu.VMEM((4 * CHUNK, FF_COLS), BF)
    pieces = (4, CHUNK, D)
    return pl.pallas_call(
        ff_kernel,
        out_shape=(
            HELD((CHUNK, D), F32),
            HELD(pieces, BF),
            HELD((96, PADDED), BF),
            HELD((96, D), BF),
        ),
        in_specs=[pl.BlockSpec(memory_space=pltpu.SMEM)] + [ANY] * 9,
        out_specs=(ANY,) * 4,
        scratch_shapes=[
            pltpu.VMEM((96, PADDED), BF), pltpu.VMEM((96, D), BF),
            pltpu.VMEM((2,) + pieces, BF), pltpu.VMEM((2,) + pieces, BF),
            weight, pltpu.VMEM((32, 48, FF_COLS), BF), weight,
            pltpu.VMEM((2, 2, 16, FF_COLS), BF), pltpu.VMEM((2, 16, FF_COLS), BF),
            rows, rows, rows,
            pltpu.VMEM((2, 4 * CHUNK, FF_COLS), F32),
            pltpu.VMEM((CHUNK, D), BF),
            pltpu.VMEM((2, 2) + pieces, BF), pltpu.VMEM((2,) + pieces, BF),
            pltpu.VMEM((CHUNK, D), F32), pltpu.VMEM(pieces, BF),
            pltpu.VMEM((2, 32, D), BF), pltpu.VMEM((2, 16, D), BF),
            pltpu.VMEM((2, SETS, 16, D), BF), pltpu.VMEM((SETS, 16, FF_COLS), BF),
            pltpu.VMEM((SETS, 16, D), BF), pltpu.VMEM((2, SETS, 16, FF_COLS), BF),
            dma((8,)), dma((4,)), dma((2, 4)), dma((2, 4)),
            dma((2, Ring.sends)), dma((2, 16)), dma((2, 4)),
        ]
        + SPREAD_SEMS
        + RingSum.scratch(),
        compiler_params=pltpu.CompilerParams(
            collective_id=4, has_side_effects=True, vmem_limit_bytes=62 * 2**20
        ),
        name="feed_forward",
    )(*args)


def backward_blocks(slot, first, last, turned_ref, rows_ref, dot_ref, kv_ref, limit_ref, lse_ref, dkv_ref, acc_ref):
    limit = limit_ref[slot, 0:1, :]
    lse = lse_ref[slot, 0:1, :]
    row_dot = dot_ref[slot, 0:1, :]

    def step(n, carry):
        keys, values = key_block(kv_ref, n, KEYS_BACK)
        scores = jnp.where(key_places(n, KEYS_BACK) <= limit, dot(keys, turned_ref[0, slot]), -1e30)
        probs = jnp.exp2(scores - lse)
        grad_probs = dot(values, turned_ref[1, slot])
        grad_scores = (probs * (grad_probs - row_dot)).astype(BF)
        acc_ref[slot] += dot(keys.T, grad_scores)
        at = pl.ds(pl.multiple_of(n * KEYS_BACK, KEYS_BACK), KEYS_BACK)
        dkv_ref[at, :HEAD] += dot(grad_scores, rows_ref[0, slot])
        dkv_ref[at, HEAD:] += dot(probs.astype(BF), rows_ref[1, slot])
        return carry

    lax.fori_loop(first, last, step, 0)


class Reduce:
    @staticmethod
    def scratch(shape):
        return [
            pltpu.VMEM((2, 3, 2, 4) + shape, BF),
            pltpu.VMEM((2, 3, 2) + shape, BF),
            pltpu.VMEM((2,) + shape, BF),
            pltpu.VMEM((2, 4, 2) + shape, BF),
            pltpu.VMEM((2, 2) + shape, BF),
            pltpu.SemaphoreType.DMA((2, 10)),
            pltpu.SemaphoreType.DMA((2, 10)),
        ]

    scratches = 7

    def __init__(self, part, scratch):
        self.part = part
        self.buf_q, self.buf_p, self.buf_y, self.sum_p, self.sum_y, self.send_sem, self.recv_sem = scratch
        self.y, self.z, self.x, self.blk, self.uly = place()
        self.pq = ((self.x, self.z), (self.z, self.x))
        self.flying = []

    def send(self, src, dst, half, n, y, p, q):
        target = blk_of(y, q, p) if half == 0 else blk_of(y, p, q)
        copy = remote(
            src, dst, self.send_sem.at[half, n], self.recv_sem.at[half, n], (target, self.uly)
        )
        copy.start()
        self.flying.append(copy)

    def land(self):
        for copy in self.flying:
            copy.wait()
        self.flying = []

    def first(self):
        for d in (2, 1, 3):
            for half in (0, 1):
                p, q = self.pq[half]
                to = (q + d) % 4
                for y in (0, 1):
                    src = self.part.at[0, y, to] if half == 0 else self.part.at[1, y, :, to]
                    self.send(
                        src, self.buf_q.at[half, d - 1, y], half, (d - 1) * 2 + y, self.y, p, to
                    )

    def second(self):
        self.land()
        for d in (2, 1, 3, 0):
            for half in (0, 1):
                p, q = self.pq[half]
                to = (p + d) % 4
                for y in (0, 1):
                    own = self.part[0, y, q, to] if half == 0 else self.part[1, y, to, q]
                    total = own.astype(F32)
                    for n in range(3):
                        total += self.buf_q[half, n, y, to].astype(F32)
                    self.sum_p[half, d, y] = total.astype(BF)
                if d > 0:
                    self.send(
                        self.sum_p.at[half, d], self.buf_p.at[half, d - 1], half, 5 + d, self.y, to, q
                    )

    def third(self):
        self.land()
        for k in (1, 0):
            for half in (0, 1):
                p, q = self.pq[half]
                y = self.y if k == 0 else 1 - self.y
                total = self.sum_p[half, 0, y].astype(F32)
                for n in range(3):
                    total += self.buf_p[half, n, y].astype(F32)
                self.sum_y[half, k] = total.astype(BF)
                if k == 1:
                    self.send(self.sum_y.at[half, 1], self.buf_y.at[half], half, 9, 1 - self.y, p, q)

    def fourth(self):
        self.land()
        return [self.sum_y[half, 0].astype(F32) + self.buf_y[half].astype(F32) for half in (0, 1)]


class Shed:
    @staticmethod
    def scratch(shape):
        return [
            pltpu.VMEM((2, 4) + shape, BF),
            pltpu.VMEM((2, 4) + shape, BF),
            pltpu.VMEM((2, 2, 4) + shape, BF),
            pltpu.VMEM((4, 2) + shape, BF),
            pltpu.VMEM((3, 2) + shape, BF),
            pltpu.VMEM((2,) + shape, BF),
            pltpu.VMEM(shape, BF),
            pltpu.SemaphoreType.DMA((10,)),
            pltpu.SemaphoreType.DMA((10,)),
        ]

    scratches = 9

    def __init__(self, part, half, rows, order, scratch):
        self.part, self.half, self.rows, self.order = part, half, rows, order
        (
            self.buf_far, self.sum_mid, self.buf_in, self.sum_p, self.buf_p, self.sum_y, self.buf_y,
            self.send_sem, self.recv_sem,
        ) = scratch
        self.y, self.z, self.x, self.blk, self.uly = place()
        self.p, self.q = (self.x, self.z) if order == 0 else (self.z, self.x)
        self.flying = []

    def line(self, y, q):
        rows = pl.ds(*self.rows)
        if self.order == 0:
            return self.part.at[self.half, y, q, :, rows]
        return self.part.at[self.half, y, :, q, rows]

    def value(self, y, q, p):
        start, size = self.rows
        z, x = (q, p) if self.order == 0 else (p, q)
        return self.part[self.half, y, z, x, start : start + size].astype(F32)

    def send(self, src, dst, n, y, p, q):
        target = blk_of(y, q, p) if self.order == 0 else blk_of(y, p, q)
        copy = remote(src, dst, self.send_sem.at[n], self.recv_sem.at[n], (target, self.uly))
        copy.start()
        self.flying.append(copy)

    def land(self):
        for copy in self.flying:
            copy.wait()
        self.flying = []

    def first(self):
        for y, d in ((0, 1), (1, 3)):
            to = (self.q + d) % 4
            self.send(self.line(y, (self.q + 2) % 4), self.buf_far.at[y], y, self.y, self.p, to)
        for y, d in ((1, 1), (0, 3)):
            to = (self.q + d) % 4
            self.send(self.line(y, to), self.buf_in.at[d // 2, y], 2 + d // 2, self.y, self.p, to)

    def second(self):
        direct = self.flying[2:]
        self.flying = self.flying[:2]
        self.land()
        for y, d in ((0, 1), (1, 3)):
            to = (self.q + d) % 4
            for p in range(4):
                total = self.value(y, to, p) + self.buf_far[y, p].astype(F32)
                self.sum_mid[y, p] = total.astype(BF)
            self.send(self.sum_mid.at[y], self.buf_in.at[d // 2, y], 4 + y, self.y, self.p, to)
        self.flying += direct

    def third(self):
        self.land()
        for d in (2, 1, 3, 0):
            to = (self.p + d) % 4
            for y in (0, 1):
                total = self.value(y, self.q, to)
                for n in (0, 1):
                    total += self.buf_in[n, y, to].astype(F32)
                self.sum_p[d, y] = total.astype(BF)
            if d > 0:
                self.send(self.sum_p.at[d], self.buf_p.at[d - 1], 5 + d, self.y, to, self.q)

    def fourth(self):
        self.land()
        for k in (1, 0):
            y = self.y if k == 0 else 1 - self.y
            total = self.sum_p[0, y].astype(F32)
            for n in range(3):
                total += self.buf_p[n, y].astype(F32)
            self.sum_y[k] = total.astype(BF)
            if k == 1:
                self.send(self.sum_y.at[1], self.buf_y, 9, 1 - self.y, self.p, self.q)

    def last(self):
        self.land()
        return self.sum_y[0].astype(F32) + self.buf_y[...].astype(F32)


def reduce_others():
    y, z, x, blk, uly = place()
    return (
        [(blk_of(1 - y, z, x), uly)]
        + [(blk_of(y, z, (x + d) % 4), uly) for d in (1, 2, 3)]
        + [(blk_of(y, (z + d) % 4, x), uly) for d in (1, 2, 3)]
    )


UNIT = (16, 128)


class Total:
    @staticmethod
    def scratch(kept, summed):
        shape = (kept + summed,) + UNIT
        return (
            [pltpu.VMEM((2, 2, 4, 4) + shape, BF)]
            + Reduce.scratch(shape)
            + [
                pltpu.VMEM((2,) + shape, BF),
                pltpu.VMEM((3, 2) + shape, BF),
                pltpu.VMEM((2, 4 * kept + summed) + UNIT, BF),
                pltpu.SemaphoreType.DMA((3,)),
                pltpu.SemaphoreType.DMA((3,)),
                pltpu.SemaphoreType.DMA((31,)),
                pltpu.SemaphoreType.DMA((31,)),
                pltpu.SemaphoreType.DMA,
                pltpu.SemaphoreType.DMA,
                pltpu.SemaphoreType.DMA,
            ]
        )

    scratches = 18

    @staticmethod
    def shape(kept, summed):
        return HELD((2, 2, 4, 4, 4 * kept + summed) + UNIT, BF)

    def __init__(self, kept, summed, all_ref, scratch):
        self.kept, self.summed, self.all_ref = kept, summed, all_ref
        self.part = scratch[0]
        self.reduce = Reduce(self.part, scratch[1:8])
        self.own, self.buf, self.full, self.send_sem, self.recv_sem = scratch[8:13]
        self.all_send, self.all_recv, self.local_sem, self.pair_send, self.pair_recv = scratch[13:18]
        self.y, self.z, self.x, self.blk, self.uly = place()
        self.core = self.uly % 2
        self.flying = []

    def pack(self, values, first, per, at):
        for n, value in enumerate(values, first):
            item = n // per
            self.part[item // 32, item // 16 % 2, item // 4 % 4, item % 4, at + n % per] = value.astype(BF)

    def pack_kept(self, values, first=0):
        self.pack(values, first, self.kept, 0)

    def pack_summed(self, values, first=0):
        self.pack(values, first, self.summed, self.kept)

    def clear(self, kept, summed):
        nothing = jnp.zeros(UNIT, BF)
        self.pack_kept([nothing] * (64 * self.kept - kept), kept)
        self.pack_summed([nothing] * (64 * self.summed - summed), summed)

    def across(self):
        for half, total in enumerate(self.reduce.fourth()):
            self.own[half] = total.astype(BF)
        self.copies = []
        for n, other in enumerate(uly_others()):
            copy = remote(self.own, self.buf.at[n], self.send_sem.at[n], self.recv_sem.at[n], other)
            copy.start()
            self.copies.append(copy)

    def send(self, src, dst, n, y, z, x):
        copy = remote(src, dst, self.all_send.at[n], self.all_recv.at[n], (blk_of(y, z, x), self.uly))
        copy.start()
        self.flying.append(copy)

    def item(self, y, d=0, e=0):
        dz, dx = self.core * d + (1 - self.core) * e, self.core * e + (1 - self.core) * d
        return self.all_ref.at[self.core, y, (self.z + dz) % 4, (self.x + dx) % 4]

    def along(self, y, src, n, d, e):
        dz, dx = self.core * d + (1 - self.core) * e, self.core * e + (1 - self.core) * d
        self.send(src[0], src[1], n, self.y, (self.z + dz) % 4, (self.x + dx) % 4)

    def along_first(self, y, src, first):
        for d in (1, 2, 3):
            self.along(y, (src, self.item(y)), first + d, d, 0)

    def join(self):
        for copy in self.copies:
            copy.wait()
        kept = self.kept
        terms = [self.own] + [self.buf.at[n] for n in range(3)]
        who = [self.uly] + [other[1] for other in uly_others()]
        for half in (0, 1):
            for term, uly in zip(terms, who):
                self.full[half, pl.ds(uly * kept, kept)] = term[half, :kept]
            if self.summed:
                self.full[half, 4 * kept :] = sum(
                    term[half, kept:].astype(F32) for term in terms
                ).astype(BF)
        own = self.full.at[self.core]
        self.send(own, self.item(self.y), 0, 1 - self.y, self.z, self.x)
        self.along_first(self.y, own, 0)
        self.local = pltpu.make_async_copy(own, self.item(self.y), self.local_sem)
        self.local.start()

    def onward(self):
        other = self.item(1 - self.y)
        wait_arrival(other, self.all_recv.at[0])
        self.along_first(1 - self.y, other, 3)

    def spread(self):
        self.local.wait()
        for k, y in enumerate((self.y, 1 - self.y)):
            for d in range(4):
                if d > 0:
                    wait_arrival(self.item(y, 4 - d), self.all_recv.at[3 * k + d])
                for e in (1, 2, 3):
                    ref = self.item(y, (4 - d) % 4)
                    self.along(y, (ref, ref), 7 + k * 12 + d * 3 + e - 1, 0, e)

    def hand(self):
        for k, y in enumerate((self.y, 1 - self.y)):
            for d in range(4):
                for e in (1, 2, 3):
                    wait_arrival(
                        self.item(y, (4 - d) % 4, 4 - e), self.all_recv.at[7 + k * 12 + d * 3 + e - 1]
                    )
        self.pair(self.core).start()

    def pair(self, core):
        return remote(
            self.all_ref.at[core], self.all_ref.at[core], self.pair_send, self.pair_recv, uly_others()[1]
        )

    def end(self):
        for copy in self.flying:
            copy.wait_send()
        self.pair(self.core).wait_send()
        wait_arrival(self.all_ref.at[1 - self.core], self.pair_recv)

    def steps(self):
        return [
            self.reduce.first, self.reduce.second, self.reduce.third, self.across, self.join,
            self.onward, self.spread, self.hand, self.end,
        ]


def units(value):
    rows, columns = value.shape
    return [
        value[n * 16 : (n + 1) * 16, t * 128 : (t + 1) * 128]
        for n in range(rows // 16) for t in range(columns // 128)
    ]


FF_KEPT, FF_SUMMED, QKV_KEPT = 2, 2, 1
COL_TILES = PADDED // 128
D_TILES = D // 128
DKV_ROWS = CHUNK // 2
DKV_STREAMS = 2


def backward_kernel(
    gains_hbm, total_hbm, down_hbm, cols_hbm, ff_hbm, resid_hbm, cot_hbm, ao_hbm, mixed_hbm, wo_hbm, kv_hbm, q_hbm, limit_hbm, lse_hbm,
    wq_hbm, rows_hbm, normed_hbm, b_qkv_hbm, cos_hbm, sin_hbm, a_hbm, bo_hbm,
    result_ref, input_grad_ref, ff_all, qkv_all,
    gains_ref, total_ref, down_ref, cols_ref, ff_ref, resid_ref, cot_ref, ao_ref, mixed_ref, wo_ref, kv_ref, q_ref, limit_ref,
    lse_ref, wq_ref, rows_ref, normed_ref, b_qkv_ref, cos_ref, sin_ref, a_ref, bo_ref, dkv_ref, acc_ref, part, dq_ref, grad_ref, grad_attn, grad_resid, grad_qkv,
    cross_out, cross_in, home_out, home_in, turned_ref, by_rows_ref, dot_ref, copy_sem, cross_sem, home_send,
    home_recv, *scratch,
):
    y, z, x, blk, uly = place()
    core, h = uly % 2, uly // 2
    scratch = list(scratch)

    def take(count):
        got = scratch[:count]
        del scratch[:count]
        return got

    chunk = 2 * blk + h
    upper = chunk // 32
    home = (1 - h) * blk + h * (31 - blk)
    home_from = [(home, upper * 2 + s) for s in (0, 1)]
    lower = low_chunk(blk)
    own_chunk = (1 - h) * lower + h * (63 - lower)
    home_to = [(own_chunk // 2, (own_chunk % 2) * 2 + half) for half in (0, 1)]
    copies = [
        pltpu.make_async_copy(src, dst, copy_sem.at[n])
        for n, (src, dst) in enumerate(
            (
                (total_hbm, total_ref), (resid_hbm, resid_ref), (cot_hbm, cot_ref), (gains_hbm, gains_ref),
                (cols_hbm, cols_ref), (ff_hbm, ff_ref), (down_hbm, down_ref), (ao_hbm, ao_ref), (mixed_hbm, mixed_ref),
                (wo_hbm, wo_ref), (bo_hbm, bo_ref), (kv_hbm, kv_ref),
                (q_hbm, q_ref), (limit_hbm, limit_ref), (lse_hbm, lse_ref), (wq_hbm, wq_ref),
                (rows_hbm, rows_ref), (normed_hbm, normed_ref), (b_qkv_hbm, b_qkv_ref),
                (cos_hbm, cos_ref), (sin_hbm, sin_ref), (a_hbm, a_ref),
            )
        )
    ]
    for copy in copies:
        copy.start()
    greet(
        reduce_others() + uly_others() + [(blk_of(1 - y, z, x), (uly + 2) % 4)] + home_from + home_to
    )
    collect_out = RingSum(
        lambda d: down_ref[(ring_at() + d) % 4].astype(F32), take(RingSum.scratches)
    )
    low, high = (
        [
            Shed(part, half, (n * DKV_ROWS, DKV_ROWS), n, take(Shed.scratches))
            for n in range(DKV_STREAMS)
        ]
        for half in (0, 1)
    )
    ff_total = Total(FF_KEPT, FF_SUMMED, ff_all, take(Total.scratches))
    qkv_total = Total(QKV_KEPT, 0, qkv_all, take(Total.scratches))
    deliver = Deliver()

    def send_home(n, value):
        home_out[n] = value.astype(BF)
        for half in (0, 1):
            deliver.send(
                home_out.at[n, pl.ds(half * 64, 64)], home_in.at[n, core],
                home_send.at[n, half], home_recv.at[n, core], home_to[half],
            )

    def arrived_home(n):
        for s in (0, 1):
            wait_arrival(home_in.at[n, s], home_recv.at[n, s])
        return home_in[n].astype(F32)

    def ready(first, last):
        for copy in copies[first:last]:
            copy.wait()

    ready(0, 4)
    residual = resid_ref[...]
    value = cot_ref[...].astype(F32) + norm_back(
        residual, norm_scale(residual), gain(gains_ref, D_TILES), total_ref[...]
    )
    grad_resid[...] = value
    own_rows = pl.ds(pl.multiple_of(h * CHUNK, CHUNK), CHUNK)
    other_rows = pl.ds(pl.multiple_of((1 - h) * CHUNK, CHUNK), CHUNK)
    grad_attn[own_rows, :] = value.astype(BF)
    partner = uly_others()[0]
    cross = remote(
        grad_attn.at[own_rows], grad_attn.at[own_rows], cross_sem.at[0], cross_sem.at[1], partner
    )
    cross.start()
    ready(4, 11)
    ff_total.pack_kept(units(cols_ref))
    ff_total.pack_summed(units(ff_ref))
    ff_total.clear(6 * COL_TILES, 6 * D_TILES)
    steps = ff_total.steps()

    def beside(*more):
        for step in more:
            step()
        if steps:
            steps.pop(0)()

    beside()
    at_o = 3 * D_TILES + D_TILES // 2 + 2
    qkv_total.clear(at_o + D_TILES // 2 + D_TILES, 0)
    dkv_ref[...] = jnp.zeros_like(dkv_ref)
    acc_ref[...] = jnp.zeros_like(acc_ref)
    latent_o = dot_nt(ao_ref[...], mixed_ref[...]).astype(BF)
    cross.wait_send()
    wait_arrival(grad_attn.at[other_rows], cross_sem.at[1])
    back_o = dot_nt(grad_attn[...], bo_ref[...]).astype(BF)
    grad_ref[...] = (dot_nt(grad_attn[...], wo_ref[...]) + dot(back_o, ao_ref[...])).astype(BF)
    back_o = dot_nt(bo_ref[...], grad_attn[...]).astype(BF)
    qkv_total.pack_kept(
        units(dot(back_o, mixed_ref[...])) + units(dot(latent_o, grad_attn[...])), at_o
    )
    beside()

    ready(11, 15)
    def pack(half):
        def one(n, carry):
            chunk = low_chunk(n) if half == 0 else 63 - low_chunk(n)
            rows = dkv_ref[pl.ds(pl.multiple_of(chunk * CHUNK, CHUNK), CHUNK), :]
            both = jnp.concatenate([rows[:, :HEAD] * LN2, rows[:, HEAD:]], axis=1)
            part[half, n // 16, n // 4 % 4, n % 4] = both.astype(BF)
            return carry

        lax.fori_loop(0, 32, one, 0)

    def shed(streams, name):
        def run():
            for stream in streams:
                getattr(stream, name)()

        return run

    args = (turned_ref, by_rows_ref, dot_ref, kv_ref, limit_ref, lse_ref, dkv_ref, acc_ref)
    step = KEYS_BACK // CHUNK
    middle = CHUNKS // 2 // step
    beside()
    for slot in (0, 1):
        for n, ref in enumerate((q_ref, grad_ref)):
            turned_ref[n, slot] = head_columns(ref, slot)
            by_rows_ref[n, slot] = head_rows(ref, slot)
        row_dot = turned_ref[1, slot].astype(F32) * head_columns(mixed_ref, slot).astype(F32)
        dot_ref[slot] = jnp.broadcast_to(jnp.sum(row_dot, axis=0, keepdims=True), (8, ROWS))
    backward_blocks(1, middle, (63 - lower) // step + 1, *args)
    backward_blocks(0, 0, lower // step + 1, *args)
    pack(1)
    beside(shed(high, "first"))
    names = ["second", "third", "fourth"]
    extra = [collect_out.first, collect_out.second]
    for n in range(0, middle, 2):
        backward_blocks(1, n, n + 2, *args)
        more = [shed(high, names.pop(0))] if names else []
        more += [extra.pop(0)] if extra else []
        if n < middle - 2:
            beside(*more)
    pack(0)
    for stream in low:
        stream.first()
    for slot in (0, 1):
        for n in range(GROUP):
            dq_ref[slot * CHUNK : (slot + 1) * CHUNK, n * HEAD : (n + 1) * HEAD] = (
                acc_ref[slot, :, n * CHUNK : (n + 1) * CHUNK].T * HEAD ** (-0.5)
            )
    ready(15, 22)
    a_qkv = a_ref[...].reshape(48, D)
    for stream in low:
        stream.second()
    beside()
    cos_table, sine_table = cos_ref[...], sin_ref[...]

    def turn_back(value, rows=slice(None)):
        return value * cos_table[rows] - pltpu.roll(value, HEAD // 2, 1) * sine_table[rows]

    for n in range(GROUP):
        at = slice(n * HEAD, (n + 1) * HEAD)
        grad_qkv[:, at] = turn_back(dq_ref[:, at]).astype(BF)
    group = GROUP * HEAD

    def key_value(half, streams):
        for n, stream in enumerate(streams):
            rows = slice(half * CHUNK + n * DKV_ROWS, half * CHUNK + (n + 1) * DKV_ROWS)
            value = stream.last()
            grad_qkv[rows, group : group + HEAD] = turn_back(value[:, :HEAD], rows).astype(BF)
            grad_qkv[rows, group + HEAD :] = value[:, HEAD:].astype(BF)

    key_value(1, high)
    for stream in low:
        stream.third()
    send_home(0, resid_ref[...] + collect_out.third())
    latent_qkv = dot_nt(a_qkv, normed_ref[...]).astype(BF)
    for stream in low:
        stream.fourth()
    key_value(0, low)

    def project_back(rows):
        grads = grad_qkv[rows, :]
        lifted = dot(dot_nt(grads, b_qkv_ref[...]).astype(BF), a_qkv)
        return dot_nt(grads[:, :512], wq_ref[0]) + dot_nt(grads[:, 512:], wq_ref[1]) + lifted

    cross_out[...] = project_back(other_rows).astype(BF)
    cross = remote(cross_out, cross_in, cross_sem.at[2], cross_sem.at[3], partner)
    cross.start()
    back_qkv = dot_nt(b_qkv_ref[...], grad_qkv[...]).astype(BF)
    grad_b = dot(latent_qkv, grad_qkv[...])
    qkv_total.pack_kept(
        units(dot(back_qkv, normed_ref[...]))
        + units(grad_b[:16, :group])
        + units(grad_b[16:32, group : group + HEAD])
        + units(grad_b[32:, group + HEAD :])
    )
    last_steps = qkv_total.steps()
    last_steps.pop(0)()
    mine = project_back(own_rows)
    last_steps.pop(0)()
    beside()
    cross.wait()
    mine = mine + cross_in[...].astype(F32)
    tokens = rows_ref[own_rows, :].astype(F32)
    send_home(1, grad_resid[...] + norm_back(tokens, norm_scale(tokens), gain(gains_ref, 0), mine))
    for step in last_steps + steps:
        step()
    result_ref[...] = arrived_home(0).astype(BF)
    input_grad_ref[...] = arrived_home(1).astype(BF)
    deliver.end()


def backward(*args):
    dma = pltpu.SemaphoreType.DMA
    group = GROUP * HEAD
    return pl.pallas_call(
        backward_kernel,
        out_shape=(
            jax.ShapeDtypeStruct((2, CHUNK // 2, D), BF),
            jax.ShapeDtypeStruct((2, CHUNK // 2, D), BF),
            Total.shape(FF_KEPT, FF_SUMMED),
            Total.shape(QKV_KEPT, 0),
        ),
        in_specs=[ANY] * 22,
        out_specs=(IN_VMEM, IN_VMEM, ANY, ANY),
        scratch_shapes=[
            pltpu.VMEM((40, 128), F32),
            pltpu.VMEM((CHUNK, D), F32),
            pltpu.VMEM((4, CHUNK, D), BF),
            pltpu.VMEM((96, PADDED), BF),
            pltpu.VMEM((96, D), BF),
            pltpu.VMEM((CHUNK, D), F32),
            pltpu.VMEM((CHUNK, D), BF),
            pltpu.VMEM((16, group), BF),
            pltpu.VMEM((2 * CHUNK, group), BF),
            pltpu.VMEM((D // 2, D), BF),
            pltpu.VMEM((CHUNKS, CHUNK, 2 * HEAD), BF),
            pltpu.VMEM((2 * CHUNK, group), BF),
            pltpu.VMEM((2, 8, ROWS), jnp.int32),
            pltpu.VMEM((2, 8, ROWS), F32),
            pltpu.VMEM((2, D, 512), BF),
            pltpu.VMEM((2 * CHUNK, D), BF),
            pltpu.VMEM((2 * CHUNK, D), BF),
            pltpu.VMEM((48, 1024), BF),
            pltpu.VMEM((2 * CHUNK, HEAD), F32),
            pltpu.VMEM((2 * CHUNK, HEAD), F32),
            pltpu.VMEM((3, 16, D), BF),
            pltpu.VMEM((16, D), BF),
            pltpu.VMEM((CHUNKS * CHUNK, 2 * HEAD), F32),
            pltpu.VMEM((2, HEAD, ROWS), F32),
            pltpu.VMEM((2, 2, 4, 4, CHUNK, 2 * HEAD), BF),
            pltpu.VMEM((2 * CHUNK, group), F32),
            pltpu.VMEM((2 * CHUNK, group), BF),
            pltpu.VMEM((2 * CHUNK, D), BF),
            pltpu.VMEM((CHUNK, D), F32),
            pltpu.VMEM((2 * CHUNK, 1024), BF),
            pltpu.VMEM((CHUNK, D), BF),
            pltpu.VMEM((CHUNK, D), BF),
            pltpu.VMEM((2, CHUNK, D), BF),
            pltpu.VMEM((2, 2, CHUNK // 2, D), BF),
            pltpu.VMEM((2, 2, HEAD, ROWS), BF),
            pltpu.VMEM((2, 2, ROWS, HEAD), BF),
            pltpu.VMEM((2, 8, ROWS), F32),
            dma((22,)), dma((4,)), dma((2, 2)), dma((2, 2)),
        ]
        + RingSum.scratch()
        + Shed.scratch((DKV_ROWS, 2 * HEAD)) * (2 * DKV_STREAMS)
        + Total.scratch(FF_KEPT, FF_SUMMED)
        + Total.scratch(QKV_KEPT, 0),
        compiler_params=pltpu.CompilerParams(
            collective_id=2, has_side_effects=True, vmem_limit_bytes=60 * 2**20
        ),
        name="backward",
    )(*args)


def fold_kernel(
    set_ref, result_in, grad_in, ff_hbm, qkv_hbm, result_ref, input_grad_ref, a_wide, a_down, b_wide, b_kv, b_ff,
    ff_ref, qkv_ref, sems,
):
    c = pl.program_id(0)
    share = [jnp.where(set_ref[s] == c, 1.0, 0.0) for s in (0, 1)]

    @pl.when(c == 0)
    def _():
        copies = [
            pltpu.make_async_copy(src, dst, sems.at[n])
            for n, (src, dst) in enumerate(((ff_hbm, ff_ref), (qkv_hbm, qkv_ref)))
        ]
        for copy in copies:
            copy.start()
        result_ref[...] = result_in[...]
        input_grad_ref[...] = grad_in[...].astype(F32)
        for copy in copies:
            copy.wait()

    chosen = jnp.logical_or(set_ref[0] == c, set_ref[1] == c)

    @pl.when(jnp.logical_not(chosen))
    def _():
        for ref in (a_wide, a_down, b_wide, b_kv, b_ff):
            ref[...] = jnp.zeros_like(ref)

    @pl.when(chosen)
    def _():
        fold_set(share, ff_ref, qkv_ref, a_wide, a_down, b_wide, b_kv, b_ff)


def fold_set(share, ff_ref, qkv_ref, a_wide, a_down, b_wide, b_kv, b_ff):
    def kept(ref, per, n, u):
        item = n // per
        return ref[item // 32, item // 16 % 2, item // 4 % 4, item % 4, u * per + n % per].astype(F32)

    def ff_kept(n, u):
        return kept(ff_ref, FF_KEPT, n, u)

    def qkv_kept(n, u):
        return kept(qkv_ref, QKV_KEPT, n, u)

    def summed(n):
        item = n // FF_SUMMED
        return ff_ref[
            item // 32, item // 16 % 2, item // 4 % 4, item % 4, 4 * FF_KEPT + n % FF_SUMMED
        ].astype(F32)

    def put(ref, at, tile, value):
        ref[at + (slice(None), slice(tile * 128, (tile + 1) * 128))] = (
            share[0] * value(0) + share[1] * value(1)
        )

    for n in range(3):
        for t in range(D_TILES):
            put(a_wide, (n, 0), t, lambda s: qkv_kept(n * D_TILES + t, s) + qkv_kept(n * D_TILES + t, 2 + s))
    half = D_TILES // 2
    at_o = 3 * D_TILES + half + 2
    for t in range(D_TILES):
        h, part = t // half, t % half
        put(a_wide, (3, 0), t, lambda s: qkv_kept(at_o + part, 2 * h + s))
        put(b_wide, (0, 0), t, lambda s: qkv_kept(3 * D_TILES + part, 2 * h + s))
        put(
            b_wide, (1, 0), t,
            lambda s: qkv_kept(at_o + half + t, s) + qkv_kept(at_o + half + t, 2 + s),
        )
        for n, (ref, at) in enumerate(((a_wide, (4, 0)), (a_wide, (5, 0)), (b_wide, (2, 0)))):
            put(ref, at, t, lambda s: summed((2 * n + s) * D_TILES + t))
    for n in (0, 1):
        for h in (0, 1):
            put(b_kv, (n, 0), h, lambda s: qkv_kept(3 * D_TILES + half + n, 2 * h + s))
    for n, (ref, at) in enumerate(((a_down, (0,)), (b_ff, (0, 0)), (b_ff, (1, 0)))):
        for t in range(FF // 128):
            where = [
                (u, t - start) for u, start in enumerate((0, 17, 35, 52)) if 0 <= t - start < COL_TILES
            ]
            put(
                ref, at, t,
                lambda s: sum(ff_kept((2 * n + s) * COL_TILES + tile, u) for u, tile in where),
            )


def fold(set_index, result, input_grad, ff_all, qkv_all):
    rows = pl.BlockSpec(result.shape, lambda c: (0, 0, 0))

    def by_set(lead, columns):
        shape = lead + (1, 16, columns)
        return pl.BlockSpec(shape, lambda c: (0,) * len(lead) + (c, 0, 0))

    def out(lead, columns):
        return jax.ShapeDtypeStruct(lead + (SETS, 16, columns), F32)

    outs = (((6,), D), ((), FF), ((3,), D), ((2,), 2 * HEAD), ((2,), FF))
    return pl.pallas_call(
        fold_kernel,
        grid=(SETS,),
        out_shape=(
            jax.ShapeDtypeStruct(result.shape, BF),
            jax.ShapeDtypeStruct(result.shape, F32),
        )
        + tuple(out(*o) for o in outs),
        in_specs=[pl.BlockSpec(memory_space=pltpu.SMEM), rows, rows, ANY, ANY],
        out_specs=(rows, rows) + tuple(by_set(*o) for o in outs),
        scratch_shapes=[
            pltpu.VMEM(ff_all.shape, BF), pltpu.VMEM(qkv_all.shape, BF), pltpu.SemaphoreType.DMA((2,))
        ],
        compiler_params=pltpu.CompilerParams(vmem_limit_bytes=40 * 2**20),
        name="fold",
    )(set_index, result, input_grad, ff_all, qkv_all)


def norm_scale(hidden):
    return lax.rsqrt(jnp.mean(hidden * hidden, axis=-1, keepdims=True) + EPS)


def norm_back(hidden, scaled, gain_vec, upstream):
    normed = hidden * scaled
    weighted = upstream * gain_vec
    return scaled * (weighted - normed * jnp.mean(weighted * normed, axis=-1, keepdims=True))


def held(*arrays):
    return [pltpu.with_memory_space_constraint(v, pltpu.HBM) for v in arrays]


def body(
    tokens, cotangent, lengths, set_index, norm_in, norm_ff, qkv_bias, w_qkv, w_out, w_gate_up, w_down,
    a_wide, a_down, b_wide, b_kv, b_ff,
):
    frequencies = np.float64(THETA) ** (-np.arange(0, HEAD, 2, dtype=np.float64) / HEAD)
    frequencies = jnp.asarray(np.concatenate([frequencies, frequencies])[None].astype(np.float32))
    gains = jnp.concatenate([norm_in, norm_ff, qkv_bias]).reshape(40, 128)
    (
        q, mixed, lse, kv_all, qkv_w, out_w, gate_w, up_w, down_w, rows, normed, residual, grad_out,
        normed_ff, grad_gathered, limit, cos_table, sine_table, b_qkv, ao, a_own, bo,
    ) = forward(
        *held(
            tokens, cotangent, lengths, set_index, w_qkv, w_out, w_gate_up, w_down.T, gains, frequencies,
            a_wide, b_wide, b_kv,
        )
    )
    gate_w, down_w = (w.reshape(D, FF_COLS) for w in (gate_w, down_w))
    grad_normed_ff, down_sum, cols, ff_wide = feed_forward(
        set_index, normed_ff, grad_gathered, gate_w, up_w, down_w, *held(a_wide, a_down, b_wide, b_ff)
    )
    result, input_grad, ff_all, qkv_all = backward(
        gains,
        grad_normed_ff, down_sum, cols, ff_wide, residual, grad_out, ao, mixed, out_w, kv_all, q, limit, lse,
        qkv_w, rows, normed, b_qkv, cos_table, sine_table, a_own, bo,
    )
    return tuple(fold(set_index, *held(result, input_grad, ff_all, qkv_all)))


def solution(mesh):
    spread = P(None, ("blk", "uly"), None)
    in_specs = (
        spread, spread, P(), P(), P(), P(), P(),
        P(("blk", "uly"), None), P(("blk", "uly"), None), P(None, "blk", "uly"), P("uly", "blk"),
        P(), P(), P(), P(), P(),
    )
    out_specs = (spread, spread, P(), P(), P(), P(), P())
    return jax.shard_map(body, mesh=mesh, in_specs=in_specs, out_specs=out_specs, check_vma=False)
```

```python
import functools

import jax
import jax.numpy as jnp
import numpy as np
from jax import lax
from jax.experimental import pallas as pl
from jax.experimental.pallas import tpu as pltpu
from jax.sharding import PartitionSpec as P

HEADS = 12
KV_HEADS = 2
HEAD = 128
GROUP = HEADS // KV_HEADS
FF = 8960
SETS = 8
D = 1536
CHUNK = 128
CHUNKS = 64
PADDED = 2304
EPS = 1e-06
THETA = 1000000.0
LOG2E = 1.4426950408889634
LN2 = 0.6931471805599453
MESH = pl.DeviceIdType.MESH
BF = jnp.bfloat16
F32 = jnp.float32
ANY = pl.BlockSpec(memory_space=pltpu.HBM)
IN_VMEM = pl.BlockSpec(memory_space=pltpu.VMEM)
HELD = pltpu.HBM


def blk_of(y, z, x):
    return y * 16 + z * 4 + x


def low_chunk(blk):
    return (1 - blk // 16) * 2 * blk + blk // 16 * (63 - 2 * blk)


def place():
    blk = lax.axis_index("blk")
    return blk // 16, (blk // 4) % 4, blk % 4, blk, lax.axis_index("uly")


def ring_others():
    y, z, x, blk, uly = place()
    return [
        (blk_of(1 - y, z, x), uly),
        (blk_of(y, z, (x + 1) % 4), uly),
        (blk_of(y, z, (x + 3) % 4), uly),
        (blk_of(y, (z + 1) % 4, x), uly),
        (blk_of(y, (z + 3) % 4, x), uly),
    ]


def choose(number, value):
    chosen = value(0)
    for c in range(1, SETS):
        chosen = jnp.where(number == c, value(c), chosen)
    return chosen


def gain(ref, first):
    return jnp.concatenate([ref[n : n + 1, :] for n in range(first, first + D // 128)], axis=1)


def greet(others, meanwhile=None):
    barrier = pltpu.get_barrier_semaphore()
    for other in others:
        pl.semaphore_signal(barrier, inc=1, device_id=other, device_id_type=MESH)
    if meanwhile is not None:
        meanwhile()
    pl.semaphore_wait(barrier, len(others))


class Gather:
    sends = 31

    def __init__(self, src, dst, send_sem, recv_sem, local_sem, orders=(0, 1)):
        self.src, self.dst, self.orders = src, dst, orders
        self.streams = range(len(orders))
        self.send_sem, self.recv_sem, self.local_sem = send_sem, recv_sem, local_sem
        self.y, self.z, self.x, self.blk, self.uly = place()
        self.count = [0] * len(orders)
        self.sent = []
        self.local = []

    def at(self, stream, y, p, q):
        order = self.orders[stream]
        return blk_of(y, order * p + (1 - order) * q, order * q + (1 - order) * p)

    def pq(self, stream):
        order = self.orders[stream]
        return (
            order * self.z + (1 - order) * self.x,
            order * self.x + (1 - order) * self.z,
        )

    def send(self, stream, item, target, src=None):
        copy = pltpu.make_async_remote_copy(
            src_ref=self.dst(stream, item) if src is None else src,
            dst_ref=self.dst(stream, item),
            send_sem=self.send_sem.at[stream, self.count[stream]],
            recv_sem=self.recv_sem.at[stream, item],
            device_id=(target, self.uly),
            device_id_type=MESH,
        )
        self.count[stream] += 1
        copy.start()
        self.sent.append(copy)

    def wait(self, stream, item):
        ref = self.dst(stream, item)
        pltpu.make_async_remote_copy(
            src_ref=ref,
            dst_ref=ref,
            send_sem=self.send_sem.at[stream, 0],
            recv_sem=self.recv_sem.at[stream, item],
            device_id=(self.blk, self.uly),
            device_id_type=MESH,
        ).wait_recv()

    def start(self):
        for s in self.streams:
            p, q = self.pq(s)
            self.send(s, self.blk, self.at(s, 1 - self.y, p, q), self.src(s))
        for s in self.streams:
            p, q = self.pq(s)
            for d in (1, 3):
                self.send(s, self.blk, self.at(s, self.y, (p + d) % 4, q), self.src(s))
            copy = pltpu.make_async_copy(self.src(s), self.dst(s, self.blk), self.local_sem.at[s])
            copy.start()
            self.local.append(copy)

    def second(self):
        for s in self.streams:
            p, q = self.pq(s)
            item = self.at(s, 1 - self.y, p, q)
            self.wait(s, item)
            for d in (1, 3):
                self.send(s, item, self.at(s, self.y, (p + d) % 4, q))
            for d in (1, 3):
                onward = self.at(s, self.y, p, (q + d) % 4)
                self.send(s, self.blk, onward, self.src(s))
                self.send(s, item, onward)

    def spread(self, s, item):
        p, q = self.pq(s)
        for d in (1, 3):
            self.send(s, item, self.at(s, self.y, p, (q + d) % 4))

    def third(self):
        for k, y in enumerate((self.y, 1 - self.y)):
            for s in self.streams:
                p, q = self.pq(s)
                for d in (3, 1):
                    item = self.at(s, y, (p + d) % 4, q)
                    self.wait(s, item)
                    if (d == 3) == (k == 0):
                        self.send(s, item, self.at(s, self.y, (p + 4 - d) % 4, q))
                    self.spread(s, item)
        for y in (self.y, 1 - self.y):
            for s in self.streams:
                p, q = self.pq(s)
                item = self.at(s, y, (p + 2) % 4, q)
                self.wait(s, item)
                self.spread(s, item)

    def fourth(self):
        for e in (0, 1, 3, 2):
            for k, y in enumerate((self.y, 1 - self.y)):
                for s in self.streams:
                    p, q = self.pq(s)
                    for d in (3, 1):
                        item = self.at(s, y, (p + e) % 4, (q + d) % 4)
                        self.wait(s, item)
                        if (d == 3) == (k == 0):
                            self.send(s, item, self.at(s, self.y, p, (q + 4 - d) % 4))

    def last(self):
        for e in (0, 1, 3, 2):
            for y in (self.y, 1 - self.y):
                for s in self.streams:
                    p, q = self.pq(s)
                    self.wait(s, self.at(s, y, (p + e) % 4, (q + 2) % 4))
        for copy in self.local:
            copy.wait()
        for copy in self.sent:
            copy.wait_send()


GATHER_SEMS = lambda *lead: [
    pltpu.SemaphoreType.DMA(lead + (2, Gather.sends)),
    pltpu.SemaphoreType.DMA(lead + (2, 32)),
    pltpu.SemaphoreType.DMA(lead + (2,)),
]


KEYS = 1024
KEYS_BACK = 512
ROWS = GROUP * CHUNK


def head_columns(ref, slot):
    return jnp.concatenate(
        [
            ref[slot * CHUNK : (slot + 1) * CHUNK, n * HEAD : (n + 1) * HEAD].T
            for n in range(GROUP)
        ],
        axis=1,
    )


def head_rows(ref, slot):
    return jnp.concatenate(
        [
            ref[slot * CHUNK : (slot + 1) * CHUNK, n * HEAD : (n + 1) * HEAD]
            for n in range(GROUP)
        ],
        axis=0,
    )


def key_block(kv_ref, step, keys):
    count = keys // CHUNK
    rows = kv_ref[pl.ds(step * count, count)].reshape(keys, 2 * HEAD)
    return rows[:, :HEAD], rows[:, HEAD:]


def dot(a, b):
    return jnp.dot(a, b, preferred_element_type=F32)


def key_places(step, keys):
    return lax.broadcasted_iota(jnp.int32, (keys, ROWS), 0) + step * keys


def dot_nt(a, b):
    return lax.dot_general(a, b, (((1,), (1,)), ((), ())), preferred_element_type=F32)


def forward_blocks(slot, first, last, turned_ref, kv_ref, limit_ref, acc_ref, stat_ref):
    turned = turned_ref[slot]
    limit = limit_ref[slot, 0:1, :]

    def step(n, carry):
        top, total = carry
        keys, values = key_block(kv_ref, n, KEYS)
        scores = jnp.where(key_places(n, KEYS) <= limit, dot(keys, turned), -1e30)
        new_top = jnp.maximum(top, jnp.max(scores, axis=0, keepdims=True))
        fade = jnp.exp2(top - new_top)
        probs = jnp.exp2(scores - new_top)
        total = total * fade + jnp.sum(probs, axis=0, keepdims=True)
        acc_ref[slot] = acc_ref[slot] * fade + dot(values.T, probs.astype(BF))
        return new_top, total

    top, total = lax.fori_loop(
        first, last, step, (stat_ref[slot, 0, 0:1, :], stat_ref[slot, 1, 0:1, :])
    )
    stat_ref[slot, 0, 0:1, :] = top
    stat_ref[slot, 1, 0:1, :] = total


def forward_end(slot, mixed_ref, lse_ref, acc_ref, stat_ref):
    top, total = stat_ref[slot, 0, 0:1, :], stat_ref[slot, 1, 0:1, :]
    out = acc_ref[slot] / total
    for n in range(GROUP):
        mixed_ref[slot * CHUNK : (slot + 1) * CHUNK, n * HEAD : (n + 1) * HEAD] = out[
            :, n * CHUNK : (n + 1) * CHUNK
        ].T.astype(BF)
    lse_ref[slot] = jnp.broadcast_to(top + jnp.log2(total), (8, ROWS))


def uly_others():
    y, z, x, blk, uly = place()
    return [(blk, (uly + 2) % 4), (blk, uly + 1 - 2 * (uly % 2)), (blk, 3 - uly)]


def ring_place(w):
    y, z, x, blk, uly = place()
    return (blk_of(w % 2, z, x), (w // 2) * 2 + uly % 2)


def ring_at():
    y, z, x, blk, uly = place()
    return (uly // 2) * 2 + y


def wait_arrival(ref, sem):
    pltpu.make_async_copy(ref, ref, sem).wait()


def remote(src, dst, send, recv, device):
    return pltpu.make_async_remote_copy(
        src_ref=src, dst_ref=dst, send_sem=send, recv_sem=recv, device_id=device, device_id_type=MESH
    )


class Deliver:
    def __init__(self):
        self.sent = []

    def send(self, src, dst, send, recv, device):
        y, z, x, blk, uly = place()
        here = jnp.logical_and(device[0] == blk, device[1] == uly)

        @pl.when(here)
        def _():
            pltpu.make_async_copy(src, dst, recv).start()

        @pl.when(jnp.logical_not(here))
        def _():
            remote(src, dst, send, recv, device).start()

        self.sent.append((here, src, dst, send, recv, device))

    def end(self):
        for here, *copy in self.sent:

            @pl.when(jnp.logical_not(here))
            def _():
                remote(*copy).wait_send()


class Ring:
    sends = 15

    def __init__(self, src, dst, y, order, way, send_sem, recv_sem):
        self.src, self.dst, self.y, self.order, self.way = src, dst, y, order, way
        self.send_sem, self.recv_sem = send_sem, recv_sem
        self.own_y, self.z, self.x, self.blk, self.uly = place()
        self.p = order * self.z + (1 - order) * self.x
        self.q = order * self.x + (1 - order) * self.z
        self.sent = []

    def at(self, y, p, q):
        order = self.order
        return blk_of(y, order * p + (1 - order) * q, order * q + (1 - order) * p)

    def index(self, p, q):
        return self.at(0, p, q)

    def send(self, p, q, dp, dq, src=None):
        ref = self.dst(self.at(self.y, p, q))
        target = self.at(self.own_y, (self.p + dp) % 4, (self.q + dq) % 4)
        copy = remote(
            ref if src is None else src, ref, self.send_sem.at[len(self.sent)],
            self.recv_sem.at[self.index(p, q)], (target, self.uly),
        )
        copy.start()
        self.sent.append(copy)

    def wait(self, p, q):
        wait_arrival(self.dst(self.at(self.y, p, q)), self.recv_sem.at[self.index(p, q)])

    def start(self):
        for d in (1, 3):
            self.send(self.p, self.q, d, 0, self.src)

    def second(self):
        for d in (4 - self.way, self.way):
            p = (self.p + d) % 4
            self.wait(p, self.q)
            if d == 4 - self.way:
                self.send(p, self.q, self.way, 0)

    def third(self):
        self.wait((self.p + 2) % 4, self.q)

    def spread(self, e):
        p = (self.p + e) % 4
        for d in (1, 3):
            self.send(p, self.q, 0, d, self.src if e == 0 else None)

    def fourth(self, e):
        p = (self.p + e) % 4
        way = self.way if e % 2 == 0 else 4 - self.way
        for d in (4 - way, way):
            q = (self.q + d) % 4
            self.wait(p, q)
            if d == 4 - way:
                self.send(p, q, 0, way)

    def last(self):
        for e in (0, 1, 3, 2):
            self.wait((self.p + e) % 4, (self.q + 2) % 4)
        self.end()

    def end(self):
        for copy in self.sent:
            copy.wait_send()


class Spread:
    def __init__(self, own, all_ref, send_sem, recv_sem, local_sem):
        self.own, self.all_ref = own, all_ref
        self.send_sem, self.recv_sem, self.local_sem = send_sem, recv_sem, local_sem
        self.w = ring_at()
        self.core = lax.axis_index("uly") % 2
        self.sibling = uly_others()[1]
        self.sent = []

    def piece(self, d, rows=slice(None), core=None):
        core = self.core if core is None else core
        ref = self.all_ref.at[core, (self.w + d) % 4]
        return ref if rows == slice(None) else ref.at[pl.ds(rows.start, rows.stop - rows.start)]

    def send(self, src, dst, recv, device):
        copy = remote(src, dst, self.send_sem.at[len(self.sent)], self.recv_sem.at[recv], device)
        copy.start()
        self.sent.append(copy)

    def pair(self, d, src=None):
        self.send(self.piece(d) if src is None else src, self.piece(d), 4 + d, self.sibling)

    def start(self):
        self.local = pltpu.make_async_copy(self.own, self.piece(0), self.local_sem)
        self.local.start()
        self.send(self.own, self.piece(0), 0, ring_place((self.w + 1) % 4))
        self.send(self.own, self.piece(0), 1, ring_place((self.w + 3) % 4))
        self.pair(0, self.own)

    def second(self):
        half = CHUNK // 2
        wait_arrival(self.piece(3), self.recv_sem.at[0])
        low = self.piece(3, slice(0, half))
        self.send(low, low, 2, ring_place((self.w + 1) % 4))
        self.pair(3)
        wait_arrival(self.piece(1), self.recv_sem.at[1])
        high = self.piece(1, slice(half, CHUNK))
        self.send(high, high, 3, ring_place((self.w + 3) % 4))
        self.pair(1)

    def third(self):
        half = CHUNK // 2
        wait_arrival(self.piece(2, slice(0, half)), self.recv_sem.at[2])
        wait_arrival(self.piece(2, slice(half, CHUNK)), self.recv_sem.at[3])
        self.pair(2)

    def last(self):
        for d in range(4):
            wait_arrival(self.piece(d, core=1 - self.core), self.recv_sem.at[4 + d])
        for copy in self.sent:
            copy.wait_send()
        self.local.wait()


SPREAD_SEMS = [pltpu.SemaphoreType.DMA((8,)), pltpu.SemaphoreType.DMA((8,)), pltpu.SemaphoreType.DMA]
FF_COLS = PADDED // 2


def forward_kernel(
    tokens_ref, cot_ref, length_hbm, set_hbm, qkv_hbm, w_out_hbm, gate_up_hbm, down_hbm, gains_hbm, freq_hbm,
    a_hbm, b_hbm, bkv_hbm,
    q_out, mixed_out, lse_out, kv_out, wq_out, wo_out, gate_all, up_all, down_all, rows_hbm, normed_out,
    resid_out, cot_out, nf_out, cot_all, limit_out, cos_out, sin_out, b_qkv_out, ao_out, a_out, bo_out,
    q_ref, mixed_ref, lse_ref, rows_out, normed_ref, resid_ref, cot_own, limit_ref, cos_ref, sin_ref,
    b_qkv_ref, ao_ref, a_ref, b_ref, bkv_ref, a_sets, b_sets, bkv_sets, turned_ref,
    length_ref, set_ref, qkv_ref, out_ref, gate_up_ref, down_ref, gains_ref, freq_ref, kv_all, wq_all, wo_all, rows, cot_in, kv_part, acc_ref, stat_ref, qkv_in, out_in, qkv_part, out_part,
    nf_own, cross_out, cross_in, qkv_pieces, out_pieces, ff_ref,
    *sems,
):
    y, z, x, blk, uly = place()
    core, h = uly % 2, uly // 2
    sems = list(sems)

    def take(count):
        got = sems[:count]
        del sems[:count]
        return got

    chunk = 2 * blk + h
    upper = chunk // 32
    home = (1 - h) * blk + h * (31 - blk)
    row_to = [[(home, hh * 2 + s) for hh in (0, 1)] for s in (0, 1)]
    row_from = [(b, hh * 2 + half) for b, hh in ((blk, 0), (31 - blk, 1)) for half in (0, 1)]
    lower = low_chunk(blk)
    out_to = [(2 * (blk % 16) + q // 2, (blk // 16) * 2 + q % 2) for q in range(4)]
    out_from = [(16 * h + blk // 2, u) for u in range(4)]
    sibling = uly_others()[1]
    set_sem = sems.pop()
    in_sem = sems.pop()
    in_copies = [
        pltpu.make_async_copy(src, dst, in_sem.at[n])
        for n, (src, dst) in enumerate(
            (
                (qkv_hbm, qkv_ref), (w_out_hbm, out_ref), (gate_up_hbm, gate_up_ref), (down_hbm, down_ref),
                (length_hbm, length_ref), (set_hbm, set_ref), (gains_hbm, gains_ref), (freq_hbm, freq_ref),
            )
        )
    ]
    for copy in in_copies:
        copy.start()
    set_copies = [
        pltpu.make_async_copy(src, dst, set_sem.at[n])
        for n, (src, dst) in enumerate(
            ((a_hbm.at[pl.ds(0, 4)], a_sets), (b_hbm.at[pl.ds(0, 2)], b_sets), (bkv_hbm, bkv_sets))
        )
    ]
    for copy in set_copies:
        copy.start()

    def prepare():
        qkv_pieces[...] = jnp.zeros_like(qkv_pieces)
        out_pieces[...] = jnp.zeros_like(out_pieces)
        for copy in in_copies:
            copy.wait()
        group = GROUP * HEAD
        for hh in (0, 1):
            qkv_pieces[2 * hh, :12] = qkv_ref[:, hh * group : hh * group + 512]
            for place_at, start, size in (
                (0, hh * group + 512, 256),
                (256, HEADS * HEAD + hh * HEAD, HEAD),
                (384, HEADS * HEAD + 256 + hh * HEAD, HEAD),
            ):
                qkv_pieces[2 * hh + 1, :12, place_at : place_at + size] = qkv_ref[:, start : start + size]
        for q in range(4):
            out_pieces[q, :12] = out_ref[:, q * 384 : (q + 1) * 384]
        for n in range(3):
            part = (gate_up_ref[n] if n < 2 else down_ref[...]).astype(F32)
            none = jnp.zeros((48, 64), F32)
            left = jnp.concatenate([part, none], axis=1)
            right = jnp.concatenate([none, part], axis=1)
            ff_ref[n] = jnp.where(jnp.broadcast_to(core, (48, PADDED)) == 1, right, left).astype(BF)

    greet(
        ring_others() + uly_others() + [(blk_of(1 - y, z, x), (uly + 2) % 4)]
        + row_to[0] + row_to[1] + row_from + out_to + out_from,
        prepare,
    )

    length = length_ref[0] * (1 - core) + length_ref[1] * core

    deliver = Deliver()
    piece_send, piece_recv, row_send, row_recv = take(4)
    for q in range(4):
        deliver.send(qkv_pieces.at[q], qkv_in.at[uly], piece_send.at[q], piece_recv.at[uly], (blk, q))
    for q in range(4):
        deliver.send(out_pieces.at[q], out_in.at[uly], piece_send.at[4 + q], piece_recv.at[4 + uly], out_to[q])
    for s in (0, 1):
        for hh in (0, 1):
            deliver.send(
                tokens_ref.at[s], rows.at[upper, core], row_send.at[s * 2 + hh],
                row_recv.at[upper * 2 + core], row_to[s][hh],
            )

    wide = PADDED // 2
    gathered = (gate_all, up_all, down_all)
    ff_send, ff_recv, y_send, y_recv, y_local = take(5)
    other_blk = blk_of(1 - y, z, x)

    def ff_part(n, half):
        return ff_ref.at[n, :, pl.ds(pl.multiple_of(half * wide, 128), wide)]

    y_copies = []
    for n, ref in enumerate(gathered):
        copy = remote(ff_part(n, 1 - y), ref.at[blk], y_send.at[n], y_recv.at[n], (other_blk, uly))
        copy.start()
        y_copies.append(copy)
        copy = pltpu.make_async_copy(ff_part(n, y), ref.at[blk], y_local.at[n])
        copy.start()
        y_copies.append(copy)
    own_ff, other_ff = (
        [
            Ring(
                ff_part(n, y) if k == 0 else ref.at[other_blk],
                lambda item, ref=ref: ref.at[item],
                y if k == 0 else 1 - y,
                y if k == 0 else 1 - y,
                (1, 3, 1 + 2 * k)[n],
                ff_send.at[k, n], ff_recv.at[k, n],
            )
            for n, ref in enumerate(gathered)
        ]
        for k in (0, 1)
    )
    for ring in own_ff:
        ring.start()

    picked = lax.broadcasted_iota(jnp.int32, (48, 64), 1)
    picked = jnp.where(picked % 16 < 12, picked // 16 * 12 + picked % 16, -1)
    picked = jnp.where(picked == lax.broadcasted_iota(jnp.int32, (48, 64), 0), 1.0, 0.0).astype(BF)
    for u in range(4):
        wait_arrival(qkv_in.at[u], piece_recv.at[u])
    qkv_part[...] = dot(picked, qkv_in[...].reshape(64, 512)).astype(BF)
    wq = Gather(
        lambda s: qkv_part.at[:, pl.ds(256 * s, 256)],
        lambda s, item: wq_all.at[
            core, pl.ds(pl.multiple_of(item * 48, 16), 48), pl.ds(256 * s, 256)
        ],
        *take(3),
    )
    wq.start()
    for u in range(4):
        wait_arrival(out_in.at[u], piece_recv.at[4 + u])
    out_part[...] = dot(picked, out_in[...].reshape(64, 384)).astype(BF)
    for s in (0, 1):
        deliver.send(
            cot_ref.at[s], cot_in.at[core], row_send.at[4 + s], row_recv.at[4 + core], (home, upper * 2 + s)
        )

    def out_columns(item, s):
        start = ((item % 2) * 2 + core) * 384
        return pl.ds(pl.multiple_of(start + 128 * s, 128), 128 + 128 * s)

    wo = Gather(
        lambda s: out_part.at[:, pl.ds(128 * s, 128 + 128 * s)],
        lambda s, item: wo_all.at[pl.ds(pl.multiple_of((item // 2) * 48, 16), 48), out_columns(item, s)],
        *take(3),
    )
    rings = own_ff + other_ff
    whole = [ring for n, ring in enumerate(rings) if n % 3 != 1]
    def tables(slot):
        at = lower if slot == 0 else 63 - lower
        row = lax.broadcasted_iota(jnp.int32, (CHUNK, HEAD), 0) + at * CHUNK
        angle = row.astype(F32) * freq_ref[...]
        first = lax.broadcasted_iota(jnp.int32, (CHUNK, HEAD), 1) < HEAD // 2
        sine = jnp.sin(angle)
        cos_ref[slot * CHUNK : (slot + 1) * CHUNK, :] = jnp.cos(angle)
        sin_ref[slot * CHUNK : (slot + 1) * CHUNK, :] = jnp.where(first, -sine, sine)
        row = lax.broadcasted_iota(jnp.int32, (8, ROWS), 1) % CHUNK + at * CHUNK
        limit_ref[slot] = jnp.minimum(row, length - 1)

    stat_ref[:, 0] = jnp.full((2, 8, ROWS), -1e30, F32)
    stat_ref[:, 1] = jnp.zeros((2, 8, ROWS), F32)
    acc_ref[...] = jnp.zeros_like(acc_ref)
    own_set = set_ref[0] * (1 - core) + set_ref[1] * core
    for copy in set_copies:
        copy.wait()
    for sets, ref in ((a_sets, a_ref), (b_sets, b_ref), (bkv_sets, bkv_ref)):
        for n in range(ref.shape[0]):
            ref[n] = choose(own_set, lambda c: sets[n, c])
    group = GROUP * HEAD
    group_at = pl.ds(pl.multiple_of(h * group, 128), group)
    head_at = pl.ds(pl.multiple_of(h * HEAD, 128), HEAD)
    ao_ref[...] = a_ref[3, :, group_at]
    b_qkv_ref[...] = jnp.zeros_like(b_qkv_ref)
    b_qkv_ref[:16, :group] = b_ref[0, :, group_at]
    b_qkv_ref[16:32, group : group + HEAD] = bkv_ref[0, :, head_at]
    b_qkv_ref[32:, group + HEAD :] = bkv_ref[1, :, head_at]
    a_qkv = a_ref[:3].reshape(48, D)
    bo_ref = b_ref.at[1]

    def bias(n):
        at = h * GROUP + n if n < GROUP else HEADS + 2 * (n - GROUP) + h
        return gains_ref[pl.ds(2 * D_TILES + at, 1), :]

    wq.second()
    tables(0)
    wq.third()
    tables(1)
    wq.fourth()
    for n in range(3):
        y_copies[2 * n].wait_recv()
    for ring in other_ff:
        ring.start()
    for ring in whole:
        ring.spread(0)

    for n in range(4):
        wait_arrival(rows.at[n // 2, n % 2], row_recv.at[n])
        value = rows[n // 2, n % 2].astype(F32)
        at = slice(n * 64, (n + 1) * 64)
        rows_out[at, :] = rows[n // 2, n % 2]
        normed_ref[at, :] = (value * norm_scale(value) * gain(gains_ref, 0)).astype(BF)
    latent = dot_nt(normed_ref[...], a_qkv)
    adapted = dot(latent.astype(BF), b_qkv_ref[...])
    wq.last()
    pair_send, pair_recv = take(2)

    def pair_copy(ref, n):
        return remote(ref, ref, pair_send.at[n], pair_recv.at[n], sibling)

    pair_copy(wq_all.at[core], 0).start()
    wo.start()
    pair_copy(wq_all.at[core], 0).wait_send()
    pair_copy(wq_all.at[1 - core], 0).wait_recv()

    cos_table, sine_table = cos_ref[...], sin_ref[...]

    def turn(head):
        return head * cos_table + pltpu.roll(head, HEAD // 2, 1) * sine_table

    def query(n, head):
        q_ref[:, n * HEAD : (n + 1) * HEAD] = (turn(head + bias(n)) * (HEAD ** (-0.5) * LOG2E)).astype(BF)

    pairs = dot(normed_ref[...], wq_all[1, :, 256:]) + adapted[:, 768:]
    for n, head in ((0, turn(pairs[:, :HEAD] + bias(6))), (1, pairs[:, HEAD:] + bias(7))):
        at = slice(n * HEAD, (n + 1) * HEAD)
        kv_part[0, :, at] = head[:CHUNK].astype(BF)
        kv_part[1, :, at] = head[CHUNK:].astype(BF)
    kv = Gather(
        lambda s: kv_part.at[s],
        lambda s, item: kv_all.at[low_chunk(item) if s == 0 else 63 - low_chunk(item)],
        *take(3),
    )
    kv.start()
    heads = dot(normed_ref[...], wq_all[1, :, :256]) + adapted[:, 512:768]
    for n in (4, 5):
        query(n, heads[:, (n - 4) * HEAD : (n - 3) * HEAD])
    kv.second()
    for ring in rings:
        ring.second()
    wo.second()
    heads = dot(normed_ref[...], wq_all[0]) + adapted[:, :512]
    for n in range(4):
        query(n, heads[:, n * HEAD : (n + 1) * HEAD])
    kv.third()
    for ring in rings:
        ring.third()
    wo.third()
    kv.fourth()
    wo.fourth()

    for half in (0, 1):
        wait_arrival(cot_in.at[half], row_recv.at[4 + half])
        start = ((1 - h) * lower + h * (63 - lower)) * CHUNK + half * 64
        at = lax.broadcasted_iota(jnp.int32, (64, D), 0) + start
        cot_own[half * 64 : (half + 1) * 64, :] = jnp.where(
            at < length, cot_in[half].astype(F32), 0.0
        ).astype(BF)
    cot_spread = Spread(cot_own, cot_all, *take(3))
    cot_spread.start()
    kv.last()
    for e in (1, 3, 2):
        for ring in whole:
            ring.spread(e)
    (out_sem,) = take(1)
    copies = []

    def keep(*pairs):
        for src, dst in pairs:
            copies.append(pltpu.make_async_copy(src, dst, out_sem.at[len(copies)]))
            copies[-1].start()

    keep(
        (kv_all, kv_out), (wq_all, wq_out), (q_ref, q_out), (rows_out, rows_hbm), (normed_ref, normed_out),
        (cot_own, cot_out), (limit_ref, limit_out), (cos_ref, cos_out), (sin_ref, sin_out),
        (b_qkv_ref, b_qkv_out), (ao_ref, ao_out), (a_ref.at[pl.ds(0, 3)], a_out), (b_ref.at[1], bo_out),
    )
    wo.last()

    def wo_columns(c, n):
        return wo_all.at[:, pl.ds(pl.multiple_of((2 * n + c) * 384, 128), 384)]

    for n in (0, 1):
        pair_copy(wo_columns(core, n), 1 + n).start()
    for slot in (0, 1):
        turned_ref[slot] = head_columns(q_ref, slot)
    args = (turned_ref, kv_all, limit_ref, acc_ref, stat_ref)

    def end(slot):
        forward_end(slot, mixed_ref, lse_ref, acc_ref, stat_ref)

    blocks = KEYS // CHUNK
    middle = CHUNKS // 2 // blocks
    forward_blocks(0, 0, lower // blocks + 1, *args)
    forward_blocks(1, middle, (63 - lower) // blocks + 1, *args)
    end(0)
    for ring in whole:
        ring.fourth(0)
    cot_spread.second()
    forward_blocks(1, 0, middle // 2, *args)
    for ring in whole:
        ring.fourth(1)
    cot_spread.third()
    forward_blocks(1, middle // 2, middle, *args)
    end(1)
    for n in (0, 1):
        pair_copy(wo_columns(core, n), 1 + n).wait_send()
        pair_copy(wo_columns(1 - core, n), 1 + n).wait_recv()
    keep((wo_all, wo_out), (mixed_ref, mixed_out), (lse_ref, lse_out))

    def project(slot):
        mixed = mixed_ref[pl.ds(pl.multiple_of(slot * CHUNK, CHUNK), CHUNK), :]
        lifted = dot(dot_nt(mixed, ao_ref[...]).astype(BF), bo_ref[...])
        return dot(mixed, wo_all[...]) + lifted

    (cross_sem,) = take(1)
    cross_out[...] = project(1 - h).astype(BF)
    cross = remote(cross_out, cross_in, cross_sem.at[0], cross_sem.at[1], uly_others()[0])
    cross.start()
    for ring in whole:
        ring.fourth(3)
    mine = project(h) + rows_out[pl.ds(pl.multiple_of(h * CHUNK, CHUNK), CHUNK), :].astype(F32)
    for ring in whole:
        ring.fourth(2)
    cross.wait()
    residual = mine + cross_in[...].astype(F32)
    resid_ref[...] = residual
    keep((resid_ref, resid_out))
    nf_own[...] = (residual * norm_scale(residual) * gain(gains_ref, D_TILES)).astype(BF)
    keep((nf_own, nf_out))
    cot_spread.last()
    for ring in whole:
        ring.last()
    for ring in (own_ff[1], other_ff[1]):
        ring.end()
    for n in range(3):
        y_copies[2 * n].wait_send()
        y_copies[2 * n + 1].wait()
    deliver.end()
    for copy in copies:
        copy.wait()


def forward(*args):
    weight = HELD((32, 48, FF_COLS), BF)
    group = GROUP * HEAD
    dma = pltpu.SemaphoreType.DMA
    spread = HELD((2, 4, CHUNK, D), BF)
    return pl.pallas_call(
        forward_kernel,
        out_shape=(
            HELD((2 * CHUNK, group), BF),
            HELD((2 * CHUNK, group), BF),
            HELD((2, 8, ROWS), F32),
            HELD((CHUNKS, CHUNK, 2 * HEAD), BF),
            HELD((2, D, 512), BF),
            HELD((D // 2, D), BF),
            weight, weight, weight,
            HELD((2 * CHUNK, D), BF),
            HELD((2 * CHUNK, D), BF),
            HELD((CHUNK, D), F32),
            HELD((CHUNK, D), BF),
            HELD((CHUNK, D), BF),
            spread,
            HELD((2, 8, ROWS), jnp.int32),
            HELD((2 * CHUNK, HEAD), F32),
            HELD((2 * CHUNK, HEAD), F32),
            HELD((48, 1024), BF),
            HELD((16, group), BF),
            HELD((3, 16, D), BF),
            HELD((16, D), BF),
        ),
        in_specs=[ANY] * 13,
        out_specs=(ANY,) * 22,
        scratch_shapes=[
            pltpu.VMEM((2 * CHUNK, group), BF),
            pltpu.VMEM((2 * CHUNK, group), BF),
            pltpu.VMEM((2, 8, ROWS), F32),
            pltpu.VMEM((2 * CHUNK, D), BF),
            pltpu.VMEM((2 * CHUNK, D), BF),
            pltpu.VMEM((CHUNK, D), F32),
            pltpu.VMEM((CHUNK, D), BF),
            pltpu.VMEM((2, 8, ROWS), jnp.int32),
            pltpu.VMEM((2 * CHUNK, HEAD), F32),
            pltpu.VMEM((2 * CHUNK, HEAD), F32),
            pltpu.VMEM((48, 1024), BF),
            pltpu.VMEM((16, group), BF),
            pltpu.VMEM((4, 16, D), BF),
            pltpu.VMEM((2, 16, D), BF),
            pltpu.VMEM((2, 16, 2 * HEAD), BF),
            pltpu.VMEM((4, SETS, 16, D), BF),
            pltpu.VMEM((2, SETS, 16, D), BF),
            pltpu.VMEM((2, SETS, 16, 2 * HEAD), BF),
            pltpu.VMEM((2, HEAD, ROWS), BF),
            pltpu.SMEM((2,), jnp.int32),
            pltpu.SMEM((2,), jnp.int32),
            pltpu.VMEM((12, 2048), BF),
            pltpu.VMEM((12, D), BF),
            pltpu.VMEM((2, 48, FF // 4), BF),
            pltpu.VMEM((48, FF // 4), BF),
            pltpu.VMEM((40, 128), F32),
            pltpu.VMEM((1, 128), F32),
            pltpu.VMEM((CHUNKS, CHUNK, 2 * HEAD), BF),
            pltpu.VMEM((2, D, 512), BF),
            pltpu.VMEM((D // 2, D), BF),
            pltpu.VMEM((2, 2, 64, D), BF),
            pltpu.VMEM((2, 64, D), BF),
            pltpu.VMEM((2, CHUNK, 2 * HEAD), BF),
            pltpu.VMEM((2, HEAD, ROWS), F32),
            pltpu.VMEM((2, 2, 8, ROWS), F32),
            pltpu.VMEM((4, 16, 512), BF),
            pltpu.VMEM((4, 16, 384), BF),
            pltpu.VMEM((48, 512), BF),
            pltpu.VMEM((48, 384), BF),
            pltpu.VMEM((CHUNK, D), BF),
            pltpu.VMEM((CHUNK, D), BF),
            pltpu.VMEM((CHUNK, D), BF),
            pltpu.VMEM((4, 16, 512), BF),
            pltpu.VMEM((4, 16, 384), BF),
            pltpu.VMEM((3, 48, PADDED), BF),
            dma((8,)), dma((8,)), dma((6,)), dma((6,)),
            dma((2, 3, Ring.sends)), dma((2, 3, 16)), dma((3,)), dma((3,)), dma((3,)),
        ]
        + GATHER_SEMS()
        + GATHER_SEMS()
        + [dma((3,)), dma((3,))]
        + GATHER_SEMS()
        + SPREAD_SEMS
        + [dma((18,)), dma((2,)), dma((8,)), dma((3,))],
        compiler_params=pltpu.CompilerParams(
            collective_id=1, has_side_effects=True, vmem_limit_bytes=48 * 2**20
        ),
        name="forward",
    )(*args)


class RingSum:
    @staticmethod
    def scratch():
        piece, half = (CHUNK, D), (CHUNK // 2, D)
        return [
            pltpu.VMEM((2,) + half, BF),
            pltpu.VMEM((2,) + piece, BF),
            pltpu.VMEM(piece, BF),
            pltpu.VMEM((2,) + piece, BF),
            pltpu.SemaphoreType.DMA((4,)),
            pltpu.SemaphoreType.DMA((4,)),
        ]

    scratches = 6

    def __init__(self, term, scratch):
        self.term = term
        self.halves, self.last_in, self.far, self.near, self.send_sem, self.recv_sem = scratch
        self.w = ring_at()
        self.sent = []

    def send(self, src, dst, recv, d):
        copy = remote(
            src, dst, self.send_sem.at[recv], self.recv_sem.at[recv], ring_place((self.w + d) % 4)
        )
        copy.start()
        self.sent.append(copy)

    def first(self):
        half = CHUNK // 2
        self.far[...] = self.term(2).astype(BF)
        self.send(self.far.at[pl.ds(0, half)], self.halves.at[0], 0, 1)
        self.send(self.far.at[pl.ds(half, half)], self.halves.at[1], 1, 3)

    def second(self):
        half = CHUNK // 2
        for k, d in ((0, 1), (1, 3)):
            total = self.term(d)
            wait_arrival(self.halves.at[k], self.recv_sem.at[k])
            rows = slice(k * half, (k + 1) * half)
            other = slice((1 - k) * half, (2 - k) * half)
            self.near[k, rows] = (total[rows] + self.halves[k].astype(F32)).astype(BF)
            self.near[k, other] = total[other].astype(BF)
            self.send(self.near.at[k], self.last_in.at[k], 2 + k, d)

    def third(self):
        total = self.term(0)
        for k in (0, 1):
            wait_arrival(self.last_in.at[k], self.recv_sem.at[2 + k])
            total += self.last_in[k].astype(F32)
        for copy in self.sent:
            copy.wait_send()
        return total


def ff_kernel(
    set_ref, own_hbm, cot_hbm, gate_hbm, up_hbm, down_hbm, a_wide, a_down, b_wide, b_ff,
    grad_out, down_out, cols_out, wide_out,
    cols_ref, wide_ref, x_ref, cot_ref, gate_w, up_w, down_w, b_cols, a_cols, hidden_ref, grad_gate, grad_up,
    grad_hidden, own_ref, terms, pair, total_ref, down_sum, a_ff, b_out, wide_sets, down_sets, out_sets,
    ff_sets, sems, out_sems, pair_send, pair_recv, *scratch,
):
    y, z, x, blk, uly = place()
    core = uly % 2
    scratch = list(scratch)

    def take(count):
        got = scratch[:count]
        del scratch[:count]
        return got

    first = (35 * uly) // 2 * 128 + y * FF_COLS
    columns = pl.ds(pl.multiple_of(first, 128), FF_COLS)
    pairs = (
        (own_hbm, own_ref), (down_hbm, down_w), (cot_hbm, cot_ref), (gate_hbm, gate_w),
        (a_wide.at[pl.ds(4, 2)], wide_sets), (a_down.at[:, :, columns], down_sets), (b_wide.at[2], out_sets),
        (b_ff.at[:, :, :, columns], ff_sets),
    )
    copies = [pltpu.make_async_copy(src, dst, sems.at[n]) for n, (src, dst) in enumerate(pairs)]
    for copy in copies[:1] + copies[4:] + copies[1:4]:
        copy.start()
    other_blk = blk_of(1 - y, z, x)
    up_send, up_recv, up_sem = take(3)
    rings = [
        Ring(
            up_w.at[b], lambda item: up_w.at[item], yy, yy, 1 + 2 * k, up_send.at[k], up_recv.at[k]
        )
        for k, (yy, b) in enumerate(((y, blk), (1 - y, other_blk)))
    ]
    lines = []
    for k, ring in enumerate(rings):
        for d in range(4):
            item = ring.at(ring.y, (ring.p + d) % 4, ring.q)
            lines.append(pltpu.make_async_copy(up_hbm.at[item], up_w.at[item], up_sem.at[k, d]))
            lines[-1].start()
    at = lax.broadcasted_iota(jnp.int32, (16, FF_COLS), 1) + (y * FF_COLS - 64 * core)
    inside = jnp.logical_and(at >= 0, at < FF // 4)

    def keep(v):
        return jnp.where(inside, v.astype(F32), 0.0).astype(BF)

    def prepare():
        for copy in copies[4:]:
            copy.wait()
        for s in (0, 1):
            number = set_ref[s]
            a_cols[s] = keep(choose(number, lambda c: down_sets[c]))
            b_out[s] = choose(number, lambda c: out_sets[c])
            for n in (0, 1):
                b_cols[s, n] = keep(choose(number, lambda c: ff_sets[n, c]))
                a_ff[s, 16 * n : 16 * n + 16] = choose(number, lambda c: wide_sets[n, c])
        cols_ref[...] = jnp.zeros_like(cols_ref)

    sibling = uly_others()[1]
    greet([sibling, (other_blk, (uly + 2) % 4)] + ring_others(), prepare)
    here = pl.ds(pl.multiple_of(y * FF_COLS, 128), FF_COLS)
    copies[0].wait()
    spread = Spread(own_ref, x_ref, *take(3))
    spread.start()
    for copy in lines:
        copy.wait()
    for e in (0, 1, 3, 2):
        for ring in rings:
            ring.spread(e)

    def flat(ref, s):
        return ref[s].reshape(4 * CHUNK, D)

    order = (1 - core, core)
    copies[1].wait()
    copies[2].wait()
    latent_cots = []
    for k, s in enumerate(order):
        cot = flat(cot_ref, s)
        latent_cots.append(dot_nt(cot, b_out[s]))
        grad_hidden[k] = dot(cot, down_w[...]) + dot(latent_cots[k].astype(BF), a_cols[s])
        (spread.second, spread.third)[k]()
        for ring in rings:
            ring.fourth(k)
    copies[3].wait()
    for e in (3, 2):
        for ring in rings:
            ring.fourth(e)
    spread.last()

    def pair_copy(n, d):
        at = (ring_at() + d) % 4
        return remote(
            terms.at[n, 0, at], pair.at[n, at], pair_send.at[n, d], pair_recv.at[n, d], sibling
        )

    def term(n, d):
        at = (ring_at() + d) % 4
        wait_arrival(pair.at[n, at], pair_recv.at[n, d])
        return terms[n, 1, at].astype(F32) + pair[n, at].astype(F32)

    ring = RingSum(lambda d: term(0, d), take(RingSum.scratches))

    def up_weight():
        return up_w[...].reshape(D, FF_COLS)

    for k, s in enumerate(order):
        rows = flat(x_ref, s)
        latent = dot_nt(rows, a_ff[s])
        low = latent.astype(BF)
        gate = dot(rows, gate_w[...]) + dot(low[:, :16], b_cols[s, 0])
        sigmoid = jax.nn.sigmoid(gate)
        silu = gate * sigmoid
        grad_up[...] = (grad_hidden[k] * silu).astype(BF)
        slope = grad_hidden[k] * (sigmoid * (1.0 + gate * (1.0 - sigmoid)))
        if k == 0:
            for up_ring in rings:
                up_ring.last()
        up = dot(rows, up_weight()) + dot(low[:, 16:], b_cols[s, 1])
        grad_gate[...] = (slope * up).astype(BF)
        hidden_ref[...] = (silu * up).astype(BF)
        back_gate = dot_nt(grad_gate[...], b_cols[s, 0])
        back_up = dot_nt(grad_up[...], b_cols[s, 1])
        grads = (
            dot_nt(grad_gate[...], gate_w[...])
            + dot_nt(grad_up[...], up_weight())
            + dot(back_gate.astype(BF), a_ff[s, :16])
            + dot(back_up.astype(BF), a_ff[s, 16:])
        )
        terms[0, k] = grads.astype(BF).reshape(4, CHUNK, D)
        if k == 0:
            for d in (2, 1, 3, 0):
                pair_copy(0, d).start()
        else:
            ring.first()
        latent_down = dot_nt(hidden_ref[...], a_cols[s])
        down = dot_nt(hidden_ref[...], down_w[...]) + dot(latent_down.astype(BF), b_out[s])
        terms[1, k] = down.astype(BF).reshape(4, CHUNK, D)
        if k == 0:
            for d in (2, 1, 3, 0):
                pair_copy(1, d).start()
        else:
            ring.second()

        def put(ref, n, value, at=slice(None)):
            ref[pl.ds(pl.multiple_of((2 * n + s) * 16, 16), 16), at] = value.astype(BF)

        def turned(value):
            return value.T.astype(BF)

        put(cols_ref, 0, dot(turned(latent_cots[k]), hidden_ref[...]), here)
        put(cols_ref, 1, dot(turned(latent[:, :16]), grad_gate[...]), here)
        put(cols_ref, 2, dot(turned(latent[:, 16:]), grad_up[...]), here)
        put(wide_ref, 0, dot(turned(back_gate), rows))
        put(wide_ref, 1, dot(turned(back_up), rows))
        put(wide_ref, 2, dot(turned(latent_down), flat(cot_ref, s)))
    outs = [
        pltpu.make_async_copy(src, dst, out_sems.at[n])
        for n, (src, dst) in enumerate(
            ((cols_ref, cols_out), (wide_ref, wide_out), (down_sum, down_out), (total_ref, grad_out))
        )
    ]
    outs[0].start()
    outs[1].start()
    for d in range(4):
        down_sum[(ring_at() + d) % 4] = term(1, d).astype(BF)
    outs[2].start()
    total_ref[...] = ring.third()
    outs[3].start()
    for n in (0, 1):
        for d in range(4):
            pair_copy(n, d).wait_send()
    for copy in outs:
        copy.wait()


def feed_forward(*args):
    dma = pltpu.SemaphoreType.DMA
    weight = pltpu.VMEM((D, FF_COLS), BF)
    rows = pltpu.VMEM((4 * CHUNK, FF_COLS), BF)
    pieces = (4, CHUNK, D)
    return pl.pallas_call(
        ff_kernel,
        out_shape=(
            HELD((CHUNK, D), F32),
            HELD(pieces, BF),
            HELD((96, PADDED), BF),
            HELD((96, D), BF),
        ),
        in_specs=[pl.BlockSpec(memory_space=pltpu.SMEM)] + [ANY] * 9,
        out_specs=(ANY,) * 4,
        scratch_shapes=[
            pltpu.VMEM((96, PADDED), BF), pltpu.VMEM((96, D), BF),
            pltpu.VMEM((2,) + pieces, BF), pltpu.VMEM((2,) + pieces, BF),
            weight, pltpu.VMEM((32, 48, FF_COLS), BF), weight,
            pltpu.VMEM((2, 2, 16, FF_COLS), BF), pltpu.VMEM((2, 16, FF_COLS), BF),
            rows, rows, rows,
            pltpu.VMEM((2, 4 * CHUNK, FF_COLS), F32),
            pltpu.VMEM((CHUNK, D), BF),
            pltpu.VMEM((2, 2) + pieces, BF), pltpu.VMEM((2,) + pieces, BF),
            pltpu.VMEM((CHUNK, D), F32), pltpu.VMEM(pieces, BF),
            pltpu.VMEM((2, 32, D), BF), pltpu.VMEM((2, 16, D), BF),
            pltpu.VMEM((2, SETS, 16, D), BF), pltpu.VMEM((SETS, 16, FF_COLS), BF),
            pltpu.VMEM((SETS, 16, D), BF), pltpu.VMEM((2, SETS, 16, FF_COLS), BF),
            dma((8,)), dma((4,)), dma((2, 4)), dma((2, 4)),
            dma((2, Ring.sends)), dma((2, 16)), dma((2, 4)),
        ]
        + SPREAD_SEMS
        + RingSum.scratch(),
        compiler_params=pltpu.CompilerParams(
            collective_id=4, has_side_effects=True, vmem_limit_bytes=62 * 2**20
        ),
        name="feed_forward",
    )(*args)


def backward_blocks(slot, first, last, turned_ref, rows_ref, dot_ref, kv_ref, limit_ref, lse_ref, dkv_ref, acc_ref):
    limit = limit_ref[slot, 0:1, :]
    lse = lse_ref[slot, 0:1, :]
    row_dot = dot_ref[slot, 0:1, :]

    def step(n, carry):
        keys, values = key_block(kv_ref, n, KEYS_BACK)
        scores = jnp.where(key_places(n, KEYS_BACK) <= limit, dot(keys, turned_ref[0, slot]), -1e30)
        probs = jnp.exp2(scores - lse)
        grad_probs = dot(values, turned_ref[1, slot])
        grad_scores = (probs * (grad_probs - row_dot)).astype(BF)
        acc_ref[slot] += dot(keys.T, grad_scores)
        at = pl.ds(pl.multiple_of(n * KEYS_BACK, KEYS_BACK), KEYS_BACK)
        dkv_ref[at, :HEAD] += dot(grad_scores, rows_ref[0, slot])
        dkv_ref[at, HEAD:] += dot(probs.astype(BF), rows_ref[1, slot])
        return carry

    lax.fori_loop(first, last, step, 0)


class Reduce:
    @staticmethod
    def scratch(shape):
        return [
            pltpu.VMEM((2, 3, 2, 4) + shape, BF),
            pltpu.VMEM((2, 3, 2) + shape, BF),
            pltpu.VMEM((2, 4, 2) + shape, BF),
            pltpu.SemaphoreType.DMA((2, 9)),
            pltpu.SemaphoreType.DMA((2, 9)),
        ]

    scratches = 5

    def __init__(self, part, scratch):
        self.part = part
        self.buf_q, self.buf_p, self.sum_p, self.send_sem, self.recv_sem = scratch
        self.y, self.z, self.x, self.blk, self.uly = place()
        self.pq = ((self.x, self.z), (self.z, self.x))
        self.flying = []

    def send(self, src, dst, half, n, y, p, q):
        target = blk_of(y, q, p) if half == 0 else blk_of(y, p, q)
        copy = remote(
            src, dst, self.send_sem.at[half, n], self.recv_sem.at[half, n], (target, self.uly)
        )
        copy.start()
        self.flying.append(copy)

    def land(self):
        for copy in self.flying:
            copy.wait()
        self.flying = []

    def first(self):
        for d in (2, 1, 3):
            for half in (0, 1):
                p, q = self.pq[half]
                to = (q + d) % 4
                for y in (0, 1):
                    src = self.part.at[0, y, to] if half == 0 else self.part.at[1, y, :, to]
                    self.send(
                        src, self.buf_q.at[half, d - 1, y], half, (d - 1) * 2 + y, self.y, p, to
                    )

    def second(self):
        self.land()
        for d in (2, 1, 3, 0):
            for half in (0, 1):
                p, q = self.pq[half]
                to = (p + d) % 4
                for y in (0, 1):
                    own = self.part[0, y, q, to] if half == 0 else self.part[1, y, to, q]
                    total = own.astype(F32)
                    for n in range(3):
                        total += self.buf_q[half, n, y, to].astype(F32)
                    self.sum_p[half, d, y] = total.astype(BF)
                if d > 0:
                    self.send(
                        self.sum_p.at[half, d], self.buf_p.at[half, d - 1], half, 5 + d, self.y, to, q
                    )

    def third(self):
        self.land()
        return [
            [
                self.sum_p[half, 0, y].astype(F32)
                + sum(self.buf_p[half, n, y].astype(F32) for n in range(3))
                for y in (0, 1)
            ]
            for half in (0, 1)
        ]


class Shed:
    @staticmethod
    def scratch(shape):
        return [
            pltpu.VMEM((2, 4) + shape, BF),
            pltpu.VMEM((2, 4) + shape, BF),
            pltpu.VMEM((2, 2, 4) + shape, BF),
            pltpu.VMEM((4, 2) + shape, BF),
            pltpu.VMEM((3, 2) + shape, BF),
            pltpu.VMEM((2,) + shape, BF),
            pltpu.VMEM(shape, BF),
            pltpu.SemaphoreType.DMA((10,)),
            pltpu.SemaphoreType.DMA((10,)),
        ]

    scratches = 9

    def __init__(self, part, half, rows, order, scratch):
        self.part, self.half, self.rows, self.order = part, half, rows, order
        (
            self.buf_far, self.sum_mid, self.buf_in, self.sum_p, self.buf_p, self.sum_y, self.buf_y,
            self.send_sem, self.recv_sem,
        ) = scratch
        self.y, self.z, self.x, self.blk, self.uly = place()
        self.p, self.q = (self.x, self.z) if order == 0 else (self.z, self.x)
        self.flying = []

    def line(self, y, q):
        rows = pl.ds(*self.rows)
        if self.order == 0:
            return self.part.at[self.half, y, q, :, rows]
        return self.part.at[self.half, y, :, q, rows]

    def value(self, y, q, p):
        start, size = self.rows
        z, x = (q, p) if self.order == 0 else (p, q)
        return self.part[self.half, y, z, x, start : start + size].astype(F32)

    def send(self, src, dst, n, y, p, q):
        target = blk_of(y, q, p) if self.order == 0 else blk_of(y, p, q)
        copy = remote(src, dst, self.send_sem.at[n], self.recv_sem.at[n], (target, self.uly))
        copy.start()
        self.flying.append(copy)

    def land(self):
        for copy in self.flying:
            copy.wait()
        self.flying = []

    def first(self):
        for y, d in ((0, 1), (1, 3)):
            to = (self.q + d) % 4
            self.send(self.line(y, (self.q + 2) % 4), self.buf_far.at[y], y, self.y, self.p, to)
        for y, d in ((1, 1), (0, 3)):
            to = (self.q + d) % 4
            self.send(self.line(y, to), self.buf_in.at[d // 2, y], 2 + d // 2, self.y, self.p, to)

    def second(self):
        direct = self.flying[2:]
        self.flying = self.flying[:2]
        self.land()
        for y, d in ((0, 1), (1, 3)):
            to = (self.q + d) % 4
            for p in range(4):
                total = self.value(y, to, p) + self.buf_far[y, p].astype(F32)
                self.sum_mid[y, p] = total.astype(BF)
            self.send(self.sum_mid.at[y], self.buf_in.at[d // 2, y], 4 + y, self.y, self.p, to)
        self.flying += direct

    def third(self):
        self.land()
        for d in (2, 1, 3, 0):
            to = (self.p + d) % 4
            for y in (0, 1):
                total = self.value(y, self.q, to)
                for n in (0, 1):
                    total += self.buf_in[n, y, to].astype(F32)
                self.sum_p[d, y] = total.astype(BF)
            if d > 0:
                self.send(self.sum_p.at[d], self.buf_p.at[d - 1], 5 + d, self.y, to, self.q)

    def fourth(self):
        self.land()
        for k in (1, 0):
            y = self.y if k == 0 else 1 - self.y
            total = self.sum_p[0, y].astype(F32)
            for n in range(3):
                total += self.buf_p[n, y].astype(F32)
            self.sum_y[k] = total.astype(BF)
            if k == 1:
                self.send(self.sum_y.at[1], self.buf_y, 9, 1 - self.y, self.p, self.q)

    def last(self):
        self.land()
        return self.sum_y[0].astype(F32) + self.buf_y[...].astype(F32)


def reduce_others():
    y, z, x, blk, uly = place()
    return (
        [(blk_of(1 - y, z, x), uly)]
        + [(blk_of(y, z, (x + d) % 4), uly) for d in (1, 2, 3)]
        + [(blk_of(y, (z + d) % 4, x), uly) for d in (1, 2, 3)]
    )


UNIT = (16, 128)


class Total:
    @staticmethod
    def scratch(kept, summed):
        shape = (kept + summed,) + UNIT
        return (
            [pltpu.VMEM((2, 2, 4, 4) + shape, BF)]
            + Reduce.scratch(shape)
            + [
                pltpu.VMEM((2, 2) + shape, BF),
                pltpu.VMEM((4, 2, 2) + shape, BF),
                pltpu.VMEM((2, 4 * kept + summed) + UNIT, BF),
                pltpu.SemaphoreType.DMA((7,)),
                pltpu.SemaphoreType.DMA((8,)),
                pltpu.SemaphoreType.DMA((15,)),
                pltpu.SemaphoreType.DMA((15,)),
                pltpu.SemaphoreType.DMA,
                pltpu.SemaphoreType.DMA,
                pltpu.SemaphoreType.DMA,
            ]
        )

    scratches = 16

    @staticmethod
    def shape(kept, summed):
        return HELD((2, 2, 4, 4, 4 * kept + summed) + UNIT, BF)

    def __init__(self, kept, summed, all_ref, scratch):
        self.kept, self.summed, self.all_ref = kept, summed, all_ref
        self.part = scratch[0]
        self.reduce = Reduce(self.part, scratch[1:6])
        self.own, self.buf, self.full, self.send_sem, self.recv_sem = scratch[6:11]
        self.all_send, self.all_recv, self.local_sem, self.pair_send, self.pair_recv = scratch[11:16]
        self.y, self.z, self.x, self.blk, self.uly = place()
        self.core = self.uly % 2
        self.w = ring_at()
        self.flying = []

    def pack(self, values, first, per, at):
        for n, value in enumerate(values, first):
            item = n // per
            self.part[item // 32, item // 16 % 2, item // 4 % 4, item % 4, at + n % per] = value.astype(BF)

    def pack_kept(self, values, first=0):
        self.pack(values, first, self.kept, 0)

    def pack_summed(self, values, first=0):
        self.pack(values, first, self.summed, self.kept)

    def clear(self, kept, summed):
        nothing = jnp.zeros(UNIT, BF)
        self.pack_kept([nothing] * (64 * self.kept - kept), kept)
        self.pack_summed([nothing] * (64 * self.summed - summed), summed)

    def others(self):
        return [
            ((self.w + d) % 4, self.core if c == 0 else 1 - self.core)
            for d in range(4) for c in (0, 1) if (d, c) != (0, 0)
        ]

    def across(self):
        for half, totals in enumerate(self.reduce.third()):
            for y, total in enumerate(totals):
                self.own[half, y] = total.astype(BF)
        self.copies = []
        for n, (w, core) in enumerate(self.others()):
            copy = remote(
                self.own.at[core], self.buf.at[self.w, self.core],
                self.send_sem.at[n], self.recv_sem.at[self.w * 2 + self.core],
                (blk_of(w % 2, self.z, self.x), w // 2 * 2 + core),
            )
            copy.start()
            self.copies.append(copy)
        self.buf[self.w, self.core] = self.own[self.core]

    def send(self, src, dst, n, d, e):
        z, x = self.at(d, e)
        copy = remote(
            src, dst, self.all_send.at[n], self.all_recv.at[n], (blk_of(self.y, z, x), self.uly)
        )
        copy.start()
        self.flying.append(copy)

    def at(self, d, e):
        dz, dx = self.core * d + (1 - self.core) * e, self.core * e + (1 - self.core) * d
        return (self.z + dz) % 4, (self.x + dx) % 4

    def items(self, d=0, e=0):
        z, x = self.at(d, e)
        return self.all_ref.at[self.core, :, z, x]

    def join(self):
        for w, core in self.others():
            wait_arrival(self.buf.at[w, core], self.recv_sem.at[w * 2 + core])
        kept = self.kept

        def term(w, core, y):
            return self.buf[w, core, y].astype(F32)

        for y in (0, 1):
            for uly in range(4):
                w, core = uly // 2 * 2, uly % 2
                value = term(w, core, y)[:kept] + term(w + 1, core, y)[:kept]
                self.full[y, uly * kept : (uly + 1) * kept] = value.astype(BF)
            if self.summed:
                self.full[y, 4 * kept :] = sum(
                    term(w, core, y)[kept:] for w in range(4) for core in (0, 1)
                ).astype(BF)
        for d in (1, 2, 3):
            self.send(self.full, self.items(), d - 1, d, 0)
        self.local = pltpu.make_async_copy(self.full, self.items(), self.local_sem)
        self.local.start()

    def spread(self):
        self.local.wait()
        for d in range(4):
            ref = self.items((4 - d) % 4)
            if d > 0:
                wait_arrival(ref, self.all_recv.at[d - 1])
            for e in (1, 2, 3):
                self.send(ref, ref, 2 + d * 3 + e, 0, e)

    def hand(self):
        for d in range(4):
            for e in (1, 2, 3):
                wait_arrival(self.items((4 - d) % 4, 4 - e), self.all_recv.at[2 + d * 3 + e])
        self.pair(self.core).start()

    def pair(self, core):
        return remote(
            self.all_ref.at[core], self.all_ref.at[core], self.pair_send, self.pair_recv, uly_others()[1]
        )

    def end(self):
        for copy in self.copies + self.flying:
            copy.wait_send()
        self.pair(self.core).wait_send()
        wait_arrival(self.all_ref.at[1 - self.core], self.pair_recv)

    def steps(self):
        return [
            self.reduce.first, self.reduce.second, self.across, self.join, self.spread, self.hand, self.end,
        ]


def units(value):
    rows, columns = value.shape
    return [
        value[n * 16 : (n + 1) * 16, t * 128 : (t + 1) * 128]
        for n in range(rows // 16) for t in range(columns // 128)
    ]


FF_KEPT, FF_SUMMED, QKV_KEPT = 2, 2, 1
COL_TILES = PADDED // 128
D_TILES = D // 128
DKV_ROWS = CHUNK // 2
DKV_STREAMS = 2


def backward_kernel(
    gains_hbm, total_hbm, down_hbm, cols_hbm, ff_hbm, resid_hbm, cot_hbm, ao_hbm, mixed_hbm, wo_hbm, kv_hbm, q_hbm, limit_hbm, lse_hbm,
    wq_hbm, rows_hbm, normed_hbm, b_qkv_hbm, cos_hbm, sin_hbm, a_hbm, bo_hbm,
    result_ref, input_grad_ref, ff_all, qkv_all,
    gains_ref, total_ref, down_ref, cols_ref, ff_ref, resid_ref, cot_ref, ao_ref, mixed_ref, wo_ref, kv_ref, q_ref, limit_ref,
    lse_ref, wq_ref, rows_ref, normed_ref, b_qkv_ref, cos_ref, sin_ref, a_ref, bo_ref, dkv_ref, acc_ref, part, dq_ref, grad_ref, grad_attn, grad_resid, grad_qkv,
    cross_out, cross_in, home_out, home_in, turned_ref, by_rows_ref, dot_ref, back, copy_sem, cross_sem, home_send,
    home_recv, *scratch,
):
    y, z, x, blk, uly = place()
    core, h = uly % 2, uly // 2
    scratch = list(scratch)

    def take(count):
        got = scratch[:count]
        del scratch[:count]
        return got

    chunk = 2 * blk + h
    upper = chunk // 32
    home = (1 - h) * blk + h * (31 - blk)
    home_from = [(home, upper * 2 + s) for s in (0, 1)]
    lower = low_chunk(blk)
    own_chunk = (1 - h) * lower + h * (63 - lower)
    home_to = [(own_chunk // 2, (own_chunk % 2) * 2 + half) for half in (0, 1)]
    copies = [
        pltpu.make_async_copy(src, dst, copy_sem.at[n])
        for n, (src, dst) in enumerate(
            (
                (total_hbm, total_ref), (resid_hbm, resid_ref), (cot_hbm, cot_ref), (gains_hbm, gains_ref),
                (cols_hbm, cols_ref), (ff_hbm, ff_ref), (down_hbm, down_ref), (ao_hbm, ao_ref), (mixed_hbm, mixed_ref),
                (wo_hbm, wo_ref), (bo_hbm, bo_ref), (kv_hbm, kv_ref),
                (q_hbm, q_ref), (limit_hbm, limit_ref), (lse_hbm, lse_ref), (wq_hbm, wq_ref),
                (rows_hbm, rows_ref), (normed_hbm, normed_ref), (b_qkv_hbm, b_qkv_ref),
                (cos_hbm, cos_ref), (sin_hbm, sin_ref), (a_hbm, a_ref),
            )
        )
    ]
    for copy in copies:
        copy.start()
    greet(
        reduce_others()
        + uly_others()
        + [(blk_of(1 - y, z, x), other[1]) for other in uly_others()]
        + home_from
        + home_to
    )
    collect_out = RingSum(
        lambda d: down_ref[(ring_at() + d) % 4].astype(F32), take(RingSum.scratches)
    )
    low, high = (
        [
            Shed(part, half, (n * DKV_ROWS, DKV_ROWS), n, take(Shed.scratches))
            for n in range(DKV_STREAMS)
        ]
        for half in (0, 1)
    )
    ff_total = Total(FF_KEPT, FF_SUMMED, ff_all, take(Total.scratches))
    qkv_total = Total(QKV_KEPT, 0, qkv_all, take(Total.scratches))
    deliver = Deliver()

    def send_home(n, value):
        home_out[n] = value.astype(BF)
        for half in (0, 1):
            deliver.send(
                home_out.at[n, pl.ds(half * 64, 64)], home_in.at[n, core],
                home_send.at[n, half], home_recv.at[n, core], home_to[half],
            )

    def arrived_home(n):
        for s in (0, 1):
            wait_arrival(home_in.at[n, s], home_recv.at[n, s])
        return home_in[n].astype(F32)

    def ready(first, last):
        for copy in copies[first:last]:
            copy.wait()

    ready(0, 4)
    residual = resid_ref[...]
    value = cot_ref[...].astype(F32) + norm_back(
        residual, norm_scale(residual), gain(gains_ref, D_TILES), total_ref[...]
    )
    grad_resid[...] = value
    own_rows = pl.ds(pl.multiple_of(h * CHUNK, CHUNK), CHUNK)
    other_rows = pl.ds(pl.multiple_of((1 - h) * CHUNK, CHUNK), CHUNK)
    grad_attn[own_rows, :] = value.astype(BF)
    partner = uly_others()[0]
    cross = remote(
        grad_attn.at[own_rows], grad_attn.at[own_rows], cross_sem.at[0], cross_sem.at[1], partner
    )
    cross.start()
    ready(4, 11)
    ff_total.pack_kept(units(cols_ref))
    ff_total.pack_summed(units(ff_ref))
    ff_total.clear(6 * COL_TILES, 6 * D_TILES)
    steps = ff_total.steps()

    def beside(*more):
        for step in more:
            step()
        if steps:
            steps.pop(0)()

    beside()
    at_o = 3 * D_TILES + D_TILES // 2 + 2
    qkv_total.clear(at_o + D_TILES // 2 + D_TILES, 0)
    dkv_ref[...] = jnp.zeros_like(dkv_ref)
    acc_ref[...] = jnp.zeros_like(acc_ref)
    latent_o = dot_nt(ao_ref[...], mixed_ref[...]).astype(BF)
    cross.wait_send()
    wait_arrival(grad_attn.at[other_rows], cross_sem.at[1])
    back_o = dot_nt(grad_attn[...], bo_ref[...]).astype(BF)
    grad_ref[...] = (dot_nt(grad_attn[...], wo_ref[...]) + dot(back_o, ao_ref[...])).astype(BF)
    back_o = dot_nt(bo_ref[...], grad_attn[...]).astype(BF)
    qkv_total.pack_kept(
        units(dot(back_o, mixed_ref[...])) + units(dot(latent_o, grad_attn[...])), at_o
    )
    beside()

    ready(11, 15)
    def pack(half):
        def one(n, carry):
            chunk = low_chunk(n) if half == 0 else 63 - low_chunk(n)
            rows = dkv_ref[pl.ds(pl.multiple_of(chunk * CHUNK, CHUNK), CHUNK), :]
            both = jnp.concatenate([rows[:, :HEAD] * LN2, rows[:, HEAD:]], axis=1)
            part[half, n // 16, n // 4 % 4, n % 4] = both.astype(BF)
            return carry

        lax.fori_loop(0, 32, one, 0)

    def shed(streams, name):
        def run():
            for stream in streams:
                getattr(stream, name)()

        return run

    args = (turned_ref, by_rows_ref, dot_ref, kv_ref, limit_ref, lse_ref, dkv_ref, acc_ref)
    step = KEYS_BACK // CHUNK
    middle = CHUNKS // 2 // step
    beside()
    for slot in (0, 1):
        for n, ref in enumerate((q_ref, grad_ref)):
            turned_ref[n, slot] = head_columns(ref, slot)
            by_rows_ref[n, slot] = head_rows(ref, slot)
        row_dot = turned_ref[1, slot].astype(F32) * head_columns(mixed_ref, slot).astype(F32)
        dot_ref[slot] = jnp.broadcast_to(jnp.sum(row_dot, axis=0, keepdims=True), (8, ROWS))
    backward_blocks(1, middle, (63 - lower) // step + 1, *args)
    backward_blocks(0, 0, lower // step + 1, *args)
    pack(1)
    beside(shed(high, "first"))
    names = ["second", "third", "fourth"]
    extra = [collect_out.first, collect_out.second]
    for n in range(0, middle, 2):
        backward_blocks(1, n, n + 2, *args)
        more = [shed(high, names.pop(0))] if names else []
        more += [extra.pop(0)] if extra else []
        for one in more:
            one()
        if n == 2:
            beside()
    pack(0)
    for stream in low:
        stream.first()
    for slot in (0, 1):
        for n in range(GROUP):
            dq_ref[slot * CHUNK : (slot + 1) * CHUNK, n * HEAD : (n + 1) * HEAD] = (
                acc_ref[slot, :, n * CHUNK : (n + 1) * CHUNK].T * HEAD ** (-0.5)
            )
    ready(15, 22)
    a_qkv = a_ref[...].reshape(48, D)
    for stream in low:
        stream.second()
    cos_table, sine_table = cos_ref[...], sin_ref[...]

    def turn_back(value, rows=slice(None)):
        return value * cos_table[rows] - pltpu.roll(value, HEAD // 2, 1) * sine_table[rows]

    for n in range(GROUP):
        at = slice(n * HEAD, (n + 1) * HEAD)
        grad_qkv[:, at] = turn_back(dq_ref[:, at]).astype(BF)
    group = GROUP * HEAD

    def key_value(half, streams):
        for n, stream in enumerate(streams):
            rows = slice(half * CHUNK + n * DKV_ROWS, half * CHUNK + (n + 1) * DKV_ROWS)
            value = stream.last()
            grad_qkv[rows, group : group + HEAD] = turn_back(value[:, :HEAD], rows).astype(BF)
            grad_qkv[rows, group + HEAD :] = value[:, HEAD:].astype(BF)

    latent_qkv = dot_nt(a_qkv, normed_ref[...]).astype(BF)

    def project_back(slot):
        rows = slice(slot * CHUNK, (slot + 1) * CHUNK)
        grads = grad_qkv[rows, :]
        lifted = dot(dot_nt(grads, b_qkv_ref[...]).astype(BF), a_qkv)
        back[slot] = dot_nt(grads[:, :512], wq_ref[0]) + dot_nt(grads[:, 512:], wq_ref[1]) + lifted
        latent_grad = dot_nt(b_qkv_ref[...], grads).astype(BF)
        return dot(latent_grad, normed_ref[rows, :]), dot(latent_qkv[:, rows], grads)

    key_value(1, high)
    for stream in low:
        stream.third()
    send_home(0, resid_ref[...] + collect_out.third())
    grad_a, grad_b = project_back(1)
    for stream in low:
        stream.fourth()
    key_value(0, low)
    more_a, more_b = project_back(0)
    cross_out[...] = back[1 - h].astype(BF)
    cross = remote(cross_out, cross_in, cross_sem.at[2], cross_sem.at[3], partner)
    cross.start()
    grad_a, grad_b = grad_a + more_a, grad_b + more_b
    qkv_total.pack_kept(
        units(grad_a)
        + units(grad_b[:16, :group])
        + units(grad_b[16:32, group : group + HEAD])
        + units(grad_b[32:, group + HEAD :])
    )
    last_steps = qkv_total.steps()
    last_steps.pop(0)()
    last_steps.pop(0)()
    beside()
    cross.wait()
    mine = back[h] + cross_in[...].astype(F32)
    tokens = rows_ref[own_rows, :].astype(F32)
    send_home(1, grad_resid[...] + norm_back(tokens, norm_scale(tokens), gain(gains_ref, 0), mine))
    for step in last_steps + steps:
        step()
    result_ref[...] = arrived_home(0).astype(BF)
    input_grad_ref[...] = arrived_home(1).astype(BF)
    deliver.end()


def backward(*args):
    dma = pltpu.SemaphoreType.DMA
    group = GROUP * HEAD
    return pl.pallas_call(
        backward_kernel,
        out_shape=(
            jax.ShapeDtypeStruct((2, CHUNK // 2, D), BF),
            jax.ShapeDtypeStruct((2, CHUNK // 2, D), BF),
            Total.shape(FF_KEPT, FF_SUMMED),
            Total.shape(QKV_KEPT, 0),
        ),
        in_specs=[ANY] * 22,
        out_specs=(IN_VMEM, IN_VMEM, ANY, ANY),
        scratch_shapes=[
            pltpu.VMEM((40, 128), F32),
            pltpu.VMEM((CHUNK, D), F32),
            pltpu.VMEM((4, CHUNK, D), BF),
            pltpu.VMEM((96, PADDED), BF),
            pltpu.VMEM((96, D), BF),
            pltpu.VMEM((CHUNK, D), F32),
            pltpu.VMEM((CHUNK, D), BF),
            pltpu.VMEM((16, group), BF),
            pltpu.VMEM((2 * CHUNK, group), BF),
            pltpu.VMEM((D // 2, D), BF),
            pltpu.VMEM((CHUNKS, CHUNK, 2 * HEAD), BF),
            pltpu.VMEM((2 * CHUNK, group), BF),
            pltpu.VMEM((2, 8, ROWS), jnp.int32),
            pltpu.VMEM((2, 8, ROWS), F32),
            pltpu.VMEM((2, D, 512), BF),
            pltpu.VMEM((2 * CHUNK, D), BF),
            pltpu.VMEM((2 * CHUNK, D), BF),
            pltpu.VMEM((48, 1024), BF),
            pltpu.VMEM((2 * CHUNK, HEAD), F32),
            pltpu.VMEM((2 * CHUNK, HEAD), F32),
            pltpu.VMEM((3, 16, D), BF),
            pltpu.VMEM((16, D), BF),
            pltpu.VMEM((CHUNKS * CHUNK, 2 * HEAD), F32),
            pltpu.VMEM((2, HEAD, ROWS), F32),
            pltpu.VMEM((2, 2, 4, 4, CHUNK, 2 * HEAD), BF),
            pltpu.VMEM((2 * CHUNK, group), F32),
            pltpu.VMEM((2 * CHUNK, group), BF),
            pltpu.VMEM((2 * CHUNK, D), BF),
            pltpu.VMEM((CHUNK, D), F32),
            pltpu.VMEM((2 * CHUNK, 1024), BF),
            pltpu.VMEM((CHUNK, D), BF),
            pltpu.VMEM((CHUNK, D), BF),
            pltpu.VMEM((2, CHUNK, D), BF),
            pltpu.VMEM((2, 2, CHUNK // 2, D), BF),
            pltpu.VMEM((2, 2, HEAD, ROWS), BF),
            pltpu.VMEM((2, 2, ROWS, HEAD), BF),
            pltpu.VMEM((2, 8, ROWS), F32),
            pltpu.VMEM((2, CHUNK, D), F32),
            dma((22,)), dma((4,)), dma((2, 2)), dma((2, 2)),
        ]
        + RingSum.scratch()
        + Shed.scratch((DKV_ROWS, 2 * HEAD)) * (2 * DKV_STREAMS)
        + Total.scratch(FF_KEPT, FF_SUMMED)
        + Total.scratch(QKV_KEPT, 0),
        compiler_params=pltpu.CompilerParams(
            collective_id=2, has_side_effects=True, vmem_limit_bytes=60 * 2**20
        ),
        name="backward",
    )(*args)


def fold_kernel(
    set_ref, result_in, grad_in, ff_hbm, qkv_hbm, result_ref, input_grad_ref, a_wide, a_down, b_wide, b_kv, b_ff,
    ff_ref, qkv_ref, sems,
):
    c = pl.program_id(0)
    share = [jnp.where(set_ref[s] == c, 1.0, 0.0) for s in (0, 1)]

    @pl.when(c == 0)
    def _():
        copies = [
            pltpu.make_async_copy(src, dst, sems.at[n])
            for n, (src, dst) in enumerate(((ff_hbm, ff_ref), (qkv_hbm, qkv_ref)))
        ]
        for copy in copies:
            copy.start()
        result_ref[...] = result_in[...]
        input_grad_ref[...] = grad_in[...].astype(F32)
        for copy in copies:
            copy.wait()

    chosen = jnp.logical_or(set_ref[0] == c, set_ref[1] == c)

    @pl.when(jnp.logical_not(chosen))
    def _():
        for ref in (a_wide, a_down, b_wide, b_kv, b_ff):
            ref[...] = jnp.zeros_like(ref)

    @pl.when(chosen)
    def _():
        fold_set(share, ff_ref, qkv_ref, a_wide, a_down, b_wide, b_kv, b_ff)


def fold_set(share, ff_ref, qkv_ref, a_wide, a_down, b_wide, b_kv, b_ff):
    def kept(ref, per, n, u):
        item = n // per
        return ref[item // 32, item // 16 % 2, item // 4 % 4, item % 4, u * per + n % per].astype(F32)

    def ff_kept(n, u):
        return kept(ff_ref, FF_KEPT, n, u)

    def qkv_kept(n, u):
        return kept(qkv_ref, QKV_KEPT, n, u)

    def summed(n):
        item = n // FF_SUMMED
        return ff_ref[
            item // 32, item // 16 % 2, item // 4 % 4, item % 4, 4 * FF_KEPT + n % FF_SUMMED
        ].astype(F32)

    def put(ref, at, tile, value):
        ref[at + (slice(None), slice(tile * 128, (tile + 1) * 128))] = (
            share[0] * value(0) + share[1] * value(1)
        )

    for n in range(3):
        for t in range(D_TILES):
            put(a_wide, (n, 0), t, lambda s: qkv_kept(n * D_TILES + t, s) + qkv_kept(n * D_TILES + t, 2 + s))
    half = D_TILES // 2
    at_o = 3 * D_TILES + half + 2
    for t in range(D_TILES):
        h, part = t // half, t % half
        put(a_wide, (3, 0), t, lambda s: qkv_kept(at_o + part, 2 * h + s))
        put(b_wide, (0, 0), t, lambda s: qkv_kept(3 * D_TILES + part, 2 * h + s))
        put(
            b_wide, (1, 0), t,
            lambda s: qkv_kept(at_o + half + t, s) + qkv_kept(at_o + half + t, 2 + s),
        )
        for n, (ref, at) in enumerate(((a_wide, (4, 0)), (a_wide, (5, 0)), (b_wide, (2, 0)))):
            put(ref, at, t, lambda s: summed((2 * n + s) * D_TILES + t))
    for n in (0, 1):
        for h in (0, 1):
            put(b_kv, (n, 0), h, lambda s: qkv_kept(3 * D_TILES + half + n, 2 * h + s))
    for n, (ref, at) in enumerate(((a_down, (0,)), (b_ff, (0, 0)), (b_ff, (1, 0)))):
        for t in range(FF // 128):
            where = [
                (u, t - start) for u, start in enumerate((0, 17, 35, 52)) if 0 <= t - start < COL_TILES
            ]
            put(
                ref, at, t,
                lambda s: sum(ff_kept((2 * n + s) * COL_TILES + tile, u) for u, tile in where),
            )


def fold(set_index, result, input_grad, ff_all, qkv_all):
    rows = pl.BlockSpec(result.shape, lambda c: (0, 0, 0))

    def by_set(lead, columns):
        shape = lead + (1, 16, columns)
        return pl.BlockSpec(shape, lambda c: (0,) * len(lead) + (c, 0, 0))

    def out(lead, columns):
        return jax.ShapeDtypeStruct(lead + (SETS, 16, columns), F32)

    outs = (((6,), D), ((), FF), ((3,), D), ((2,), 2 * HEAD), ((2,), FF))
    return pl.pallas_call(
        fold_kernel,
        grid=(SETS,),
        out_shape=(
            jax.ShapeDtypeStruct(result.shape, BF),
            jax.ShapeDtypeStruct(result.shape, F32),
        )
        + tuple(out(*o) for o in outs),
        in_specs=[pl.BlockSpec(memory_space=pltpu.SMEM), rows, rows, ANY, ANY],
        out_specs=(rows, rows) + tuple(by_set(*o) for o in outs),
        scratch_shapes=[
            pltpu.VMEM(ff_all.shape, BF), pltpu.VMEM(qkv_all.shape, BF), pltpu.SemaphoreType.DMA((2,))
        ],
        compiler_params=pltpu.CompilerParams(vmem_limit_bytes=40 * 2**20),
        name="fold",
    )(set_index, result, input_grad, ff_all, qkv_all)


def norm_scale(hidden):
    return lax.rsqrt(jnp.mean(hidden * hidden, axis=-1, keepdims=True) + EPS)


def norm_back(hidden, scaled, gain_vec, upstream):
    normed = hidden * scaled
    weighted = upstream * gain_vec
    return scaled * (weighted - normed * jnp.mean(weighted * normed, axis=-1, keepdims=True))


def held(*arrays):
    return [pltpu.with_memory_space_constraint(v, pltpu.HBM) for v in arrays]


def body(
    tokens, cotangent, lengths, set_index, norm_in, norm_ff, qkv_bias, w_qkv, w_out, w_gate_up, w_down,
    a_wide, a_down, b_wide, b_kv, b_ff,
):
    frequencies = np.float64(THETA) ** (-np.arange(0, HEAD, 2, dtype=np.float64) / HEAD)
    frequencies = jnp.asarray(np.concatenate([frequencies, frequencies])[None].astype(np.float32))
    gains = jnp.concatenate([norm_in, norm_ff, qkv_bias]).reshape(40, 128)
    (
        q, mixed, lse, kv_all, qkv_w, out_w, gate_w, up_w, down_w, rows, normed, residual, grad_out,
        normed_ff, grad_gathered, limit, cos_table, sine_table, b_qkv, ao, a_own, bo,
    ) = forward(
        *held(
            tokens, cotangent, lengths, set_index, w_qkv, w_out, w_gate_up, w_down.T, gains, frequencies,
            a_wide, b_wide, b_kv,
        )
    )
    gate_w, down_w = (w.reshape(D, FF_COLS) for w in (gate_w, down_w))
    grad_normed_ff, down_sum, cols, ff_wide = feed_forward(
        set_index, normed_ff, grad_gathered, gate_w, up_w, down_w, *held(a_wide, a_down, b_wide, b_ff)
    )
    result, input_grad, ff_all, qkv_all = backward(
        gains,
        grad_normed_ff, down_sum, cols, ff_wide, residual, grad_out, ao, mixed, out_w, kv_all, q, limit, lse,
        qkv_w, rows, normed, b_qkv, cos_table, sine_table, a_own, bo,
    )
    return tuple(fold(set_index, *held(result, input_grad, ff_all, qkv_all)))


def solution(mesh):
    spread = P(None, ("blk", "uly"), None)
    in_specs = (
        spread, spread, P(), P(), P(), P(), P(),
        P(("blk", "uly"), None), P(("blk", "uly"), None), P(None, "blk", "uly"), P("uly", "blk"),
        P(), P(), P(), P(), P(),
    )
    out_specs = (spread, spread, P(), P(), P(), P(), P())
    return jax.shard_map(body, mesh=mesh, in_specs=in_specs, out_specs=out_specs, check_vma=False)
```

```python
import functools

import jax
import jax.numpy as jnp
import numpy as np
from jax import lax
from jax.experimental import pallas as pl
from jax.experimental.pallas import tpu as pltpu
from jax.sharding import PartitionSpec as P

HEADS = 12
KV_HEADS = 2
HEAD = 128
GROUP = HEADS // KV_HEADS
FF = 8960
SETS = 8
D = 1536
CHUNK = 128
CHUNKS = 64
PADDED = 2304
EPS = 1e-06
THETA = 1000000.0
LOG2E = 1.4426950408889634
LN2 = 0.6931471805599453
MESH = pl.DeviceIdType.MESH
BF = jnp.bfloat16
F32 = jnp.float32
ANY = pl.BlockSpec(memory_space=pltpu.HBM)
IN_VMEM = pl.BlockSpec(memory_space=pltpu.VMEM)
HELD = pltpu.HBM


def blk_of(y, z, x):
    return y * 16 + z * 4 + x


def low_chunk(blk):
    return (1 - blk // 16) * 2 * blk + blk // 16 * (63 - 2 * blk)


def place():
    blk = lax.axis_index("blk")
    return blk // 16, (blk // 4) % 4, blk % 4, blk, lax.axis_index("uly")


def ring_others():
    y, z, x, blk, uly = place()
    return [
        (blk_of(1 - y, z, x), uly),
        (blk_of(y, z, (x + 1) % 4), uly),
        (blk_of(y, z, (x + 3) % 4), uly),
        (blk_of(y, (z + 1) % 4, x), uly),
        (blk_of(y, (z + 3) % 4, x), uly),
    ]


def choose(number, value):
    chosen = value(0)
    for c in range(1, SETS):
        chosen = jnp.where(number == c, value(c), chosen)
    return chosen


def gain(ref, first):
    return jnp.concatenate([ref[n : n + 1, :] for n in range(first, first + D // 128)], axis=1)


def greet(others, meanwhile=None):
    barrier = pltpu.get_barrier_semaphore()
    for other in others:
        pl.semaphore_signal(barrier, inc=1, device_id=other, device_id_type=MESH)
    if meanwhile is not None:
        meanwhile()
    pl.semaphore_wait(barrier, len(others))


class Gather:
    sends = 31

    def __init__(self, src, dst, send_sem, recv_sem, local_sem, orders=(0, 1)):
        self.src, self.dst, self.orders = src, dst, orders
        self.streams = range(len(orders))
        self.send_sem, self.recv_sem, self.local_sem = send_sem, recv_sem, local_sem
        self.y, self.z, self.x, self.blk, self.uly = place()
        self.count = [0] * len(orders)
        self.sent = []
        self.local = []

    def at(self, stream, y, p, q):
        order = self.orders[stream]
        return blk_of(y, order * p + (1 - order) * q, order * q + (1 - order) * p)

    def pq(self, stream):
        order = self.orders[stream]
        return (
            order * self.z + (1 - order) * self.x,
            order * self.x + (1 - order) * self.z,
        )

    def send(self, stream, item, target, src=None):
        copy = pltpu.make_async_remote_copy(
            src_ref=self.dst(stream, item) if src is None else src,
            dst_ref=self.dst(stream, item),
            send_sem=self.send_sem.at[stream, self.count[stream]],
            recv_sem=self.recv_sem.at[stream, item],
            device_id=(target, self.uly),
            device_id_type=MESH,
        )
        self.count[stream] += 1
        copy.start()
        self.sent.append(copy)

    def wait(self, stream, item):
        ref = self.dst(stream, item)
        pltpu.make_async_remote_copy(
            src_ref=ref,
            dst_ref=ref,
            send_sem=self.send_sem.at[stream, 0],
            recv_sem=self.recv_sem.at[stream, item],
            device_id=(self.blk, self.uly),
            device_id_type=MESH,
        ).wait_recv()

    def start(self):
        for s in self.streams:
            p, q = self.pq(s)
            self.send(s, self.blk, self.at(s, 1 - self.y, p, q), self.src(s))
        for s in self.streams:
            p, q = self.pq(s)
            for d in (1, 3):
                self.send(s, self.blk, self.at(s, self.y, (p + d) % 4, q), self.src(s))
            copy = pltpu.make_async_copy(self.src(s), self.dst(s, self.blk), self.local_sem.at[s])
            copy.start()
            self.local.append(copy)

    def second(self):
        for s in self.streams:
            p, q = self.pq(s)
            item = self.at(s, 1 - self.y, p, q)
            self.wait(s, item)
            for d in (1, 3):
                self.send(s, item, self.at(s, self.y, (p + d) % 4, q))
            for d in (1, 3):
                onward = self.at(s, self.y, p, (q + d) % 4)
                self.send(s, self.blk, onward, self.src(s))
                self.send(s, item, onward)

    def spread(self, s, item):
        p, q = self.pq(s)
        for d in (1, 3):
            self.send(s, item, self.at(s, self.y, p, (q + d) % 4))

    def third(self):
        for k, y in enumerate((self.y, 1 - self.y)):
            for s in self.streams:
                p, q = self.pq(s)
                for d in (3, 1):
                    item = self.at(s, y, (p + d) % 4, q)
                    self.wait(s, item)
                    if (d == 3) == (k == 0):
                        self.send(s, item, self.at(s, self.y, (p + 4 - d) % 4, q))
                    self.spread(s, item)
        for y in (self.y, 1 - self.y):
            for s in self.streams:
                p, q = self.pq(s)
                item = self.at(s, y, (p + 2) % 4, q)
                self.wait(s, item)
                self.spread(s, item)

    def fourth(self):
        for e in (0, 1, 3, 2):
            for k, y in enumerate((self.y, 1 - self.y)):
                for s in self.streams:
                    p, q = self.pq(s)
                    for d in (3, 1):
                        item = self.at(s, y, (p + e) % 4, (q + d) % 4)
                        self.wait(s, item)
                        if (d == 3) == (k == 0):
                            self.send(s, item, self.at(s, self.y, p, (q + 4 - d) % 4))

    def last(self):
        for e in (0, 1, 3, 2):
            for y in (self.y, 1 - self.y):
                for s in self.streams:
                    p, q = self.pq(s)
                    self.wait(s, self.at(s, y, (p + e) % 4, (q + 2) % 4))
        for copy in self.local:
            copy.wait()
        for copy in self.sent:
            copy.wait_send()


GATHER_SEMS = lambda *lead: [
    pltpu.SemaphoreType.DMA(lead + (2, Gather.sends)),
    pltpu.SemaphoreType.DMA(lead + (2, 32)),
    pltpu.SemaphoreType.DMA(lead + (2,)),
]


KEYS = 1024
KEYS_BACK = 512
ROWS = GROUP * CHUNK


def head_columns(ref, slot):
    return jnp.concatenate(
        [
            ref[slot * CHUNK : (slot + 1) * CHUNK, n * HEAD : (n + 1) * HEAD].T
            for n in range(GROUP)
        ],
        axis=1,
    )


def head_rows(ref, slot):
    return jnp.concatenate(
        [
            ref[slot * CHUNK : (slot + 1) * CHUNK, n * HEAD : (n + 1) * HEAD]
            for n in range(GROUP)
        ],
        axis=0,
    )


def key_block(kv_ref, step, keys):
    count = keys // CHUNK
    rows = kv_ref[pl.ds(step * count, count)].reshape(keys, 2 * HEAD)
    return rows[:, :HEAD], rows[:, HEAD:]


def dot(a, b):
    return jnp.dot(a, b, preferred_element_type=F32)


def key_places(step, keys):
    return lax.broadcasted_iota(jnp.int32, (keys, ROWS), 0) + step * keys


def dot_nt(a, b):
    return lax.dot_general(a, b, (((1,), (1,)), ((), ())), preferred_element_type=F32)


def forward_blocks(slot, first, last, turned_ref, kv_ref, limit_ref, acc_ref, stat_ref):
    turned = turned_ref[slot]
    limit = limit_ref[slot, 0:1, :]

    def step(n, carry):
        top, total = carry
        keys, values = key_block(kv_ref, n, KEYS)
        scores = jnp.where(key_places(n, KEYS) <= limit, dot(keys, turned), -1e30)
        new_top = jnp.maximum(top, jnp.max(scores, axis=0, keepdims=True))
        fade = jnp.exp2(top - new_top)
        probs = jnp.exp2(scores - new_top)
        total = total * fade + jnp.sum(probs, axis=0, keepdims=True)
        acc_ref[slot] = acc_ref[slot] * fade + dot(values.T, probs.astype(BF))
        return new_top, total

    top, total = lax.fori_loop(
        first, last, step, (stat_ref[slot, 0, 0:1, :], stat_ref[slot, 1, 0:1, :])
    )
    stat_ref[slot, 0, 0:1, :] = top
    stat_ref[slot, 1, 0:1, :] = total


def forward_end(slot, mixed_ref, lse_ref, acc_ref, stat_ref):
    top, total = stat_ref[slot, 0, 0:1, :], stat_ref[slot, 1, 0:1, :]
    out = acc_ref[slot] / total
    for n in range(GROUP):
        mixed_ref[slot * CHUNK : (slot + 1) * CHUNK, n * HEAD : (n + 1) * HEAD] = out[
            :, n * CHUNK : (n + 1) * CHUNK
        ].T.astype(BF)
    lse_ref[slot] = jnp.broadcast_to(top + jnp.log2(total), (8, ROWS))


def uly_others():
    y, z, x, blk, uly = place()
    return [(blk, (uly + 2) % 4), (blk, uly + 1 - 2 * (uly % 2)), (blk, 3 - uly)]


def ring_place(w):
    y, z, x, blk, uly = place()
    return (blk_of(w % 2, z, x), (w // 2) * 2 + uly % 2)


def ring_at():
    y, z, x, blk, uly = place()
    return (uly // 2) * 2 + y


def wait_arrival(ref, sem):
    pltpu.make_async_copy(ref, ref, sem).wait()


def remote(src, dst, send, recv, device):
    return pltpu.make_async_remote_copy(
        src_ref=src, dst_ref=dst, send_sem=send, recv_sem=recv, device_id=device, device_id_type=MESH
    )


class Deliver:
    def __init__(self):
        self.sent = []

    def send(self, src, dst, send, recv, device):
        y, z, x, blk, uly = place()
        here = jnp.logical_and(device[0] == blk, device[1] == uly)

        @pl.when(here)
        def _():
            pltpu.make_async_copy(src, dst, recv).start()

        @pl.when(jnp.logical_not(here))
        def _():
            remote(src, dst, send, recv, device).start()

        self.sent.append((here, src, dst, send, recv, device))

    def end(self):
        for here, *copy in self.sent:

            @pl.when(jnp.logical_not(here))
            def _():
                remote(*copy).wait_send()


class Ring:
    sends = 15

    def __init__(self, src, dst, y, order, way, send_sem, recv_sem):
        self.src, self.dst, self.y, self.order, self.way = src, dst, y, order, way
        self.send_sem, self.recv_sem = send_sem, recv_sem
        self.own_y, self.z, self.x, self.blk, self.uly = place()
        self.p = order * self.z + (1 - order) * self.x
        self.q = order * self.x + (1 - order) * self.z
        self.sent = []

    def at(self, y, p, q):
        order = self.order
        return blk_of(y, order * p + (1 - order) * q, order * q + (1 - order) * p)

    def index(self, p, q):
        return self.at(0, p, q)

    def send(self, p, q, dp, dq, src=None):
        ref = self.dst(self.at(self.y, p, q))
        target = self.at(self.own_y, (self.p + dp) % 4, (self.q + dq) % 4)
        copy = remote(
            ref if src is None else src, ref, self.send_sem.at[len(self.sent)],
            self.recv_sem.at[self.index(p, q)], (target, self.uly),
        )
        copy.start()
        self.sent.append(copy)

    def wait(self, p, q):
        wait_arrival(self.dst(self.at(self.y, p, q)), self.recv_sem.at[self.index(p, q)])

    def start(self):
        for d in (1, 3):
            self.send(self.p, self.q, d, 0, self.src)

    def second(self):
        for d in (4 - self.way, self.way):
            p = (self.p + d) % 4
            self.wait(p, self.q)
            if d == 4 - self.way:
                self.send(p, self.q, self.way, 0)

    def third(self):
        self.wait((self.p + 2) % 4, self.q)

    def spread(self, e):
        p = (self.p + e) % 4
        for d in (1, 3):
            self.send(p, self.q, 0, d, self.src if e == 0 else None)

    def fourth(self, e):
        p = (self.p + e) % 4
        way = self.way if e % 2 == 0 else 4 - self.way
        for d in (4 - way, way):
            q = (self.q + d) % 4
            self.wait(p, q)
            if d == 4 - way:
                self.send(p, q, 0, way)

    def last(self):
        for e in (0, 1, 3, 2):
            self.wait((self.p + e) % 4, (self.q + 2) % 4)
        self.end()

    def end(self):
        for copy in self.sent:
            copy.wait_send()


class Spread:
    def __init__(self, own, all_ref, send_sem, recv_sem, local_sem):
        self.own, self.all_ref = own, all_ref
        self.send_sem, self.recv_sem, self.local_sem = send_sem, recv_sem, local_sem
        self.w = ring_at()
        self.core = lax.axis_index("uly") % 2
        self.sibling = uly_others()[1]
        self.sent = []

    def piece(self, d, rows=slice(None), core=None):
        core = self.core if core is None else core
        ref = self.all_ref.at[core, (self.w + d) % 4]
        return ref if rows == slice(None) else ref.at[pl.ds(rows.start, rows.stop - rows.start)]

    def send(self, src, dst, recv, device):
        copy = remote(src, dst, self.send_sem.at[len(self.sent)], self.recv_sem.at[recv], device)
        copy.start()
        self.sent.append(copy)

    def pair(self, d, src=None):
        self.send(self.piece(d) if src is None else src, self.piece(d), 4 + d, self.sibling)

    def start(self):
        self.local = pltpu.make_async_copy(self.own, self.piece(0), self.local_sem)
        self.local.start()
        self.send(self.own, self.piece(0), 0, ring_place((self.w + 1) % 4))
        self.send(self.own, self.piece(0), 1, ring_place((self.w + 3) % 4))
        self.pair(0, self.own)

    def second(self):
        half = CHUNK // 2
        wait_arrival(self.piece(3), self.recv_sem.at[0])
        low = self.piece(3, slice(0, half))
        self.send(low, low, 2, ring_place((self.w + 1) % 4))
        self.pair(3)
        wait_arrival(self.piece(1), self.recv_sem.at[1])
        high = self.piece(1, slice(half, CHUNK))
        self.send(high, high, 3, ring_place((self.w + 3) % 4))
        self.pair(1)

    def third(self):
        half = CHUNK // 2
        wait_arrival(self.piece(2, slice(0, half)), self.recv_sem.at[2])
        wait_arrival(self.piece(2, slice(half, CHUNK)), self.recv_sem.at[3])
        self.pair(2)

    def last(self):
        for d in range(4):
            wait_arrival(self.piece(d, core=1 - self.core), self.recv_sem.at[4 + d])
        for copy in self.sent:
            copy.wait_send()
        self.local.wait()


SPREAD_SEMS = [pltpu.SemaphoreType.DMA((8,)), pltpu.SemaphoreType.DMA((8,)), pltpu.SemaphoreType.DMA]
FF_COLS = PADDED // 2


def forward_kernel(
    tokens_ref, cot_ref, length_hbm, set_hbm, qkv_hbm, w_out_hbm, gate_up_hbm, down_hbm, gains_hbm, freq_hbm,
    a_hbm, b_hbm, bkv_hbm,
    q_out, mixed_out, lse_out, kv_out, wq_out, wo_out, gate_all, up_all, down_all, rows_hbm, normed_out,
    resid_out, cot_out, nf_out, cot_all, limit_out, cos_out, sin_out, b_qkv_out, ao_out, a_out, bo_out,
    q_ref, mixed_ref, lse_ref, rows_out, normed_ref, resid_ref, cot_own, limit_ref, cos_ref, sin_ref,
    b_qkv_ref, ao_ref, a_ref, b_ref, bkv_ref, a_sets, b_sets, bkv_sets, turned_ref,
    length_ref, set_ref, qkv_ref, out_ref, gate_up_ref, down_ref, gains_ref, freq_ref, kv_all, wq_all, wo_all, rows, cot_in, kv_part, acc_ref, stat_ref, qkv_in, out_in, qkv_part, out_part,
    nf_own, cross_out, cross_in, qkv_pieces, out_pieces, ff_ref,
    *sems,
):
    y, z, x, blk, uly = place()
    core, h = uly % 2, uly // 2
    sems = list(sems)

    def take(count):
        got = sems[:count]
        del sems[:count]
        return got

    chunk = 2 * blk + h
    upper = chunk // 32
    home = (1 - h) * blk + h * (31 - blk)
    row_to = [[(home, hh * 2 + s) for hh in (0, 1)] for s in (0, 1)]
    row_from = [(b, hh * 2 + half) for b, hh in ((blk, 0), (31 - blk, 1)) for half in (0, 1)]
    lower = low_chunk(blk)
    out_to = [(2 * (blk % 16) + q // 2, (blk // 16) * 2 + q % 2) for q in range(4)]
    out_from = [(16 * h + blk // 2, u) for u in range(4)]
    sibling = uly_others()[1]
    set_sem = sems.pop()
    in_sem = sems.pop()
    in_copies = [
        pltpu.make_async_copy(src, dst, in_sem.at[n])
        for n, (src, dst) in enumerate(
            (
                (qkv_hbm, qkv_ref), (w_out_hbm, out_ref), (gate_up_hbm, gate_up_ref), (down_hbm, down_ref),
                (length_hbm, length_ref), (set_hbm, set_ref), (gains_hbm, gains_ref), (freq_hbm, freq_ref),
            )
        )
    ]
    for copy in in_copies:
        copy.start()
    set_copies = [
        pltpu.make_async_copy(src, dst, set_sem.at[n])
        for n, (src, dst) in enumerate(
            ((a_hbm.at[pl.ds(0, 4)], a_sets), (b_hbm.at[pl.ds(0, 2)], b_sets), (bkv_hbm, bkv_sets))
        )
    ]
    for copy in set_copies:
        copy.start()

    def prepare():
        qkv_pieces[...] = jnp.zeros_like(qkv_pieces)
        out_pieces[...] = jnp.zeros_like(out_pieces)
        for copy in in_copies:
            copy.wait()
        group = GROUP * HEAD
        for hh in (0, 1):
            qkv_pieces[2 * hh, :12] = qkv_ref[:, hh * group : hh * group + 512]
            for place_at, start, size in (
                (0, hh * group + 512, 256),
                (256, HEADS * HEAD + hh * HEAD, HEAD),
                (384, HEADS * HEAD + 256 + hh * HEAD, HEAD),
            ):
                qkv_pieces[2 * hh + 1, :12, place_at : place_at + size] = qkv_ref[:, start : start + size]
        for q in range(4):
            out_pieces[q, :12] = out_ref[:, q * 384 : (q + 1) * 384]
        for n in range(3):
            part = (gate_up_ref[n] if n < 2 else down_ref[...]).astype(F32)
            none = jnp.zeros((48, 64), F32)
            left = jnp.concatenate([part, none], axis=1)
            right = jnp.concatenate([none, part], axis=1)
            ff_ref[n] = jnp.where(jnp.broadcast_to(core, (48, PADDED)) == 1, right, left).astype(BF)

    greet(
        ring_others() + uly_others() + [(blk_of(1 - y, z, x), (uly + 2) % 4)]
        + row_to[0] + row_to[1] + row_from + out_to + out_from,
        prepare,
    )

    length = length_ref[0] * (1 - core) + length_ref[1] * core

    deliver = Deliver()
    piece_send, piece_recv, row_send, row_recv = take(4)
    for q in range(4):
        deliver.send(qkv_pieces.at[q], qkv_in.at[uly], piece_send.at[q], piece_recv.at[uly], (blk, q))
    for q in range(4):
        deliver.send(out_pieces.at[q], out_in.at[uly], piece_send.at[4 + q], piece_recv.at[4 + uly], out_to[q])
    for s in (0, 1):
        for hh in (0, 1):
            deliver.send(
                tokens_ref.at[s], rows.at[upper, core], row_send.at[s * 2 + hh],
                row_recv.at[upper * 2 + core], row_to[s][hh],
            )

    wide = PADDED // 2
    gathered = (gate_all, up_all, down_all)
    ff_send, ff_recv, y_send, y_recv, y_local = take(5)
    other_blk = blk_of(1 - y, z, x)

    def ff_part(n, half):
        return ff_ref.at[n, :, pl.ds(pl.multiple_of(half * wide, 128), wide)]

    y_copies = []
    for n, ref in enumerate(gathered):
        copy = remote(ff_part(n, 1 - y), ref.at[blk], y_send.at[n], y_recv.at[n], (other_blk, uly))
        copy.start()
        y_copies.append(copy)
        copy = pltpu.make_async_copy(ff_part(n, y), ref.at[blk], y_local.at[n])
        copy.start()
        y_copies.append(copy)
    own_ff, other_ff = (
        [
            Ring(
                ff_part(n, y) if k == 0 else ref.at[other_blk],
                lambda item, ref=ref: ref.at[item],
                y if k == 0 else 1 - y,
                y if k == 0 else 1 - y,
                (1, 3, 1 + 2 * k)[n],
                ff_send.at[k, n], ff_recv.at[k, n],
            )
            for n, ref in enumerate(gathered)
        ]
        for k in (0, 1)
    )
    picked = lax.broadcasted_iota(jnp.int32, (48, 64), 1)
    picked = jnp.where(picked % 16 < 12, picked // 16 * 12 + picked % 16, -1)
    picked = jnp.where(picked == lax.broadcasted_iota(jnp.int32, (48, 64), 0), 1.0, 0.0).astype(BF)
    for u in range(4):
        wait_arrival(qkv_in.at[u], piece_recv.at[u])
    qkv_part[...] = dot(picked, qkv_in[...].reshape(64, 512)).astype(BF)
    wq = Gather(
        lambda s: qkv_part.at[:, pl.ds(256 * s, 256)],
        lambda s, item: wq_all.at[
            core, pl.ds(pl.multiple_of(item * 48, 16), 48), pl.ds(256 * s, 256)
        ],
        *take(3),
    )
    wq.start()
    for u in range(4):
        wait_arrival(out_in.at[u], piece_recv.at[4 + u])
    out_part[...] = dot(picked, out_in[...].reshape(64, 384)).astype(BF)
    for s in (0, 1):
        deliver.send(
            cot_ref.at[s], cot_in.at[core], row_send.at[4 + s], row_recv.at[4 + core], (home, upper * 2 + s)
        )

    def out_columns(item, s):
        start = ((item % 2) * 2 + core) * 384
        return pl.ds(pl.multiple_of(start + 128 * s, 128), 128 + 128 * s)

    wo = Gather(
        lambda s: out_part.at[:, pl.ds(128 * s, 128 + 128 * s)],
        lambda s, item: wo_all.at[pl.ds(pl.multiple_of((item // 2) * 48, 16), 48), out_columns(item, s)],
        *take(3),
    )
    rings = own_ff + other_ff
    whole = [ring for n, ring in enumerate(rings) if n % 3 != 1]
    def tables(slot):
        at = lower if slot == 0 else 63 - lower
        row = lax.broadcasted_iota(jnp.int32, (CHUNK, HEAD), 0) + at * CHUNK
        angle = row.astype(F32) * freq_ref[...]
        first = lax.broadcasted_iota(jnp.int32, (CHUNK, HEAD), 1) < HEAD // 2
        sine = jnp.sin(angle)
        cos_ref[slot * CHUNK : (slot + 1) * CHUNK, :] = jnp.cos(angle)
        sin_ref[slot * CHUNK : (slot + 1) * CHUNK, :] = jnp.where(first, -sine, sine)
        row = lax.broadcasted_iota(jnp.int32, (8, ROWS), 1) % CHUNK + at * CHUNK
        limit_ref[slot] = jnp.minimum(row, length - 1)

    stat_ref[:, 0] = jnp.full((2, 8, ROWS), -1e30, F32)
    stat_ref[:, 1] = jnp.zeros((2, 8, ROWS), F32)
    acc_ref[...] = jnp.zeros_like(acc_ref)
    own_set = set_ref[0] * (1 - core) + set_ref[1] * core
    for copy in set_copies:
        copy.wait()
    for sets, ref in ((a_sets, a_ref), (b_sets, b_ref), (bkv_sets, bkv_ref)):
        for n in range(ref.shape[0]):
            ref[n] = choose(own_set, lambda c: sets[n, c])
    group = GROUP * HEAD
    group_at = pl.ds(pl.multiple_of(h * group, 128), group)
    head_at = pl.ds(pl.multiple_of(h * HEAD, 128), HEAD)
    ao_ref[...] = a_ref[3, :, group_at]
    b_qkv_ref[...] = jnp.zeros_like(b_qkv_ref)
    b_qkv_ref[:16, :group] = b_ref[0, :, group_at]
    b_qkv_ref[16:32, group : group + HEAD] = bkv_ref[0, :, head_at]
    b_qkv_ref[32:, group + HEAD :] = bkv_ref[1, :, head_at]
    a_qkv = a_ref[:3].reshape(48, D)
    bo_ref = b_ref.at[1]

    def bias(n):
        at = h * GROUP + n if n < GROUP else HEADS + 2 * (n - GROUP) + h
        return gains_ref[pl.ds(2 * D_TILES + at, 1), :]

    wq.second()
    tables(0)
    wq.third()
    tables(1)
    wq.fourth()
    for ring in own_ff:
        ring.start()
    for n in range(3):
        y_copies[2 * n].wait_recv()
    for ring in other_ff:
        ring.start()

    for n in range(4):
        wait_arrival(rows.at[n // 2, n % 2], row_recv.at[n])
        value = rows[n // 2, n % 2].astype(F32)
        at = slice(n * 64, (n + 1) * 64)
        rows_out[at, :] = rows[n // 2, n % 2]
        normed_ref[at, :] = (value * norm_scale(value) * gain(gains_ref, 0)).astype(BF)
    latent = dot_nt(normed_ref[...], a_qkv)
    adapted = dot(latent.astype(BF), b_qkv_ref[...])
    wq.last()
    pair_send, pair_recv = take(2)

    def pair_copy(ref, n):
        return remote(ref, ref, pair_send.at[n], pair_recv.at[n], sibling)

    pair_copy(wq_all.at[core], 0).start()
    wo.start()
    pair_copy(wq_all.at[core], 0).wait_send()
    pair_copy(wq_all.at[1 - core], 0).wait_recv()

    cos_table, sine_table = cos_ref[...], sin_ref[...]

    def turn(head):
        return head * cos_table + pltpu.roll(head, HEAD // 2, 1) * sine_table

    def query(n, head):
        q_ref[:, n * HEAD : (n + 1) * HEAD] = (turn(head + bias(n)) * (HEAD ** (-0.5) * LOG2E)).astype(BF)

    pairs = dot(normed_ref[...], wq_all[1, :, 256:]) + adapted[:, 768:]
    for n, head in ((0, turn(pairs[:, :HEAD] + bias(6))), (1, pairs[:, HEAD:] + bias(7))):
        at = slice(n * HEAD, (n + 1) * HEAD)
        kv_part[0, :, at] = head[:CHUNK].astype(BF)
        kv_part[1, :, at] = head[CHUNK:].astype(BF)
    kv = Gather(
        lambda s: kv_part.at[s],
        lambda s, item: kv_all.at[low_chunk(item) if s == 0 else 63 - low_chunk(item)],
        *take(3),
    )
    kv.start()
    heads = dot(normed_ref[...], wq_all[1, :, :256]) + adapted[:, 512:768]
    for n in (4, 5):
        query(n, heads[:, (n - 4) * HEAD : (n - 3) * HEAD])
    kv.second()
    for ring in rings:
        ring.second()
    wo.second()
    heads = dot(normed_ref[...], wq_all[0]) + adapted[:, :512]
    for n in range(4):
        query(n, heads[:, n * HEAD : (n + 1) * HEAD])
    kv.third()
    for ring in rings:
        ring.third()
    wo.third()
    kv.fourth()
    wo.fourth()

    for half in (0, 1):
        wait_arrival(cot_in.at[half], row_recv.at[4 + half])
        start = ((1 - h) * lower + h * (63 - lower)) * CHUNK + half * 64
        at = lax.broadcasted_iota(jnp.int32, (64, D), 0) + start
        cot_own[half * 64 : (half + 1) * 64, :] = jnp.where(
            at < length, cot_in[half].astype(F32), 0.0
        ).astype(BF)
    cot_spread = Spread(cot_own, cot_all, *take(3))
    cot_spread.start()
    kv.last()
    for e in (0, 1, 3, 2):
        for ring in whole:
            ring.spread(e)
    (out_sem,) = take(1)
    copies = []

    def keep(*pairs):
        for src, dst in pairs:
            copies.append(pltpu.make_async_copy(src, dst, out_sem.at[len(copies)]))
            copies[-1].start()

    keep(
        (kv_all, kv_out), (wq_all, wq_out), (q_ref, q_out), (rows_out, rows_hbm), (normed_ref, normed_out),
        (cot_own, cot_out), (limit_ref, limit_out), (cos_ref, cos_out), (sin_ref, sin_out),
        (b_qkv_ref, b_qkv_out), (ao_ref, ao_out), (a_ref.at[pl.ds(0, 3)], a_out), (b_ref.at[1], bo_out),
    )
    wo.last()

    def wo_columns(c, n):
        return wo_all.at[:, pl.ds(pl.multiple_of((2 * n + c) * 384, 128), 384)]

    for n in (0, 1):
        pair_copy(wo_columns(core, n), 1 + n).start()
    for slot in (0, 1):
        turned_ref[slot] = head_columns(q_ref, slot)
    args = (turned_ref, kv_all, limit_ref, acc_ref, stat_ref)

    def end(slot):
        forward_end(slot, mixed_ref, lse_ref, acc_ref, stat_ref)

    blocks = KEYS // CHUNK
    middle = CHUNKS // 2 // blocks
    forward_blocks(0, 0, lower // blocks + 1, *args)
    forward_blocks(1, middle, (63 - lower) // blocks + 1, *args)
    end(0)
    for ring in whole:
        ring.fourth(0)
    cot_spread.second()
    forward_blocks(1, 0, middle // 2, *args)
    for ring in whole:
        ring.fourth(1)
    cot_spread.third()
    forward_blocks(1, middle // 2, middle, *args)
    end(1)
    for n in (0, 1):
        pair_copy(wo_columns(core, n), 1 + n).wait_send()
        pair_copy(wo_columns(1 - core, n), 1 + n).wait_recv()
    keep((wo_all, wo_out), (mixed_ref, mixed_out), (lse_ref, lse_out))

    def project(slot):
        mixed = mixed_ref[pl.ds(pl.multiple_of(slot * CHUNK, CHUNK), CHUNK), :]
        lifted = dot(dot_nt(mixed, ao_ref[...]).astype(BF), bo_ref[...])
        return dot(mixed, wo_all[...]) + lifted

    (cross_sem,) = take(1)
    cross_out[...] = project(1 - h).astype(BF)
    cross = remote(cross_out, cross_in, cross_sem.at[0], cross_sem.at[1], uly_others()[0])
    cross.start()
    for ring in whole:
        ring.fourth(3)
    mine = project(h) + rows_out[pl.ds(pl.multiple_of(h * CHUNK, CHUNK), CHUNK), :].astype(F32)
    for ring in whole:
        ring.fourth(2)
    cross.wait()
    residual = mine + cross_in[...].astype(F32)
    resid_ref[...] = residual
    keep((resid_ref, resid_out))
    nf_own[...] = (residual * norm_scale(residual) * gain(gains_ref, D_TILES)).astype(BF)
    keep((nf_own, nf_out))
    cot_spread.last()
    for ring in whole:
        ring.last()
    for ring in (own_ff[1], other_ff[1]):
        ring.end()
    for n in range(3):
        y_copies[2 * n].wait_send()
        y_copies[2 * n + 1].wait()
    deliver.end()
    for copy in copies:
        copy.wait()


def forward(*args):
    weight = HELD((32, 48, FF_COLS), BF)
    group = GROUP * HEAD
    dma = pltpu.SemaphoreType.DMA
    spread = HELD((2, 4, CHUNK, D), BF)
    return pl.pallas_call(
        forward_kernel,
        out_shape=(
            HELD((2 * CHUNK, group), BF),
            HELD((2 * CHUNK, group), BF),
            HELD((2, 8, ROWS), F32),
            HELD((CHUNKS, CHUNK, 2 * HEAD), BF),
            HELD((2, D, 512), BF),
            HELD((D // 2, D), BF),
            weight, weight, weight,
            HELD((2 * CHUNK, D), BF),
            HELD((2 * CHUNK, D), BF),
            HELD((CHUNK, D), F32),
            HELD((CHUNK, D), BF),
            HELD((CHUNK, D), BF),
            spread,
            HELD((2, 8, ROWS), jnp.int32),
            HELD((2 * CHUNK, HEAD), F32),
            HELD((2 * CHUNK, HEAD), F32),
            HELD((48, 1024), BF),
            HELD((16, group), BF),
            HELD((3, 16, D), BF),
            HELD((16, D), BF),
        ),
        in_specs=[ANY] * 13,
        out_specs=(ANY,) * 22,
        scratch_shapes=[
            pltpu.VMEM((2 * CHUNK, group), BF),
            pltpu.VMEM((2 * CHUNK, group), BF),
            pltpu.VMEM((2, 8, ROWS), F32),
            pltpu.VMEM((2 * CHUNK, D), BF),
            pltpu.VMEM((2 * CHUNK, D), BF),
            pltpu.VMEM((CHUNK, D), F32),
            pltpu.VMEM((CHUNK, D), BF),
            pltpu.VMEM((2, 8, ROWS), jnp.int32),
            pltpu.VMEM((2 * CHUNK, HEAD), F32),
            pltpu.VMEM((2 * CHUNK, HEAD), F32),
            pltpu.VMEM((48, 1024), BF),
            pltpu.VMEM((16, group), BF),
            pltpu.VMEM((4, 16, D), BF),
            pltpu.VMEM((2, 16, D), BF),
            pltpu.VMEM((2, 16, 2 * HEAD), BF),
            pltpu.VMEM((4, SETS, 16, D), BF),
            pltpu.VMEM((2, SETS, 16, D), BF),
            pltpu.VMEM((2, SETS, 16, 2 * HEAD), BF),
            pltpu.VMEM((2, HEAD, ROWS), BF),
            pltpu.SMEM((2,), jnp.int32),
            pltpu.SMEM((2,), jnp.int32),
            pltpu.VMEM((12, 2048), BF),
            pltpu.VMEM((12, D), BF),
            pltpu.VMEM((2, 48, FF // 4), BF),
            pltpu.VMEM((48, FF // 4), BF),
            pltpu.VMEM((40, 128), F32),
            pltpu.VMEM((1, 128), F32),
            pltpu.VMEM((CHUNKS, CHUNK, 2 * HEAD), BF),
            pltpu.VMEM((2, D, 512), BF),
            pltpu.VMEM((D // 2, D), BF),
            pltpu.VMEM((2, 2, 64, D), BF),
            pltpu.VMEM((2, 64, D), BF),
            pltpu.VMEM((2, CHUNK, 2 * HEAD), BF),
            pltpu.VMEM((2, HEAD, ROWS), F32),
            pltpu.VMEM((2, 2, 8, ROWS), F32),
            pltpu.VMEM((4, 16, 512), BF),
            pltpu.VMEM((4, 16, 384), BF),
            pltpu.VMEM((48, 512), BF),
            pltpu.VMEM((48, 384), BF),
            pltpu.VMEM((CHUNK, D), BF),
            pltpu.VMEM((CHUNK, D), BF),
            pltpu.VMEM((CHUNK, D), BF),
            pltpu.VMEM((4, 16, 512), BF),
            pltpu.VMEM((4, 16, 384), BF),
            pltpu.VMEM((3, 48, PADDED), BF),
            dma((8,)), dma((8,)), dma((6,)), dma((6,)),
            dma((2, 3, Ring.sends)), dma((2, 3, 16)), dma((3,)), dma((3,)), dma((3,)),
        ]
        + GATHER_SEMS()
        + GATHER_SEMS()
        + [dma((3,)), dma((3,))]
        + GATHER_SEMS()
        + SPREAD_SEMS
        + [dma((18,)), dma((2,)), dma((8,)), dma((3,))],
        compiler_params=pltpu.CompilerParams(
            collective_id=1, has_side_effects=True, vmem_limit_bytes=48 * 2**20
        ),
        name="forward",
    )(*args)


class RingSum:
    @staticmethod
    def scratch():
        piece, half = (CHUNK, D), (CHUNK // 2, D)
        return [
            pltpu.VMEM((2,) + half, BF),
            pltpu.VMEM((2,) + piece, BF),
            pltpu.VMEM(piece, BF),
            pltpu.VMEM((2,) + piece, BF),
            pltpu.SemaphoreType.DMA((4,)),
            pltpu.SemaphoreType.DMA((4,)),
        ]

    scratches = 6

    def __init__(self, term, scratch):
        self.term = term
        self.halves, self.last_in, self.far, self.near, self.send_sem, self.recv_sem = scratch
        self.w = ring_at()
        self.sent = []

    def send(self, src, dst, recv, d):
        copy = remote(
            src, dst, self.send_sem.at[recv], self.recv_sem.at[recv], ring_place((self.w + d) % 4)
        )
        copy.start()
        self.sent.append(copy)

    def first(self):
        half = CHUNK // 2
        self.far[...] = self.term(2).astype(BF)
        self.send(self.far.at[pl.ds(0, half)], self.halves.at[0], 0, 1)
        self.send(self.far.at[pl.ds(half, half)], self.halves.at[1], 1, 3)

    def second(self):
        half = CHUNK // 2
        for k, d in ((0, 1), (1, 3)):
            total = self.term(d)
            wait_arrival(self.halves.at[k], self.recv_sem.at[k])
            rows = slice(k * half, (k + 1) * half)
            other = slice((1 - k) * half, (2 - k) * half)
            self.near[k, rows] = (total[rows] + self.halves[k].astype(F32)).astype(BF)
            self.near[k, other] = total[other].astype(BF)
            self.send(self.near.at[k], self.last_in.at[k], 2 + k, d)

    def third(self):
        total = self.term(0)
        for k in (0, 1):
            wait_arrival(self.last_in.at[k], self.recv_sem.at[2 + k])
            total += self.last_in[k].astype(F32)
        for copy in self.sent:
            copy.wait_send()
        return total


def ff_kernel(
    set_ref, own_hbm, cot_hbm, gate_hbm, up_hbm, down_hbm, a_wide, a_down, b_wide, b_ff,
    grad_out, down_out, cols_out, wide_out,
    cols_ref, wide_ref, x_ref, cot_ref, gate_w, up_w, down_w, b_cols, a_cols, hidden_ref, grad_gate, grad_up,
    grad_hidden, own_ref, terms, pair, total_ref, down_sum, a_ff, b_out, wide_sets, down_sets, out_sets,
    ff_sets, sems, out_sems, pair_send, pair_recv, *scratch,
):
    y, z, x, blk, uly = place()
    core = uly % 2
    scratch = list(scratch)

    def take(count):
        got = scratch[:count]
        del scratch[:count]
        return got

    first = (35 * uly) // 2 * 128 + y * FF_COLS
    columns = pl.ds(pl.multiple_of(first, 128), FF_COLS)
    pairs = (
        (own_hbm, own_ref), (down_hbm, down_w), (cot_hbm, cot_ref), (gate_hbm, gate_w),
        (a_wide.at[pl.ds(4, 2)], wide_sets), (a_down.at[:, :, columns], down_sets), (b_wide.at[2], out_sets),
        (b_ff.at[:, :, :, columns], ff_sets),
    )
    copies = [pltpu.make_async_copy(src, dst, sems.at[n]) for n, (src, dst) in enumerate(pairs)]
    for copy in copies[:1] + copies[4:] + copies[1:4]:
        copy.start()
    other_blk = blk_of(1 - y, z, x)
    up_send, up_recv, up_sem = take(3)
    rings = [
        Ring(
            up_w.at[b], lambda item: up_w.at[item], yy, yy, 1 + 2 * k, up_send.at[k], up_recv.at[k]
        )
        for k, (yy, b) in enumerate(((y, blk), (1 - y, other_blk)))
    ]
    lines = []
    for k, ring in enumerate(rings):
        for d in range(4):
            item = ring.at(ring.y, (ring.p + d) % 4, ring.q)
            lines.append(pltpu.make_async_copy(up_hbm.at[item], up_w.at[item], up_sem.at[k, d]))
            lines[-1].start()
    at = lax.broadcasted_iota(jnp.int32, (16, FF_COLS), 1) + (y * FF_COLS - 64 * core)
    inside = jnp.logical_and(at >= 0, at < FF // 4)

    def keep(v):
        return jnp.where(inside, v.astype(F32), 0.0).astype(BF)

    def prepare():
        for copy in copies[4:]:
            copy.wait()
        for s in (0, 1):
            number = set_ref[s]
            a_cols[s] = keep(choose(number, lambda c: down_sets[c]))
            b_out[s] = choose(number, lambda c: out_sets[c])
            for n in (0, 1):
                b_cols[s, n] = keep(choose(number, lambda c: ff_sets[n, c]))
                a_ff[s, 16 * n : 16 * n + 16] = choose(number, lambda c: wide_sets[n, c])
        cols_ref[...] = jnp.zeros_like(cols_ref)

    sibling = uly_others()[1]
    greet([sibling, (other_blk, (uly + 2) % 4)] + ring_others(), prepare)
    here = pl.ds(pl.multiple_of(y * FF_COLS, 128), FF_COLS)
    copies[0].wait()
    spread = Spread(own_ref, x_ref, *take(3))
    spread.start()
    for copy in lines:
        copy.wait()
    for e in (0, 1, 3, 2):
        for ring in rings:
            ring.spread(e)

    def flat(ref, s):
        return ref[s].reshape(4 * CHUNK, D)

    order = (1 - core, core)
    copies[1].wait()
    copies[2].wait()
    latent_cots = []
    for k, s in enumerate(order):
        cot = flat(cot_ref, s)
        latent_cots.append(dot_nt(cot, b_out[s]))
        grad_hidden[k] = dot(cot, down_w[...]) + dot(latent_cots[k].astype(BF), a_cols[s])
        (spread.second, spread.third)[k]()
        for ring in rings:
            ring.fourth(k)
    copies[3].wait()
    for e in (3, 2):
        for ring in rings:
            ring.fourth(e)
    spread.last()

    def pair_copy(n, d):
        at = (ring_at() + d) % 4
        return remote(
            terms.at[n, 0, at], pair.at[n, at], pair_send.at[n, d], pair_recv.at[n, d], sibling
        )

    def term(n, d):
        at = (ring_at() + d) % 4
        wait_arrival(pair.at[n, at], pair_recv.at[n, d])
        return terms[n, 1, at].astype(F32) + pair[n, at].astype(F32)

    ring = RingSum(lambda d: term(0, d), take(RingSum.scratches))

    def up_weight():
        return up_w[...].reshape(D, FF_COLS)

    latents = []
    for k, s in enumerate(order):
        rows = flat(x_ref, s)
        latent = dot_nt(rows, a_ff[s])
        low = latent.astype(BF)
        gate = dot(rows, gate_w[...]) + dot(low[:, :16], b_cols[s, 0])
        sigmoid = jax.nn.sigmoid(gate)
        silu = gate * sigmoid
        grad_up[k] = (grad_hidden[k] * silu).astype(BF)
        slope = grad_hidden[k] * (sigmoid * (1.0 + gate * (1.0 - sigmoid)))
        if k == 0:
            for up_ring in rings:
                up_ring.last()
        up = dot(rows, up_weight()) + dot(low[:, 16:], b_cols[s, 1])
        grad_gate[k] = (slope * up).astype(BF)
        hidden_ref[k] = (silu * up).astype(BF)
        back_gate = dot_nt(grad_gate[k], b_cols[s, 0])
        back_up = dot_nt(grad_up[k], b_cols[s, 1])
        grads = (
            dot_nt(grad_gate[k], gate_w[...])
            + dot_nt(grad_up[k], up_weight())
            + dot(back_gate.astype(BF), a_ff[s, :16])
            + dot(back_up.astype(BF), a_ff[s, 16:])
        )
        terms[0, k] = grads.astype(BF).reshape(4, CHUNK, D)
        if k == 0:
            for d in (2, 1, 3, 0):
                pair_copy(0, d).start()
        else:
            ring.first()
        latents.append((latent, back_gate, back_up))

    def put(ref, n, s, value, at=slice(None)):
        ref[pl.ds(pl.multiple_of((2 * n + s) * 16, 16), 16), at] = value.astype(BF)

    def turned(value):
        return value.T.astype(BF)

    for k, s in enumerate(order):
        latent_down = dot_nt(hidden_ref[k], a_cols[s])
        down = dot_nt(hidden_ref[k], down_w[...]) + dot(latent_down.astype(BF), b_out[s])
        terms[1, k] = down.astype(BF).reshape(4, CHUNK, D)
        if k == 0:
            for d in (2, 1, 3, 0):
                pair_copy(1, d).start()
        else:
            ring.second()
        put(wide_ref, 2, s, dot(turned(latent_down), flat(cot_ref, s)))
    for k, s in enumerate(order):
        latent, back_gate, back_up = latents[k]
        rows = flat(x_ref, s)
        put(cols_ref, 0, s, dot(turned(latent_cots[k]), hidden_ref[k]), here)
        put(cols_ref, 1, s, dot(turned(latent[:, :16]), grad_gate[k]), here)
        put(cols_ref, 2, s, dot(turned(latent[:, 16:]), grad_up[k]), here)
        put(wide_ref, 0, s, dot(turned(back_gate), rows))
        put(wide_ref, 1, s, dot(turned(back_up), rows))
    outs = [
        pltpu.make_async_copy(src, dst, out_sems.at[n])
        for n, (src, dst) in enumerate(
            ((cols_ref, cols_out), (wide_ref, wide_out), (down_sum, down_out), (total_ref, grad_out))
        )
    ]
    outs[0].start()
    outs[1].start()
    for d in range(4):
        down_sum[(ring_at() + d) % 4] = term(1, d).astype(BF)
    outs[2].start()
    total_ref[...] = ring.third()
    outs[3].start()
    for n in (0, 1):
        for d in range(4):
            pair_copy(n, d).wait_send()
    for copy in outs:
        copy.wait()


def feed_forward(*args):
    dma = pltpu.SemaphoreType.DMA
    weight = pltpu.VMEM((D, FF_COLS), BF)
    rows = pltpu.VMEM((2, 4 * CHUNK, FF_COLS), BF)
    pieces = (4, CHUNK, D)
    return pl.pallas_call(
        ff_kernel,
        out_shape=(
            HELD((CHUNK, D), F32),
            HELD(pieces, BF),
            HELD((96, PADDED), BF),
            HELD((96, D), BF),
        ),
        in_specs=[pl.BlockSpec(memory_space=pltpu.SMEM)] + [ANY] * 9,
        out_specs=(ANY,) * 4,
        scratch_shapes=[
            pltpu.VMEM((96, PADDED), BF), pltpu.VMEM((96, D), BF),
            pltpu.VMEM((2,) + pieces, BF), pltpu.VMEM((2,) + pieces, BF),
            weight, pltpu.VMEM((32, 48, FF_COLS), BF), weight,
            pltpu.VMEM((2, 2, 16, FF_COLS), BF), pltpu.VMEM((2, 16, FF_COLS), BF),
            rows, rows, rows,
            pltpu.VMEM((2, 4 * CHUNK, FF_COLS), F32),
            pltpu.VMEM((CHUNK, D), BF),
            pltpu.VMEM((2, 2) + pieces, BF), pltpu.VMEM((2,) + pieces, BF),
            pltpu.VMEM((CHUNK, D), F32), pltpu.VMEM(pieces, BF),
            pltpu.VMEM((2, 32, D), BF), pltpu.VMEM((2, 16, D), BF),
            pltpu.VMEM((2, SETS, 16, D), BF), pltpu.VMEM((SETS, 16, FF_COLS), BF),
            pltpu.VMEM((SETS, 16, D), BF), pltpu.VMEM((2, SETS, 16, FF_COLS), BF),
            dma((8,)), dma((4,)), dma((2, 4)), dma((2, 4)),
            dma((2, Ring.sends)), dma((2, 16)), dma((2, 4)),
        ]
        + SPREAD_SEMS
        + RingSum.scratch(),
        compiler_params=pltpu.CompilerParams(
            collective_id=4, has_side_effects=True, vmem_limit_bytes=62 * 2**20
        ),
        name="feed_forward",
    )(*args)


def backward_blocks(slot, first, last, turned_ref, rows_ref, dot_ref, kv_ref, limit_ref, lse_ref, dkv_ref, acc_ref):
    limit = limit_ref[slot, 0:1, :]
    lse = lse_ref[slot, 0:1, :]
    row_dot = dot_ref[slot, 0:1, :]

    def step(n, carry):
        keys, values = key_block(kv_ref, n, KEYS_BACK)
        scores = jnp.where(key_places(n, KEYS_BACK) <= limit, dot(keys, turned_ref[0, slot]), -1e30)
        probs = jnp.exp2(scores - lse)
        grad_probs = dot(values, turned_ref[1, slot])
        grad_scores = (probs * (grad_probs - row_dot)).astype(BF)
        acc_ref[slot] += dot(keys.T, grad_scores)
        at = pl.ds(pl.multiple_of(n * KEYS_BACK, KEYS_BACK), KEYS_BACK)
        dkv_ref[at, :HEAD] += dot(grad_scores, rows_ref[0, slot])
        dkv_ref[at, HEAD:] += dot(probs.astype(BF), rows_ref[1, slot])
        return carry

    lax.fori_loop(first, last, step, 0)


class Reduce:
    @staticmethod
    def scratch(shape):
        return [
            pltpu.VMEM((2, 3, 2, 4) + shape, BF),
            pltpu.VMEM((2, 3, 2) + shape, BF),
            pltpu.VMEM((2, 4, 2) + shape, BF),
            pltpu.SemaphoreType.DMA((2, 9)),
            pltpu.SemaphoreType.DMA((2, 9)),
        ]

    scratches = 5

    def __init__(self, part, scratch):
        self.part = part
        self.buf_q, self.buf_p, self.sum_p, self.send_sem, self.recv_sem = scratch
        self.y, self.z, self.x, self.blk, self.uly = place()
        self.pq = ((self.x, self.z), (self.z, self.x))
        self.flying = []

    def send(self, src, dst, half, n, y, p, q):
        target = blk_of(y, q, p) if half == 0 else blk_of(y, p, q)
        copy = remote(
            src, dst, self.send_sem.at[half, n], self.recv_sem.at[half, n], (target, self.uly)
        )
        copy.start()
        self.flying.append(copy)

    def land(self):
        for copy in self.flying:
            copy.wait()
        self.flying = []

    def first(self):
        for d in (2, 1, 3):
            for half in (0, 1):
                p, q = self.pq[half]
                to = (q + d) % 4
                for y in (0, 1):
                    src = self.part.at[0, y, to] if half == 0 else self.part.at[1, y, :, to]
                    self.send(
                        src, self.buf_q.at[half, d - 1, y], half, (d - 1) * 2 + y, self.y, p, to
                    )

    def second(self):
        self.land()
        for d in (2, 1, 3, 0):
            for half in (0, 1):
                p, q = self.pq[half]
                to = (p + d) % 4
                for y in (0, 1):
                    own = self.part[0, y, q, to] if half == 0 else self.part[1, y, to, q]
                    total = own.astype(F32)
                    for n in range(3):
                        total += self.buf_q[half, n, y, to].astype(F32)
                    self.sum_p[half, d, y] = total.astype(BF)
                if d > 0:
                    self.send(
                        self.sum_p.at[half, d], self.buf_p.at[half, d - 1], half, 5 + d, self.y, to, q
                    )

    def third(self):
        self.land()
        return [
            [
                self.sum_p[half, 0, y].astype(F32)
                + sum(self.buf_p[half, n, y].astype(F32) for n in range(3))
                for y in (0, 1)
            ]
            for half in (0, 1)
        ]


class Shed:
    @staticmethod
    def scratch(shape):
        return [
            pltpu.VMEM((2, 4) + shape, BF),
            pltpu.VMEM((2, 4) + shape, BF),
            pltpu.VMEM((2, 2, 4) + shape, BF),
            pltpu.VMEM((4, 2) + shape, BF),
            pltpu.VMEM((3, 2) + shape, BF),
            pltpu.VMEM((2,) + shape, BF),
            pltpu.VMEM(shape, BF),
            pltpu.SemaphoreType.DMA((10,)),
            pltpu.SemaphoreType.DMA((10,)),
        ]

    scratches = 9

    def __init__(self, part, half, rows, order, scratch):
        self.part, self.half, self.rows, self.order = part, half, rows, order
        (
            self.buf_far, self.sum_mid, self.buf_in, self.sum_p, self.buf_p, self.sum_y, self.buf_y,
            self.send_sem, self.recv_sem,
        ) = scratch
        self.y, self.z, self.x, self.blk, self.uly = place()
        self.p, self.q = (self.x, self.z) if order == 0 else (self.z, self.x)
        self.flying = []

    def line(self, y, q):
        rows = pl.ds(*self.rows)
        if self.order == 0:
            return self.part.at[self.half, y, q, :, rows]
        return self.part.at[self.half, y, :, q, rows]

    def value(self, y, q, p):
        start, size = self.rows
        z, x = (q, p) if self.order == 0 else (p, q)
        return self.part[self.half, y, z, x, start : start + size].astype(F32)

    def send(self, src, dst, n, y, p, q):
        target = blk_of(y, q, p) if self.order == 0 else blk_of(y, p, q)
        copy = remote(src, dst, self.send_sem.at[n], self.recv_sem.at[n], (target, self.uly))
        copy.start()
        self.flying.append(copy)

    def land(self):
        for copy in self.flying:
            copy.wait()
        self.flying = []

    def first(self):
        for y, d in ((0, 1), (1, 3)):
            to = (self.q + d) % 4
            self.send(self.line(y, (self.q + 2) % 4), self.buf_far.at[y], y, self.y, self.p, to)
        for y, d in ((1, 1), (0, 3)):
            to = (self.q + d) % 4
            self.send(self.line(y, to), self.buf_in.at[d // 2, y], 2 + d // 2, self.y, self.p, to)

    def second(self):
        direct = self.flying[2:]
        self.flying = self.flying[:2]
        self.land()
        for y, d in ((0, 1), (1, 3)):
            to = (self.q + d) % 4
            for p in range(4):
                total = self.value(y, to, p) + self.buf_far[y, p].astype(F32)
                self.sum_mid[y, p] = total.astype(BF)
            self.send(self.sum_mid.at[y], self.buf_in.at[d // 2, y], 4 + y, self.y, self.p, to)
        self.flying += direct

    def third(self):
        self.land()
        for d in (2, 1, 3, 0):
            to = (self.p + d) % 4
            for y in (0, 1):
                total = self.value(y, self.q, to)
                for n in (0, 1):
                    total += self.buf_in[n, y, to].astype(F32)
                self.sum_p[d, y] = total.astype(BF)
            if d > 0:
                self.send(self.sum_p.at[d], self.buf_p.at[d - 1], 5 + d, self.y, to, self.q)

    def fourth(self):
        self.land()
        for k in (1, 0):
            y = self.y if k == 0 else 1 - self.y
            total = self.sum_p[0, y].astype(F32)
            for n in range(3):
                total += self.buf_p[n, y].astype(F32)
            self.sum_y[k] = total.astype(BF)
            if k == 1:
                self.send(self.sum_y.at[1], self.buf_y, 9, 1 - self.y, self.p, self.q)

    def last(self):
        self.land()
        return self.sum_y[0].astype(F32) + self.buf_y[...].astype(F32)


def reduce_others():
    y, z, x, blk, uly = place()
    return (
        [(blk_of(1 - y, z, x), uly)]
        + [(blk_of(y, z, (x + d) % 4), uly) for d in (1, 2, 3)]
        + [(blk_of(y, (z + d) % 4, x), uly) for d in (1, 2, 3)]
    )


UNIT = (16, 128)


class Total:
    @staticmethod
    def scratch(kept, summed):
        shape = (kept + summed,) + UNIT
        return (
            [pltpu.VMEM((2, 2, 4, 4) + shape, BF)]
            + Reduce.scratch(shape)
            + [
                pltpu.VMEM((2, 2) + shape, BF),
                pltpu.VMEM((4, 2, 2) + shape, BF),
                pltpu.VMEM((2, 4 * kept + summed) + UNIT, BF),
                pltpu.SemaphoreType.DMA((7,)),
                pltpu.SemaphoreType.DMA((8,)),
                pltpu.SemaphoreType.DMA((15,)),
                pltpu.SemaphoreType.DMA((15,)),
                pltpu.SemaphoreType.DMA,
                pltpu.SemaphoreType.DMA,
                pltpu.SemaphoreType.DMA,
            ]
        )

    scratches = 16

    @staticmethod
    def shape(kept, summed):
        return HELD((2, 2, 4, 4, 4 * kept + summed) + UNIT, BF)

    def __init__(self, kept, summed, all_ref, scratch):
        self.kept, self.summed, self.all_ref = kept, summed, all_ref
        self.part = scratch[0]
        self.reduce = Reduce(self.part, scratch[1:6])
        self.own, self.buf, self.full, self.send_sem, self.recv_sem = scratch[6:11]
        self.all_send, self.all_recv, self.local_sem, self.pair_send, self.pair_recv = scratch[11:16]
        self.y, self.z, self.x, self.blk, self.uly = place()
        self.core = self.uly % 2
        self.w = ring_at()
        self.flying = []

    def pack(self, values, first, per, at):
        for n, value in enumerate(values, first):
            item = n // per
            self.part[item // 32, item // 16 % 2, item // 4 % 4, item % 4, at + n % per] = value.astype(BF)

    def pack_kept(self, values, first=0):
        self.pack(values, first, self.kept, 0)

    def pack_summed(self, values, first=0):
        self.pack(values, first, self.summed, self.kept)

    def clear(self, kept, summed):
        nothing = jnp.zeros(UNIT, BF)
        self.pack_kept([nothing] * (64 * self.kept - kept), kept)
        self.pack_summed([nothing] * (64 * self.summed - summed), summed)

    def others(self):
        return [
            ((self.w + d) % 4, self.core if c == 0 else 1 - self.core)
            for d in range(4) for c in (0, 1) if (d, c) != (0, 0)
        ]

    def across(self):
        for half, totals in enumerate(self.reduce.third()):
            for y, total in enumerate(totals):
                self.own[half, y] = total.astype(BF)
        self.copies = []
        for n, (w, core) in enumerate(self.others()):
            copy = remote(
                self.own.at[core], self.buf.at[self.w, self.core],
                self.send_sem.at[n], self.recv_sem.at[self.w * 2 + self.core],
                (blk_of(w % 2, self.z, self.x), w // 2 * 2 + core),
            )
            copy.start()
            self.copies.append(copy)
        self.buf[self.w, self.core] = self.own[self.core]

    def send(self, src, dst, n, d, e):
        z, x = self.at(d, e)
        copy = remote(
            src, dst, self.all_send.at[n], self.all_recv.at[n], (blk_of(self.y, z, x), self.uly)
        )
        copy.start()
        self.flying.append(copy)

    def at(self, d, e):
        dz, dx = self.core * d + (1 - self.core) * e, self.core * e + (1 - self.core) * d
        return (self.z + dz) % 4, (self.x + dx) % 4

    def items(self, d=0, e=0):
        z, x = self.at(d, e)
        return self.all_ref.at[self.core, :, z, x]

    def join(self):
        for w, core in self.others():
            wait_arrival(self.buf.at[w, core], self.recv_sem.at[w * 2 + core])
        kept = self.kept

        def term(w, core, y):
            return self.buf[w, core, y].astype(F32)

        for y in (0, 1):
            for uly in range(4):
                w, core = uly // 2 * 2, uly % 2
                value = term(w, core, y)[:kept] + term(w + 1, core, y)[:kept]
                self.full[y, uly * kept : (uly + 1) * kept] = value.astype(BF)
            if self.summed:
                self.full[y, 4 * kept :] = sum(
                    term(w, core, y)[kept:] for w in range(4) for core in (0, 1)
                ).astype(BF)
        for d in (1, 2, 3):
            self.send(self.full, self.items(), d - 1, d, 0)
        self.local = pltpu.make_async_copy(self.full, self.items(), self.local_sem)
        self.local.start()

    def spread(self):
        self.local.wait()
        for d in range(4):
            ref = self.items((4 - d) % 4)
            if d > 0:
                wait_arrival(ref, self.all_recv.at[d - 1])
            for e in (1, 2, 3):
                self.send(ref, ref, 2 + d * 3 + e, 0, e)

    def hand(self):
        for d in range(4):
            for e in (1, 2, 3):
                wait_arrival(self.items((4 - d) % 4, 4 - e), self.all_recv.at[2 + d * 3 + e])
        self.pair(self.core).start()

    def pair(self, core):
        return remote(
            self.all_ref.at[core], self.all_ref.at[core], self.pair_send, self.pair_recv, uly_others()[1]
        )

    def end(self):
        for copy in self.copies + self.flying:
            copy.wait_send()
        self.pair(self.core).wait_send()
        wait_arrival(self.all_ref.at[1 - self.core], self.pair_recv)

    def steps(self):
        return [
            self.reduce.first, self.reduce.second, self.across, self.join, self.spread, self.hand, self.end,
        ]


def units(value):
    rows, columns = value.shape
    return [
        value[n * 16 : (n + 1) * 16, t * 128 : (t + 1) * 128]
        for n in range(rows // 16) for t in range(columns // 128)
    ]


FF_KEPT, FF_SUMMED, QKV_KEPT = 2, 2, 1
COL_TILES = PADDED // 128
D_TILES = D // 128
DKV_ROWS = CHUNK // 2
DKV_STREAMS = 2


def backward_kernel(
    gains_hbm, total_hbm, down_hbm, cols_hbm, ff_hbm, resid_hbm, cot_hbm, ao_hbm, mixed_hbm, wo_hbm, kv_hbm, q_hbm, limit_hbm, lse_hbm,
    wq_hbm, rows_hbm, normed_hbm, b_qkv_hbm, cos_hbm, sin_hbm, a_hbm, bo_hbm,
    result_ref, input_grad_ref, ff_all, qkv_all,
    gains_ref, total_ref, down_ref, cols_ref, ff_ref, resid_ref, cot_ref, ao_ref, mixed_ref, wo_ref, kv_ref, q_ref, limit_ref,
    lse_ref, wq_ref, rows_ref, normed_ref, b_qkv_ref, cos_ref, sin_ref, a_ref, bo_ref, dkv_ref, acc_ref, part, dq_ref, grad_ref, grad_attn, grad_resid, grad_qkv,
    cross_out, cross_in, home_out, home_in, turned_ref, by_rows_ref, dot_ref, back, copy_sem, cross_sem, home_send,
    home_recv, *scratch,
):
    y, z, x, blk, uly = place()
    core, h = uly % 2, uly // 2
    scratch = list(scratch)

    def take(count):
        got = scratch[:count]
        del scratch[:count]
        return got

    chunk = 2 * blk + h
    upper = chunk // 32
    home = (1 - h) * blk + h * (31 - blk)
    home_from = [(home, upper * 2 + s) for s in (0, 1)]
    lower = low_chunk(blk)
    own_chunk = (1 - h) * lower + h * (63 - lower)
    home_to = [(own_chunk // 2, (own_chunk % 2) * 2 + half) for half in (0, 1)]
    copies = [
        pltpu.make_async_copy(src, dst, copy_sem.at[n])
        for n, (src, dst) in enumerate(
            (
                (total_hbm, total_ref), (resid_hbm, resid_ref), (cot_hbm, cot_ref), (gains_hbm, gains_ref),
                (cols_hbm, cols_ref), (ff_hbm, ff_ref), (down_hbm, down_ref), (ao_hbm, ao_ref), (mixed_hbm, mixed_ref),
                (wo_hbm, wo_ref), (bo_hbm, bo_ref), (kv_hbm, kv_ref),
                (q_hbm, q_ref), (limit_hbm, limit_ref), (lse_hbm, lse_ref), (wq_hbm, wq_ref),
                (rows_hbm, rows_ref), (normed_hbm, normed_ref), (b_qkv_hbm, b_qkv_ref),
                (cos_hbm, cos_ref), (sin_hbm, sin_ref), (a_hbm, a_ref),
            )
        )
    ]
    for copy in copies:
        copy.start()
    greet(
        reduce_others()
        + uly_others()
        + [(blk_of(1 - y, z, x), other[1]) for other in uly_others()]
        + home_from
        + home_to
    )
    collect_out = RingSum(
        lambda d: down_ref[(ring_at() + d) % 4].astype(F32), take(RingSum.scratches)
    )
    low, high = (
        [
            Shed(part, half, (n * DKV_ROWS, DKV_ROWS), n, take(Shed.scratches))
            for n in range(DKV_STREAMS)
        ]
        for half in (0, 1)
    )
    ff_total = Total(FF_KEPT, FF_SUMMED, ff_all, take(Total.scratches))
    qkv_total = Total(QKV_KEPT, 0, qkv_all, take(Total.scratches))
    deliver = Deliver()

    def send_home(n, value):
        home_out[n] = value.astype(BF)
        for half in (0, 1):
            deliver.send(
                home_out.at[n, pl.ds(half * 64, 64)], home_in.at[n, core],
                home_send.at[n, half], home_recv.at[n, core], home_to[half],
            )

    def arrived_home(n):
        for s in (0, 1):
            wait_arrival(home_in.at[n, s], home_recv.at[n, s])
        return home_in[n].astype(F32)

    def ready(first, last):
        for copy in copies[first:last]:
            copy.wait()

    ready(0, 4)
    residual = resid_ref[...]
    value = cot_ref[...].astype(F32) + norm_back(
        residual, norm_scale(residual), gain(gains_ref, D_TILES), total_ref[...]
    )
    grad_resid[...] = value
    own_rows = pl.ds(pl.multiple_of(h * CHUNK, CHUNK), CHUNK)
    other_rows = pl.ds(pl.multiple_of((1 - h) * CHUNK, CHUNK), CHUNK)
    grad_attn[own_rows, :] = value.astype(BF)
    partner = uly_others()[0]
    cross = remote(
        grad_attn.at[own_rows], grad_attn.at[own_rows], cross_sem.at[0], cross_sem.at[1], partner
    )
    cross.start()
    ready(4, 11)
    ff_total.pack_kept(units(cols_ref))
    ff_total.pack_summed(units(ff_ref))
    ff_total.clear(6 * COL_TILES, 6 * D_TILES)
    steps = ff_total.steps()

    def beside(*more):
        for step in more:
            step()
        if steps:
            steps.pop(0)()

    beside()
    at_o = 3 * D_TILES + D_TILES // 2 + 2
    qkv_total.clear(at_o + D_TILES // 2 + D_TILES, 0)
    dkv_ref[...] = jnp.zeros_like(dkv_ref)
    acc_ref[...] = jnp.zeros_like(acc_ref)
    latent_o = dot_nt(ao_ref[...], mixed_ref[...]).astype(BF)
    cross.wait_send()
    wait_arrival(grad_attn.at[other_rows], cross_sem.at[1])
    back_o = dot_nt(grad_attn[...], bo_ref[...]).astype(BF)
    grad_ref[...] = (dot_nt(grad_attn[...], wo_ref[...]) + dot(back_o, ao_ref[...])).astype(BF)
    back_o = dot_nt(bo_ref[...], grad_attn[...]).astype(BF)
    qkv_total.pack_kept(
        units(dot(back_o, mixed_ref[...])) + units(dot(latent_o, grad_attn[...])), at_o
    )
    beside()

    ready(11, 15)
    def pack(half):
        def one(n, carry):
            chunk = low_chunk(n) if half == 0 else 63 - low_chunk(n)
            rows = dkv_ref[pl.ds(pl.multiple_of(chunk * CHUNK, CHUNK), CHUNK), :]
            both = jnp.concatenate([rows[:, :HEAD] * LN2, rows[:, HEAD:]], axis=1)
            part[half, n // 16, n // 4 % 4, n % 4] = both.astype(BF)
            return carry

        lax.fori_loop(0, 32, one, 0)

    def shed(streams, name):
        def run():
            for stream in streams:
                getattr(stream, name)()

        return run

    args = (turned_ref, by_rows_ref, dot_ref, kv_ref, limit_ref, lse_ref, dkv_ref, acc_ref)
    step = KEYS_BACK // CHUNK
    middle = CHUNKS // 2 // step
    beside()
    for slot in (0, 1):
        for n, ref in enumerate((q_ref, grad_ref)):
            turned_ref[n, slot] = head_columns(ref, slot)
            by_rows_ref[n, slot] = head_rows(ref, slot)
        row_dot = turned_ref[1, slot].astype(F32) * head_columns(mixed_ref, slot).astype(F32)
        dot_ref[slot] = jnp.broadcast_to(jnp.sum(row_dot, axis=0, keepdims=True), (8, ROWS))
    backward_blocks(1, middle, (63 - lower) // step + 1, *args)
    backward_blocks(0, 0, lower // step + 1, *args)
    pack(1)
    beside(shed(high, "first"))
    names = ["second", "third", "fourth"]
    extra = [collect_out.first, collect_out.second]
    for n in range(0, middle, 2):
        backward_blocks(1, n, n + 2, *args)
        more = [shed(high, names.pop(0))] if names else []
        more += [extra.pop(0)] if extra else []
        for one in more:
            one()
        if n == 2:
            beside()
    pack(0)
    for stream in low:
        stream.first()
    for slot in (0, 1):
        for n in range(GROUP):
            dq_ref[slot * CHUNK : (slot + 1) * CHUNK, n * HEAD : (n + 1) * HEAD] = (
                acc_ref[slot, :, n * CHUNK : (n + 1) * CHUNK].T * HEAD ** (-0.5)
            )
    ready(15, 22)
    a_qkv = a_ref[...].reshape(48, D)
    for stream in low:
        stream.second()
    cos_table, sine_table = cos_ref[...], sin_ref[...]

    def turn_back(value, rows=slice(None)):
        return value * cos_table[rows] - pltpu.roll(value, HEAD // 2, 1) * sine_table[rows]

    for n in range(GROUP):
        at = slice(n * HEAD, (n + 1) * HEAD)
        grad_qkv[:, at] = turn_back(dq_ref[:, at]).astype(BF)
    group = GROUP * HEAD

    def key_value(half, streams):
        for n, stream in enumerate(streams):
            rows = slice(half * CHUNK + n * DKV_ROWS, half * CHUNK + (n + 1) * DKV_ROWS)
            value = stream.last()
            grad_qkv[rows, group : group + HEAD] = turn_back(value[:, :HEAD], rows).astype(BF)
            grad_qkv[rows, group + HEAD :] = value[:, HEAD:].astype(BF)

    latent_qkv = dot_nt(a_qkv, normed_ref[...]).astype(BF)

    def project_back(slot):
        rows = slice(slot * CHUNK, (slot + 1) * CHUNK)
        grads = grad_qkv[rows, :]
        lifted = dot(dot_nt(grads, b_qkv_ref[...]).astype(BF), a_qkv)
        back[slot] = dot_nt(grads[:, :512], wq_ref[0]) + dot_nt(grads[:, 512:], wq_ref[1]) + lifted
        latent_grad = dot_nt(b_qkv_ref[...], grads).astype(BF)
        return dot(latent_grad, normed_ref[rows, :]), dot(latent_qkv[:, rows], grads)

    key_value(1, high)
    for stream in low:
        stream.third()
    send_home(0, resid_ref[...] + collect_out.third())
    grad_a, grad_b = project_back(1)
    for stream in low:
        stream.fourth()
    key_value(0, low)
    more_a, more_b = project_back(0)
    cross_out[...] = back[1 - h].astype(BF)
    cross = remote(cross_out, cross_in, cross_sem.at[2], cross_sem.at[3], partner)
    cross.start()
    grad_a, grad_b = grad_a + more_a, grad_b + more_b
    qkv_total.pack_kept(
        units(grad_a)
        + units(grad_b[:16, :group])
        + units(grad_b[16:32, group : group + HEAD])
        + units(grad_b[32:, group + HEAD :])
    )
    last_steps = qkv_total.steps()
    last_steps.pop(0)()
    last_steps.pop(0)()
    beside()
    cross.wait()
    mine = back[h] + cross_in[...].astype(F32)
    tokens = rows_ref[own_rows, :].astype(F32)
    send_home(1, grad_resid[...] + norm_back(tokens, norm_scale(tokens), gain(gains_ref, 0), mine))
    for step in last_steps + steps:
        step()
    result_ref[...] = arrived_home(0).astype(BF)
    input_grad_ref[...] = arrived_home(1).astype(BF)
    deliver.end()


def backward(*args):
    dma = pltpu.SemaphoreType.DMA
    group = GROUP * HEAD
    return pl.pallas_call(
        backward_kernel,
        out_shape=(
            jax.ShapeDtypeStruct((2, CHUNK // 2, D), BF),
            jax.ShapeDtypeStruct((2, CHUNK // 2, D), BF),
            Total.shape(FF_KEPT, FF_SUMMED),
            Total.shape(QKV_KEPT, 0),
        ),
        in_specs=[ANY] * 22,
        out_specs=(IN_VMEM, IN_VMEM, ANY, ANY),
        scratch_shapes=[
            pltpu.VMEM((40, 128), F32),
            pltpu.VMEM((CHUNK, D), F32),
            pltpu.VMEM((4, CHUNK, D), BF),
            pltpu.VMEM((96, PADDED), BF),
            pltpu.VMEM((96, D), BF),
            pltpu.VMEM((CHUNK, D), F32),
            pltpu.VMEM((CHUNK, D), BF),
            pltpu.VMEM((16, group), BF),
            pltpu.VMEM((2 * CHUNK, group), BF),
            pltpu.VMEM((D // 2, D), BF),
            pltpu.VMEM((CHUNKS, CHUNK, 2 * HEAD), BF),
            pltpu.VMEM((2 * CHUNK, group), BF),
            pltpu.VMEM((2, 8, ROWS), jnp.int32),
            pltpu.VMEM((2, 8, ROWS), F32),
            pltpu.VMEM((2, D, 512), BF),
            pltpu.VMEM((2 * CHUNK, D), BF),
            pltpu.VMEM((2 * CHUNK, D), BF),
            pltpu.VMEM((48, 1024), BF),
            pltpu.VMEM((2 * CHUNK, HEAD), F32),
            pltpu.VMEM((2 * CHUNK, HEAD), F32),
            pltpu.VMEM((3, 16, D), BF),
            pltpu.VMEM((16, D), BF),
            pltpu.VMEM((CHUNKS * CHUNK, 2 * HEAD), F32),
            pltpu.VMEM((2, HEAD, ROWS), F32),
            pltpu.VMEM((2, 2, 4, 4, CHUNK, 2 * HEAD), BF),
            pltpu.VMEM((2 * CHUNK, group), F32),
            pltpu.VMEM((2 * CHUNK, group), BF),
            pltpu.VMEM((2 * CHUNK, D), BF),
            pltpu.VMEM((CHUNK, D), F32),
            pltpu.VMEM((2 * CHUNK, 1024), BF),
            pltpu.VMEM((CHUNK, D), BF),
            pltpu.VMEM((CHUNK, D), BF),
            pltpu.VMEM((2, CHUNK, D), BF),
            pltpu.VMEM((2, 2, CHUNK // 2, D), BF),
            pltpu.VMEM((2, 2, HEAD, ROWS), BF),
            pltpu.VMEM((2, 2, ROWS, HEAD), BF),
            pltpu.VMEM((2, 8, ROWS), F32),
            pltpu.VMEM((2, CHUNK, D), F32),
            dma((22,)), dma((4,)), dma((2, 2)), dma((2, 2)),
        ]
        + RingSum.scratch()
        + Shed.scratch((DKV_ROWS, 2 * HEAD)) * (2 * DKV_STREAMS)
        + Total.scratch(FF_KEPT, FF_SUMMED)
        + Total.scratch(QKV_KEPT, 0),
        compiler_params=pltpu.CompilerParams(
            collective_id=2, has_side_effects=True, vmem_limit_bytes=60 * 2**20
        ),
        name="backward",
    )(*args)


def fold_kernel(
    set_ref, result_in, grad_in, ff_hbm, qkv_hbm, result_ref, input_grad_ref, a_wide, a_down, b_wide, b_kv, b_ff,
    ff_ref, qkv_ref, sems,
):
    c = pl.program_id(0)
    share = [jnp.where(set_ref[s] == c, 1.0, 0.0) for s in (0, 1)]

    @pl.when(c == 0)
    def _():
        copies = [
            pltpu.make_async_copy(src, dst, sems.at[n])
            for n, (src, dst) in enumerate(((ff_hbm, ff_ref), (qkv_hbm, qkv_ref)))
        ]
        for copy in copies:
            copy.start()
        result_ref[...] = result_in[...]
        input_grad_ref[...] = grad_in[...].astype(F32)
        for copy in copies:
            copy.wait()

    chosen = jnp.logical_or(set_ref[0] == c, set_ref[1] == c)

    @pl.when(jnp.logical_not(chosen))
    def _():
        for ref in (a_wide, a_down, b_wide, b_kv, b_ff):
            ref[...] = jnp.zeros_like(ref)

    @pl.when(chosen)
    def _():
        fold_set(share, ff_ref, qkv_ref, a_wide, a_down, b_wide, b_kv, b_ff)


def fold_set(share, ff_ref, qkv_ref, a_wide, a_down, b_wide, b_kv, b_ff):
    def kept(ref, per, n, u):
        item = n // per
        return ref[item // 32, item // 16 % 2, item // 4 % 4, item % 4, u * per + n % per].astype(F32)

    def ff_kept(n, u):
        return kept(ff_ref, FF_KEPT, n, u)

    def qkv_kept(n, u):
        return kept(qkv_ref, QKV_KEPT, n, u)

    def summed(n):
        item = n // FF_SUMMED
        return ff_ref[
            item // 32, item // 16 % 2, item // 4 % 4, item % 4, 4 * FF_KEPT + n % FF_SUMMED
        ].astype(F32)

    def put(ref, at, tile, value):
        ref[at + (slice(None), slice(tile * 128, (tile + 1) * 128))] = (
            share[0] * value(0) + share[1] * value(1)
        )

    for n in range(3):
        for t in range(D_TILES):
            put(a_wide, (n, 0), t, lambda s: qkv_kept(n * D_TILES + t, s) + qkv_kept(n * D_TILES + t, 2 + s))
    half = D_TILES // 2
    at_o = 3 * D_TILES + half + 2
    for t in range(D_TILES):
        h, part = t // half, t % half
        put(a_wide, (3, 0), t, lambda s: qkv_kept(at_o + part, 2 * h + s))
        put(b_wide, (0, 0), t, lambda s: qkv_kept(3 * D_TILES + part, 2 * h + s))
        put(
            b_wide, (1, 0), t,
            lambda s: qkv_kept(at_o + half + t, s) + qkv_kept(at_o + half + t, 2 + s),
        )
        for n, (ref, at) in enumerate(((a_wide, (4, 0)), (a_wide, (5, 0)), (b_wide, (2, 0)))):
            put(ref, at, t, lambda s: summed((2 * n + s) * D_TILES + t))
    for n in (0, 1):
        for h in (0, 1):
            put(b_kv, (n, 0), h, lambda s: qkv_kept(3 * D_TILES + half + n, 2 * h + s))
    for n, (ref, at) in enumerate(((a_down, (0,)), (b_ff, (0, 0)), (b_ff, (1, 0)))):
        for t in range(FF // 128):
            where = [
                (u, t - start) for u, start in enumerate((0, 17, 35, 52)) if 0 <= t - start < COL_TILES
            ]
            put(
                ref, at, t,
                lambda s: sum(ff_kept((2 * n + s) * COL_TILES + tile, u) for u, tile in where),
            )


def fold(set_index, result, input_grad, ff_all, qkv_all):
    rows = pl.BlockSpec(result.shape, lambda c: (0, 0, 0))

    def by_set(lead, columns):
        shape = lead + (1, 16, columns)
        return pl.BlockSpec(shape, lambda c: (0,) * len(lead) + (c, 0, 0))

    def out(lead, columns):
        return jax.ShapeDtypeStruct(lead + (SETS, 16, columns), F32)

    outs = (((6,), D), ((), FF), ((3,), D), ((2,), 2 * HEAD), ((2,), FF))
    return pl.pallas_call(
        fold_kernel,
        grid=(SETS,),
        out_shape=(
            jax.ShapeDtypeStruct(result.shape, BF),
            jax.ShapeDtypeStruct(result.shape, F32),
        )
        + tuple(out(*o) for o in outs),
        in_specs=[pl.BlockSpec(memory_space=pltpu.SMEM), rows, rows, ANY, ANY],
        out_specs=(rows, rows) + tuple(by_set(*o) for o in outs),
        scratch_shapes=[
            pltpu.VMEM(ff_all.shape, BF), pltpu.VMEM(qkv_all.shape, BF), pltpu.SemaphoreType.DMA((2,))
        ],
        compiler_params=pltpu.CompilerParams(vmem_limit_bytes=40 * 2**20),
        name="fold",
    )(set_index, result, input_grad, ff_all, qkv_all)


def norm_scale(hidden):
    return lax.rsqrt(jnp.mean(hidden * hidden, axis=-1, keepdims=True) + EPS)


def norm_back(hidden, scaled, gain_vec, upstream):
    normed = hidden * scaled
    weighted = upstream * gain_vec
    return scaled * (weighted - normed * jnp.mean(weighted * normed, axis=-1, keepdims=True))


def held(*arrays):
    return [pltpu.with_memory_space_constraint(v, pltpu.HBM) for v in arrays]


def body(
    tokens, cotangent, lengths, set_index, norm_in, norm_ff, qkv_bias, w_qkv, w_out, w_gate_up, w_down,
    a_wide, a_down, b_wide, b_kv, b_ff,
):
    frequencies = np.float64(THETA) ** (-np.arange(0, HEAD, 2, dtype=np.float64) / HEAD)
    frequencies = jnp.asarray(np.concatenate([frequencies, frequencies])[None].astype(np.float32))
    gains = jnp.concatenate([norm_in, norm_ff, qkv_bias]).reshape(40, 128)
    (
        q, mixed, lse, kv_all, qkv_w, out_w, gate_w, up_w, down_w, rows, normed, residual, grad_out,
        normed_ff, grad_gathered, limit, cos_table, sine_table, b_qkv, ao, a_own, bo,
    ) = forward(
        *held(
            tokens, cotangent, lengths, set_index, w_qkv, w_out, w_gate_up, w_down.T, gains, frequencies,
            a_wide, b_wide, b_kv,
        )
    )
    gate_w, down_w = (w.reshape(D, FF_COLS) for w in (gate_w, down_w))
    grad_normed_ff, down_sum, cols, ff_wide = feed_forward(
        set_index, normed_ff, grad_gathered, gate_w, up_w, down_w, *held(a_wide, a_down, b_wide, b_ff)
    )
    result, input_grad, ff_all, qkv_all = backward(
        gains,
        grad_normed_ff, down_sum, cols, ff_wide, residual, grad_out, ao, mixed, out_w, kv_all, q, limit, lse,
        qkv_w, rows, normed, b_qkv, cos_table, sine_table, a_own, bo,
    )
    return tuple(fold(set_index, *held(result, input_grad, ff_all, qkv_all)))


def solution(mesh):
    spread = P(None, ("blk", "uly"), None)
    in_specs = (
        spread, spread, P(), P(), P(), P(), P(),
        P(("blk", "uly"), None), P(("blk", "uly"), None), P(None, "blk", "uly"), P("uly", "blk"),
        P(), P(), P(), P(), P(),
    )
    out_specs = (spread, spread, P(), P(), P(), P(), P())
    return jax.shard_map(body, mesh=mesh, in_specs=in_specs, out_specs=out_specs, check_vma=False)
```
